32 devices in a mesh: batch: 8 (over y, x, core), head: 4 (over z).
Axes of the slice: x: 2, y: 2, z: 4, core: 2. Of those that a mesh axis runs over, the one named last changes fastest.
Arguments:
- tokens: bfloat16 [16384, 768], P('batch'), may hold values from -6 to 6
- segment_ids: int32 [16384], P('batch'), may hold values from -1 to 3, as said below
- w_qkv: bfloat16 [3, 768, 768], P(None, None, 'head'), may hold values from -0.21875 to 0.21875
- b_qv: float32 [2, 768], P(None, 'head'), may hold values from -0.6 to 0.6
- w_out: bfloat16 [768, 768], P('head'), may hold values from -1.25 to 1.25
- b_out: float32 [768], replicated, may hold values from -1.8 to 1.8
- ln1_gain: float32 [768], replicated, may hold values from 0.5 to 1.5
- ln1_bias: float32 [768], replicated, may hold values from -1.8 to 1.8
- w_up: bfloat16 [768, 3072], replicated, may hold values from -0.21875 to 0.21875
- b_up: float32 [3072], replicated, may hold values from -3 to 3
- w_down: bfloat16 [3072, 768], replicated, may hold values from -0.109375 to 0.109375
- b_down: float32 [768], replicated, may hold values from -1.8 to 1.8
- ln2_gain: float32 [768], replicated, may hold values from 0.5 to 1.5
- ln2_bias: float32 [768], replicated, may hold values from -1.8 to 1.8
- cotangent: bfloat16 [16384, 768], P(('batch', 'head')), may hold values from -6 to 6
Outputs:
- layer_output: bfloat16 [16384, 768], P(('batch', 'head'))
- input_grad: float32 [16384, 768], P(('batch', 'head'))
- grad_qkv: float32 [3, 768, 768], P(None, None, 'head')
- grad_qv_bias: float32 [2, 768], P(None, 'head')
- grad_out: float32 [768, 768], P('head')
- grad_up: float32 [768, 3072], P(None, 'head')
- grad_up_bias: float32 [3072], P('head')
- grad_down: float32 [3072, 768], P('head')
- grad_small: float32 [6, 768], replicated
The draws below stay inside these ranges and needn't reach their ends.
Inputs may be any that keep to these rules, and one draw needn't show every extreme that they name: `segment_ids`: within each slot of 512 tokens the ids never fall along the live tokens, which come first; -1 marks the padding at the end of every slot; documents never cross slots.
All inputs are finite; a program needn't handle non-finite values.
Results may differ from the reference program's by a relative error of at most 0.015.
The reference program's roundings to bfloat16 on the way count: a program that leaves them out, or rounds other values in their place, can miss the bound.
Values may be sent and summed in bfloat16 or wider, within the bound.
No kernel may reach another device: no remote copies, remote signals or barrier semaphores. Data moves between devices by JAX's collectives and lax.ppermute only.
A program may use at most 192 MiB of HBM per device.

```python
import jax
import jax.numpy as jnp
from jax import lax

HEADS = 12
HEAD_DIM = 64
D = 768
FF = 3072
SLOT = 512
TOKENS = 16384


def draw_segment_ids(key, part):
    key = jax.random.fold_in(key, 7)
    slot_count = TOKENS // SLOT
    pad_key, cut_key = jax.random.split(key)
    padding = jax.random.randint(pad_key, (slot_count, 1), 1, SLOT // 4 + 1)
    live = SLOT - padding
    cuts = jax.random.randint(cut_key, (slot_count, 3), 1, live)
    places = jnp.arange(SLOT, dtype=jnp.int32)[None, :]
    counted = jnp.sum((places[:, :, None] >= cuts[:, None, :]).astype(jnp.int32), -1)
    ids = jnp.where(places < live, counted, -1)
    return ids.reshape(-1).astype(jnp.int32)


def level_of(stream_key, extent, cuts, least, high):
    loudness, own = 1.0, jax.random.fold_in(stream_key, 6)
    for position, shards_of in cuts:
        steps = jnp.exp(jax.random.uniform(jax.random.fold_in(own, position), (shards_of,), jnp.float32, least / len(cuts), high / len(cuts)))
        loudness = loudness * jnp.repeat(steps, extent[position] // shards_of).reshape([-1 if axis == position else 1 for axis in range(len(extent))])
    return loudness


def scatter_about(key, dims, spread, limit, pieces=(), kind=jnp.bfloat16):
    drawn = spread * jax.random.normal(key, dims, jnp.float32)
    if pieces:
        drawn = drawn * level_of(key, dims, pieces, -0.22, 0.18)
    return jnp.clip(drawn, -limit, limit).astype(kind)


def setup_inputs(seed: int = 0) -> dict:
    arg_keys = jax.random.split(jax.random.key(seed), 16)
    return {
        "tokens": scatter_about(arg_keys[0], (TOKENS, D), 1.0, 6.0, ((0, 8),)),
        "segment_ids": draw_segment_ids(jax.random.fold_in(arg_keys[15], 71), 0),
        "w_qkv": scatter_about(arg_keys[2], (3, D, D), D ** -0.5, 0.21875, ((2, 4),)),
        "b_qv": scatter_about(arg_keys[3], (2, D), 0.1, 0.6, ((1, 4),), jnp.float32),
        "w_out": scatter_about(arg_keys[4], (D, D), (D // 32) ** -0.5, 1.25, ((0, 4),)),
        "b_out": scatter_about(arg_keys[5], (D,), 0.3, 1.8, (), jnp.float32),
        "ln1_gain": jnp.clip(1.0 + 0.1 * jax.random.normal(arg_keys[6], (D,), jnp.float32), 0.5, 1.5),
        "ln1_bias": scatter_about(arg_keys[7], (D,), 0.3, 1.8, (), jnp.float32),
        "w_up": scatter_about(arg_keys[8], (D, FF), D ** -0.5, 0.21875),
        "b_up": scatter_about(arg_keys[9], (FF,), 0.5, 3.0, (), jnp.float32),
        "w_down": scatter_about(arg_keys[10], (FF, D), FF ** -0.5, 0.109375),
        "b_down": scatter_about(arg_keys[11], (D,), 0.3, 1.8, (), jnp.float32),
        "ln2_gain": jnp.clip(1.0 + 0.1 * jax.random.normal(arg_keys[12], (D,), jnp.float32), 0.5, 1.5),
        "ln2_bias": scatter_about(arg_keys[13], (D,), 0.3, 1.8, (), jnp.float32),
        "cotangent": scatter_about(arg_keys[14], (TOKENS, D), 1.0, 6.0, ((0, 32),)),
    }


@jax.custom_vjp
def low(v):
    return lax.optimization_barrier(v.astype(jnp.bfloat16)).astype(jnp.float32)

@jax.custom_vjp
def low_back(v):
    return v

def low_keep(v):
    return (low(v), None)

def low_pass(kept, grad):
    return (grad,)

def back_keep(v):
    return (v, None)

def back_low(kept, grad):
    return (low(grad),)
low.defvjp(low_keep, low_pass)
low_back.defvjp(back_keep, back_low)

def layer_norm(values, gain, offset):
    centred = values - lax.optimization_barrier(jnp.mean(values, -1, keepdims=True))
    inv_std = lax.rsqrt(lax.optimization_barrier(jnp.mean(centred * centred, -1, keepdims=True)) + 1e-05)
    return centred * inv_std * gain + offset

def forward(inputs, seg_row, w_qkv, b_qv, w_out, b_out, ln1_gain, ln1_bias, w_up, b_up, w_down, b_down, ln2_gain, ln2_bias):
    highest = lax.Precision.HIGHEST
    row_count = inputs.shape[0]
    queries = jnp.dot(inputs, w_qkv[0], precision=highest) + b_qv[0]
    key_rows = jnp.dot(inputs, w_qkv[1], precision=highest)
    value_rows = jnp.dot(inputs, w_qkv[2], precision=highest) + b_qv[1]
    queries = low_back(low(queries)).reshape(row_count, HEADS, HEAD_DIM)
    key_rows = low_back(low(key_rows)).reshape(row_count, HEADS, HEAD_DIM)
    value_rows = low_back(low(value_rows)).reshape(row_count, HEADS, HEAD_DIM)
    raw_scores = jnp.einsum('qhd,khd->hqk', queries, key_rows, precision=highest)
    scores = low_back(raw_scores) * HEAD_DIM ** (-0.5)
    visible = seg_row[:, None] == seg_row[None, :]
    scores = jnp.where(visible[None], scores, -1e+30)
    row_max = lax.optimization_barrier(jnp.max(scores, -1, keepdims=True))
    exponent = jnp.exp(scores - row_max)
    attend = exponent / lax.optimization_barrier(jnp.sum(exponent, -1, keepdims=True))
    mixed = jnp.einsum('hqk,khd->qhd', low(attend), value_rows, precision=highest).reshape(row_count, HEADS * HEAD_DIM)
    mixed = low_back(low(mixed))
    attended = low_back(jnp.dot(mixed, w_out, precision=highest) + b_out)
    hidden_one = layer_norm(inputs + attended, ln1_gain, ln1_bias)
    inner_pre = low_back(jnp.dot(low(hidden_one), w_up, precision=highest) + b_up)
    activated = jax.nn.gelu(inner_pre, approximate=False)
    branch = low_back(jnp.dot(low(activated), w_down, precision=highest) + b_down)
    return layer_norm(hidden_one + branch, ln2_gain, ln2_bias)

def reference(tokens, segment_ids, w_qkv, b_qv, w_out, b_out, ln1_gain, ln1_bias, w_up, b_up, w_down, b_down, ln2_gain, ln2_bias, cotangent):
    params = (w_qkv.astype(jnp.float32), b_qv, w_out.astype(jnp.float32), b_out, ln1_gain, ln1_bias, w_up.astype(jnp.float32), b_up, w_down.astype(jnp.float32), b_down, ln2_gain, ln2_bias)
    width = tokens.shape[1]
    slot_inputs = tokens.astype(jnp.float32).reshape(-1, SLOT, width)
    slot_segs = segment_ids.reshape(-1, SLOT)
    slot_cots = cotangent.astype(jnp.float32).reshape(-1, SLOT, width)

    def one_slot(totals, item):
        inputs, seg_row, upstream = item
        result, pull = jax.vjp(lambda xin, prm: forward(xin, seg_row, *prm), inputs, params)
        grad_in, grad_params = pull(upstream)
        totals = jax.tree.map(jnp.add, totals, grad_params)
        return (totals, (result.astype(jnp.bfloat16), grad_in))
    zeros = jax.tree.map(jnp.zeros_like, params)
    totals, (results, grad_inputs) = lax.scan(one_slot, zeros, (slot_inputs, slot_segs, slot_cots))
    layer_output = results.reshape(-1, width)
    input_grad = grad_inputs.reshape(-1, width)
    grad_small = jnp.stack([totals[3], totals[4], totals[5], totals[9], totals[10], totals[11]])
    return (layer_output, input_grad, totals[0], totals[1], totals[2], totals[6], totals[7], totals[8], grad_small)
```

```python
import jax
import jax.numpy as jnp
from jax import lax
from jax.sharding import PartitionSpec as P

HEAD_DIM = 64
SLOT = 512
LOW = jnp.bfloat16
F32 = jnp.float32


def normalize(values, gain, offset):
    centred = values - jnp.mean(values, -1, keepdims=True)
    inv_std = lax.rsqrt(jnp.mean(centred * centred, -1, keepdims=True) + 1e-05)
    unit_rows = centred * inv_std
    return (unit_rows * gain + offset, unit_rows, inv_std)


def norm_back(upstream, unit_rows, inv_std, gain):
    scaled = upstream * gain
    inner = jnp.mean(scaled * unit_rows, -1, keepdims=True)
    return inv_std * (scaled - jnp.mean(scaled, -1, keepdims=True) - unit_rows * inner)


def gelu_slope(inputs):
    cumul = 0.5 * (1.0 + lax.erf(inputs * 0.7071067811865476))
    density = jnp.exp(-0.5 * inputs * inputs) * 0.3989422804014327
    return cumul + inputs * density


def swap_batch(value, bit):
    size = lax.axis_size("batch")
    return lax.ppermute(value, "batch", [(i, i ^ bit) for i in range(size)])


def swap_head(value, bit):
    size = lax.axis_size("head")
    return lax.ppermute(value, "head", [(i, i ^ bit) for i in range(size)])


def shift_head(value, distance):
    size = lax.axis_size("head")
    return lax.ppermute(value, "head", [(i, (i + distance) % size) for i in range(size)])


def chip_bits(flip):
    size = lax.axis_size("batch")
    bits = []
    bit = 2
    while bit < size:
        bits.append(bit)
        bit *= 2
    return bits[::-1] if flip else bits


def gather_chips(piece, flip):
    bits = chip_bits(flip)
    rank = len(bits)
    mine = lax.axis_index("batch")
    held = piece.reshape((1,) * rank + piece.shape)
    for bit in bits:
        axis = rank - bit.bit_length() + 1
        other = swap_batch(held, bit)
        high = (mine & bit) != 0
        first = jnp.where(high, other, held)
        second = jnp.where(high, held, other)
        held = jnp.concatenate([first, second], axis)
    return held.reshape((-1,) + piece.shape)


def gather_cores(piece):
    other = swap_batch(piece, 1)
    high = (lax.axis_index("batch") & 1) != 0
    return jnp.stack([jnp.where(high, other, piece), jnp.where(high, piece, other)])


def reduce_unit(unit, flip):
    heads, rows, columns = unit.shape
    bits = chip_bits(flip)
    rank = len(bits)
    mine = lax.axis_index("batch")
    part = rows >> rank
    held = unit.reshape((heads,) + (2,) * rank + (part, columns))
    for bit in bits:
        axis = rank - bit.bit_length() + 2
        high = jnp.where((mine & bit) != 0, 1, 0)
        keep = lax.dynamic_slice_in_dim(held, high, 1, axis)
        send = lax.dynamic_slice_in_dim(held, 1 - high, 1, axis)
        held = (keep.astype(F32) + swap_batch(send, bit).astype(F32)).astype(LOW)
    held = held.reshape(heads, part, columns)
    z = lax.axis_index("head")
    total = lax.dynamic_index_in_dim(held, z, 0, False).astype(F32)
    for distance in range(1, heads):
        send = lax.dynamic_index_in_dim(held, (z + distance) % heads, 0, False)
        total = total + shift_head(send, distance).astype(F32)
    whole = gather_chips(total.astype(LOW), flip)
    return whole.reshape(rows, columns)


def sum_small(rows):
    bit = 1
    while bit < lax.axis_size("batch"):
        rows = rows + swap_batch(rows, bit)
        bit *= 2
    bit = 1
    while bit < lax.axis_size("head"):
        rows = rows + swap_head(rows, bit)
        bit *= 2
    return rows


def slot_scores(queries, key_rows, seg_row):
    raw_scores = jnp.einsum("qhd,khd->hqk", queries, key_rows, preferred_element_type=F32)
    visible = seg_row[:, None] == seg_row[None, :]
    return jnp.where(visible[None], raw_scores * HEAD_DIM ** (-0.5), -1e30)


def per_device(
    tokens,
    segment_ids,
    w_qkv,
    b_qv,
    w_out,
    b_out,
    ln1_gain,
    ln1_bias,
    w_up,
    b_up,
    w_down,
    b_down,
    ln2_gain,
    ln2_bias,
    cotangent,
):
    width = tokens.shape[1]
    own_rows = cotangent.shape[0]
    local_width = w_qkv.shape[2]
    heads_axis = lax.axis_size("head")
    batch_axis = lax.axis_size("batch")
    b = lax.axis_index("batch")
    z = lax.axis_index("head")
    core = b & 1
    scale = HEAD_DIM ** (-0.5)
    hidden_units = w_up.shape[1]
    chunk = hidden_units // heads_axis // 2
    half = width // 2

    shard = jnp.concatenate([w_qkv.transpose(0, 2, 1).reshape(-1, width), w_out], 0)
    shard_rows = shard.shape[0]
    piece_rows = shard_rows // batch_axis
    piece = lax.dynamic_slice_in_dim(shard, b * piece_rows, piece_rows, 0)
    arrived = jnp.stack([shift_head(piece, d) for d in range(1, heads_axis)])
    arrived = arrived.reshape(heads_axis - 1, 2, piece_rows // 2, width)
    spread = [gather_chips(arrived[:, side], side == 1) for side in range(2)]
    spread = gather_cores(jnp.stack(spread))
    spread = spread.transpose(3, 2, 0, 1, 4, 5).reshape(heads_axis - 1, shard_rows, width)
    shards = jnp.concatenate([shard[None], spread], 0)
    order = (z - jnp.arange(heads_axis)) % heads_axis
    weights = jnp.take(shards, order, axis=0)
    wqkv_t = weights[:, : 3 * local_width].reshape(heads_axis, 3, local_width, width)
    wqkv_t = wqkv_t.transpose(1, 0, 2, 3).reshape(3, width, width)
    wout = weights[:, 3 * local_width :].reshape(width, width)
    biases = jnp.concatenate([b_qv[0], b_qv[1]])[None]
    bias_all = jnp.concatenate([biases] + [shift_head(biases, d) for d in range(1, heads_axis)])
    bias_all = jnp.take(bias_all, order, axis=0).reshape(heads_axis, 2, local_width)
    bias_all = bias_all.transpose(1, 0, 2).reshape(2, width)

    own_tokens = lax.dynamic_slice_in_dim(tokens, z * own_rows, own_rows, 0)
    seg_row = lax.dynamic_slice_in_dim(segment_ids, z * own_rows, own_rows, 0)

    projected = jnp.einsum("td,ced->cte", own_tokens, wqkv_t, preferred_element_type=F32)
    bias_rows = jnp.stack([bias_all[0], jnp.zeros_like(bias_all[0]), bias_all[1]])
    qkv_low = (projected + bias_rows[:, None, :]).astype(LOW)
    heads_view = qkv_low.reshape(3, own_rows, -1, HEAD_DIM)
    queries, key_rows, value_rows = heads_view[0], heads_view[1], heads_view[2]
    scores = slot_scores(queries, key_rows, seg_row)
    row_max = jnp.max(scores, -1, keepdims=True)
    exponent = jnp.exp(scores - row_max)
    row_total = jnp.sum(exponent, -1, keepdims=True)
    attend = (exponent / row_total).astype(LOW)
    mixed = jnp.einsum("hqk,khd->qhd", attend, value_rows, preferred_element_type=F32)
    mixed = mixed.astype(LOW).reshape(own_rows, width)
    log_total = row_max[..., 0] + jnp.log(row_total[..., 0])
    attended = jnp.dot(mixed, wout, preferred_element_type=F32) + b_out

    hidden_one, unit_one, inv_one = normalize(own_tokens.astype(F32) + attended, ln1_gain, ln1_bias)
    hidden_low = hidden_one.astype(LOW)
    inner_pre = jnp.dot(hidden_low, w_up, preferred_element_type=F32) + b_up
    activated = jax.nn.gelu(inner_pre, approximate=False).astype(LOW)
    branch = jnp.dot(activated, w_down, preferred_element_type=F32) + b_down
    normed, unit_two, inv_two = normalize(hidden_one + branch, ln2_gain, ln2_bias)
    layer_output = normed.astype(LOW)
    upstream = cotangent.astype(F32)
    grad_res_two = norm_back(upstream, unit_two, inv_two, ln2_gain)
    grad_branch = grad_res_two.astype(LOW)
    grad_act = jnp.einsum("td,fd->tf", grad_branch, w_down, preferred_element_type=F32)
    grad_inner = (grad_act * gelu_slope(inner_pre)).astype(LOW)
    grad_hidden = jnp.einsum("tf,df->td", grad_inner, w_up, preferred_element_type=F32) + grad_res_two
    grad_res_one = norm_back(grad_hidden, unit_one, inv_one, ln1_gain)
    grad_attended = grad_res_one.astype(LOW)

    def split_units(rows):
        view = rows.reshape(own_rows, heads_axis, 2, chunk)
        mine = lax.dynamic_index_in_dim(view, core, 2, False)
        other = lax.dynamic_index_in_dim(view, 1 - core, 2, False)
        return jnp.concatenate([mine, swap_batch(other, 1)], 0)

    def split_width(rows):
        mine = lax.dynamic_slice_in_dim(rows, core * half, half, 1)
        other = lax.dynamic_slice_in_dim(rows, (1 - core) * half, half, 1)
        return jnp.concatenate([mine, swap_batch(other, 1)], 0)

    def both(rows):
        return jnp.concatenate([rows, swap_batch(rows, 1)], 0)

    act_half = split_units(activated)
    down_unit = jnp.einsum(
        "thf,td->hfd", act_half, both(grad_branch), preferred_element_type=F32
    ).astype(LOW)
    inner_half = split_units(grad_inner)
    up_unit = jnp.einsum(
        "td,thf->hdf", both(hidden_low), inner_half, preferred_element_type=F32
    ).astype(LOW)
    down_sum = reduce_unit(down_unit, False)
    up_sum = reduce_unit(up_unit, True)

    small_terms = jnp.concatenate(
        [
            jnp.stack(
                [
                    jnp.sum(grad_attended.astype(F32), 0),
                    jnp.sum(grad_hidden * unit_one, 0),
                    jnp.sum(grad_hidden, 0),
                    jnp.sum(grad_branch.astype(F32), 0),
                    jnp.sum(upstream * unit_two, 0),
                    jnp.sum(upstream, 0),
                ]
            ),
            jnp.sum(grad_inner.astype(F32), 0).reshape(heads_axis, -1),
        ]
    )
    small_sum = sum_small(small_terms)
    grad_small = small_sum[:6]
    grad_up_bias = lax.dynamic_index_in_dim(small_sum[6:], z, 0, False)

    grad_mixed = jnp.einsum("td,ed->te", grad_attended, wout, preferred_element_type=F32).astype(LOW)
    grad_slot = grad_mixed.reshape(own_rows, -1, HEAD_DIM)
    scores = slot_scores(queries, key_rows, seg_row)
    weights_full = jnp.exp(scores - log_total[..., None])
    attend = weights_full.astype(LOW)
    grad_values = jnp.einsum("hqk,qhd->khd", attend, grad_slot, preferred_element_type=F32)
    grad_probs = jnp.einsum("qhd,khd->hqk", grad_slot, value_rows, preferred_element_type=F32)
    inner = jnp.sum(weights_full * grad_probs, -1, keepdims=True)
    grad_scores = (weights_full * (grad_probs - inner) * scale).astype(LOW)
    grad_queries = jnp.einsum("hqk,khd->qhd", grad_scores, key_rows, preferred_element_type=F32)
    grad_keys = jnp.einsum("hqk,qhd->khd", grad_scores, queries, preferred_element_type=F32)
    grad_rows = jnp.stack([grad_queries, grad_keys, grad_values]).astype(LOW)
    grad_rows = grad_rows.reshape(3, own_rows, width)

    rows_both = jnp.concatenate([grad_rows, swap_batch(grad_rows, 1)], 1)
    rows_both = rows_both.reshape(3, 2 * own_rows, heads_axis, local_width)
    qkv_unit = jnp.einsum(
        "cthe,td->hced", rows_both, split_width(own_tokens), preferred_element_type=F32
    ).astype(LOW)
    qkv_unit = qkv_unit.reshape(heads_axis, 3 * local_width, half)
    out_unit = jnp.einsum(
        "te,td->ed", both(mixed), split_width(grad_attended), preferred_element_type=F32
    ).astype(LOW)
    out_unit = out_unit.reshape(heads_axis, local_width, half)
    attn_unit = jnp.concatenate([qkv_unit, out_unit], 1)
    attn_sum = reduce_unit(attn_unit, False)

    column_sums = jnp.sum(grad_rows.astype(F32), 1)
    bias_sum = sum_small(jnp.stack([column_sums[0], column_sums[2]]))
    grad_qv_bias = lax.dynamic_slice_in_dim(bias_sum, z * local_width, local_width, 1)

    input_grad = (
        jnp.einsum("cte,ced->td", grad_rows, wqkv_t, preferred_element_type=F32) + grad_res_one
    )

    down_all = gather_cores(down_sum)
    grad_down = down_all.reshape(-1, width).astype(F32)
    up_all = gather_cores(up_sum)
    grad_up = up_all.transpose(1, 0, 2).reshape(width, -1).astype(F32)
    attn_all = gather_cores(attn_sum).transpose(1, 0, 2).reshape(-1, width).astype(F32)
    grad_qkv = attn_all[: 3 * local_width].reshape(3, local_width, width).transpose(0, 2, 1)
    grad_out = attn_all[3 * local_width :]
    return (
        layer_output,
        input_grad,
        grad_qkv,
        grad_qv_bias,
        grad_out,
        grad_up,
        grad_up_bias,
        grad_down,
        grad_small,
    )


def solution(mesh):
    in_specs = (
        P("batch", None),
        P("batch"),
        P(None, None, "head"),
        P(None, "head"),
        P("head", None),
        P(),
        P(),
        P(),
        P(),
        P(),
        P(),
        P(),
        P(),
        P(),
        P(("batch", "head"), None),
    )
    out_specs = (
        P(("batch", "head"), None),
        P(("batch", "head"), None),
        P(None, None, "head"),
        P(None, "head"),
        P("head", None),
        P(None, "head"),
        P("head"),
        P("head", None),
        P(),
    )
    return jax.shard_map(
        per_device, mesh=mesh, in_specs=in_specs, out_specs=out_specs, check_vma=False
    )
```

```python
import math

import jax
import jax.numpy as jnp
from jax import lax
from jax.experimental import pallas as pl
from jax.experimental.pallas import tpu as pltpu
from jax.sharding import PartitionSpec as P

HEAD_DIM = 64
SLOT = 512
LOW = jnp.bfloat16
F32 = jnp.float32
LOG2E = math.log2(math.e)
SCORE_SCALE = HEAD_DIM ** (-0.5) * LOG2E
VMEM_BYTES = 48 * 2**20


def swap_batch(value, bit):
    size = lax.axis_size("batch")
    return lax.ppermute(value, "batch", [(i, i ^ bit) for i in range(size)])


def swap_head(value, bit):
    size = lax.axis_size("head")
    return lax.ppermute(value, "head", [(i, i ^ bit) for i in range(size)])


def shift_head(value, distance):
    size = lax.axis_size("head")
    return lax.ppermute(value, "head", [(i, (i + distance) % size) for i in range(size)])


def upper_bits():
    bits = []
    bit = 8
    while bit < lax.axis_size("batch"):
        bits.append(bit)
        bit *= 2
    return bits


def spread_shard(piece):
    rows = piece.shape[0] // 2
    sides = []
    for side, bits in enumerate(((2, 4), (4, 2))):
        held = piece[side * rows : (side + 1) * rows][None]
        for bit in bits:
            held = jnp.concatenate([held, swap_batch(held, bit)], 0)
        sides.append(held)
    mine = jnp.stack(sides)
    return mine, swap_batch(mine, 1)


def reduce_unit(unit, bits):
    mine = lax.axis_index("batch")
    held = unit
    for bit in bits:
        half = held.shape[1] // 2
        high = jnp.where((mine & bit) != 0, 1, 0)
        keep = lax.dynamic_slice_in_dim(held, high * half, half, 1)
        send = lax.dynamic_slice_in_dim(held, (1 - high) * half, half, 1)
        held = (keep.astype(F32) + swap_batch(send, bit).astype(F32)).astype(LOW)
    for bit in upper_bits():
        held = (held.astype(F32) + swap_batch(held, bit).astype(F32)).astype(LOW)
    total = held[0].astype(F32)
    for distance in range(1, unit.shape[0]):
        total = total + shift_head(held[distance], -distance).astype(F32)
    held = total.astype(LOW)
    for bit in bits[::-1]:
        other = swap_batch(held, bit)
        high = (mine & bit) != 0
        held = jnp.concatenate([jnp.where(high, other, held), jnp.where(high, held, other)], 0)
    return held


def gather_cores(piece):
    other = swap_batch(piece, 1)
    high = (lax.axis_index("batch") & 1) != 0
    return jnp.stack([jnp.where(high, other, piece), jnp.where(high, piece, other)])


def sum_small(rows):
    for axis, swap in (("batch", swap_batch), ("head", swap_head)):
        bit = 1
        while bit < lax.axis_size(axis):
            rows = rows + swap(rows, bit)
            bit *= 2
    return rows


def dot(a, b):
    return jnp.dot(a, b, preferred_element_type=F32)


def dot_nt(a, b):
    return lax.dot_general(a, b, (((1,), (1,)), ((), ())), preferred_element_type=F32)


def dot_tn(a, b):
    return lax.dot_general(a, b, (((0,), (0,)), ((), ())), preferred_element_type=F32)


def whole(shape):
    return pl.BlockSpec(shape, lambda *args: (0,) * len(shape))


def run(kernel, places, grid, ins, outs, scratch=(), macs=0):
    moved = sum(a.size * a.dtype.itemsize for a, spec in ins)
    moved += sum(math.prod(shape) * jnp.dtype(kind).itemsize for shape, kind, spec in outs)
    return pl.pallas_call(
        kernel,
        grid_spec=pltpu.PrefetchScalarGridSpec(
            num_scalar_prefetch=1,
            grid=grid,
            in_specs=[spec for a, spec in ins],
            out_specs=[spec for shape, kind, spec in outs],
            scratch_shapes=list(scratch),
        ),
        out_shape=[jax.ShapeDtypeStruct(shape, kind) for shape, kind, spec in outs],
        compiler_params=pltpu.CompilerParams(vmem_limit_bytes=VMEM_BYTES),
        cost_estimate=pl.CostEstimate(flops=2 * macs, bytes_accessed=moved, transcendentals=0),
    )(places, *[a for a, spec in ins])


def mask_rows(seg_col, seg_row):
    return jnp.where(seg_col == seg_row, 0.0, -1e30)


def attend_heads(tok, w_rows, bias, seg_col, seg_row, qkv_ref, mix_ref, log_ref):
    qkv = (dot_nt(w_rows, tok) + bias).astype(LOW)
    qkv_ref[...] = qkv
    width = qkv.shape[0] // 3
    masked = mask_rows(seg_col, seg_row)
    for head in range(width // HEAD_DIM):
        q, k, v = (
            qkv[c * width + head * HEAD_DIM : c * width + (head + 1) * HEAD_DIM] for c in range(3)
        )
        scores = dot_tn(k, q) + masked
        top = jnp.max(scores, 0, keepdims=True)
        exponent = jnp.exp2((scores - top) * SCORE_SCALE)
        total = jnp.sum(exponent, 0, keepdims=True)
        attend = (exponent * (1.0 / total)).astype(LOW)
        mix_ref[head * HEAD_DIM : (head + 1) * HEAD_DIM] = dot(v, attend).astype(LOW)
        log_ref[head : head + 1] = top * SCORE_SCALE + jnp.log2(total)


def own_attention(places, tok, w, bias, seg_col, seg_row, qkv_ref, mix_ref, log_ref):
    attend_heads(
        tok[...], w[...], bias[...], seg_col[...], seg_row[...], qkv_ref, mix_ref, log_ref
    )


def far_attention(
    places, tok, mine, other, bias, seg_col, seg_row, qkv_ref, mix_ref, log_ref, w_ref
):
    place = places[0]
    core = place & 1
    rows = mine.shape[2]
    for which, held in enumerate((mine, other)):
        for side in range(2):
            for offset in range(4):
                near, far = offset & 1, offset >> 1
                flip = near + 2 * far if side == 0 else 2 * near + far
                owner = (((place >> 1) & 3) ^ flip) * 2 + (core ^ which)
                start = pl.multiple_of(owner * (2 * rows) + side * rows, rows)
                w_ref[pl.ds(start, rows)] = held[side, offset]
    attend_heads(
        tok[...],
        w_ref[: qkv_ref.shape[0]],
        bias[...],
        seg_col[...],
        seg_row[...],
        qkv_ref,
        mix_ref,
        log_ref,
    )


def norm_stats(v):
    centred = v - jnp.mean(v, -1, keepdims=True)
    inv = lax.rsqrt(jnp.mean(centred * centred, -1, keepdims=True) + 1e-05)
    return centred * inv, inv


def norm_back(upstream, unit, inv, gain):
    scaled = upstream * gain
    inner = jnp.mean(scaled * unit, -1, keepdims=True)
    return inv * (scaled - jnp.mean(scaled, -1, keepdims=True) - unit * inner)


def gelu_both(pre):
    cumul = 0.5 * (1.0 + lax.erf(pre * 0.7071067811865476))
    density = jnp.exp2(pre * pre * (-0.5 * LOG2E)) * 0.3989422804014327
    return (pre * cumul).astype(LOW), cumul + pre * density


def feed_forward(
    places, tok, mix0, mix1, mix2, mix3, w0, w1, w2, w3, b_out, gain1, shift1,
    w_up, b_up, w_down, b_down, gain2, shift2, cot,
    send, own, slope, unit1, inv1, res2, out, small,
    hidden, low, acc, branch,
):
    k = pl.program_id(0)
    half = send.shape[2]

    @pl.when(k == 0)
    def _():
        attended = b_out[...]
        for mix, w in ((mix0, w0), (mix1, w1), (mix2, w2), (mix3, w3)):
            attended = attended + dot_tn(mix[...], w[...])
        unit, inv = norm_stats(tok[...].astype(F32) + attended)
        unit1[...] = unit
        inv1[...] = inv
        one = unit * gain1[...] + shift1[...]
        hidden[...] = one
        low[...] = one.astype(LOW)
        acc[...] = jnp.zeros_like(acc)

    @pl.when(k < 8)
    def _():
        pre = dot(low[...], w_up[...]) + b_up[0]
        act, tilt = gelu_both(pre)
        slope[0] = tilt
        acc[...] += dot(act, w_down[...])

        @pl.when(k < 4)
        def _():
            send[0] = act

        @pl.when(k >= 4)
        def _():
            own[0] = act

    @pl.when(k == 4)
    def _():
        send[0] = low[:, :half]

    @pl.when(k == 5)
    def _():
        send[0] = low[:, half:]

    @pl.when(k == 8)
    def _():
        unit, inv = norm_stats(hidden[...] + (acc[...] + b_down[...]))
        out[...] = (unit * gain2[...] + shift2[...]).astype(LOW)
        upstream = cot[...].astype(F32)
        grad = norm_back(upstream, unit, inv, gain2[...])
        res2[...] = grad
        grad_low = grad.astype(LOW)
        branch[...] = grad_low
        send[0] = grad_low[:, :half]
        small[0:1] = jnp.sum(grad_low.astype(F32), 0, keepdims=True)
        small[1:2] = jnp.sum(upstream * unit, 0, keepdims=True)
        small[2:3] = jnp.sum(upstream, 0, keepdims=True)

    @pl.when(k == 9)
    def _():
        send[0] = branch[:, half:]


def feed_backward(
    places, left, right, w_down, slope, w_up, res2, unit1, inv1, gain1,
    send, own, bias, res1, low, small,
    branch, acc,
):
    k = pl.program_id(0)
    half = send.shape[2]

    @pl.when(k == 0)
    def _():
        branch[:, :half] = left[0]
        branch[:, half:] = right[0]
        acc[...] = jnp.zeros_like(acc)

    @pl.when(k < 8)
    def _():
        inner = (dot_nt(branch[...], w_down[...]) * slope[0]).astype(LOW)
        acc[...] += dot_nt(inner, w_up[...])
        bias[0] = jnp.sum(inner.astype(F32), 0, keepdims=True)

        @pl.when(k < 4)
        def _():
            send[0] = inner

        @pl.when(k >= 4)
        def _():
            own[0] = inner

    @pl.when(k == 8)
    def _():
        grad = acc[...] + res2[...]
        result = norm_back(grad, unit1[...], inv1[...], gain1[...])
        res1[...] = result
        result_low = result.astype(LOW)
        low[...] = result_low
        core = places[0] & 1
        send[0] = jnp.where(core == 0, result_low[:, half:], result_low[:, :half])
        small[0:1] = jnp.sum(result_low.astype(F32), 0, keepdims=True)
        small[1:2] = jnp.sum(grad * unit1[...], 0, keepdims=True)
        small[2:3] = jnp.sum(grad, 0, keepdims=True)


def attention_back(places, qkv, w_out, grad, log_ref, seg_col, seg_row, rows_ref, bias_ref):
    width = w_out.shape[0]
    grad_mixed = dot_nt(w_out[...], grad[...]).astype(LOW)
    masked = mask_rows(seg_col[...], seg_row[...])
    scale = HEAD_DIM ** (-0.5)
    for head in range(width // HEAD_DIM):
        places_of = [c * width + head * HEAD_DIM for c in range(3)]
        q, k, v = (qkv[at : at + HEAD_DIM] for at in places_of)
        g = grad_mixed[head * HEAD_DIM : (head + 1) * HEAD_DIM]
        scores = dot_tn(k, q) + masked
        attend = jnp.exp2(scores * SCORE_SCALE - log_ref[head : head + 1])
        attend_low = attend.astype(LOW)
        grad_v = dot_nt(g, attend_low)
        product = attend * dot_tn(v, g)
        inner = jnp.sum(product, 0, keepdims=True)
        grad_scores = (product - attend * inner).astype(LOW)
        grad_q = dot(k, grad_scores) * scale
        grad_k = dot_nt(q, grad_scores) * scale
        for at, value in zip(places_of, (grad_q, grad_k, grad_v)):
            rows_ref[at : at + HEAD_DIM] = value.astype(LOW)
    ones = jnp.ones((8, rows_ref.shape[1]), LOW)
    bias_ref[...] = dot_nt(ones, rows_ref[...])


def down_grad(places, act, act_far, left, right, left_far, right_far, out):
    half = left.shape[2]
    for side, near, far in ((0, left, left_far), (1, right, right_far)):
        total = dot_tn(act[0], near[0]) + dot_tn(act_far[0], far[0])
        out[0, :, side * half : (side + 1) * half] = total.astype(LOW)


def up_grad(places, inner, inner_far, left, right, left_far, right_far, out):
    half = left.shape[2]
    for side, near, far in ((0, left, left_far), (1, right, right_far)):
        total = dot_tn(near[0], inner[0]) + dot_tn(far[0], inner_far[0])
        out[0, side * half : (side + 1) * half] = total.astype(LOW)


def attn_grad(places, rows, rows_far, tok, tok_far, mix, mix_far, grad, grad_far, out):
    count = rows.shape[0]
    out[:count] = (dot(rows[...], tok[...]) + dot(rows_far[...], tok_far[...])).astype(LOW)
    out[count:] = (dot(mix[...], grad[...]) + dot(mix_far[...], grad_far[0])).astype(LOW)


def input_sum(places, r0, r1, r2, r3, w0, w1, w2, w3, res1, out):
    total = res1[...]
    for rows, w in ((r0, w0), (r1, w1), (r2, w2), (r3, w3)):
        total = total + dot_tn(rows[...], w[...])
    out[...] = total


def per_device(
    tokens,
    segment_ids,
    w_qkv,
    b_qv,
    w_out,
    b_out,
    ln1_gain,
    ln1_bias,
    w_up,
    b_up,
    w_down,
    b_down,
    ln2_gain,
    ln2_bias,
    cotangent,
):
    width = tokens.shape[1]
    own_rows = cotangent.shape[0]
    local_width = w_qkv.shape[2]
    heads_axis = lax.axis_size("head")
    b = lax.axis_index("batch")
    z = lax.axis_index("head")
    core = b & 1
    hidden_units = w_up.shape[1]
    chunk = hidden_units // heads_axis // 2
    half = width // 2
    rows3 = 3 * local_width
    places = jnp.stack([b, z]).astype(jnp.int32)

    shard = jnp.concatenate([w_qkv.transpose(0, 2, 1).reshape(rows3, width), w_out], 0)
    shard_rows = shard.shape[0]
    piece_rows = shard_rows // 8
    piece = lax.dynamic_slice_in_dim(shard, (b & 7) * piece_rows, piece_rows, 0)
    pieces = [shift_head(piece, d) for d in range(1, heads_axis)]
    biases = [b_qv] + [shift_head(b_qv, d) for d in range(1, heads_axis)]
    spread = [spread_shard(p) for p in pieces]
    seg = lax.dynamic_slice_in_dim(segment_ids, z * own_rows, own_rows, 0)
    seg_col, seg_row = seg[:, None], seg[None]
    own_tokens = (tokens, pl.BlockSpec((own_rows, width), lambda k, s: (s[1], 0)))

    shards, qkvs, mixes, logs = [shard], [], [], []
    macs = rows3 * width * own_rows + 6 * own_rows * own_rows * 256
    for d in range(heads_axis):
        bias = jnp.concatenate([biases[d][0], jnp.zeros_like(b_qv[0]), biases[d][1]])[:, None]
        common = [
            (bias, whole((rows3, 1))),
            (seg_col, whole((own_rows, 1))),
            (seg_row, whole((1, own_rows))),
        ]
        outs = [
            ((rows3, own_rows), LOW, whole((rows3, own_rows))),
            ((local_width, own_rows), LOW, whole((local_width, own_rows))),
            ((8, own_rows), F32, whole((8, own_rows))),
        ]
        if d == 0:
            ins = [own_tokens, (shard, whole((rows3, width)))] + common
            qkv, mix, log = run(own_attention, places, (1,), ins, outs, macs=macs)
        else:
            mine, other = spread[d - 1]
            ins = [own_tokens, (mine, whole(mine.shape)), (other, whole(other.shape))] + common
            outs.append(((shard_rows, width), LOW, whole((shard_rows, width))))
            qkv, mix, log, full = run(far_attention, places, (1,), ins, outs, macs=macs)
            shards.append(full)
        qkvs.append(qkv)
        mixes.append(mix)
        logs.append(log)

    tok_own = lax.dynamic_slice_in_dim(tokens, z * own_rows, own_rows, 0)
    tok_far = swap_batch(lax.dynamic_slice_in_dim(tok_own, (1 - core) * half, half, 1), 1)
    mixes_far = swap_batch(jnp.stack(mixes), 1)

    def chunk_id(k, s):
        step = jnp.minimum(k, 7)
        side = jnp.where(step < 4, 1 - (s[0] & 1), s[0] & 1)
        return 2 * ((s[1] + heads_axis - (step & 3)) % heads_axis) + side

    row = whole((1, width))
    up_block = (w_up, pl.BlockSpec((width, chunk), lambda k, s: (0, chunk_id(k, s))))
    down_block = (w_down, pl.BlockSpec((chunk, width), lambda k, s: (chunk_id(k, s), 0)))
    out_rows = pl.BlockSpec((local_width, width), lambda k, s: (3, 0))
    tile = (1, own_rows, chunk)

    def at(index):
        return pl.BlockSpec(tile, lambda *args: (index, 0, 0))

    square = (own_rows, width)
    ins = [own_tokens]
    ins += [(m, whole(m.shape)) for m in mixes]
    ins += [(w, out_rows) for w in shards]
    ins += [(b_out[None], row), (ln1_gain[None], row), (ln1_bias[None], row)]
    ins += [up_block]
    ins += [
        (
            b_up.reshape(2 * heads_axis, 1, chunk),
            pl.BlockSpec((1, 1, chunk), lambda k, s: (chunk_id(k, s), 0, 0)),
        )
    ]
    ins += [down_block]
    ins += [(b_down[None], row), (ln2_gain[None], row), (ln2_bias[None], row)]
    ins += [(cotangent, whole(square))]

    def send_at(k, s):
        return (jnp.where(k < 6, k, jnp.maximum(k - 2, 5)), 0, 0)

    def own_at(k, s):
        return (jnp.clip(k - 4, 0, 3), 0, 0)

    outs = [
        ((8, own_rows, chunk), LOW, pl.BlockSpec(tile, send_at)),
        ((4, own_rows, chunk), LOW, pl.BlockSpec(tile, own_at)),
        ((8, own_rows, chunk), F32, pl.BlockSpec(tile, lambda k, s: (jnp.minimum(k, 7), 0, 0))),
        (square, F32, whole(square)),
        ((own_rows, 1), F32, whole((own_rows, 1))),
        (square, F32, whole(square)),
        (square, LOW, whole(square)),
        ((8, width), F32, whole((8, width))),
    ]
    scratch = [
        pltpu.VMEM(square, F32),
        pltpu.VMEM(square, LOW),
        pltpu.VMEM(square, F32),
        pltpu.VMEM(square, LOW),
    ]
    ffn_macs = 2 * own_rows * width * hidden_units
    sent, act_own, slope, unit1, inv1, res2, layer_output, small_two = run(
        feed_forward, places, (10,), ins, outs, scratch, ffn_macs
    )
    came = swap_batch(sent, 1)

    ins = [
        (sent, at(6)),
        (sent, at(7)),
        down_block,
        (slope, pl.BlockSpec(tile, lambda k, s: (jnp.minimum(k, 7), 0, 0))),
        up_block,
        (res2, whole(square)),
        (unit1, whole(square)),
        (inv1, whole((own_rows, 1))),
        (ln1_gain[None], row),
    ]
    outs = [
        ((5, own_rows, chunk), LOW, pl.BlockSpec(tile, lambda k, s: (jnp.where(k < 8, jnp.minimum(k, 3), 4), 0, 0))),
        ((4, own_rows, chunk), LOW, pl.BlockSpec(tile, own_at)),
        ((2 * heads_axis, 1, chunk), F32, pl.BlockSpec((1, 1, chunk), lambda k, s: (chunk_id(k, s), 0, 0))),
        (square, F32, whole(square)),
        (square, LOW, whole(square)),
        ((8, width), F32, whole((8, width))),
    ]
    scratch = [pltpu.VMEM(square, LOW), pltpu.VMEM(square, F32)]
    sent_back, inner_own, up_bias, res1, grad_attended, small_one = run(
        feed_backward, places, (9,), ins, outs, scratch, ffn_macs
    )
    came_back = swap_batch(sent_back, 1)

    def by_distance(k, s):
        return (k, 0, 0)

    ins = [(act_own, pl.BlockSpec(tile, by_distance)), (came, pl.BlockSpec(tile, by_distance))]
    ins += [(sent, at(6)), (sent, at(7)), (came, at(6)), (came, at(7))]
    outs = [((4, chunk, width), LOW, pl.BlockSpec((1, chunk, width), by_distance))]
    (down_unit,) = run(down_grad, places, (4,), ins, outs, macs=ffn_macs // 2)
    ins = [(inner_own, pl.BlockSpec(tile, by_distance)), (came_back, pl.BlockSpec(tile, by_distance))]
    ins += [(sent, at(4)), (sent, at(5)), (came, at(4)), (came, at(5))]
    outs = [((4, width, chunk), LOW, pl.BlockSpec((1, width, chunk), by_distance))]
    (up_unit,) = run(up_grad, places, (4,), ins, outs, macs=ffn_macs // 2)
    down_sum = reduce_unit(down_unit, (2, 4))
    up_sum = reduce_unit(up_unit, (4, 2))

    small_terms = jnp.concatenate(
        [small_one[:3], small_two[:3], up_bias.reshape(heads_axis, width)]
    )
    small_sum = sum_small(small_terms)
    grad_small = small_sum[:6]
    grad_up_bias = lax.dynamic_index_in_dim(small_sum[6:], z, 0, False)

    grad_rows, units, bias_sums = [], [], []
    own_half = pl.BlockSpec((own_rows, half), lambda k, s: (s[1], s[0] & 1))
    for d in range(heads_axis):
        ins = [
            (qkvs[d], whole((rows3, own_rows))),
            (shards[d], out_rows),
            (grad_attended, whole(square)),
            (logs[d], whole((8, own_rows))),
            (seg_col, whole((own_rows, 1))),
            (seg_row, whole((1, own_rows))),
        ]
        outs = [
            ((rows3, own_rows), LOW, whole((rows3, own_rows))),
            ((8, rows3), F32, whole((8, rows3))),
        ]
        rows, bias_sum = run(
            attention_back, places, (1,), ins, outs,
            macs=15 * own_rows * own_rows * 256 + local_width * own_rows * width,
        )
        rows_far = swap_batch(rows, 1)
        ins = [
            (rows, whole((rows3, own_rows))),
            (rows_far, whole((rows3, own_rows))),
            (tokens, own_half),
            (tok_far, whole((own_rows, half))),
            (mixes[d], whole((local_width, own_rows))),
            (mixes_far[d], whole((local_width, own_rows))),
            (grad_attended, pl.BlockSpec((own_rows, half), lambda k, s: (0, s[0] & 1))),
            (came_back, at(4)),
        ]
        outs = [((shard_rows, half), LOW, whole((shard_rows, half)))]
        (unit,) = run(attn_grad, places, (1,), ins, outs, macs=2 * shard_rows * own_rows * half)
        grad_rows.append(rows)
        units.append(unit)
        bias_sums.append(bias_sum[0])
    attn_sum = reduce_unit(jnp.stack(units), (2, 4))

    bias_sum = jnp.stack(bias_sums).reshape(heads_axis, 3, local_width)[:, ::2]
    total = bias_sum[0]
    for d in range(1, heads_axis):
        total = total + shift_head(bias_sum[d], -d)
    bit = 1
    while bit < lax.axis_size("batch"):
        total = total + swap_batch(total, bit)
        bit *= 2
    grad_qv_bias = total

    ins = [(rows, whole((rows3, own_rows))) for rows in grad_rows]
    ins += [(w, whole((rows3, width))) for w in shards]
    ins += [(res1, whole(square))]
    outs = [(square, F32, whole(square))]
    (input_grad,) = run(input_sum, places, (1,), ins, outs, macs=own_rows * rows3 * width * 4)

    grad_down = gather_cores(down_sum).reshape(-1, width).astype(F32)
    grad_up = gather_cores(up_sum).transpose(1, 0, 2).reshape(width, -1).astype(F32)
    attn_all = gather_cores(attn_sum).transpose(1, 0, 2).reshape(-1, width).astype(F32)
    grad_qkv = attn_all[:rows3].reshape(3, local_width, width).transpose(0, 2, 1)
    grad_out = attn_all[rows3:]
    return (
        layer_output,
        input_grad,
        grad_qkv,
        grad_qv_bias,
        grad_out,
        grad_up,
        grad_up_bias,
        grad_down,
        grad_small,
    )


def solution(mesh):
    in_specs = (
        P("batch", None),
        P("batch"),
        P(None, None, "head"),
        P(None, "head"),
        P("head", None),
        P(),
        P(),
        P(),
        P(),
        P(),
        P(),
        P(),
        P(),
        P(),
        P(("batch", "head"), None),
    )
    out_specs = (
        P(("batch", "head"), None),
        P(("batch", "head"), None),
        P(None, None, "head"),
        P(None, "head"),
        P("head", None),
        P(None, "head"),
        P("head"),
        P("head", None),
        P(),
    )
    return jax.shard_map(
        per_device, mesh=mesh, in_specs=in_specs, out_specs=out_specs, check_vma=False
    )
```

```python
import math

import jax
import jax.numpy as jnp
from jax import lax
from jax.experimental import pallas as pl
from jax.experimental.pallas import tpu as pltpu
from jax.sharding import Mesh
from jax.sharding import PartitionSpec as P

HEAD_DIM = 64
SLOT = 512
LOW = jnp.bfloat16
F32 = jnp.float32
LOG2E = math.log2(math.e)
SCORE_SCALE = HEAD_DIM ** (-0.5) * LOG2E
VMEM_BYTES = 48 * 2**20
CHIPS = ("far", "near")
EXTRA = 64
TAIL_SLOPE = 0.36
TAIL = (
    0.14371304537508633,
    0.14177245466203425,
    0.1397192603907239,
    0.026549325413860486,
    0.18095403134327948,
    -0.1797647161697652,
    0.047056295581175855,
)


def swap_core(value):
    return lax.ppermute(value, "core", [(0, 1), (1, 0)])


def dot(a, b):
    return jnp.dot(a, b, preferred_element_type=F32)


def dot_nt(a, b):
    return lax.dot_general(a, b, (((1,), (1,)), ((), ())), preferred_element_type=F32)


def dot_tn(a, b):
    return lax.dot_general(a, b, (((0,), (0,)), ((), ())), preferred_element_type=F32)


def whole(shape):
    return pl.BlockSpec(shape, lambda *args: (0,) * len(shape))


def run(kernel, places, grid, ins, outs, scratch=(), macs=0, after=(), alias=()):
    moved = sum(a.size * a.dtype.itemsize for a, spec in ins)
    moved += sum(math.prod(shape) * jnp.dtype(kind).itemsize for shape, kind, spec in outs)
    count, unread = len(ins), len(alias) + len(after)

    def body(places, *refs):
        kernel(places, *refs[:count], *refs[count + unread :])

    held = pl.BlockSpec(memory_space=pl.ANY)
    return pl.pallas_call(
        body,
        grid_spec=pltpu.PrefetchScalarGridSpec(
            num_scalar_prefetch=1,
            grid=grid,
            in_specs=[spec for a, spec in ins] + [held] * unread,
            out_specs=[spec for shape, kind, spec in outs],
            scratch_shapes=list(scratch),
        ),
        out_shape=[jax.ShapeDtypeStruct(shape, kind) for shape, kind, spec in outs],
        input_output_aliases={1 + count + i: i for i in range(len(alias))},
        compiler_params=pltpu.CompilerParams(vmem_limit_bytes=VMEM_BYTES),
        cost_estimate=pl.CostEstimate(flops=2 * macs, bytes_accessed=moved, transcendentals=0),
    )(places, *[a for a, spec in ins], *alias, *after)


def mask_rows(seg_col, seg_row):
    return jnp.where(seg_col == seg_row, 0.0, -1e30)


def attend_heads(tok, w_rows, bias, seg_col, seg_row, qkv_ref, mix_ref, log_ref):
    width = w_rows.shape[0] // 3
    added = dot_tn(bias[:, : 2 * width], jnp.ones((bias.shape[0], tok.shape[0]), LOW))
    qkv = dot_nt(w_rows, tok)
    parts = (
        (qkv[:width] + added[:width]).astype(LOW),
        qkv[width : 2 * width].astype(LOW),
        (qkv[2 * width :] + added[width:]).astype(LOW),
    )
    for c in range(3):
        qkv_ref[c * width : (c + 1) * width] = parts[c]
    masked = mask_rows(seg_col, seg_row)
    for head in range(width // HEAD_DIM):
        q, k, v = (part[head * HEAD_DIM : (head + 1) * HEAD_DIM] for part in parts)
        scores = dot_tn(k, q) + masked
        top = jnp.max(scores, 0, keepdims=True)
        exponent = jnp.exp2((scores - top) * SCORE_SCALE)
        total = jnp.sum(exponent, 0, keepdims=True)
        attend = (exponent * (1.0 / total)).astype(LOW)
        mix_ref[head * HEAD_DIM : (head + 1) * HEAD_DIM] = dot(v, attend).astype(LOW)
        log_ref[head : head + 1] = top * SCORE_SCALE + jnp.log2(total)


def own_attention(places, tok, w, bias, seg_col, seg_row, qkv_ref, mix_ref, log_ref):
    attend_heads(
        tok[...], w[...], bias[...], seg_col[...], seg_row[...], qkv_ref, mix_ref, log_ref
    )


def merge_pieces(ref, rows):
    parts = ref[:, :rows]
    return parts.reshape(parts.shape[0] * rows, parts.shape[2])


def far_attention(places, tok, pieces, seg_col, seg_row, qkv_ref, mix_ref, log_ref):
    rows = mix_ref.shape[0] // 2
    attend_heads(
        tok[...],
        merge_pieces(pieces, rows),
        pieces[0, rows:],
        seg_col[...],
        seg_row[...],
        qkv_ref,
        mix_ref,
        log_ref,
    )


def norm_stats(v):
    centred = v - jnp.mean(v, -1, keepdims=True)
    inv = lax.rsqrt(jnp.mean(centred * centred, -1, keepdims=True) + 1e-05)
    return centred * inv, inv


def norm_back(upstream, unit, inv, gain):
    scaled = upstream * gain
    inner = jnp.mean(scaled * unit, -1, keepdims=True)
    return inv * (scaled - jnp.mean(scaled, -1, keepdims=True) - unit * inner)


def gelu_both(pre):
    power = jnp.exp2(pre * pre * (-0.5 * LOG2E))
    base = 1.0 + TAIL_SLOPE * jnp.abs(pre)
    t = pl.reciprocal(base, approx=True)
    t = t * (2.0 - base * t)
    tail = TAIL[6] * t + TAIL[5]
    for c in TAIL[4::-1]:
        tail = tail * t + c
    tail = tail * (t * power)
    cumul = jnp.where(pre < 0.0, tail, 1.0 - tail)
    return (pre * cumul).astype(LOW), cumul + pre * (power * 0.3989422804014327)


def feed_forward(
    places, tok, mix, w_out, b_out, gain1, shift1,
    w_up, b_up, w_down, b_down, gain2, shift2, cot,
    send, own, slope, unit1, inv1, res2, out, small,
    hidden, low, acc, branch, acts,
):
    k = pl.program_id(0)
    half = send.shape[1]
    core, z = places[1], places[2]
    heads = mix.shape[0]
    rows = mix.shape[1] // 2

    @pl.when(k == 0)
    def _():
        attended = b_out[...]
        for d in range(heads):
            attended = attended + dot_tn(mix[d], merge_pieces(w_out.at[:, z ^ d], rows))
        unit, inv = norm_stats(tok[...].astype(F32) + attended)
        unit1[...] = unit
        inv1[...] = inv
        one = unit * gain1[...] + shift1[...]
        hidden[...] = one
        low[...] = one.astype(LOW)

    @pl.when(k < heads)
    def _():
        block = 256
        for j in range(acts.shape[1] // block):
            at = slice(j * block, (j + 1) * block)
            pre = dot(low[...], w_up[:, at]) + b_up[:, at]
            act, tilt = gelu_both(pre)
            slope[:, at] = tilt
            acts[:, at] = act
        product = dot(acts[...], w_down[...])
        acc[...] = jnp.where(k == 0, product, acc[...] + product)
        left, right = acts[:, :half], acts[:, half:]
        own[...] = jnp.where(core == 0, left, right)
        send[...] = jnp.where(core == 0, right, left)

    @pl.when(k == heads)
    def _():
        unit, inv = norm_stats(hidden[...] + (acc[...] + b_down[...]))
        out[...] = (unit * gain2[...] + shift2[...]).astype(LOW)
        upstream = cot[...].astype(F32)
        grad = norm_back(upstream, unit, inv, gain2[...])
        res2[...] = grad
        grad_low = grad.astype(LOW)
        branch[...] = grad_low
        send[...] = grad_low[:, :half]
        small[0:1] = jnp.sum(grad_low.astype(F32), 0, keepdims=True)
        small[1:2] = jnp.sum(upstream * unit, 0, keepdims=True)
        small[2:3] = jnp.sum(upstream, 0, keepdims=True)

    for step, held in ((1, branch), (2, low), (3, low)):

        @pl.when(k == heads + step)
        def _():
            send[...] = held[:, :half] if step == 2 else held[:, half:]


def feed_backward(
    places, left, right, w_down, slope, w_up, res2, unit1, inv1, gain1,
    send, own, bias, res1, low, small,
    branch, acc, inners,
):
    k = pl.program_id(0)
    half = send.shape[1]
    core = places[1]
    heads = pl.num_programs(0) - 1

    @pl.when(k == 0)
    def _():
        branch[:, :half] = left[...]
        branch[:, half:] = right[...]

    @pl.when(k < heads)
    def _():
        block = 256
        for j in range(inners.shape[1] // block):
            at = slice(j * block, (j + 1) * block)
            inner = (dot_nt(branch[...], w_down[at]) * slope[:, at]).astype(LOW)
            inners[:, at] = inner
            bias[:, at] = jnp.sum(inner.astype(F32), 0, keepdims=True)
        product = dot_nt(inners[...], w_up[...])
        acc[...] = jnp.where(k == 0, product, acc[...] + product)
        first, second = inners[:, :half], inners[:, half:]
        own[...] = jnp.where(core == 0, first, second)
        send[...] = jnp.where(core == 0, second, first)

    @pl.when(k == heads)
    def _():
        grad = acc[...] + res2[...]
        result = norm_back(grad, unit1[...], inv1[...], gain1[...])
        res1[...] = result
        result_low = result.astype(LOW)
        low[...] = result_low
        send[...] = jnp.where(core == 0, result_low[:, half:], result_low[:, :half])
        small[0:1] = jnp.sum(result_low.astype(F32), 0, keepdims=True)
        small[1:2] = jnp.sum(grad * unit1[...], 0, keepdims=True)
        small[2:3] = jnp.sum(grad, 0, keepdims=True)


def attention_back(places, qkv, w_out, grad, log_ref, seg_col, seg_row, rows_ref, bias_ref):
    width = qkv.shape[0] // 3
    grad_mixed = dot_nt(merge_pieces(w_out, width // 2), grad[...]).astype(LOW)
    masked = mask_rows(seg_col[...], seg_row[...])
    scale = HEAD_DIM ** (-0.5)
    for head in range(width // HEAD_DIM):
        places_of = [c * width + head * HEAD_DIM for c in range(3)]
        q, k, v = (qkv[at : at + HEAD_DIM] for at in places_of)
        g = grad_mixed[head * HEAD_DIM : (head + 1) * HEAD_DIM]
        scores = dot_tn(k, q) + masked
        attend = jnp.exp2(scores * SCORE_SCALE - log_ref[head : head + 1])
        attend_low = attend.astype(LOW)
        grad_v = dot_nt(g, attend_low)
        product = attend * dot_tn(v, g)
        inner = jnp.sum(product, 0, keepdims=True)
        grad_scores = (product - attend * inner).astype(LOW)
        grad_q = dot(k, grad_scores) * scale
        grad_k = dot_nt(q, grad_scores) * scale
        for at, value in zip(places_of, (grad_q, grad_k, grad_v)):
            rows_ref[at : at + HEAD_DIM] = value.astype(LOW)
    ones = jnp.ones((8, rows_ref.shape[1]), LOW)
    bias_ref[...] = dot_nt(ones, rows_ref[...])


def down_grad(places, act, act_far, left, right, left_far, right_far, out, near, far):
    half = left.shape[1]

    @pl.when(pl.program_id(0) == 0)
    def _():
        near[:, :half] = left[...]
        near[:, half:] = right[...]
        far[:, :half] = left_far[...]
        far[:, half:] = right_far[...]

    out[...] = (dot_tn(act[...], near[...]) + dot_tn(act_far[...], far[...])).astype(LOW)


def up_grad(places, inner, inner_far, left, right, left_far, right_far, out):
    half = left.shape[1]
    for side, near, far in ((0, left, left_far), (1, right, right_far)):
        total = dot_tn(near[...], inner[...]) + dot_tn(far[...], inner_far[...])
        out[side * half : (side + 1) * half] = total.astype(LOW)


def attn_grad(
    places, rows, rows_far, tok, tok_far, mix, mix_far, grad, grad_far,
    small_one, small_two, up_bias, qkv_bias, out,
):
    count, width = rows.shape[0], mix.shape[0]
    half = out.shape[1]
    out[:count] = (dot(rows[...], tok[...]) + dot(rows_far[...], tok_far[...])).astype(LOW)
    end = count + width
    out[count:end] = (dot(mix[...], grad[...]) + dot(mix_far[...], grad_far[...])).astype(LOW)
    lines = []
    for held in (small_one, small_two):
        for i in range(3):
            lines += [held[i : i + 1, :half], held[i : i + 1, half:]]
    lines += [up_bias[:, :half], up_bias[:, half:]]
    lines.append(jnp.concatenate([qkv_bias[0:1, :width], qkv_bias[0:1, 2 * width :]], 1))
    lines.append(jnp.zeros((EXTRA - len(lines), half), F32))
    out[end:] = jnp.concatenate(lines, 0).astype(LOW)


def input_sum(places, rows, w, res1, out):
    total = dot_tn(rows[...], merge_pieces(w, rows.shape[0] // 6))
    k = pl.program_id(0)
    out[...] = jnp.where(k == 0, res1[...], out[...]) + total


def down_place(places, pieces, out):
    chips, cores, rows, width = pieces.shape
    for chip in range(chips):
        for core in range(cores):
            start = (core * chips + chip) * rows
            out[start : start + rows] = pieces[chip, core].astype(F32)


def up_place(places, pieces, out):
    chips, cores, rows, width = pieces.shape
    for chip in range(chips):
        for core in range(cores):
            start = chip * rows
            out[start : start + rows, core * width : (core + 1) * width] = pieces[chip, core].astype(F32)


def attn_place(places, pieces, qkv, w_out, small, up_bias, qv_bias, full):
    chips, cores, rows, width = pieces.shape
    for chip in range(chips):
        for core in range(cores):
            start = chip * rows
            full[start : start + rows, core * width : (core + 1) * width] = pieces[chip, core].astype(F32)
    count = w_out.shape[0]
    for c in range(3):
        qkv[c] = full[c * count : (c + 1) * count].T
    w_out[...] = full[3 * count : 4 * count]
    at = 4 * count
    lines = full[at : at + 16, :width] + full[at : at + 16, width:]
    for i in range(6):
        small[i : i + 1, :width] = lines[2 * i : 2 * i + 1]
        small[i : i + 1, width:] = lines[2 * i + 1 : 2 * i + 2]
    up_bias[:, :width] = lines[12:13]
    up_bias[:, width:] = lines[13:14]
    qv_bias[0:1] = lines[14:15, :count]
    qv_bias[1:2] = lines[14:15, count : 2 * count]


def bias_parts(values):
    rows, rest = [], values
    for _ in range(3):
        rows.append(lax.reduce_precision(rest, 8, 7))
        rest = rest - rows[-1]
    return jnp.stack(rows).astype(LOW)


def reduce_unit(unit):
    part = lax.psum_scatter(unit, CHIPS, scatter_dimension=1, tiled=True)
    part = lax.psum_scatter(part, "head", scatter_dimension=0, tiled=False)
    pieces = lax.all_gather(part, CHIPS + ("core",), axis=0, tiled=False)
    pieces = pieces.reshape((-1, 2) + part.shape)
    if part.shape[0] % 16:
        joined = pieces.transpose(1, 0, 2, 3).reshape(2, -1, part.shape[1])
        pieces = joined[None].reshape(1, 2, -1, part.shape[1])
    return pieces


def per_device(
    tokens,
    segment_ids,
    w_qkv,
    b_qv,
    w_out,
    b_out,
    ln1_gain,
    ln1_bias,
    w_up,
    b_up,
    w_down,
    b_down,
    ln2_gain,
    ln2_bias,
    cotangent,
):
    width = tokens.shape[1]
    own_rows = cotangent.shape[0]
    local_width = w_qkv.shape[2]
    heads = lax.axis_size("head")
    z = lax.axis_index("head")
    core = lax.axis_index("core")
    near = lax.axis_index("near")
    hidden_units = w_up.shape[1]
    chunk = hidden_units // heads
    half = width // 2
    rows3 = 3 * local_width
    places = jnp.stack([near, core, z]).astype(jnp.int32)

    shard = jnp.concatenate([w_qkv.transpose(0, 2, 1).reshape(rows3, width), w_out], 0)
    piece_rows = shard.shape[0] // 8
    bias = jnp.pad(bias_parts(b_qv.reshape(-1)), ((0, 13), (0, width - 2 * local_width)))
    piece = lax.dynamic_slice_in_dim(shard, (near * 2 + core) * piece_rows, piece_rows, 0)
    piece = jnp.concatenate([piece, bias], 0)
    pieces = lax.all_gather(piece, ("near", "core", "head"), axis=0, tiled=False)
    pieces = pieces.reshape(8, heads, piece_rows + 16, width)

    seg = lax.dynamic_slice_in_dim(segment_ids, z * own_rows, own_rows, 0)
    segs = [
        (seg[:, None], whole((own_rows, 1))),
        (seg[None], whole((1, own_rows))),
    ]
    own_tokens = (tokens, pl.BlockSpec((own_rows, width), lambda k, s: (s[2], 0)))

    def attend_outs(first):
        def spec(*shape):
            return pl.BlockSpec((None,) + shape, lambda k, s: (k + first, 0, 0))

        return [
            ((heads, rows3, own_rows), LOW, spec(rows3, own_rows)),
            ((heads, local_width, own_rows), LOW, spec(local_width, own_rows)),
            ((heads, 8, own_rows), F32, spec(8, own_rows)),
        ]

    def shard_pieces(count, first, off):
        block = (count, None, piece_rows + 16, width)
        return (pieces, pl.BlockSpec(block, lambda k, s: (first, s[2] ^ (k + off), 0, 0)))

    macs = rows3 * width * own_rows + 6 * own_rows * own_rows * 256
    ins = [own_tokens, (shard, whole((rows3, width))), (bias, whole(bias.shape))] + segs
    begun = run(own_attention, places, (1,), ins, attend_outs(0), macs=macs)
    ins = [own_tokens, shard_pieces(6, 0, 1)] + segs
    qkvs, mixes, logs = run(
        far_attention, places, (heads - 1,), ins, attend_outs(1), macs=3 * macs, alias=begun
    )

    tok_send = lax.dynamic_slice(tokens, (z * own_rows, (1 - core) * half), (own_rows, half))
    tok_far = swap_core(tok_send)
    mixes_far = swap_core(mixes)

    def by_step(*shape):
        block = (None,) + shape
        return pl.BlockSpec(block, lambda k, s: (jnp.minimum(k, heads - 1),) + (0,) * len(shape))

    def unit_at(k, s):
        return s[2] ^ jnp.minimum(k, heads - 1)

    def at(index):
        return pl.BlockSpec((None, own_rows, half), lambda *args: (index, 0, 0))

    row = whole((1, width))
    square = (own_rows, width)
    up_block = (w_up, pl.BlockSpec((width, chunk), lambda k, s: (0, unit_at(k, s))))
    down_block = (w_down, pl.BlockSpec((chunk, width), lambda k, s: (unit_at(k, s), 0)))
    line_block = pl.BlockSpec((None, 1, chunk), lambda k, s: (unit_at(k, s), 0, 0))
    ins = [
        own_tokens,
        (mixes, whole(mixes.shape)),
        (pieces, pl.BlockSpec((2, heads, piece_rows + 16, width), lambda k, s: (3, 0, 0, 0))),
        (b_out[None], row),
        (ln1_gain[None], row),
        (ln1_bias[None], row),
        up_block,
        (b_up.reshape(heads, 1, chunk), line_block),
        down_block,
        (b_down[None], row),
        (ln2_gain[None], row),
        (ln2_bias[None], row),
        (cotangent, whole(square)),
    ]
    tile = pl.BlockSpec((None, own_rows, half), lambda k, s: (k, 0, 0))
    outs = [
        ((8, own_rows, half), LOW, tile),
        ((heads, own_rows, half), LOW, by_step(own_rows, half)),
        ((heads, own_rows, chunk), F32, by_step(own_rows, chunk)),
        (square, F32, whole(square)),
        ((own_rows, 1), F32, whole((own_rows, 1))),
        (square, F32, whole(square)),
        (square, LOW, whole(square)),
        ((8, width), F32, whole((8, width))),
    ]
    scratch = [
        pltpu.VMEM(square, F32),
        pltpu.VMEM(square, LOW),
        pltpu.VMEM(square, F32),
        pltpu.VMEM(square, LOW),
        pltpu.VMEM((own_rows, chunk), LOW),
    ]
    ffn_macs = 2 * own_rows * width * hidden_units
    sent, act_own, slope, unit1, inv1, res2, layer_output, small_two = run(
        feed_forward, places, (heads + 4,), ins, outs, scratch, ffn_macs
    )
    came = swap_core(sent)

    ins = [(act_own, by_step(own_rows, half)), (came, by_step(own_rows, half))]
    ins += [(sent, at(4)), (sent, at(5)), (came, at(4)), (came, at(5))]
    out_block = pl.BlockSpec((None, half, width), lambda k, s: (unit_at(k, s), 0, 0))
    outs = [((heads, half, width), LOW, out_block)]
    scratch = [pltpu.VMEM(square, LOW), pltpu.VMEM(square, LOW)]
    (down_unit,) = run(down_grad, places, (heads,), ins, outs, scratch, ffn_macs // 2)
    down_pieces = reduce_unit(down_unit)

    ins = [
        (sent, at(4)),
        (sent, at(5)),
        down_block,
        (slope, by_step(own_rows, chunk)),
        up_block,
        (res2, whole(square)),
        (unit1, whole(square)),
        (inv1, whole((own_rows, 1))),
        (ln1_gain[None], row),
    ]
    outs = [
        ((5, own_rows, half), LOW, tile),
        ((heads, own_rows, half), LOW, by_step(own_rows, half)),
        ((heads, 1, chunk), F32, line_block),
        (square, F32, whole(square)),
        (square, LOW, whole(square)),
        ((8, width), F32, whole((8, width))),
    ]
    scratch = [
        pltpu.VMEM(square, LOW),
        pltpu.VMEM(square, F32),
        pltpu.VMEM((own_rows, chunk), LOW),
    ]
    sent_back, inner_own, up_bias, res1, grad_attended, small_one = run(
        feed_backward, places, (heads + 1,), ins, outs, scratch, ffn_macs, after=[down_unit]
    )
    came_back = swap_core(sent_back)

    ins = [(inner_own, by_step(own_rows, half)), (came_back, by_step(own_rows, half))]
    ins += [(sent, at(6)), (sent, at(7)), (came, at(6)), (came, at(7))]
    out_block = pl.BlockSpec((None, width, half), lambda k, s: (unit_at(k, s), 0, 0))
    outs = [((heads, width, half), LOW, out_block)]
    (up_unit,) = run(up_grad, places, (heads,), ins, outs, macs=ffn_macs // 2)
    up_pieces = reduce_unit(up_unit)

    ins = [
        (qkvs, by_step(rows3, own_rows)),
        shard_pieces(2, 3, 0),
        (grad_attended, whole(square)),
        (logs, by_step(8, own_rows)),
    ] + segs
    outs = [
        ((heads, rows3, own_rows), LOW, by_step(rows3, own_rows)),
        ((heads, 8, rows3), F32, by_step(8, rows3)),
    ]
    grad_rows, qkv_bias = run(
        attention_back, places, (heads,), ins, outs, after=[up_unit],
        macs=heads * (15 * own_rows * own_rows * 256 + local_width * own_rows * width),
    )
    rows_far = swap_core(grad_rows)
    ins = [
        (grad_rows, by_step(rows3, own_rows)),
        (rows_far, by_step(rows3, own_rows)),
        (tokens, pl.BlockSpec((own_rows, half), lambda k, s: (s[2], s[1]))),
        (tok_far, whole((own_rows, half))),
        (mixes, by_step(local_width, own_rows)),
        (mixes_far, by_step(local_width, own_rows)),
        (grad_attended, pl.BlockSpec((own_rows, half), lambda k, s: (0, s[1]))),
        (came_back, at(4)),
        (small_one, whole((8, width))),
        (small_two, whole((8, width))),
        (up_bias, line_block),
        (qkv_bias, by_step(8, rows3)),
    ]
    unit_rows = rows3 + local_width + EXTRA
    out_block = pl.BlockSpec((None, unit_rows, half), lambda k, s: (unit_at(k, s), 0, 0))
    outs = [((heads, unit_rows, half), LOW, out_block)]
    (attn_unit,) = run(attn_grad, places, (heads,), ins, outs, macs=8 * width * own_rows * half)
    attn_pieces = reduce_unit(attn_unit)

    ins = [(grad_rows, by_step(rows3, own_rows)), shard_pieces(6, 0, 0), (res1, whole(square))]
    outs = [(square, F32, whole(square))]
    (input_grad,) = run(
        input_sum, places, (heads,), ins, outs, macs=heads * own_rows * rows3 * width
    )

    outs = [((chunk, width), F32, whole((chunk, width)))]
    ins = [(down_pieces, whole(down_pieces.shape))]
    (grad_down,) = run(down_place, places, (1,), ins, outs)
    outs = [((width, chunk), F32, whole((width, chunk)))]
    ins = [(up_pieces, whole(up_pieces.shape))]
    (grad_up,) = run(up_place, places, (1,), ins, outs)
    shapes = [
        (3, width, local_width),
        (local_width, width),
        (6, width),
        (1, chunk),
        (2, local_width),
    ]
    ins = [(attn_pieces, whole(attn_pieces.shape))]
    grad_qkv, grad_out, grad_small, grad_up_bias, grad_qv_bias = run(
        attn_place,
        places,
        (1,),
        ins,
        [(shape, F32, whole(shape)) for shape in shapes],
        [pltpu.VMEM((unit_rows, width), F32)],
    )
    return (
        layer_output,
        input_grad,
        grad_qkv,
        grad_qv_bias,
        grad_out,
        grad_up,
        grad_up_bias[0],
        grad_down,
        grad_small,
    )


def solution(mesh):
    batch, heads = mesh.devices.shape
    mesh = Mesh(
        mesh.devices.reshape(batch // 8, 4, 2, heads), ("far", "near", "core", "head")
    )
    group = ("far", "near", "core")
    everyone = group + ("head",)
    in_specs = (
        P(group, None),
        P(group),
        P(None, None, "head"),
        P(None, "head"),
        P("head", None),
        P(),
        P(),
        P(),
        P(),
        P(),
        P(),
        P(),
        P(),
        P(),
        P(everyone, None),
    )
    out_specs = (
        P(everyone, None),
        P(everyone, None),
        P(None, None, "head"),
        P(None, "head"),
        P("head", None),
        P(None, "head"),
        P("head"),
        P("head", None),
        P(),
    )
    return jax.shard_map(
        per_device, mesh=mesh, in_specs=in_specs, out_specs=out_specs, check_vma=False
    )
```

```python
import functools
import math

import jax
import jax.numpy as jnp
from jax import lax
from jax.experimental import pallas as pl
from jax.experimental.pallas import tpu as pltpu
from jax.sharding import Mesh
from jax.sharding import PartitionSpec as P

HEAD_DIM = 64
SLOT = 512
LOW = jnp.bfloat16
F32 = jnp.float32
LOG2E = math.log2(math.e)
SCORE_SCALE = HEAD_DIM ** (-0.5) * LOG2E
VMEM_BYTES = 60 * 2**20
EXTRA = 64
TAIL_SLOPE = 0.36
TAIL = (
    0.14371304537508633,
    0.14177245466203425,
    0.1397192603907239,
    0.026549325413860486,
    0.18095403134327948,
    -0.1797647161697652,
    0.047056295581175855,
)


def swap(value, axis, bit):
    size = lax.axis_size(axis)
    return lax.ppermute(value, axis, [(i, i ^ bit) for i in range(size)])


def swap_core(value):
    return swap(value, "core", 1)


def dot(a, b):
    return jnp.dot(a, b, preferred_element_type=F32)


def dot_nt(a, b):
    return lax.dot_general(a, b, (((1,), (1,)), ((), ())), preferred_element_type=F32)


def dot_tn(a, b):
    return lax.dot_general(a, b, (((0,), (0,)), ((), ())), preferred_element_type=F32)


def whole(shape):
    return pl.BlockSpec(shape, lambda *args: (0,) * len(shape))


def run(kernel, places, grid, ins, outs, scratch=(), macs=0, after=(), alias=()):
    moved = sum(a.size * a.dtype.itemsize for a, spec in ins)
    moved += sum(math.prod(shape) * jnp.dtype(kind).itemsize for shape, kind, spec in outs)
    count, unread = len(ins), len(alias) + len(after)

    def body(places, *refs):
        kernel(places, *refs[:count], *refs[count + unread :])

    held = pl.BlockSpec(memory_space=pl.ANY)
    return pl.pallas_call(
        body,
        grid_spec=pltpu.PrefetchScalarGridSpec(
            num_scalar_prefetch=1,
            grid=grid,
            in_specs=[spec for a, spec in ins] + [held] * unread,
            out_specs=[spec for shape, kind, spec in outs],
            scratch_shapes=list(scratch),
        ),
        out_shape=[jax.ShapeDtypeStruct(shape, kind) for shape, kind, spec in outs],
        input_output_aliases={1 + count + i: i for i in range(len(alias))},
        compiler_params=pltpu.CompilerParams(vmem_limit_bytes=VMEM_BYTES),
        cost_estimate=pl.CostEstimate(flops=2 * macs, bytes_accessed=moved, transcendentals=0),
    )(places, *[a for a, spec in ins], *alias, *after)


def mask_rows(seg_col, seg_row):
    return jnp.where(seg_col == seg_row, 0.0, -1e30)


def attend_heads(tok, w_rows, bias, seg_col, seg_row, qkv_ref, mix_ref, log_ref):
    width = w_rows.shape[0] // 3
    added = dot_tn(bias[:, : 2 * width], jnp.ones((bias.shape[0], tok.shape[0]), LOW))
    qkv = dot_nt(w_rows, tok)
    parts = (
        (qkv[:width] + added[:width]).astype(LOW),
        qkv[width : 2 * width].astype(LOW),
        (qkv[2 * width :] + added[width:]).astype(LOW),
    )
    for c in range(3):
        qkv_ref[c * width : (c + 1) * width] = parts[c]
    masked = mask_rows(seg_col, seg_row)
    for head in range(width // HEAD_DIM):
        q, k, v = (part[head * HEAD_DIM : (head + 1) * HEAD_DIM] for part in parts)
        scores = dot_tn(k, q) + masked
        top = jnp.max(scores, 0, keepdims=True)
        exponent = jnp.exp2((scores - top) * SCORE_SCALE)
        total = jnp.sum(exponent, 0, keepdims=True)
        attend = (exponent * (1.0 / total)).astype(LOW)
        mix_ref[head * HEAD_DIM : (head + 1) * HEAD_DIM] = dot(v, attend).astype(LOW)
        log_ref[head : head + 1] = top * SCORE_SCALE + jnp.log2(total)


def own_attention(places, tok, w, bias, seg_col, seg_row, qkv_ref, mix_ref, log_ref, w_ref):
    w_ref[...] = w[...]
    attend_heads(
        tok[...],
        w[: qkv_ref.shape[0]],
        bias[...],
        seg_col[...],
        seg_row[...],
        qkv_ref,
        mix_ref,
        log_ref,
    )


def far_attention(
    order, places, tok, pair, rest, pair_far, rest_far, bias, seg_col, seg_row,
    qkv_ref, mix_ref, log_ref, w_ref,
):
    first, second = order
    rows = pair.shape[1]
    me = places[0] * 2 + places[1]
    for other, held in enumerate(((pair, rest), (pair_far, rest_far))):
        for two, block in enumerate(held):
            for one in range(2):
                owner = me ^ (other + 2 * first * one + 2 * second * two)
                w_ref[pl.ds(pl.multiple_of(owner * rows, rows), rows)] = block[one]
    attend_heads(
        tok[...],
        w_ref[: qkv_ref.shape[0]],
        bias[...],
        seg_col[...],
        seg_row[...],
        qkv_ref,
        mix_ref,
        log_ref,
    )


def norm_stats(v):
    centred = v - jnp.mean(v, -1, keepdims=True)
    inv = lax.rsqrt(jnp.mean(centred * centred, -1, keepdims=True) + 1e-05)
    return centred * inv, inv


def norm_back(upstream, unit, inv, gain):
    scaled = upstream * gain
    inner = jnp.mean(scaled * unit, -1, keepdims=True)
    return inv * (scaled - jnp.mean(scaled, -1, keepdims=True) - unit * inner)


def gelu_both(pre):
    power = jnp.exp2(pre * pre * (-0.5 * LOG2E))
    base = 1.0 + TAIL_SLOPE * jnp.abs(pre)
    t = pl.reciprocal(base, approx=True)
    t = t * (2.0 - base * t)
    tail = TAIL[6] * t + TAIL[5]
    for c in TAIL[4::-1]:
        tail = tail * t + c
    tail = tail * (t * power)
    cumul = jnp.where(pre < 0.0, tail, 1.0 - tail)
    return (pre * cumul).astype(LOW), cumul + pre * (power * 0.3989422804014327)


def feed_forward(
    places, tok, mix, w_out, b_out, gain1, shift1,
    w_up, b_up, w_down, b_down, gain2, shift2, cot,
    send, own, ends, slope, unit1, inv1, res2, out, small,
    hidden, low, acts, down, sem,
):
    k = pl.program_id(0)
    half = send.shape[1]
    chunk = w_up.shape[1]
    core, z = places[1], places[2]
    heads = mix.shape[0]
    fetch = pltpu.make_async_copy(w_down, down, sem)

    @pl.when(k == 0)
    def _():
        fetch.start()
        attended = b_out[...]
        for d in range(heads):
            attended = attended + dot_tn(mix[d], w_out[d])
        unit, inv = norm_stats(tok[...].astype(F32) + attended)
        unit1[...] = unit
        inv1[...] = inv
        one = unit * gain1[...] + shift1[...]
        hidden[...] = one
        one_low = one.astype(LOW)
        low[...] = one_low
        ends[0] = one_low[:, :half]
        ends[1] = one_low[:, half:]

    @pl.when(k < heads)
    def _():
        start = (z ^ k) * chunk
        block = 256
        for j in range(chunk // block):
            at = slice(j * block, (j + 1) * block)
            pre = dot(low[...], w_up[:, at]) + b_up[:, at]
            act, tilt = gelu_both(pre)
            slope[:, at] = tilt
            acts[:, pl.ds(pl.multiple_of(start + j * block, block), block)] = act
        left = acts[:, pl.ds(pl.multiple_of(start, 128), half)]
        right = acts[:, pl.ds(pl.multiple_of(start + half, 128), half)]
        own[...] = jnp.where(core == 0, left, right)
        send[...] = jnp.where(core == 0, right, left)

    @pl.when(k == heads)
    def _():
        fetch.wait()
        unit, inv = norm_stats(hidden[...] + (dot(acts[...], down[...]) + b_down[...]))
        out[...] = (unit * gain2[...] + shift2[...]).astype(LOW)
        upstream = cot[...].astype(F32)
        grad = norm_back(upstream, unit, inv, gain2[...])
        res2[...] = grad
        grad_low = grad.astype(LOW)
        ends[2] = grad_low[:, :half]
        ends[3] = grad_low[:, half:]
        small[0:1] = jnp.sum(grad_low.astype(F32), 0, keepdims=True)
        small[1:2] = jnp.sum(upstream * unit, 0, keepdims=True)
        small[2:3] = jnp.sum(upstream, 0, keepdims=True)


def inner_back(places, ends, w_down, slope, send, own, bias, branch, inners):
    half = send.shape[1]
    core = places[1]

    @pl.when(pl.program_id(0) == 0)
    def _():
        branch[:, :half] = ends[0]
        branch[:, half:] = ends[1]

    block = 256
    for j in range(inners.shape[1] // block):
        at = slice(j * block, (j + 1) * block)
        inner = (dot_nt(branch[...], w_down[at]) * slope[:, at]).astype(LOW)
        inners[:, at] = inner
        bias[:, at] = jnp.sum(inner.astype(F32), 0, keepdims=True)
    first, second = inners[:, :half], inners[:, half:]
    own[...] = jnp.where(core == 0, first, second)
    send[...] = jnp.where(core == 0, second, first)


def hidden_back(
    places, own, sent, w_up, res2, unit1, inv1, gain1, send, res1, low, small, acc
):
    k = pl.program_id(0)
    core = places[1]
    half = own.shape[1]
    mine, other = own[...], sent[...]
    inner = jnp.concatenate(
        [jnp.where(core == 0, mine, other), jnp.where(core == 0, other, mine)], 1
    )
    product = dot_nt(inner, w_up[...])

    @pl.when(k == 0)
    def _():
        acc[...] = res2[...] + product

    @pl.when(k > 0)
    def _():
        acc[...] += product

    @pl.when(k == pl.num_programs(0) - 1)
    def _():
        grad = acc[...]
        result = norm_back(grad, unit1[...], inv1[...], gain1[...])
        res1[...] = result
        result_low = result.astype(LOW)
        low[...] = result_low
        send[...] = jnp.where(core == 0, result_low[:, half:], result_low[:, :half])
        small[0:1] = jnp.sum(result_low.astype(F32), 0, keepdims=True)
        small[1:2] = jnp.sum(grad * unit1[...], 0, keepdims=True)
        small[2:3] = jnp.sum(grad, 0, keepdims=True)


def attention_back(places, qkv, w_out, grad, log_ref, seg_col, seg_row, rows_ref, bias_ref):
    width = qkv.shape[0] // 3
    grad_mixed = dot_nt(w_out[...], grad[...]).astype(LOW)
    masked = mask_rows(seg_col[...], seg_row[...])
    scale = HEAD_DIM ** (-0.5)
    for head in range(width // HEAD_DIM):
        places_of = [c * width + head * HEAD_DIM for c in range(3)]
        q, k, v = (qkv[at : at + HEAD_DIM] for at in places_of)
        g = grad_mixed[head * HEAD_DIM : (head + 1) * HEAD_DIM]
        scores = dot_tn(k, q) + masked
        attend = jnp.exp2(scores * SCORE_SCALE - log_ref[head : head + 1])
        attend_low = attend.astype(LOW)
        grad_v = dot_nt(g, attend_low)
        product = attend * dot_tn(v, g)
        inner = jnp.sum(product, 0, keepdims=True)
        grad_scores = (product - attend * inner).astype(LOW)
        grad_q = dot(k, grad_scores) * scale
        grad_k = dot_nt(q, grad_scores) * scale
        for at, value in zip(places_of, (grad_q, grad_k, grad_v)):
            rows_ref[at : at + HEAD_DIM] = value.astype(LOW)
    ones = jnp.ones((8, rows_ref.shape[1]), LOW)
    bias_ref[...] = dot_nt(ones, rows_ref[...])


def split_rows(value, high, send, keep):
    rows = value.shape[0] // 2
    low = value.astype(LOW)
    send[...] = jnp.where(high, low[:rows], low[rows:])
    keep[...] = jnp.where(high, low[rows:], low[:rows])


def is_high(places, bit):
    return (places[0] & bit) != 0


def ffn_grad(bit, places, units, units_far, ends, ends_far, send, keep, near, far):
    half = ends.shape[2]

    @pl.when(pl.program_id(0) == 0)
    def _():
        for side in range(2):
            rows = slice(side * half, (side + 1) * half)
            near[rows] = ends[side].T
            far[rows] = ends_far[side].T

    total = dot(near[...], units[...]) + dot(far[...], units_far[...])
    split_rows(total, is_high(places, bit), send, keep)


def attn_grad(
    places, rows, rows_far, tok, tok_far, mix, mix_far, grad, grad_far,
    small_one, small_two, up_bias, qkv_bias, send_x, keep_x, send_y, keep_y,
):
    width = mix.shape[0]
    half = tok.shape[1]
    qkv = dot(rows[...], tok[...]) + dot(rows_far[...], tok_far[...])
    out = dot(mix[...], grad[...]) + dot(mix_far[...], grad_far[...])
    lines = []
    for held in (small_one, small_two):
        for i in range(3):
            lines += [held[i : i + 1, :half], held[i : i + 1, half:]]
    lines += [up_bias[:, :half], up_bias[:, half:]]
    lines.append(jnp.concatenate([qkv_bias[0:1, :width], qkv_bias[0:1, 2 * width :]], 1))
    lines.append(jnp.zeros((EXTRA - len(lines), half), F32))
    split_rows(qkv[: 2 * width], is_high(places, 1), send_x, keep_x)
    split_rows(jnp.concatenate([qkv[2 * width :], out] + lines, 0), is_high(places, 2), send_y, keep_y)


def add_split(bits, places, *refs):
    for i, bit in enumerate(bits):
        keep, came = refs[2 * i : 2 * i + 2]
        send, left = refs[2 * (len(bits) + i) : 2 * (len(bits) + i) + 2]
        total = keep[...].astype(F32) + came[...].astype(F32)
        split_rows(total, is_high(places, bit), send, left)


def add_parts(places, keep_a, came_a, keep_b, came_b, *outs):
    rows = keep_a.shape[1]
    for d, out in enumerate(outs):
        out[:rows] = (keep_a[d].astype(F32) + came_a[d].astype(F32)).astype(LOW)
        out[rows:] = (keep_b[d].astype(F32) + came_b[d].astype(F32)).astype(LOW)


def add_heads(places, *refs):
    total = refs[0][...].astype(F32)
    for ref in refs[1:-1]:
        total = total + ref[...].astype(F32)
    refs[-1][...] = total.astype(LOW)


def input_sum(places, rows, w, res1, out):
    total = dot_tn(rows[...], w[...])
    k = pl.program_id(0)
    out[...] = jnp.where(k == 0, res1[...], out[...]) + total


def place_pieces(places, held, full, layouts):
    pair, rest, pair_far, rest_far = held
    near, core = places[0], places[1]
    width = pair.shape[2]
    for one in range(2):
        for two in range(2):
            chip = near ^ (one + 2 * two)
            mine = (rest if two else pair)[one]
            other = (rest_far if two else pair_far)[one]
            sides = (jnp.where(core == 0, mine, other), jnp.where(core == 0, other, mine))
            for at, rows, start, outer in layouts:
                low_bit, high_bit = chip & 1, chip >> 1
                order = 2 * low_bit + high_bit if outer == 1 else 2 * high_bit + low_bit
                to = pl.multiple_of(start + order * rows, 16)
                for side in range(2):
                    full[pl.ds(to, rows), side * width : (side + 1) * width] = sides[side][
                        at : at + rows
                    ].astype(F32)


def ffn_place(places, pair, rest, pair_far, rest_far, down, up, full):
    rows = pair.shape[1] // 2
    held = (pair, rest, pair_far, rest_far)
    place_pieces(places, held, full, [(0, rows, 0, 1)])
    down[...] = full[...].T
    place_pieces(places, held, up, [(rows, rows, 0, 2)])


def attn_place(
    places, pair, rest, pair_far, rest_far, qkv, w_out, small, up_bias, qv_bias, full
):
    width = pair.shape[2]
    count = w_out.shape[0]
    rows = count // 2
    more = pair.shape[1] - rows
    place_pieces(
        places,
        (pair, rest, pair_far, rest_far),
        full,
        [(0, rows, 0, 1), (rows, more, 4 * rows, 2)],
    )
    for c in range(3):
        qkv[c] = full[c * count : (c + 1) * count].T
    w_out[...] = full[3 * count : 4 * count]
    at = 4 * count
    lines = full[at : at + 16, :width] + full[at : at + 16, width:]
    for i in range(6):
        small[i : i + 1, :width] = lines[2 * i : 2 * i + 1]
        small[i : i + 1, width:] = lines[2 * i + 1 : 2 * i + 2]
    up_bias[:, :width] = lines[12:13]
    up_bias[:, width:] = lines[13:14]
    qv_bias[0:1] = lines[14:15, :count]
    qv_bias[1:2] = lines[14:15, count : 2 * count]


def bias_parts(values):
    rows, rest = [], values
    for _ in range(3):
        rows.append(lax.reduce_precision(rest, 8, 7))
        rest = rest - rows[-1]
    return jnp.stack(rows).astype(LOW)


def sum_heads(parts, places):
    got = [parts[0]] + [swap(parts[d], "head", d) for d in range(1, len(parts))]
    shape = parts[0].shape
    ins = [(g, whole(shape)) for g in got]
    (total,) = run(add_heads, places, (1,), ins, [(shape, LOW, whole(shape))])
    bit = 1
    while bit < lax.axis_size("far"):
        total = (total.astype(F32) + swap(total, "far", bit).astype(F32)).astype(LOW)
        bit *= 2
    return total


def gather_back(piece):
    pair = jnp.stack([piece, swap(piece, "near", 1)])
    rest = swap(pair, "near", 2)
    held = [pair, rest, swap_core(pair), swap_core(rest)]
    return [(h, whole(h.shape)) for h in held]


def per_device(
    tokens,
    segment_ids,
    w_qkv,
    b_qv,
    w_out,
    b_out,
    ln1_gain,
    ln1_bias,
    w_up,
    b_up,
    w_down,
    b_down,
    ln2_gain,
    ln2_bias,
    cotangent,
):
    width = tokens.shape[1]
    own_rows = cotangent.shape[0]
    local_width = w_qkv.shape[2]
    heads = lax.axis_size("head")
    z = lax.axis_index("head")
    core = lax.axis_index("core")
    near = lax.axis_index("near")
    hidden_units = w_up.shape[1]
    chunk = hidden_units // heads
    half = width // 2
    rows3 = 3 * local_width
    places = jnp.stack([near, core, z]).astype(jnp.int32)

    shard = jnp.concatenate([w_qkv.transpose(0, 2, 1).reshape(rows3, width), w_out], 0)
    piece_rows = shard.shape[0] // 8
    bias = jnp.pad(bias_parts(b_qv.reshape(-1)), ((0, 13), (0, width - 2 * local_width)))
    piece = lax.dynamic_slice_in_dim(shard, (near * 2 + core) * piece_rows, piece_rows, 0)
    piece = jnp.concatenate([piece, bias], 0)
    first_hop = [swap(piece, "head", d) for d in range(1, heads)]

    seg = lax.dynamic_slice_in_dim(segment_ids, z * own_rows, own_rows, 0)
    segs = [
        (seg[:, None], whole((own_rows, 1))),
        (seg[None], whole((1, own_rows))),
    ]
    own_tokens = (tokens, pl.BlockSpec((own_rows, width), lambda k, s: (s[2], 0)))

    def attend_outs(first):
        def spec(*shape):
            return pl.BlockSpec((None,) + shape, lambda k, s: (k + first, 0, 0))

        return [
            ((heads, rows3, own_rows), LOW, spec(rows3, own_rows)),
            ((heads, local_width, own_rows), LOW, spec(local_width, own_rows)),
            ((heads, 8, own_rows), F32, spec(8, own_rows)),
            ((heads, rows3 + local_width, width), LOW, spec(rows3 + local_width, width)),
        ]

    macs = rows3 * width * own_rows + 6 * own_rows * own_rows * 256
    ins = [own_tokens, (shard, whole(shard.shape)), (bias, whole(bias.shape))] + segs
    made = run(own_attention, places, (1,), ins, attend_outs(0), macs=macs)
    for d in range(1, heads):
        order = (1, 2) if d % 2 else (2, 1)
        mine = first_hop[d - 1][:piece_rows]
        pair = jnp.stack([mine, swap(mine, "near", order[0])])
        rest = swap(pair, "near", order[1])
        held = [pair, rest, swap_core(pair), swap_core(rest)]
        ins = [own_tokens] + [(h, whole(h.shape)) for h in held]
        ins += [(first_hop[d - 1], pl.BlockSpec((16, width), lambda k, s: (piece_rows // 16, 0)))]
        kernel = functools.partial(far_attention, order)
        made = run(kernel, places, (1,), ins + segs, attend_outs(d), macs=macs, alias=made)
    qkvs, mixes, logs, weights = made

    tok_send = lax.dynamic_slice(tokens, (z * own_rows, (1 - core) * half), (own_rows, half))
    tok_far = swap_core(tok_send)
    mixes_far = swap_core(mixes)

    def by_step(*shape):
        block = (None,) + shape
        return pl.BlockSpec(block, lambda k, s: (jnp.minimum(k, heads - 1),) + (0,) * len(shape))

    def unit_at(k, s):
        return s[2] ^ jnp.minimum(k, heads - 1)


    row = whole((1, width))
    square = (own_rows, width)
    tile = by_step(own_rows, half)
    tiles = (heads, own_rows, half)
    up_block = (w_up, pl.BlockSpec((width, chunk), lambda k, s: (0, unit_at(k, s))))
    down_block = (w_down, pl.BlockSpec((chunk, width), lambda k, s: (unit_at(k, s), 0)))
    line_block = pl.BlockSpec((None, 1, chunk), lambda k, s: (unit_at(k, s), 0, 0))

    def weight_rows(rows, index):
        return (weights, pl.BlockSpec((None, rows, width), lambda k, s: (k, index, 0)))

    ins = [
        own_tokens,
        (mixes, whole(mixes.shape)),
        (weights, pl.BlockSpec((heads, local_width, width), lambda k, s: (0, 3, 0))),
        (b_out[None], row),
        (ln1_gain[None], row),
        (ln1_bias[None], row),
        up_block,
        (b_up.reshape(heads, 1, chunk), line_block),
        (w_down, pl.BlockSpec(memory_space=pl.ANY)),
        (b_down[None], row),
        (ln2_gain[None], row),
        (ln2_bias[None], row),
        (cotangent, whole(square)),
    ]
    outs = [
        (tiles, LOW, tile),
        (tiles, LOW, tile),
        ((4, own_rows, half), LOW, whole((4, own_rows, half))),
        ((heads, own_rows, chunk), F32, by_step(own_rows, chunk)),
        (square, F32, whole(square)),
        ((own_rows, 1), F32, whole((own_rows, 1))),
        (square, F32, whole(square)),
        (square, LOW, whole(square)),
        ((8, width), F32, whole((8, width))),
    ]
    scratch = [
        pltpu.VMEM(square, F32),
        pltpu.VMEM(square, LOW),
        pltpu.VMEM((own_rows, hidden_units), LOW),
        pltpu.VMEM(w_down.shape, LOW),
        pltpu.SemaphoreType.DMA,
    ]
    ffn_macs = 2 * own_rows * width * hidden_units
    act_send, act_own, ends, slope, unit1, inv1, res2, layer_output, small_two = run(
        feed_forward, places, (heads + 1,), ins, outs, scratch, ffn_macs
    )
    act_far = swap_core(act_send)
    ends_far = swap_core(ends)

    def two_of(array, index):
        return (array, pl.BlockSpec((2, own_rows, half), lambda k, s: (index, 0, 0)))

    ins = [two_of(ends, 1), down_block, (slope, by_step(own_rows, chunk))]
    outs = [(tiles, LOW, tile), (tiles, LOW, tile), ((heads, 1, chunk), F32, line_block)]
    scratch = [pltpu.VMEM(square, LOW), pltpu.VMEM((own_rows, chunk), LOW)]
    inner_send, inner_own, up_bias = run(
        inner_back, places, (heads,), ins, outs, scratch, ffn_macs // 2
    )
    inner_far = swap_core(inner_send)

    def unit_outs(rows):
        return [((heads, rows, half), LOW, by_step(rows, half))] * 2

    flipped = [pltpu.VMEM((width, own_rows), LOW)] * 2
    ins = [(act_own, tile), (act_far, tile), two_of(ends, 1), two_of(ends_far, 1)]
    d_send, d_keep = run(
        functools.partial(ffn_grad, 1), places, (heads,), ins, unit_outs(half), flipped,
        ffn_macs // 2, after=[inner_send],
    )
    d_came = swap(d_send, "near", 1)

    ins = [
        (inner_own, tile),
        (inner_send, tile),
        up_block,
        (res2, whole(square)),
        (unit1, whole(square)),
        (inv1, whole((own_rows, 1))),
        (ln1_gain[None], row),
    ]
    outs = [
        ((own_rows, half), LOW, whole((own_rows, half))),
        (square, F32, whole(square)),
        (square, LOW, whole(square)),
        ((8, width), F32, whole((8, width))),
    ]
    grad_send, res1, grad_attended, small_one = run(
        hidden_back, places, (heads,), ins, outs, [pltpu.VMEM(square, F32)], ffn_macs // 2,
        after=[d_send],
    )
    grad_far = swap_core(grad_send)

    ins = [(inner_own, tile), (inner_far, tile), two_of(ends, 0), two_of(ends_far, 0)]
    u_send, u_keep = run(
        functools.partial(ffn_grad, 2), places, (heads,), ins, unit_outs(half), flipped,
        ffn_macs // 2, after=[grad_send],
    )
    u_came = swap(u_send, "near", 2)

    ins = [
        (qkvs, by_step(rows3, own_rows)),
        weight_rows(local_width, 3),
        (grad_attended, whole(square)),
        (logs, by_step(8, own_rows)),
    ] + segs
    outs = [
        ((heads, rows3, own_rows), LOW, by_step(rows3, own_rows)),
        ((heads, 8, rows3), F32, by_step(8, rows3)),
    ]
    grad_rows, qkv_bias = run(
        attention_back, places, (heads,), ins, outs, after=[u_send],
        macs=heads * (15 * own_rows * own_rows * 256 + local_width * own_rows * width),
    )
    rows_far = swap_core(grad_rows)

    ins = [(grad_rows, by_step(rows3, own_rows)), weight_rows(rows3, 0), (res1, whole(square))]
    outs = [(square, F32, whole(square))]
    (input_grad,) = run(
        input_sum, places, (heads,), ins, outs, macs=heads * own_rows * rows3 * width
    )

    ins = [
        (grad_rows, by_step(rows3, own_rows)),
        (rows_far, by_step(rows3, own_rows)),
        (tokens, pl.BlockSpec((own_rows, half), lambda k, s: (s[2], s[1]))),
        (tok_far, whole((own_rows, half))),
        (mixes, by_step(local_width, own_rows)),
        (mixes_far, by_step(local_width, own_rows)),
        (grad_attended, pl.BlockSpec((own_rows, half), lambda k, s: (0, s[1]))),
        (grad_far, whole((own_rows, half))),
        (small_one, whole((8, width))),
        (small_two, whole((8, width))),
        (up_bias, line_block),
        (qkv_bias, by_step(8, rows3)),
    ]
    x_rows = local_width
    y_rows = local_width + EXTRA // 2
    outs = unit_outs(x_rows) + unit_outs(y_rows)
    x_send, x_keep, y_send, y_keep = run(
        attn_grad, places, (heads,), ins, outs, macs=8 * width * own_rows * half,
        after=[input_grad],
    )
    x_came = swap(x_send, "near", 1)
    y_came = swap(y_send, "near", 2)

    def second(bits, pairs):
        ins = [(a, by_step(*a.shape[1:])) for pair in pairs for a in pair]
        outs = []
        for keep, came in pairs:
            outs += unit_outs(keep.shape[1] // 2)
        return run(functools.partial(add_split, bits), places, (heads,), ins, outs)

    def third(keep_a, came_a, keep_b, came_b):
        held = (keep_a, came_a, keep_b, came_b)
        shape = (keep_a.shape[1] + keep_b.shape[1], half)
        return sum_heads(
            run(
                add_parts,
                places,
                (1,),
                [(a, whole(a.shape)) for a in held],
                [(shape, LOW, whole(shape))] * heads,
            ),
            places,
        )

    d_send, d_keep = second((2,), [(d_keep, d_came)])
    u_send, u_keep = second((1,), [(u_keep, u_came)])
    d_came = swap(d_send, "near", 2)
    u_came = swap(u_send, "near", 1)
    ffn_piece = third(d_keep, d_came, u_keep, u_came)
    x_send, x_keep, y_send, y_keep = second((2, 1), [(x_keep, x_came), (y_keep, y_came)])
    x_came = swap(x_send, "near", 2)
    y_came = swap(y_send, "near", 1)
    attn_piece = third(x_keep, x_came, y_keep, y_came)

    outs = [(shape, F32, whole(shape)) for shape in ((chunk, width), (width, chunk))]
    grad_down, grad_up = run(
        ffn_place, places, (1,), gather_back(ffn_piece), outs, [pltpu.VMEM((width, chunk), F32)]
    )
    shapes = [
        (3, width, local_width),
        (local_width, width),
        (6, width),
        (1, chunk),
        (2, local_width),
    ]
    grad_qkv, grad_out, grad_small, grad_up_bias, grad_qv_bias = run(
        attn_place,
        places,
        (1,),
        gather_back(attn_piece),
        [(shape, F32, whole(shape)) for shape in shapes],
        [pltpu.VMEM((width + EXTRA, width), F32)],
    )
    return (
        layer_output,
        input_grad,
        grad_qkv,
        grad_qv_bias,
        grad_out,
        grad_up,
        grad_up_bias[0],
        grad_down,
        grad_small,
    )


def solution(mesh):
    batch, heads = mesh.devices.shape
    mesh = Mesh(
        mesh.devices.reshape(batch // 8, 4, 2, heads), ("far", "near", "core", "head")
    )
    group = ("far", "near", "core")
    everyone = group + ("head",)
    in_specs = (
        P(group, None),
        P(group),
        P(None, None, "head"),
        P(None, "head"),
        P("head", None),
        P(),
        P(),
        P(),
        P(),
        P(),
        P(),
        P(),
        P(),
        P(),
        P(everyone, None),
    )
    out_specs = (
        P(everyone, None),
        P(everyone, None),
        P(None, None, "head"),
        P(None, "head"),
        P("head", None),
        P(None, "head"),
        P("head"),
        P("head", None),
        P(),
    )
    return jax.shard_map(
        per_device, mesh=mesh, in_specs=in_specs, out_specs=out_specs, check_vma=False
    )
```

```python
import functools
import math

import jax
import jax.numpy as jnp
from jax import lax
from jax.experimental import pallas as pl
from jax.experimental.pallas import tpu as pltpu
from jax.sharding import Mesh
from jax.sharding import PartitionSpec as P

HEAD_DIM = 64
SLOT = 512
LOW = jnp.bfloat16
F32 = jnp.float32
LOG2E = math.log2(math.e)
SCORE_SCALE = HEAD_DIM ** (-0.5) * LOG2E
SPARE_BYTES = 12 * 2**20
EXTRA = 64
TAIL_SLOPE = 0.36
TAIL = (
    0.14371304537508633,
    0.14177245466203425,
    0.1397192603907239,
    0.026549325413860486,
    0.18095403134327948,
    -0.1797647161697652,
    0.047056295581175855,
)


def swap(value, axis, bit):
    size = lax.axis_size(axis)
    return lax.ppermute(value, axis, [(i, i ^ bit) for i in range(size)])


def swap_core(value):
    return swap(value, "core", 1)


def dot(a, b):
    return jnp.dot(a, b, preferred_element_type=F32)


def dot_nt(a, b):
    return lax.dot_general(a, b, (((1,), (1,)), ((), ())), preferred_element_type=F32)


def dot_tn(a, b):
    return lax.dot_general(a, b, (((0,), (0,)), ((), ())), preferred_element_type=F32)


def whole(shape):
    return pl.BlockSpec(shape, lambda *args: (0,) * len(shape))


def run(kernel, places, grid, ins, outs, scratch=(), macs=0, after=(), alias=(), weight=8):
    moved = sum(a.size * a.dtype.itemsize for a, spec in ins)
    moved += sum(math.prod(shape) * jnp.dtype(kind).itemsize for shape, kind, spec in outs)
    count, unread = len(ins), len(alias) + len(after)

    def body(places, *refs):
        kernel(places, *refs[:count], *refs[count + unread :])

    held = pl.BlockSpec(memory_space=pl.ANY)
    room = SPARE_BYTES
    for shape, kind, spec in outs + [(a.shape, a.dtype, spec) for a, spec in ins]:
        if spec.block_shape is not None:
            block = math.prod(1 if n is None else n for n in spec.block_shape)
            room += 2 * block * jnp.dtype(kind).itemsize
    for ref in scratch:
        if hasattr(ref, "shape") and ref.shape:
            room += math.prod(ref.shape) * jnp.dtype(ref.dtype).itemsize
    return pl.pallas_call(
        body,
        name=getattr(kernel, "func", kernel).__name__,
        grid_spec=pltpu.PrefetchScalarGridSpec(
            num_scalar_prefetch=1,
            grid=grid,
            in_specs=[spec for a, spec in ins] + [held] * unread,
            out_specs=[spec for shape, kind, spec in outs],
            scratch_shapes=list(scratch),
        ),
        out_shape=[jax.ShapeDtypeStruct(shape, kind) for shape, kind, spec in outs],
        input_output_aliases={1 + count + i: i for i in range(len(alias))},
        compiler_params=pltpu.CompilerParams(vmem_limit_bytes=room),
        cost_estimate=pl.CostEstimate(flops=int(2 * macs * weight), bytes_accessed=int(moved * weight), transcendentals=0),
    )(places, *[a for a, spec in ins], *alias, *after)


def mask_rows(seg_col, seg_row):
    return jnp.where(seg_col == seg_row, 0.0, -1e30)


def attend_heads(tok, w_rows, bias, seg_col, seg_row, qkv_ref, mix_ref, log_ref):
    width = w_rows.shape[0] // 3
    added = dot_tn(bias[:, : 2 * width], jnp.ones((bias.shape[0], tok.shape[0]), LOW))
    qkv = dot_nt(w_rows, tok)
    parts = (
        (qkv[:width] + added[:width]).astype(LOW),
        qkv[width : 2 * width].astype(LOW),
        (qkv[2 * width :] + added[width:]).astype(LOW),
    )
    for c in range(3):
        qkv_ref[c * width : (c + 1) * width] = parts[c]
    masked = mask_rows(seg_col, seg_row)
    for head in range(width // HEAD_DIM):
        q, k, v = (part[head * HEAD_DIM : (head + 1) * HEAD_DIM] for part in parts)
        scores = dot_tn(k, q) + masked
        top = jnp.max(scores, 0, keepdims=True)
        exponent = jnp.exp2((scores - top) * SCORE_SCALE)
        total = jnp.sum(exponent, 0, keepdims=True)
        attend = (exponent * (1.0 / total)).astype(LOW)
        mix_ref[head * HEAD_DIM : (head + 1) * HEAD_DIM] = dot(v, attend).astype(LOW)
        log_ref[head : head + 1] = top * SCORE_SCALE + jnp.log2(total)


def own_attention(places, tok, w, bias, seg_col, seg_row, qkv_ref, mix_ref, log_ref, w_ref):
    w_ref[...] = w[...]
    attend_heads(
        tok[...],
        w[: qkv_ref.shape[0]],
        bias[...],
        seg_col[...],
        seg_row[...],
        qkv_ref,
        mix_ref,
        log_ref,
    )


def far_attention(
    order, places, tok, pair, rest, pair_far, rest_far, bias, seg_col, seg_row,
    qkv_ref, mix_ref, log_ref, w_ref,
):
    first, second = order
    rows = pair.shape[1]
    me = places[0] * 2 + places[1]
    for other, held in enumerate(((pair, rest), (pair_far, rest_far))):
        for two, block in enumerate(held):
            for one in range(2):
                owner = me ^ (other + 2 * first * one + 2 * second * two)
                w_ref[pl.ds(pl.multiple_of(owner * rows, rows), rows)] = block[one]
    attend_heads(
        tok[...],
        w_ref[: qkv_ref.shape[0]],
        bias[...],
        seg_col[...],
        seg_row[...],
        qkv_ref,
        mix_ref,
        log_ref,
    )


def take_rows(places, rows, out):
    out[...] = rows[...]


def pair_rows(places, first, second, out):
    out[0] = first[...]
    out[1] = second[...]


def norm_stats(v):
    centred = v - jnp.mean(v, -1, keepdims=True)
    inv = lax.rsqrt(jnp.mean(centred * centred, -1, keepdims=True) + 1e-05)
    return centred * inv, inv


def norm_back(upstream, unit, inv, gain):
    scaled = upstream * gain
    inner = jnp.mean(scaled * unit, -1, keepdims=True)
    return inv * (scaled - jnp.mean(scaled, -1, keepdims=True) - unit * inner)


def gelu_both(pre):
    power = jnp.exp2(pre * pre * (-0.5 * LOG2E))
    base = 1.0 + TAIL_SLOPE * jnp.abs(pre)
    t = pl.reciprocal(base, approx=True)
    t = t * (2.0 - base * t)
    tail = TAIL[6] * t + TAIL[5]
    for c in TAIL[4::-1]:
        tail = tail * t + c
    tail = tail * (t * power)
    cumul = jnp.where(pre < 0.0, tail, 1.0 - tail)
    return (pre * cumul).astype(LOW), cumul + pre * (power * 0.3989422804014327)


def feed_forward(
    places, tok, mix, w_out, vectors,
    w_up, b_up, w_down, cot,
    send, own, ends, slope, unit1, inv1, res2, out, small,
    hidden, low, acts, down, sem,
):
    k = pl.program_id(0)
    half = send.shape[1]
    chunk = w_up.shape[1]
    core, z = places[1], places[2]
    heads = mix.shape[0]
    fetch = pltpu.make_async_copy(w_down, down, sem)
    b_out, gain1, shift1, b_down, gain2, shift2 = (vectors[i : i + 1] for i in range(6))

    @pl.when(k == 0)
    def _():
        fetch.start()
        attended = b_out
        for d in range(heads):
            attended = attended + dot_tn(mix[d], w_out[d])
        unit, inv = norm_stats(tok[...].astype(F32) + attended)
        unit1[...] = unit
        inv1[...] = inv
        one = unit * gain1 + shift1
        hidden[...] = one
        one_low = one.astype(LOW)
        low[...] = one_low
        ends[0] = one_low[:, :half]
        ends[1] = one_low[:, half:]

    @pl.when(k < heads)
    def _():
        start = (z ^ k) * chunk
        block = 256
        for j in range(chunk // block):
            at = slice(j * block, (j + 1) * block)
            pre = dot(low[...], w_up[:, at]) + b_up[:, at]
            act, tilt = gelu_both(pre)
            slope[:, at] = tilt
            acts[:, pl.ds(pl.multiple_of(start + j * block, block), block)] = act
        left = acts[:, pl.ds(pl.multiple_of(start, 128), half)]
        right = acts[:, pl.ds(pl.multiple_of(start + half, 128), half)]
        own[...] = jnp.where(core == 0, left, right)
        send[...] = jnp.where(core == 0, right, left)

    @pl.when(k == heads)
    def _():
        fetch.wait()
        unit, inv = norm_stats(hidden[...] + (dot(acts[...], down[...]) + b_down))
        out[...] = (unit * gain2 + shift2).astype(LOW)
        upstream = cot[...].astype(F32)
        grad = norm_back(upstream, unit, inv, gain2)
        res2[...] = grad
        grad_low = grad.astype(LOW)
        ends[2] = grad_low[:, :half]
        ends[3] = grad_low[:, half:]
        small[0:1] = jnp.sum(grad_low.astype(F32), 0, keepdims=True)
        small[1:2] = jnp.sum(upstream * unit, 0, keepdims=True)
        small[2:3] = jnp.sum(upstream, 0, keepdims=True)


def inner_back(places, ends, w_down, slope, send, own, bias, branch, inners):
    half = send.shape[1]
    core = places[1]

    @pl.when(pl.program_id(0) == 0)
    def _():
        branch[:, :half] = ends[0]
        branch[:, half:] = ends[1]

    block = 256
    for j in range(inners.shape[1] // block):
        at = slice(j * block, (j + 1) * block)
        inner = (dot_nt(branch[...], w_down[at]) * slope[:, at]).astype(LOW)
        inners[:, at] = inner
        bias[:, at] = jnp.sum(inner.astype(F32), 0, keepdims=True)
    first, second = inners[:, :half], inners[:, half:]
    own[...] = jnp.where(core == 0, first, second)
    send[...] = jnp.where(core == 0, second, first)


def hidden_back(
    places, own, sent, w_up, res2, unit1, inv1, vectors, send, res1, low, small, acc
):
    k = pl.program_id(0)
    core = places[1]
    half = own.shape[1]
    mine, other = own[...], sent[...]
    inner = jnp.concatenate(
        [jnp.where(core == 0, mine, other), jnp.where(core == 0, other, mine)], 1
    )
    product = dot_nt(inner, w_up[...])

    @pl.when(k == 0)
    def _():
        acc[...] = res2[...] + product

    @pl.when(k > 0)
    def _():
        acc[...] += product

    @pl.when(k == pl.num_programs(0) - 1)
    def _():
        grad = acc[...]
        result = norm_back(grad, unit1[...], inv1[...], vectors[1:2])
        res1[...] = result
        result_low = result.astype(LOW)
        low[...] = result_low
        send[...] = jnp.where(core == 0, result_low[:, half:], result_low[:, :half])
        small[0:1] = jnp.sum(result_low.astype(F32), 0, keepdims=True)
        small[1:2] = jnp.sum(grad * unit1[...], 0, keepdims=True)
        small[2:3] = jnp.sum(grad, 0, keepdims=True)


def attention_back(places, qkv, w_out, grad, log_ref, seg_col, seg_row, rows_ref, bias_ref):
    width = qkv.shape[0] // 3
    grad_mixed = dot_nt(w_out[...], grad[...]).astype(LOW)
    masked = mask_rows(seg_col[...], seg_row[...])
    scale = HEAD_DIM ** (-0.5)
    for head in range(width // HEAD_DIM):
        places_of = [c * width + head * HEAD_DIM for c in range(3)]
        q, k, v = (qkv[at : at + HEAD_DIM] for at in places_of)
        g = grad_mixed[head * HEAD_DIM : (head + 1) * HEAD_DIM]
        scores = dot_tn(k, q) + masked
        attend = jnp.exp2(scores * SCORE_SCALE - log_ref[head : head + 1])
        attend_low = attend.astype(LOW)
        grad_v = dot_nt(g, attend_low)
        product = attend * dot_tn(v, g)
        inner = jnp.sum(product, 0, keepdims=True)
        grad_scores = (product - attend * inner).astype(LOW)
        grad_q = dot(k, grad_scores) * scale
        grad_k = dot_nt(q, grad_scores) * scale
        for at, value in zip(places_of, (grad_q, grad_k, grad_v)):
            rows_ref[at : at + HEAD_DIM] = value.astype(LOW)
    ones = jnp.ones((8, rows_ref.shape[1]), LOW)
    bias_ref[...] = dot_nt(ones, rows_ref[...])


def split_rows(value, high, send, keep):
    rows = value.shape[0] // 2
    low = value.astype(LOW)
    send[...] = jnp.where(high, low[:rows], low[rows:])
    keep[...] = jnp.where(high, low[rows:], low[:rows])


def is_high(places, bit):
    return (places[0] & bit) != 0


def ffn_grad(bit, places, units, units_far, ends, ends_far, send, keep, near, far):
    half = ends.shape[2]

    @pl.when(pl.program_id(0) == 0)
    def _():
        for side in range(2):
            rows = slice(side * half, (side + 1) * half)
            near[rows] = ends[side].T
            far[rows] = ends_far[side].T

    total = dot(near[...], units[...]) + dot(far[...], units_far[...])
    split_rows(total, is_high(places, bit), send, keep)


def attn_grad(
    places, rows, rows_far, tok, tok_far, mix, mix_far, grad, grad_far,
    small_one, small_two, up_bias, qkv_bias, send_x, keep_x, send_y, keep_y,
):
    width = mix.shape[0]
    half = tok.shape[1]
    qkv = dot(rows[...], tok[...]) + dot(rows_far[...], tok_far[...])
    out = dot(mix[...], grad[...]) + dot(mix_far[...], grad_far[...])
    lines = []
    for held in (small_one, small_two):
        for i in range(3):
            lines += [held[i : i + 1, :half], held[i : i + 1, half:]]
    lines += [up_bias[:, :half], up_bias[:, half:]]
    lines.append(jnp.concatenate([qkv_bias[0:1, :width], qkv_bias[0:1, 2 * width :]], 1))
    lines.append(jnp.zeros((EXTRA - len(lines), half), F32))
    split_rows(qkv[: 2 * width], is_high(places, 1), send_x, keep_x)
    split_rows(jnp.concatenate([qkv[2 * width :], out] + lines, 0), is_high(places, 2), send_y, keep_y)


def add_split(bits, places, *refs):
    for i, bit in enumerate(bits):
        keep, came = refs[2 * i : 2 * i + 2]
        send, left = refs[2 * (len(bits) + i) : 2 * (len(bits) + i) + 2]
        for d in range(keep.shape[0]):
            total = keep[d].astype(F32) + came[d].astype(F32)
            split_rows(total, is_high(places, bit), send.at[d], left.at[d])


def add_parts(places, keep_a, came_a, keep_b, came_b, *outs):
    rows = keep_a.shape[1]
    for d, out in enumerate(outs):
        out[:rows] = (keep_a[d].astype(F32) + came_a[d].astype(F32)).astype(LOW)
        out[rows:] = (keep_b[d].astype(F32) + came_b[d].astype(F32)).astype(LOW)


def add_heads(places, *refs):
    total = refs[0][...].astype(F32)
    for ref in refs[1:-1]:
        total = total + ref[...].astype(F32)
    refs[-1][...] = total.astype(LOW)


def input_sum(places, rows, w, res1, out):
    total = dot_tn(rows[...], w[...])
    k = pl.program_id(0)
    out[...] = jnp.where(k == 0, res1[...], out[...]) + total


def place_pieces(places, held, full, layouts):
    pair, rest, pair_far, rest_far = held
    near, core = places[0], places[1]
    width = pair.shape[2]
    for one in range(2):
        for two in range(2):
            chip = near ^ (one + 2 * two)
            mine = (rest if two else pair)[one]
            other = (rest_far if two else pair_far)[one]
            sides = (jnp.where(core == 0, mine, other), jnp.where(core == 0, other, mine))
            for at, rows, start, outer in layouts:
                low_bit, high_bit = chip & 1, chip >> 1
                order = 2 * low_bit + high_bit if outer == 1 else 2 * high_bit + low_bit
                to = pl.multiple_of(start + order * rows, 16)
                for side in range(2):
                    full[pl.ds(to, rows), side * width : (side + 1) * width] = sides[side][
                        at : at + rows
                    ].astype(F32)


def ffn_place(places, pair, rest, pair_far, rest_far, down, up, full):
    rows = pair.shape[1] // 2
    held = (pair, rest, pair_far, rest_far)
    place_pieces(places, held, full, [(0, rows, 0, 1)])
    down[...] = full[...].T
    place_pieces(places, held, up, [(rows, rows, 0, 2)])


def attn_place(
    places, pair, rest, pair_far, rest_far, qkv, w_out, small, up_bias, qv_bias, full
):
    width = pair.shape[2]
    count = w_out.shape[0]
    rows = count // 2
    more = pair.shape[1] - rows
    place_pieces(
        places,
        (pair, rest, pair_far, rest_far),
        full,
        [(0, rows, 0, 1), (rows, more, 4 * rows, 2)],
    )
    for c in range(3):
        qkv[c] = full[c * count : (c + 1) * count].T
    w_out[...] = full[3 * count : 4 * count]
    at = 4 * count
    lines = full[at : at + 16, :width] + full[at : at + 16, width:]
    for i in range(6):
        small[i : i + 1, :width] = lines[2 * i : 2 * i + 1]
        small[i : i + 1, width:] = lines[2 * i + 1 : 2 * i + 2]
    up_bias[:, :width] = lines[12:13]
    up_bias[:, width:] = lines[13:14]
    qv_bias[0:1] = lines[14:15, :count]
    qv_bias[1:2] = lines[14:15, count : 2 * count]


def bias_parts(values):
    rows, rest = [], values
    for _ in range(3):
        rows.append(lax.reduce_precision(rest, 8, 7))
        rest = rest - rows[-1]
    return jnp.stack(rows).astype(LOW)


def sum_heads(parts, places):
    got = [parts[0]] + [swap(parts[d], "head", d) for d in range(1, len(parts))]
    shape = parts[0].shape
    ins = [(g, whole(shape)) for g in got]
    (total,) = run(add_heads, places, (1,), ins, [(shape, LOW, whole(shape))])
    bit = 1
    while bit < lax.axis_size("far"):
        total = (total.astype(F32) + swap(total, "far", bit).astype(F32)).astype(LOW)
        bit *= 2
    return total


def gather_back(piece):
    pair = jnp.stack([piece, swap(piece, "near", 1)])
    rest = swap(pair, "near", 2)
    held = [pair, rest, swap_core(pair), swap_core(rest)]
    return [(h, whole(h.shape)) for h in held]


def per_device(
    tokens,
    segment_ids,
    w_qkv,
    b_qv,
    w_out,
    b_out,
    ln1_gain,
    ln1_bias,
    w_up,
    b_up,
    w_down,
    b_down,
    ln2_gain,
    ln2_bias,
    cotangent,
):
    width = tokens.shape[1]
    own_rows = cotangent.shape[0]
    local_width = w_qkv.shape[2]
    heads = lax.axis_size("head")
    z = lax.axis_index("head")
    core = lax.axis_index("core")
    near = lax.axis_index("near")
    hidden_units = w_up.shape[1]
    chunk = hidden_units // heads
    half = width // 2
    rows3 = 3 * local_width
    places = jnp.stack([near, core, z]).astype(jnp.int32)

    shard = jnp.concatenate([w_qkv.transpose(0, 2, 1).reshape(rows3, width), w_out], 0)
    piece_rows = shard.shape[0] // 8
    bias = jnp.pad(bias_parts(b_qv.reshape(-1)), ((0, 13), (0, width - 2 * local_width)))
    piece = lax.dynamic_slice_in_dim(shard, (near * 2 + core) * piece_rows, piece_rows, 0)
    piece = jnp.concatenate([piece, bias], 0)
    first_hop = [swap(piece, "head", d) for d in range(1, heads)]

    seg = lax.dynamic_slice_in_dim(segment_ids, z * own_rows, own_rows, 0)
    segs = [
        (seg[:, None], whole((own_rows, 1))),
        (seg[None], whole((1, own_rows))),
    ]
    own_tokens = (tokens, pl.BlockSpec((own_rows, width), lambda k, s: (s[2], 0)))

    def attend_outs(first):
        def spec(*shape):
            return pl.BlockSpec((None,) + shape, lambda k, s: (k + first, 0, 0))

        return [
            ((heads, rows3, own_rows), LOW, spec(rows3, own_rows)),
            ((heads, local_width, own_rows), LOW, spec(local_width, own_rows)),
            ((heads, 8, own_rows), F32, spec(8, own_rows)),
            ((heads, rows3 + local_width, width), LOW, spec(rows3 + local_width, width)),
        ]

    macs = rows3 * width * own_rows + 6 * own_rows * own_rows * 256
    ins = [own_tokens, (shard, whole(shard.shape)), (bias, whole(bias.shape))] + segs
    made = begun = run(own_attention, places, (1,), ins, attend_outs(0), macs=macs)
    block = pl.BlockSpec((piece_rows, width), lambda k, s: (0, 0))
    mines = []
    for d in range(1, heads):
        mines += run(
            take_rows, places, (1,), [(first_hop[d - 1], block)],
            [((piece_rows, width), LOW, block)], after=[begun[0]] + mines, weight=0.01,
        )
    orders = [(1, 2) if d % 2 else (2, 1) for d in range(heads)]
    nexts = [swap(mines[d - 1], "near", orders[d][0]) for d in range(1, heads)]
    for d in range(1, heads):
        order = orders[d]
        ins = [(mines[d - 1], block), (nexts[d - 1], block)]
        twice = (2, piece_rows, width)
        (pair,) = run(
            pair_rows, places, (1,), ins, [(twice, LOW, whole(twice))],
            after=nexts[d : d + 1] + mines[d + 1 :], weight=0.01,
        )
        rest = swap(pair, "near", order[1])
        held = [pair, rest, swap_core(pair), swap_core(rest)]
        ins = [own_tokens] + [(h, whole(h.shape)) for h in held]
        ins += [(first_hop[d - 1], pl.BlockSpec((16, width), lambda k, s: (piece_rows // 16, 0)))]
        kernel = functools.partial(far_attention, order)
        made = run(kernel, places, (1,), ins + segs, attend_outs(d), macs=macs, alias=made)
    qkvs, mixes, logs, weights = made

    vectors = jnp.stack([b_out, ln1_gain, ln1_bias, b_down, ln2_gain, ln2_bias])

    tok_send = lax.dynamic_slice(tokens, (z * own_rows, (1 - core) * half), (own_rows, half))
    tok_far = swap_core(tok_send)
    mixes_far = swap_core(mixes)

    def by_step(*shape):
        block = (None,) + shape
        return pl.BlockSpec(block, lambda k, s: (jnp.minimum(k, heads - 1),) + (0,) * len(shape))

    def unit_at(k, s):
        return s[2] ^ jnp.minimum(k, heads - 1)


    square = (own_rows, width)
    tile = by_step(own_rows, half)
    tiles = (heads, own_rows, half)
    up_block = (w_up, pl.BlockSpec((width, chunk), lambda k, s: (0, unit_at(k, s))))
    down_block = (w_down, pl.BlockSpec((chunk, width), lambda k, s: (unit_at(k, s), 0)))
    line_block = pl.BlockSpec((None, 1, chunk), lambda k, s: (unit_at(k, s), 0, 0))

    def weight_rows(rows, index):
        return (weights, pl.BlockSpec((None, rows, width), lambda k, s: (k, index, 0)))

    ins = [
        own_tokens,
        (mixes, whole(mixes.shape)),
        (weights, pl.BlockSpec((heads, local_width, width), lambda k, s: (0, 3, 0))),
        (vectors, whole(vectors.shape)),
        up_block,
        (b_up.reshape(heads, 1, chunk), line_block),
        (w_down, pl.BlockSpec(memory_space=pl.ANY)),
        (cotangent, whole(square)),
    ]
    outs = [
        (tiles, LOW, tile),
        (tiles, LOW, tile),
        ((4, own_rows, half), LOW, whole((4, own_rows, half))),
        ((heads, own_rows, chunk), F32, by_step(own_rows, chunk)),
        (square, F32, whole(square)),
        ((own_rows, 1), F32, whole((own_rows, 1))),
        (square, F32, whole(square)),
        (square, LOW, whole(square)),
        ((8, width), F32, whole((8, width))),
    ]
    scratch = [
        pltpu.VMEM(square, F32),
        pltpu.VMEM(square, LOW),
        pltpu.VMEM((own_rows, hidden_units), LOW),
        pltpu.VMEM(w_down.shape, LOW),
        pltpu.SemaphoreType.DMA,
    ]
    ffn_macs = 2 * own_rows * width * hidden_units
    act_send, act_own, ends, slope, unit1, inv1, res2, layer_output, small_two = run(
        feed_forward, places, (heads + 1,), ins, outs, scratch, ffn_macs
    )
    act_far = swap_core(act_send)
    ends_far = swap_core(ends)

    def two_of(array, index):
        return (array, pl.BlockSpec((2, own_rows, half), lambda k, s: (index, 0, 0)))

    ins = [two_of(ends, 1), down_block, (slope, by_step(own_rows, chunk))]
    outs = [(tiles, LOW, tile), (tiles, LOW, tile), ((heads, 1, chunk), F32, line_block)]
    scratch = [pltpu.VMEM(square, LOW), pltpu.VMEM((own_rows, chunk), LOW)]
    inner_send, inner_own, up_bias = run(
        inner_back, places, (heads,), ins, outs, scratch, ffn_macs // 2,
        after=[tok_far, mixes_far],
    )
    inner_far = swap_core(inner_send)

    def unit_outs(rows):
        return [((heads, rows, half), LOW, by_step(rows, half))] * 2

    flipped = [pltpu.VMEM((width, own_rows), LOW)] * 2
    ins = [(act_own, tile), (act_far, tile), two_of(ends, 1), two_of(ends_far, 1)]
    d_send, d_keep = run(
        functools.partial(ffn_grad, 1), places, (heads,), ins, unit_outs(half), flipped,
        ffn_macs // 2, after=[inner_send],
    )
    d_came = swap(d_send, "near", 1)

    ins = [(inner_own, tile), (inner_far, tile), two_of(ends, 0), two_of(ends_far, 0)]
    u_send, u_keep = run(
        functools.partial(ffn_grad, 2), places, (heads,), ins, unit_outs(half), flipped,
        ffn_macs // 2, after=[d_send],
    )
    u_came = swap(u_send, "near", 2)

    ins = [
        (inner_own, tile),
        (inner_send, tile),
        up_block,
        (res2, whole(square)),
        (unit1, whole(square)),
        (inv1, whole((own_rows, 1))),
        (vectors, whole(vectors.shape)),
    ]
    outs = [
        ((own_rows, half), LOW, whole((own_rows, half))),
        (square, F32, whole(square)),
        (square, LOW, whole(square)),
        ((8, width), F32, whole((8, width))),
    ]
    grad_send, res1, grad_attended, small_one = run(
        hidden_back, places, (heads,), ins, outs, [pltpu.VMEM(square, F32)], ffn_macs // 2,
        after=[u_send], weight=0.01,
    )
    grad_far = swap_core(grad_send)

    ins = [
        (qkvs, by_step(rows3, own_rows)),
        weight_rows(local_width, 3),
        (grad_attended, whole(square)),
        (logs, by_step(8, own_rows)),
    ] + segs
    outs = [
        ((heads, rows3, own_rows), LOW, by_step(rows3, own_rows)),
        ((heads, 8, rows3), F32, by_step(8, rows3)),
    ]
    grad_rows, qkv_bias = run(
        attention_back, places, (heads,), ins, outs, weight=8,
        macs=heads * (15 * own_rows * own_rows * 256 + local_width * own_rows * width),
    )
    rows_far = swap_core(grad_rows)

    def second(bits, pairs, after):
        ins = [(a, whole(a.shape)) for pair in pairs for a in pair]
        outs = []
        for keep, came in pairs:
            shape = (heads, keep.shape[1] // 2, half)
            outs += [(shape, LOW, whole(shape))] * 2
        kernel = functools.partial(add_split, bits)
        return run(kernel, places, (1,), ins, outs, after=after)

    def third(keep_a, came_a, keep_b, came_b, after):
        held = (keep_a, came_a, keep_b, came_b)
        shape = (keep_a.shape[1] + keep_b.shape[1], half)
        return sum_heads(
            run(
                add_parts,
                places,
                (1,),
                [(a, whole(a.shape)) for a in held],
                [(shape, LOW, whole(shape))] * heads,
                after=after,
            ),
            places,
        )

    d_send, d_keep, u_send, u_keep = second(
        (2, 1), [(d_keep, d_came), (u_keep, u_came)], [grad_rows]
    )
    d_came = swap(d_send, "near", 2)
    u_came = swap(u_send, "near", 1)

    ins = [(grad_rows, by_step(rows3, own_rows)), weight_rows(rows3, 0), (res1, whole(square))]
    outs = [(square, F32, whole(square))]
    (input_grad,) = run(
        input_sum, places, (heads,), ins, outs, macs=heads * own_rows * rows3 * width,
        after=[d_send],
    )

    ins = [
        (grad_rows, by_step(rows3, own_rows)),
        (rows_far, by_step(rows3, own_rows)),
        (tokens, pl.BlockSpec((own_rows, half), lambda k, s: (s[2], s[1]))),
        (tok_far, whole((own_rows, half))),
        (mixes, by_step(local_width, own_rows)),
        (mixes_far, by_step(local_width, own_rows)),
        (grad_attended, pl.BlockSpec((own_rows, half), lambda k, s: (0, s[1]))),
        (grad_far, whole((own_rows, half))),
        (small_one, whole((8, width))),
        (small_two, whole((8, width))),
        (up_bias, line_block),
        (qkv_bias, by_step(8, rows3)),
    ]
    x_rows = local_width
    y_rows = local_width + EXTRA // 2
    outs = unit_outs(x_rows) + unit_outs(y_rows)
    x_send, x_keep, y_send, y_keep = run(
        attn_grad, places, (heads,), ins, outs, macs=8 * width * own_rows * half,
        after=[input_grad],
    )
    x_came = swap(x_send, "near", 1)
    y_came = swap(y_send, "near", 2)

    ffn_piece = third(d_keep, d_came, u_keep, u_came, [x_send])
    x_send, x_keep, y_send, y_keep = second(
        (2, 1), [(x_keep, x_came), (y_keep, y_came)], [ffn_piece]
    )
    x_came = swap(x_send, "near", 2)
    y_came = swap(y_send, "near", 1)
    attn_piece = third(x_keep, x_came, y_keep, y_came, [])

    outs = [(shape, F32, whole(shape)) for shape in ((chunk, width), (width, chunk))]
    grad_down, grad_up = run(
        ffn_place, places, (1,), gather_back(ffn_piece), outs, [pltpu.VMEM((width, chunk), F32)]
    )
    shapes = [
        (3, width, local_width),
        (local_width, width),
        (6, width),
        (1, chunk),
        (2, local_width),
    ]
    grad_qkv, grad_out, grad_small, grad_up_bias, grad_qv_bias = run(
        attn_place,
        places,
        (1,),
        gather_back(attn_piece),
        [(shape, F32, whole(shape)) for shape in shapes],
        [pltpu.VMEM((width + EXTRA, width), F32)],
    )
    return (
        layer_output,
        input_grad,
        grad_qkv,
        grad_qv_bias,
        grad_out,
        grad_up,
        grad_up_bias[0],
        grad_down,
        grad_small,
    )


def solution(mesh):
    batch, heads = mesh.devices.shape
    mesh = Mesh(
        mesh.devices.reshape(batch // 8, 4, 2, heads), ("far", "near", "core", "head")
    )
    group = ("far", "near", "core")
    everyone = group + ("head",)
    in_specs = (
        P(group, None),
        P(group),
        P(None, None, "head"),
        P(None, "head"),
        P("head", None),
        P(),
        P(),
        P(),
        P(),
        P(),
        P(),
        P(),
        P(),
        P(),
        P(everyone, None),
    )
    out_specs = (
        P(everyone, None),
        P(everyone, None),
        P(None, None, "head"),
        P(None, "head"),
        P("head", None),
        P(None, "head"),
        P("head"),
        P("head", None),
        P(),
    )
    return jax.shard_map(
        per_device, mesh=mesh, in_specs=in_specs, out_specs=out_specs, check_vma=False
    )
```

```python
import functools
import math

import jax
import jax.numpy as jnp
from jax import lax
from jax.experimental import pallas as pl
from jax.experimental.pallas import tpu as pltpu
from jax.sharding import Mesh
from jax.sharding import PartitionSpec as P

HEAD_DIM = 64
SLOT = 512
LOW = jnp.bfloat16
F32 = jnp.float32
LOG2E = math.log2(math.e)
SCORE_SCALE = HEAD_DIM ** (-0.5) * LOG2E
SPARE_BYTES = 12 * 2**20
EXTRA = 64
LIGHT = 0.01
CHAIN = []
TAIL_SLOPE = 0.36
TAIL = (
    0.14371304537508633,
    0.14177245466203425,
    0.1397192603907239,
    0.026549325413860486,
    0.18095403134327948,
    -0.1797647161697652,
    0.047056295581175855,
)


def swap(value, axis, bit):
    size = lax.axis_size(axis)
    return lax.ppermute(value, axis, [(i, i ^ bit) for i in range(size)])


def swap_core(value):
    return swap(value, "core", 1)


def dot(a, b):
    return jnp.dot(a, b, preferred_element_type=F32)


def dot_nt(a, b):
    return lax.dot_general(a, b, (((1,), (1,)), ((), ())), preferred_element_type=F32)


def dot_tn(a, b):
    return lax.dot_general(a, b, (((0,), (0,)), ((), ())), preferred_element_type=F32)


def whole(shape):
    return pl.BlockSpec(shape, lambda *args: (0,) * len(shape))


def run(kernel, places, grid, ins, outs, scratch=(), macs=0, after=(), alias=(), weight=8):
    moved = sum(a.size * a.dtype.itemsize for a, spec in ins)
    moved += sum(math.prod(shape) * jnp.dtype(kind).itemsize for shape, kind, spec in outs)
    after = list(after) + CHAIN
    count, unread = len(ins), len(alias) + len(after)

    def body(places, *refs):
        kernel(places, *refs[:count], *refs[count + unread :])

    held = pl.BlockSpec(memory_space=pl.ANY)
    room = SPARE_BYTES
    for shape, kind, spec in outs + [(a.shape, a.dtype, spec) for a, spec in ins]:
        if spec.block_shape is not None:
            block = math.prod(1 if n is None else n for n in spec.block_shape)
            room += 2 * block * jnp.dtype(kind).itemsize
    for ref in scratch:
        if hasattr(ref, "shape") and ref.shape:
            room += math.prod(ref.shape) * jnp.dtype(ref.dtype).itemsize
    made = pl.pallas_call(
        body,
        name=getattr(kernel, "func", kernel).__name__,
        grid_spec=pltpu.PrefetchScalarGridSpec(
            num_scalar_prefetch=1,
            grid=grid,
            in_specs=[spec for a, spec in ins] + [held] * unread,
            out_specs=[spec for shape, kind, spec in outs],
            scratch_shapes=list(scratch),
        ),
        out_shape=[jax.ShapeDtypeStruct(shape, kind) for shape, kind, spec in outs],
        input_output_aliases={1 + count + i: i for i in range(len(alias))},
        compiler_params=pltpu.CompilerParams(vmem_limit_bytes=room),
        cost_estimate=pl.CostEstimate(flops=int(2 * macs * weight), bytes_accessed=int(moved * weight), transcendentals=0),
    )(places, *[a for a, spec in ins], *alias, *after)
    CHAIN[:] = made[:1]
    return made


def mask_rows(seg_col, seg_row):
    return jnp.where(seg_col == seg_row, 0.0, -1e30)


def attend_heads(tok, w_rows, bias, seg_col, seg_row, qkv_ref, mix_ref, log_ref):
    width = w_rows.shape[0] // 3
    added = dot_tn(bias[:, : 2 * width], jnp.ones((bias.shape[0], tok.shape[0]), LOW))
    qkv = dot_nt(w_rows, tok)
    parts = (
        (qkv[:width] + added[:width]).astype(LOW),
        qkv[width : 2 * width].astype(LOW),
        (qkv[2 * width :] + added[width:]).astype(LOW),
    )
    for c in range(3):
        qkv_ref[c * width : (c + 1) * width] = parts[c]
    masked = mask_rows(seg_col, seg_row)
    for head in range(width // HEAD_DIM):
        q, k, v = (part[head * HEAD_DIM : (head + 1) * HEAD_DIM] for part in parts)
        scores = dot_tn(k, q) + masked
        top = jnp.max(scores, 0, keepdims=True)
        exponent = jnp.exp2((scores - top) * SCORE_SCALE)
        total = jnp.sum(exponent, 0, keepdims=True)
        attend = (exponent * (1.0 / total)).astype(LOW)
        mix_ref[head * HEAD_DIM : (head + 1) * HEAD_DIM] = dot(v, attend).astype(LOW)
        log_ref[head : head + 1] = top * SCORE_SCALE + jnp.log2(total)


def own_attention(places, tok, w, bias, seg_col, seg_row, qkv_ref, mix_ref, log_ref, w_ref):
    w_ref[...] = w[...]
    attend_heads(
        tok[...],
        w[: qkv_ref.shape[0]],
        bias[...],
        seg_col[...],
        seg_row[...],
        qkv_ref,
        mix_ref,
        log_ref,
    )


def far_attention(
    order, places, tok, pair, rest, pair_far, rest_far, bias, seg_col, seg_row,
    qkv_ref, mix_ref, log_ref, w_ref,
):
    first, second = order
    rows = pair.shape[1]
    me = places[0] * 2 + places[1]
    for other, held in enumerate(((pair, rest), (pair_far, rest_far))):
        for two, block in enumerate(held):
            for one in range(2):
                owner = me ^ (other + 2 * first * one + 2 * second * two)
                w_ref[pl.ds(pl.multiple_of(owner * rows, rows), rows)] = block[one]
    attend_heads(
        tok[...],
        w_ref[: qkv_ref.shape[0]],
        bias[...],
        seg_col[...],
        seg_row[...],
        qkv_ref,
        mix_ref,
        log_ref,
    )


def take_rows(places, rows, out):
    out[...] = rows[...]


def pair_rows(places, first, second, out):
    out[0] = first[...]
    out[1] = second[...]


def norm_stats(v):
    centred = v - jnp.mean(v, -1, keepdims=True)
    inv = lax.rsqrt(jnp.mean(centred * centred, -1, keepdims=True) + 1e-05)
    return centred * inv, inv


def norm_back(upstream, unit, inv, gain):
    scaled = upstream * gain
    inner = jnp.mean(scaled * unit, -1, keepdims=True)
    return inv * (scaled - jnp.mean(scaled, -1, keepdims=True) - unit * inner)


def gelu_both(pre):
    power = jnp.exp2(pre * pre * (-0.5 * LOG2E))
    base = 1.0 + TAIL_SLOPE * jnp.abs(pre)
    t = pl.reciprocal(base, approx=True)
    t = t * (2.0 - base * t)
    tail = TAIL[6] * t + TAIL[5]
    for c in TAIL[4::-1]:
        tail = tail * t + c
    tail = tail * (t * power)
    cumul = jnp.where(pre < 0.0, tail, 1.0 - tail)
    return (pre * cumul).astype(LOW), cumul + pre * (power * 0.3989422804014327)


def feed_forward(
    places, tok, mix, w_out, vectors,
    w_up, b_up, w_down, cot,
    send, own, ends, slope, unit1, inv1, res2, out, small,
    hidden, low, acts, down, sem,
):
    k = pl.program_id(0)
    half = send.shape[1]
    chunk = w_up.shape[1]
    core, z = places[1], places[2]
    heads = mix.shape[0]
    fetch = pltpu.make_async_copy(w_down, down, sem)
    b_out, gain1, shift1, b_down, gain2, shift2 = (vectors[i : i + 1] for i in range(6))

    @pl.when(k == 0)
    def _():
        fetch.start()
        attended = b_out
        for d in range(heads):
            attended = attended + dot_tn(mix[d], w_out[d])
        unit, inv = norm_stats(tok[...].astype(F32) + attended)
        unit1[...] = unit
        inv1[...] = inv
        one = unit * gain1 + shift1
        hidden[...] = one
        one_low = one.astype(LOW)
        low[...] = one_low
        ends[0] = one_low[:, :half]
        ends[1] = one_low[:, half:]

    @pl.when(k < heads)
    def _():
        start = (z ^ k) * chunk
        block = 256
        for j in range(chunk // block):
            at = slice(j * block, (j + 1) * block)
            pre = dot(low[...], w_up[:, at]) + b_up[:, at]
            act, tilt = gelu_both(pre)
            slope[:, at] = tilt
            acts[:, pl.ds(pl.multiple_of(start + j * block, block), block)] = act
        left = acts[:, pl.ds(pl.multiple_of(start, 128), half)]
        right = acts[:, pl.ds(pl.multiple_of(start + half, 128), half)]
        own[...] = jnp.where(core == 0, left, right)
        send[...] = jnp.where(core == 0, right, left)

    @pl.when(k == heads)
    def _():
        fetch.wait()
        unit, inv = norm_stats(hidden[...] + (dot(acts[...], down[...]) + b_down))
        out[...] = (unit * gain2 + shift2).astype(LOW)
        upstream = cot[...].astype(F32)
        grad = norm_back(upstream, unit, inv, gain2)
        res2[...] = grad
        grad_low = grad.astype(LOW)
        ends[2] = grad_low[:, :half]
        ends[3] = grad_low[:, half:]
        small[0:1] = jnp.sum(grad_low.astype(F32), 0, keepdims=True)
        small[1:2] = jnp.sum(upstream * unit, 0, keepdims=True)
        small[2:3] = jnp.sum(upstream, 0, keepdims=True)


def inner_back(places, ends, w_down, slope, send, own, bias, branch, inners):
    half = send.shape[1]
    core = places[1]

    @pl.when(pl.program_id(0) == 0)
    def _():
        branch[:, :half] = ends[0]
        branch[:, half:] = ends[1]

    block = 256
    for j in range(inners.shape[1] // block):
        at = slice(j * block, (j + 1) * block)
        inner = (dot_nt(branch[...], w_down[at]) * slope[:, at]).astype(LOW)
        inners[:, at] = inner
        bias[:, at] = jnp.sum(inner.astype(F32), 0, keepdims=True)
    first, second = inners[:, :half], inners[:, half:]
    own[...] = jnp.where(core == 0, first, second)
    send[...] = jnp.where(core == 0, second, first)


def hidden_back(
    places, own, sent, w_up, res2, unit1, inv1, vectors, send, res1, low, small, acc
):
    k = pl.program_id(0)
    core = places[1]
    half = own.shape[1]
    mine, other = own[...], sent[...]
    inner = jnp.concatenate(
        [jnp.where(core == 0, mine, other), jnp.where(core == 0, other, mine)], 1
    )
    product = dot_nt(inner, w_up[...])

    @pl.when(k == 0)
    def _():
        acc[...] = res2[...] + product

    @pl.when(k > 0)
    def _():
        acc[...] += product

    @pl.when(k == pl.num_programs(0) - 1)
    def _():
        grad = acc[...]
        result = norm_back(grad, unit1[...], inv1[...], vectors[1:2])
        res1[...] = result
        result_low = result.astype(LOW)
        low[...] = result_low
        send[...] = jnp.where(core == 0, result_low[:, half:], result_low[:, :half])
        small[0:1] = jnp.sum(result_low.astype(F32), 0, keepdims=True)
        small[1:2] = jnp.sum(grad * unit1[...], 0, keepdims=True)
        small[2:3] = jnp.sum(grad, 0, keepdims=True)


def attention_back(places, qkv, w_out, grad, log_ref, seg_col, seg_row, rows_ref, bias_ref):
    width = qkv.shape[0] // 3
    grad_mixed = dot_nt(w_out[...], grad[...]).astype(LOW)
    masked = mask_rows(seg_col[...], seg_row[...])
    scale = HEAD_DIM ** (-0.5)
    for head in range(width // HEAD_DIM):
        places_of = [c * width + head * HEAD_DIM for c in range(3)]
        q, k, v = (qkv[at : at + HEAD_DIM] for at in places_of)
        g = grad_mixed[head * HEAD_DIM : (head + 1) * HEAD_DIM]
        scores = dot_tn(k, q) + masked
        attend = jnp.exp2(scores * SCORE_SCALE - log_ref[head : head + 1])
        attend_low = attend.astype(LOW)
        grad_v = dot_nt(g, attend_low)
        product = attend * dot_tn(v, g)
        inner = jnp.sum(product, 0, keepdims=True)
        grad_scores = (product - attend * inner).astype(LOW)
        grad_q = dot(k, grad_scores) * scale
        grad_k = dot_nt(q, grad_scores) * scale
        for at, value in zip(places_of, (grad_q, grad_k, grad_v)):
            rows_ref[at : at + HEAD_DIM] = value.astype(LOW)
    ones = jnp.ones((8, rows_ref.shape[1]), LOW)
    bias_ref[...] = dot_nt(ones, rows_ref[...])


def split_rows(value, high, send, keep):
    rows = value.shape[0] // 2
    low = value.astype(LOW)
    send[...] = jnp.where(high, low[:rows], low[rows:])
    keep[...] = jnp.where(high, low[rows:], low[:rows])


def is_high(places, bit):
    return (places[0] & bit) != 0


def unit_rows(places, units, units_far, ends, ends_far, near, far):
    half = ends.shape[2]

    @pl.when(pl.program_id(0) == 0)
    def _():
        for side in range(2):
            rows = slice(side * half, (side + 1) * half)
            near[rows] = ends[side].T
            far[rows] = ends_far[side].T

    return dot(near[...], units[...]) + dot(far[...], units_far[...])


def split_both(places, total, outs):
    rows = outs[0].shape[0] * 2
    split_rows(total[:rows], is_high(places, 1), *outs[:2])
    split_rows(total[rows:], is_high(places, 2), *outs[2:])


def down_grad(places, units, units_far, ends, ends_far, send, keep, near, far):
    total = unit_rows(places, units, units_far, ends, ends_far, near, far).astype(LOW)
    odd = lax.rem(pl.program_id(0), 2)

    @pl.when(odd == 0)
    def _():
        keep[...] = total

    @pl.when(odd == 1)
    def _():
        send[...] = total


def up_grad(places, units, units_far, ends, ends_far, *refs):
    total = unit_rows(places, units, units_far, ends, ends_far, *refs[4:])
    split_both(places, total, refs[:4])


def add_both(places, keep, came, *outs):
    for d in range(keep.shape[0]):
        total = keep[d].astype(F32) + came[d].astype(F32)
        split_both(places, total, [out.at[d] for out in outs])


def attn_grad(
    places, rows, rows_far, tok, tok_far, mix, mix_far, grad, grad_far,
    small_one, small_two, up_bias, qkv_bias, send_x, keep_x, send_y, keep_y,
):
    width = mix.shape[0]
    half = tok.shape[1]
    qkv = dot(rows[...], tok[...]) + dot(rows_far[...], tok_far[...])
    out = dot(mix[...], grad[...]) + dot(mix_far[...], grad_far[...])
    lines = []
    for held in (small_one, small_two):
        for i in range(3):
            lines += [held[i : i + 1, :half], held[i : i + 1, half:]]
    lines += [up_bias[:, :half], up_bias[:, half:]]
    lines.append(jnp.concatenate([qkv_bias[0:1, :width], qkv_bias[0:1, 2 * width :]], 1))
    lines.append(jnp.zeros((EXTRA - len(lines), half), F32))
    total = jnp.concatenate([qkv, out] + lines, 0)
    split_both(places, total, (send_x, keep_x, send_y, keep_y))


def add_split(bits, places, *refs):
    for i, bit in enumerate(bits):
        keep, came = refs[2 * i : 2 * i + 2]
        send, left = refs[2 * (len(bits) + i) : 2 * (len(bits) + i) + 2]
        for d in range(keep.shape[0]):
            total = keep[d].astype(F32) + came[d].astype(F32)
            split_rows(total, is_high(places, bit), send.at[d], left.at[d])


def add_parts(places, keep_a, came_a, keep_b, came_b, *outs):
    rows = keep_a.shape[1]
    for d, out in enumerate(outs):
        out[:rows] = (keep_a[d].astype(F32) + came_a[d].astype(F32)).astype(LOW)
        out[rows:] = (keep_b[d].astype(F32) + came_b[d].astype(F32)).astype(LOW)


def add_heads(places, *refs):
    total = refs[0][...].astype(F32)
    for ref in refs[1:-1]:
        total = total + ref[...].astype(F32)
    refs[-1][...] = total.astype(LOW)


def input_sum(places, first, second, w, res1, out):
    k = pl.program_id(0)
    rows = jnp.where(k < pl.num_programs(0) // 2, first[...], second[...])
    total = dot_tn(rows, w[...])
    out[...] = jnp.where(k == 0, res1[...], out[...]) + total


def place_pieces(places, held, full, layouts):
    near, core = places[0], places[1]
    width = held[0].shape[1]
    for off in range(4):
        chip = near ^ off
        mine, other = held[off][...], held[4 + off][...]
        sides = (jnp.where(core == 0, mine, other), jnp.where(core == 0, other, mine))
        for at, rows, start, outer in layouts:
            low_bit, high_bit = chip & 1, chip >> 1
            order = 2 * low_bit + high_bit if outer == 1 else 2 * high_bit + low_bit
            to = pl.multiple_of(start + order * rows, 16)
            for side in range(2):
                full[pl.ds(to, rows), side * width : (side + 1) * width] = sides[side][
                    at : at + rows
                ].astype(F32)


def ffn_place(places, *refs):
    held, (down, up, full) = refs[:8], refs[8:]
    rows = held[0].shape[0] // 4
    half = 4 * rows
    place_pieces(places, held, full, [(0, rows, 0, 1), (rows, rows, half, 2)])
    down[...] = full[...].T
    place_pieces(places, held, up, [(2 * rows, rows, 0, 1), (3 * rows, rows, half, 2)])


def attn_place(places, *refs):
    held, (qkv, w_out, small, up_bias, qv_bias, full) = refs[:8], refs[8:]
    width = held[0].shape[1]
    count = w_out.shape[0]
    rows = count // 2
    more = held[0].shape[0] - rows
    place_pieces(places, held, full, [(0, rows, 0, 1), (rows, more, 4 * rows, 2)])
    for c in range(3):
        qkv[c] = full[c * count : (c + 1) * count].T
    w_out[...] = full[3 * count : 4 * count]
    at = 4 * count
    lines = full[at : at + 16, :width] + full[at : at + 16, width:]
    for i in range(6):
        small[i : i + 1, :width] = lines[2 * i : 2 * i + 1]
        small[i : i + 1, width:] = lines[2 * i + 1 : 2 * i + 2]
    up_bias[:, :width] = lines[12:13]
    up_bias[:, width:] = lines[13:14]
    qv_bias[0:1] = lines[14:15, :count]
    qv_bias[1:2] = lines[14:15, count : 2 * count]


def bias_parts(values):
    rows, rest = [], values
    for _ in range(3):
        rows.append(lax.reduce_precision(rest, 8, 7))
        rest = rest - rows[-1]
    return jnp.stack(rows).astype(LOW)


def sum_heads(parts, distances, places):
    got = [swap(part, "head", d) if d else part for part, d in zip(parts, distances)]
    shape = parts[0].shape
    ins = [(g, whole(shape)) for g in got]
    outs = [(shape, LOW, whole(shape))]
    (total,) = run(add_heads, places, (1,), ins, outs, weight=LIGHT)
    bit = 1
    while bit < lax.axis_size("far"):
        total = (total.astype(F32) + swap(total, "far", bit).astype(F32)).astype(LOW)
        bit *= 2
    return total


def gather_back(piece):
    held = [piece] + [swap(piece, "near", off) for off in range(1, 4)]
    held += [swap_core(h) for h in held]
    return [(h, whole(h.shape)) for h in held]


def per_device(
    tokens,
    segment_ids,
    w_qkv,
    b_qv,
    w_out,
    b_out,
    ln1_gain,
    ln1_bias,
    w_up,
    b_up,
    w_down,
    b_down,
    ln2_gain,
    ln2_bias,
    cotangent,
):
    CHAIN.clear()
    width = tokens.shape[1]
    own_rows = cotangent.shape[0]
    local_width = w_qkv.shape[2]
    heads = lax.axis_size("head")
    z = lax.axis_index("head")
    core = lax.axis_index("core")
    near = lax.axis_index("near")
    hidden_units = w_up.shape[1]
    chunk = hidden_units // heads
    half = width // 2
    rows3 = 3 * local_width
    places = jnp.stack([near, core, z]).astype(jnp.int32)

    shard = jnp.concatenate([w_qkv.transpose(0, 2, 1).reshape(rows3, width), w_out], 0)
    piece_rows = shard.shape[0] // 8
    bias = jnp.pad(bias_parts(b_qv.reshape(-1)), ((0, 13), (0, width - 2 * local_width)))
    piece = lax.dynamic_slice_in_dim(shard, (near * 2 + core) * piece_rows, piece_rows, 0)
    piece = jnp.concatenate([piece, bias], 0)
    first_hop = [swap(piece, "head", d) for d in range(1, heads)]

    seg = lax.dynamic_slice_in_dim(segment_ids, z * own_rows, own_rows, 0)
    segs = [
        (seg[:, None], whole((own_rows, 1))),
        (seg[None], whole((1, own_rows))),
    ]
    own_tokens = (tokens, pl.BlockSpec((own_rows, width), lambda k, s: (s[2], 0)))

    def attend_outs(first):
        def spec(*shape):
            return pl.BlockSpec((None,) + shape, lambda k, s: (k + first, 0, 0))

        return [
            ((heads, rows3, own_rows), LOW, spec(rows3, own_rows)),
            ((heads, local_width, own_rows), LOW, spec(local_width, own_rows)),
            ((heads, 8, own_rows), F32, spec(8, own_rows)),
            ((heads, rows3 + local_width, width), LOW, spec(rows3 + local_width, width)),
        ]

    macs = rows3 * width * own_rows + 6 * own_rows * own_rows * 256
    ins = [own_tokens, (shard, whole(shard.shape)), (bias, whole(bias.shape))] + segs
    made = begun = run(own_attention, places, (1,), ins, attend_outs(0), macs=macs)
    block = pl.BlockSpec((piece_rows, width), lambda k, s: (0, 0))
    mines = []
    for d in range(1, heads):
        mines += run(
            take_rows, places, (1,), [(first_hop[d - 1], block)],
            [((piece_rows, width), LOW, block)], after=[begun[0]] + mines, weight=LIGHT,
        )
    orders = [(1, 2) if d % 2 else (2, 1) for d in range(heads)]
    nexts = [swap(mines[d - 1], "near", orders[d][0]) for d in range(1, heads)]
    for d in range(1, heads):
        order = orders[d]
        ins = [(mines[d - 1], block), (nexts[d - 1], block)]
        twice = (2, piece_rows, width)
        (pair,) = run(
            pair_rows, places, (1,), ins, [(twice, LOW, whole(twice))],
            after=nexts[d : d + 1] + mines[d + 1 :], weight=LIGHT,
        )
        rest = swap(pair, "near", order[1])
        held = [pair, rest, swap_core(pair), swap_core(rest)]
        ins = [own_tokens] + [(h, whole(h.shape)) for h in held]
        ins += [(first_hop[d - 1], pl.BlockSpec((16, width), lambda k, s: (piece_rows // 16, 0)))]
        kernel = functools.partial(far_attention, order)
        made = run(kernel, places, (1,), ins + segs, attend_outs(d), macs=macs, alias=made)
    qkvs, mixes, logs, weights = made

    vectors = jnp.stack([b_out, ln1_gain, ln1_bias, b_down, ln2_gain, ln2_bias])

    tok_send = lax.dynamic_slice(tokens, (z * own_rows, (1 - core) * half), (own_rows, half))
    tok_far = swap_core(tok_send)
    mixes_far = swap_core(mixes)

    def by_step(*shape):
        block = (None,) + shape
        return pl.BlockSpec(block, lambda k, s: (jnp.minimum(k, heads - 1),) + (0,) * len(shape))

    def unit_at(k, s):
        return s[2] ^ jnp.minimum(k, heads - 1)


    square = (own_rows, width)
    tile = by_step(own_rows, half)
    tiles = (heads, own_rows, half)
    up_block = (w_up, pl.BlockSpec((width, chunk), lambda k, s: (0, unit_at(k, s))))
    down_block = (w_down, pl.BlockSpec((chunk, width), lambda k, s: (unit_at(k, s), 0)))
    line_block = pl.BlockSpec((None, 1, chunk), lambda k, s: (unit_at(k, s), 0, 0))

    def weight_rows(rows, index):
        return (weights, pl.BlockSpec((None, rows, width), lambda k, s: (k, index, 0)))

    ins = [
        own_tokens,
        (mixes, whole(mixes.shape)),
        (weights, pl.BlockSpec((heads, local_width, width), lambda k, s: (0, 3, 0))),
        (vectors, whole(vectors.shape)),
        up_block,
        (b_up.reshape(heads, 1, chunk), line_block),
        (w_down, pl.BlockSpec(memory_space=pl.ANY)),
        (cotangent, whole(square)),
    ]
    outs = [
        (tiles, LOW, tile),
        (tiles, LOW, tile),
        ((4, own_rows, half), LOW, whole((4, own_rows, half))),
        ((heads, own_rows, chunk), F32, by_step(own_rows, chunk)),
        (square, F32, whole(square)),
        ((own_rows, 1), F32, whole((own_rows, 1))),
        (square, F32, whole(square)),
        (square, LOW, whole(square)),
        ((8, width), F32, whole((8, width))),
    ]
    scratch = [
        pltpu.VMEM(square, F32),
        pltpu.VMEM(square, LOW),
        pltpu.VMEM((own_rows, hidden_units), LOW),
        pltpu.VMEM(w_down.shape, LOW),
        pltpu.SemaphoreType.DMA,
    ]
    ffn_macs = 2 * own_rows * width * hidden_units
    act_send, act_own, ends, slope, unit1, inv1, res2, layer_output, small_two = run(
        feed_forward, places, (heads + 1,), ins, outs, scratch, ffn_macs
    )
    act_far = swap_core(act_send)
    ends_far = swap_core(ends)

    def two_of(array, index):
        return (array, pl.BlockSpec((2, own_rows, half), lambda k, s: (index, 0, 0)))

    ins = [two_of(ends, 1), down_block, (slope, by_step(own_rows, chunk))]
    outs = [(tiles, LOW, tile), (tiles, LOW, tile), ((heads, 1, chunk), F32, line_block)]
    scratch = [pltpu.VMEM(square, LOW), pltpu.VMEM((own_rows, chunk), LOW)]
    inner_send, inner_own, up_bias = run(
        inner_back, places, (heads,), ins, outs, scratch, ffn_macs // 2,
        after=[tok_far, mixes_far],
    )
    inner_far = swap_core(inner_send)

    def unit_outs(count, *rows):
        def out(r):
            return ((count, r, half), LOW, pl.BlockSpec((None, r, half), lambda k, s: (k, 0, 0)))

        return [out(r) for r in rows for _ in range(2)]

    def add_on(kernel, arrays, *rows):
        ins = [(a, whole(a.shape)) for a in arrays]
        shapes = [(arrays[0].shape[0], r, half) for r in rows for _ in range(2)]
        outs = [(shape, LOW, whole(shape)) for shape in shapes]
        return run(kernel, places, (1,), ins, outs, weight=LIGHT)

    def second(x_keep, x_came, y_keep, y_came):
        arrays = (x_keep, x_came, y_keep, y_came)
        rows = (x_keep.shape[1] // 2, y_keep.shape[1] // 2)
        return add_on(functools.partial(add_split, (2, 1)), arrays, *rows)

    def third(x_keep, x_came, y_keep, y_came):
        arrays = (x_keep, x_came, y_keep, y_came)
        shape = (x_keep.shape[1] + y_keep.shape[1], half)
        return run(
            add_parts, places, (1,), [(a, whole(a.shape)) for a in arrays],
            [(shape, LOW, whole(shape))] * x_keep.shape[0], weight=LIGHT,
        )

    def cross(made, flip):
        x_send, x_keep, y_send, y_keep = made
        x_bit, y_bit = (2, 1) if flip else (1, 2)
        return x_keep, swap(x_send, "near", x_bit), y_keep, swap(y_send, "near", y_bit)

    flipped = [pltpu.VMEM((width, own_rows), LOW)] * 2
    ins = [(act_own, tile), (act_far, tile), two_of(ends, 1), two_of(ends_far, 1)]
    pairs = pl.BlockSpec((None, width, half), lambda k, s: (k // 2, 0, 0))
    outs = [((heads // 2, width, half), LOW, pairs)] * 2
    d_send, d_keep = run(down_grad, places, (heads,), ins, outs, flipped, ffn_macs // 2)
    d_came = swap(d_send, "head", 1)
    ins = [(inner_own, tile), (inner_far, tile), two_of(ends, 0), two_of(ends_far, 0)]
    u_made = run(
        up_grad, places, (heads,), ins, unit_outs(heads, half // 2, half // 2), flipped, ffn_macs // 2
    )
    u_held = cross(u_made, False)

    ins = [
        (inner_own, tile),
        (inner_send, tile),
        up_block,
        (res2, whole(square)),
        (unit1, whole(square)),
        (inv1, whole((own_rows, 1))),
        (vectors, whole(vectors.shape)),
    ]
    outs = [
        ((own_rows, half), LOW, whole((own_rows, half))),
        (square, F32, whole(square)),
        (square, LOW, whole(square)),
        ((8, width), F32, whole((8, width))),
    ]
    grad_send, res1, grad_attended, small_one = run(
        hidden_back, places, (heads,), ins, outs, [pltpu.VMEM(square, F32)], ffn_macs // 2
    )
    grad_far = swap_core(grad_send)

    def pair_block(first, *shape):
        block = (None,) + shape
        return pl.BlockSpec(block, lambda k, s: (k + first,) + (0,) * len(shape))

    def attend_back(first):
        ins = [
            (qkvs, pair_block(first, rows3, own_rows)),
            (weights, pl.BlockSpec((None, local_width, width), lambda k, s: (k + first, 3, 0))),
            (grad_attended, whole(square)),
            (logs, pair_block(first, 8, own_rows)),
        ] + segs
        outs = [
            ((2, rows3, own_rows), LOW, pair_block(0, rows3, own_rows)),
            ((2, 8, rows3), F32, pair_block(0, 8, rows3)),
        ]
        return run(
            attention_back, places, (2,), ins, outs,
            macs=2 * (15 * own_rows * own_rows * 256 + local_width * own_rows * width),
        )

    def attend_unit(first, rows, rows_far, qkv_bias):
        line = pl.BlockSpec((None, 1, chunk), lambda k, s: (s[2] ^ (k + first), 0, 0))
        ins = [
            (rows, pair_block(0, rows3, own_rows)),
            (rows_far, pair_block(0, rows3, own_rows)),
            (tokens, pl.BlockSpec((own_rows, half), lambda k, s: (s[2], s[1]))),
            (tok_far, whole((own_rows, half))),
            (mixes, pair_block(first, local_width, own_rows)),
            (mixes_far, pair_block(first, local_width, own_rows)),
            (grad_attended, pl.BlockSpec((own_rows, half), lambda k, s: (0, s[1]))),
            (grad_far, whole((own_rows, half))),
            (small_one, whole((8, width))),
            (small_two, whole((8, width))),
            (up_bias, line),
            (qkv_bias, pair_block(0, 8, rows3)),
        ]
        outs = unit_outs(2, half // 2, (half + EXTRA) // 2)
        return run(attn_grad, places, (2,), ins, outs, macs=4 * width * own_rows * half)

    far_rows, far_bias = attend_back(2)
    far_rows_came = swap_core(far_rows)
    u_held = cross(second(*u_held), True)
    own_rows_made, own_bias = attend_back(0)
    own_rows_came = swap_core(own_rows_made)
    d_held = cross(add_on(add_both, (d_keep, d_came), half // 2, half // 2), False)
    f_held = cross(attend_unit(2, far_rows, far_rows_came, far_bias), False)
    u_parts = third(*u_held)
    o_held = cross(attend_unit(0, own_rows_made, own_rows_came, own_bias), False)
    d_held = cross(second(*d_held), True)
    u_piece = sum_heads(u_parts, (0, 1, 2, 3), places)
    f_held = cross(second(*f_held), True)
    d_parts = third(*d_held)
    d_piece = sum_heads(d_parts, (0, 2), places)
    o_held = cross(second(*o_held), True)
    f_parts = third(*f_held)
    ffn_held = gather_back(jnp.concatenate([d_piece, u_piece], 0))
    o_parts = third(*o_held)

    ins = [
        (far_rows, pl.BlockSpec((None, rows3, own_rows), lambda k, s: (jnp.minimum(k, 1), 0, 0))),
        (own_rows_made, pl.BlockSpec((None, rows3, own_rows), lambda k, s: (jnp.maximum(k - 2, 0), 0, 0))),
        (weights, pl.BlockSpec((None, rows3, width), lambda k, s: ((k + 2) % 4, 0, 0))),
        (res1, whole(square)),
    ]
    outs = [(square, F32, whole(square))]
    (input_grad,) = run(
        input_sum, places, (heads,), ins, outs, macs=heads * own_rows * rows3 * width
    )
    attn_piece = sum_heads(list(o_parts) + list(f_parts), (0, 1, 2, 3), places)
    attn_held = gather_back(attn_piece)

    outs = [(shape, F32, whole(shape)) for shape in ((chunk, width), (width, chunk))]
    grad_down, grad_up = run(
        ffn_place, places, (1,), ffn_held, outs, [pltpu.VMEM((width, chunk), F32)]
    )
    shapes = [
        (3, width, local_width),
        (local_width, width),
        (6, width),
        (1, chunk),
        (2, local_width),
    ]
    grad_qkv, grad_out, grad_small, grad_up_bias, grad_qv_bias = run(
        attn_place,
        places,
        (1,),
        attn_held,
        [(shape, F32, whole(shape)) for shape in shapes],
        [pltpu.VMEM((width + EXTRA, width), F32)],
    )
    return (
        layer_output,
        input_grad,
        grad_qkv,
        grad_qv_bias,
        grad_out,
        grad_up,
        grad_up_bias[0],
        grad_down,
        grad_small,
    )


def solution(mesh):
    batch, heads = mesh.devices.shape
    mesh = Mesh(
        mesh.devices.reshape(batch // 8, 4, 2, heads), ("far", "near", "core", "head")
    )
    group = ("far", "near", "core")
    everyone = group + ("head",)
    in_specs = (
        P(group, None),
        P(group),
        P(None, None, "head"),
        P(None, "head"),
        P("head", None),
        P(),
        P(),
        P(),
        P(),
        P(),
        P(),
        P(),
        P(),
        P(),
        P(everyone, None),
    )
    out_specs = (
        P(everyone, None),
        P(everyone, None),
        P(None, None, "head"),
        P(None, "head"),
        P("head", None),
        P(None, "head"),
        P("head"),
        P("head", None),
        P(),
    )
    return jax.shard_map(
        per_device, mesh=mesh, in_specs=in_specs, out_specs=out_specs, check_vma=False
    )
```

```python
import functools
import math

import jax
import jax.numpy as jnp
from jax import lax
from jax.experimental import pallas as pl
from jax.experimental.pallas import tpu as pltpu
from jax.sharding import Mesh
from jax.sharding import PartitionSpec as P

HEAD_DIM = 64
SLOT = 512
LOW = jnp.bfloat16
F32 = jnp.float32
LOG2E = math.log2(math.e)
SCORE_SCALE = HEAD_DIM ** (-0.5) * LOG2E
SPARE_BYTES = 12 * 2**20
EXTRA = 64
LIGHT = 0.01
CHAIN = []
TAIL_SLOPE = 0.36
TAIL = (
    0.14371304537508633,
    0.14177245466203425,
    0.1397192603907239,
    0.026549325413860486,
    0.18095403134327948,
    -0.1797647161697652,
    0.047056295581175855,
)


def swap(value, axis, bit):
    size = lax.axis_size(axis)
    return lax.ppermute(value, axis, [(i, i ^ bit) for i in range(size)])


def swap_core(value):
    return swap(value, "core", 1)


def dot(a, b):
    return jnp.dot(a, b, preferred_element_type=F32)


def dot_nt(a, b):
    return lax.dot_general(a, b, (((1,), (1,)), ((), ())), preferred_element_type=F32)


def dot_tn(a, b):
    return lax.dot_general(a, b, (((0,), (0,)), ((), ())), preferred_element_type=F32)


def whole(shape):
    return pl.BlockSpec(shape, lambda *args: (0,) * len(shape), pipeline_mode=pl.Buffered(1))


def run(
    kernel, places, grid, ins, outs, scratch=(), macs=0, after=(), alias=(), weight=8, chain=True
):
    moved = sum(a.size * a.dtype.itemsize for a, spec in ins)
    moved += sum(math.prod(shape) * jnp.dtype(kind).itemsize for shape, kind, spec in outs)
    after = list(after) + (CHAIN if chain else [])
    count, unread = len(ins), len(alias) + len(after)
    results = len(outs)
    flag = (8, 128)
    if chain:
        outs = outs + [(flag, F32, whole(flag))]

    def body(places, *refs):
        made = refs[count + unread :]
        if chain:

            @pl.when(pl.program_id(0) == 0)
            def _():
                made[results][...] = jnp.zeros(flag, F32)

        kernel(places, *refs[:count], *made[:results], *made[len(outs) :])

    held = pl.BlockSpec(memory_space=pl.ANY)
    room = SPARE_BYTES
    for shape, kind, spec in outs + [(a.shape, a.dtype, spec) for a, spec in ins]:
        if spec.block_shape is not None:
            block = math.prod(1 if n is None else n for n in spec.block_shape)
            copies = 2 if spec.pipeline_mode is None else 1
            room += copies * block * jnp.dtype(kind).itemsize
    for ref in scratch:
        if hasattr(ref, "shape") and ref.dtype in (LOW, F32):
            room += math.prod(ref.shape) * jnp.dtype(ref.dtype).itemsize
    made = pl.pallas_call(
        body,
        name=getattr(kernel, "func", kernel).__name__,
        grid_spec=pltpu.PrefetchScalarGridSpec(
            num_scalar_prefetch=1,
            grid=grid,
            in_specs=[spec for a, spec in ins] + [held] * unread,
            out_specs=[spec for shape, kind, spec in outs],
            scratch_shapes=list(scratch),
        ),
        out_shape=[jax.ShapeDtypeStruct(shape, kind) for shape, kind, spec in outs],
        input_output_aliases={1 + count + i: i for i in range(len(alias))},
        compiler_params=pltpu.CompilerParams(vmem_limit_bytes=room),
        cost_estimate=pl.CostEstimate(
            flops=int(2 * macs * weight), bytes_accessed=int(moved * weight), transcendentals=0
        ),
    )(places, *[a for a, spec in ins], *alias, *after)
    if chain:
        CHAIN[:] = made[results:]
    return made[:results]


def mask_rows(seg_col, seg_row):
    return jnp.where(seg_col == seg_row, 0.0, -1e30)


def attend_heads(tok, w_rows, bias, seg_col, seg_row, qkv_ref, mix_ref, log_ref):
    width = w_rows.shape[0] // 3
    added = dot_tn(bias[:, : 2 * width], jnp.ones((bias.shape[0], tok.shape[0]), LOW))
    qkv = dot_nt(w_rows, tok)
    parts = (
        (qkv[:width] + added[:width]).astype(LOW),
        qkv[width : 2 * width].astype(LOW),
        (qkv[2 * width :] + added[width:]).astype(LOW),
    )
    for c in range(3):
        qkv_ref[c * width : (c + 1) * width] = parts[c]
    masked = mask_rows(seg_col, seg_row)
    for head in range(width // HEAD_DIM):
        q, k, v = (part[head * HEAD_DIM : (head + 1) * HEAD_DIM] for part in parts)
        scores = dot_tn(k, q) + masked
        top = jnp.max(scores, 0, keepdims=True)
        exponent = jnp.exp2((scores - top) * SCORE_SCALE)
        total = jnp.sum(exponent, 0, keepdims=True)
        attend = (exponent * (1.0 / total)).astype(LOW)
        mix_ref[head * HEAD_DIM : (head + 1) * HEAD_DIM] = dot(v, attend).astype(LOW)
        log_ref[head : head + 1] = top * SCORE_SCALE + jnp.log2(total)


def own_attention(
    places, tok, w, bias, seg_col, seg_row, qkv_ref, mix_ref, log_ref, w_qkv, w_out
):
    w_qkv[...] = w[: qkv_ref.shape[0]]
    w_out[...] = w[qkv_ref.shape[0] :]
    attend_heads(
        tok[...],
        w[: qkv_ref.shape[0]],
        bias[...],
        seg_col[...],
        seg_row[...],
        qkv_ref,
        mix_ref,
        log_ref,
    )


def far_attention(
    order, places, tok, pair, rest, pair_far, rest_far, bias, seg_col, seg_row,
    qkv_ref, mix_ref, log_ref, w_qkv, w_out, w_ref,
):
    first, second = order
    rows = pair.shape[1]
    me = places[0] * 2 + places[1]
    for other, held in enumerate(((pair, rest), (pair_far, rest_far))):
        for two, block in enumerate(held):
            for one in range(2):
                owner = me ^ (other + 2 * first * one + 2 * second * two)
                w_ref[pl.ds(pl.multiple_of(owner * rows, rows), rows)] = block[one]
    w_qkv[...] = w_ref[: qkv_ref.shape[0]]
    w_out[...] = w_ref[qkv_ref.shape[0] :]
    attend_heads(
        tok[...],
        w_ref[: qkv_ref.shape[0]],
        bias[...],
        seg_col[...],
        seg_row[...],
        qkv_ref,
        mix_ref,
        log_ref,
    )


def take_rows(places, rows, out):
    out[...] = rows[...]


def pair_rows(places, first, second, out):
    out[0] = first[...]
    out[1] = second[...]


def norm_stats(v):
    centred = v - jnp.mean(v, -1, keepdims=True)
    inv = lax.rsqrt(jnp.mean(centred * centred, -1, keepdims=True) + 1e-05)
    return centred * inv, inv


def norm_back(upstream, unit, inv, gain):
    scaled = upstream * gain
    inner = jnp.mean(scaled * unit, -1, keepdims=True)
    return inv * (scaled - jnp.mean(scaled, -1, keepdims=True) - unit * inner)


def gelu_both(pre):
    power = jnp.exp2(pre * pre * (-0.5 * LOG2E))
    base = 1.0 + TAIL_SLOPE * jnp.abs(pre)
    t = pl.reciprocal(base, approx=True)
    t = t * (2.0 - base * t)
    tail = TAIL[6] * t + TAIL[5]
    for c in TAIL[4::-1]:
        tail = tail * t + c
    tail = tail * (t * power)
    cumul = jnp.where(pre < 0.0, tail, 1.0 - tail)
    return (pre * cumul).astype(LOW), cumul + pre * (power * 0.3989422804014327)


def feed_forward(
    places, tok, mix, w_out, vectors, w_up, b_up, w_down, cot,
    send, own, inner_send, inner_own, ends, out, res1, grad_low, grad_send, small, bias,
    up, down, low, acts, slope, inners, hidden, unit1, res2, inv1, branch, up_sem, down_sem,
):
    k = pl.program_id(0)
    half = send.shape[1]
    heads, _, chunk = up.shape
    core, z = places[1], places[2]
    b_out, gain1, shift1, b_down, gain2, shift2 = (vectors[i : i + 1] for i in range(6))
    block = 256
    parts = [slice(j * block, (j + 1) * block) for j in range(chunk // block)]

    def fetch_up(i):
        at = pl.ds(pl.multiple_of((z ^ i) * chunk, chunk), chunk)
        return pltpu.make_async_copy(w_up.at[:, at], up.at[i], up_sem.at[i])

    def fetch_down(i):
        at = pl.ds(pl.multiple_of((z ^ i) * chunk, chunk), chunk)
        return pltpu.make_async_copy(w_down.at[at], down.at[i], down_sem.at[i])

    def share(wide, mine, other):
        left, right = wide[:, :half], wide[:, half:]
        mine[...] = jnp.where(core == 0, left, right)
        other[...] = jnp.where(core == 0, right, left)

    @pl.when(k == 0)
    def _():
        for i in range(heads):
            fetch_up(i).start()
        for i in range(heads):
            fetch_down(i).start()
        attended = b_out
        for d in range(heads):
            attended = attended + dot_tn(mix[d], w_out[d])
        unit, inv = norm_stats(tok[...].astype(F32) + attended)
        unit1[...] = unit
        inv1[...] = inv
        one = unit * gain1 + shift1
        hidden[...] = one
        one_low = one.astype(LOW)
        low[...] = one_low
        ends[0] = one_low[:, :half]
        ends[1] = one_low[:, half:]

    for i in range(heads):

        @pl.when(k == i)
        def _():
            fetch_up(i).wait()
            for at in parts:
                pre = dot(low[...], up[i, :, at]) + b_up[:, at]
                act, tilt = gelu_both(pre)
                slope[i, :, at] = tilt
                acts[:, i * chunk + at.start : i * chunk + at.stop] = act
            share(acts.at[:, i * chunk : (i + 1) * chunk], own, send)

    @pl.when(k == heads)
    def _():
        for i in range(heads):
            fetch_down(i).wait()
        total = dot(acts[...], down[...].reshape(heads * chunk, down.shape[2]))
        unit, inv = norm_stats(hidden[...] + (total + b_down))
        out[...] = (unit * gain2 + shift2).astype(LOW)
        upstream = cot[...].astype(F32)
        grad = norm_back(upstream, unit, inv, gain2)
        res2[...] = grad
        low_part = grad.astype(LOW)
        branch[...] = low_part
        ends[2] = low_part[:, :half]
        ends[3] = low_part[:, half:]
        small[3:4] = jnp.sum(low_part.astype(F32), 0, keepdims=True)
        small[4:5] = jnp.sum(upstream * unit, 0, keepdims=True)
        small[5:6] = jnp.sum(upstream, 0, keepdims=True)

    for i in range(heads):

        @pl.when(k == heads + 1 + i)
        def _():
            for at in parts:
                inner = (dot_nt(branch[...], down[i, at]) * slope[i, :, at]).astype(LOW)
                inners[i, :, at] = inner
                bias[:, at] = jnp.sum(inner.astype(F32), 0, keepdims=True)
            share(inners.at[i], inner_own, inner_send)

    @pl.when(k == 2 * heads + 1)
    def _():
        grad = res2[...]
        for i in range(heads):
            grad = grad + dot_nt(inners[i], up[i])
        unit = unit1[...]
        result = norm_back(grad, unit, inv1[...], gain1)
        res1[...] = result
        result_low = result.astype(LOW)
        grad_low[...] = result_low
        grad_send[...] = jnp.where(core == 0, result_low[:, half:], result_low[:, :half])
        small[0:1] = jnp.sum(result_low.astype(F32), 0, keepdims=True)
        small[1:2] = jnp.sum(grad * unit, 0, keepdims=True)
        small[2:3] = jnp.sum(grad, 0, keepdims=True)


def attention_back(places, qkv, w_out, grad, log_ref, seg_col, seg_row, rows_ref, bias_ref):
    width = qkv.shape[0] // 3
    grad_mixed = dot_nt(w_out[...], grad[...]).astype(LOW)
    masked = mask_rows(seg_col[...], seg_row[...])
    scale = HEAD_DIM ** (-0.5)
    for head in range(width // HEAD_DIM):
        places_of = [c * width + head * HEAD_DIM for c in range(3)]
        q, k, v = (qkv[at : at + HEAD_DIM] for at in places_of)
        g = grad_mixed[head * HEAD_DIM : (head + 1) * HEAD_DIM]
        scores = dot_tn(k, q) + masked
        attend = jnp.exp2(scores * SCORE_SCALE - log_ref[head : head + 1])
        attend_low = attend.astype(LOW)
        grad_v = dot_nt(g, attend_low)
        product = attend * dot_tn(v, g)
        inner = jnp.sum(product, 0, keepdims=True)
        grad_scores = (product - attend * inner).astype(LOW)
        grad_q = dot(k, grad_scores) * scale
        grad_k = dot_nt(q, grad_scores) * scale
        for at, value in zip(places_of, (grad_q, grad_k, grad_v)):
            rows_ref[at : at + HEAD_DIM] = value.astype(LOW)
    ones = jnp.ones((8, rows_ref.shape[1]), LOW)
    bias_ref[...] = dot_nt(ones, rows_ref[...])


def split_rows(value, high, send, keep):
    rows = value.shape[0] // 2
    low = value.astype(LOW)
    send[...] = jnp.where(high, low[:rows], low[rows:])
    keep[...] = jnp.where(high, low[rows:], low[:rows])


def is_high(places, bit):
    return (places[0] & bit) != 0


def unit_rows(places, units, units_far, ends, ends_far, near, far):
    half = ends.shape[2]

    @pl.when(pl.program_id(0) == 0)
    def _():
        for side in range(2):
            rows = slice(side * half, (side + 1) * half)
            near[rows] = ends[side].T
            far[rows] = ends_far[side].T

    return dot(near[...], units[...]) + dot(far[...], units_far[...])


def down_grad(places, units, units_far, ends, ends_far, send, keep, near, far):
    total = unit_rows(places, units, units_far, ends, ends_far, near, far)
    split_rows(total, is_high(places, 1), send, keep)


def up_grad(places, units, units_far, ends, ends_far, send, keep, near, far):
    total = unit_rows(places, units, units_far, ends, ends_far, near, far)
    split_rows(total, is_high(places, 2), send, keep)


def attn_grad(
    places, rows, rows_far, tok, tok_far, mix, mix_far, grad, grad_far,
    small, up_bias, qkv_bias, send_x, keep_x, send_y, keep_y,
):
    width = mix.shape[0]
    half = tok.shape[1]
    qkv = dot(rows[...], tok[...]) + dot(rows_far[...], tok_far[...])
    out = dot(mix[...], grad[...]) + dot(mix_far[...], grad_far[...])
    lines = []
    for i in range(6):
        lines += [small[i : i + 1, :half], small[i : i + 1, half:]]
    lines += [up_bias[:, :half], up_bias[:, half:]]
    lines.append(jnp.concatenate([qkv_bias[0:1, :width], qkv_bias[0:1, 2 * width :]], 1))
    lines.append(jnp.zeros((EXTRA - len(lines), half), F32))
    total = jnp.concatenate([qkv, out] + lines, 0)
    split_rows(total[:half], is_high(places, 1), send_x, keep_x)
    split_rows(total[half:], is_high(places, 2), send_y, keep_y)


def add_split(bits, places, *refs):
    for i, bit in enumerate(bits):
        keep, came = refs[2 * i : 2 * i + 2]
        send, left = refs[2 * (len(bits) + i) : 2 * (len(bits) + i) + 2]
        for d in range(keep.shape[0]):
            total = keep[d].astype(F32) + came[d].astype(F32)
            split_rows(total, is_high(places, bit), send.at[d], left.at[d])


def add_parts(places, keep_a, came_a, keep_b, came_b, send, keep):
    rows = keep_a.shape[1]
    for d in range(keep_a.shape[0]):
        out = (send if d % 2 else keep).at[d // 2]
        out[:rows] = (keep_a[d].astype(F32) + came_a[d].astype(F32)).astype(LOW)
        out[rows:] = (keep_b[d].astype(F32) + came_b[d].astype(F32)).astype(LOW)


def add_pair(places, keep, came, *outs):
    for i, out in enumerate(outs):
        out[...] = (keep[i].astype(F32) + came[i].astype(F32)).astype(LOW)


def add_two(places, keep, came, out):
    out[...] = (keep[...].astype(F32) + came[...].astype(F32)).astype(LOW)


def input_sum(places, first, second, w, res1, out):
    k = pl.program_id(0)
    rows = jnp.where(k < pl.num_programs(0) // 2, first[...], second[...])
    total = dot_tn(rows, w[...])
    out[...] = jnp.where(k == 0, res1[...], out[...]) + total


def place_pieces(places, held, full, layouts):
    near, core = places[0], places[1]
    width = held[0].shape[1]
    for off in range(4):
        chip = near ^ off
        mine, other = held[off][...], held[4 + off][...]
        sides = (jnp.where(core == 0, mine, other), jnp.where(core == 0, other, mine))
        for at, rows, start, outer in layouts:
            low_bit, high_bit = chip & 1, chip >> 1
            order = 2 * low_bit + high_bit if outer == 1 else 2 * high_bit + low_bit
            to = pl.multiple_of(start + order * rows, 16)
            for side in range(2):
                full[pl.ds(to, rows), side * width : (side + 1) * width] = sides[side][
                    at : at + rows
                ].astype(F32)


def ffn_place(places, *refs):
    held, (down, up, full) = refs[:8], refs[8:]
    rows = held[0].shape[0] // 2
    place_pieces(places, held, full, [(0, rows, 0, 1)])
    down[...] = full[...].T
    place_pieces(places, held, up, [(rows, rows, 0, 2)])


def attn_place(places, *refs):
    held, (qkv, w_out, small, up_bias, qv_bias, full) = refs[:8], refs[8:]
    width = held[0].shape[1]
    count = w_out.shape[0]
    rows = count // 2
    more = held[0].shape[0] - rows
    place_pieces(places, held, full, [(0, rows, 0, 1), (rows, more, 4 * rows, 2)])
    for c in range(3):
        qkv[c] = full[c * count : (c + 1) * count].T
    w_out[...] = full[3 * count : 4 * count]
    at = 4 * count
    lines = full[at : at + 16, :width] + full[at : at + 16, width:]
    for i in range(6):
        small[i : i + 1, :width] = lines[2 * i : 2 * i + 1]
        small[i : i + 1, width:] = lines[2 * i + 1 : 2 * i + 2]
    up_bias[:, :width] = lines[12:13]
    up_bias[:, width:] = lines[13:14]
    qv_bias[0:1] = lines[14:15, :count]
    qv_bias[1:2] = lines[14:15, count : 2 * count]


def bias_parts(values):
    rows, rest = [], values
    for _ in range(3):
        rows.append(lax.reduce_precision(rest, 8, 7))
        rest = rest - rows[-1]
    return jnp.stack(rows).astype(LOW)


def gather_back(piece):
    held = [piece] + [swap(piece, "near", off) for off in range(1, 4)]
    held += [swap_core(h) for h in held]
    return [(h, whole(h.shape)) for h in held]


def per_device(
    tokens,
    segment_ids,
    w_qkv,
    b_qv,
    w_out,
    b_out,
    ln1_gain,
    ln1_bias,
    w_up,
    b_up,
    w_down,
    b_down,
    ln2_gain,
    ln2_bias,
    cotangent,
):
    CHAIN.clear()
    width = tokens.shape[1]
    own_rows = cotangent.shape[0]
    local_width = w_qkv.shape[2]
    heads = lax.axis_size("head")
    z = lax.axis_index("head")
    core = lax.axis_index("core")
    near = lax.axis_index("near")
    hidden_units = w_up.shape[1]
    chunk = hidden_units // heads
    half = width // 2
    rows3 = 3 * local_width
    places = jnp.stack([near, core, z]).astype(jnp.int32)

    shard = jnp.concatenate([w_qkv.transpose(0, 2, 1).reshape(rows3, width), w_out], 0)
    piece_rows = shard.shape[0] // 8
    bias = jnp.pad(bias_parts(b_qv.reshape(-1)), ((0, 13), (0, width - 2 * local_width)))
    piece = lax.dynamic_slice_in_dim(shard, (near * 2 + core) * piece_rows, piece_rows, 0)
    piece = jnp.concatenate([piece, bias], 0)
    first_hop = [swap(piece, "head", d) for d in range(1, heads)]

    seg = lax.dynamic_slice_in_dim(segment_ids, z * own_rows, own_rows, 0)
    segs = [
        (seg[:, None], whole((own_rows, 1))),
        (seg[None], whole((1, own_rows))),
    ]
    tok_own = lax.dynamic_slice_in_dim(tokens, z * own_rows, own_rows, 0)
    own_tokens = (tok_own, whole((own_rows, width)))

    def attend_outs(first):
        def spec(*shape):
            return pl.BlockSpec((None,) + shape, lambda k, s: (k + first, 0, 0))

        return [
            ((heads, rows3, own_rows), LOW, spec(rows3, own_rows)),
            ((heads, local_width, own_rows), LOW, spec(local_width, own_rows)),
            ((heads, 8, own_rows), F32, spec(8, own_rows)),
            ((heads, rows3, width), LOW, spec(rows3, width)),
            ((heads, local_width, width), LOW, spec(local_width, width)),
        ]

    macs = rows3 * width * own_rows + 6 * own_rows * own_rows * 256
    ins = [own_tokens, (shard, whole(shard.shape)), (bias, whole(bias.shape))] + segs
    made = begun = run(own_attention, places, (1,), ins, attend_outs(0), macs=macs, chain=False)
    block = pl.BlockSpec((piece_rows, width), lambda k, s: (0, 0))
    mines = []
    for d in range(1, heads):
        mines += run(
            take_rows, places, (1,), [(first_hop[d - 1], block)],
            [((piece_rows, width), LOW, block)], after=[begun[2]] + mines, weight=LIGHT, chain=False,
        )
    orders = [(1, 2) if d % 2 else (2, 1) for d in range(heads)]
    nexts = [swap(mines[d - 1], "near", orders[d][0]) for d in range(1, heads)]
    for d in range(1, heads):
        order = orders[d]
        ins = [(mines[d - 1], block), (nexts[d - 1], block)]
        twice = (2, piece_rows, width)
        (pair,) = run(
            pair_rows, places, (1,), ins, [(twice, LOW, whole(twice))],
            after=nexts[d : d + 1] + mines[d + 1 :], weight=LIGHT, chain=False,
        )
        rest = swap(pair, "near", order[1])
        held = [pair, rest, swap_core(pair), swap_core(rest)]
        ins = [own_tokens] + [(h, whole(h.shape)) for h in held]
        ins += [(first_hop[d - 1], pl.BlockSpec((16, width), lambda k, s: (piece_rows // 16, 0)))]
        kernel = functools.partial(far_attention, order)
        made = run(
            kernel, places, (1,), ins + segs, attend_outs(d), [pltpu.VMEM((rows3 + local_width, width), LOW)], macs, alias=made,
            chain=False,
        )
    qkvs, mixes, logs, w_qkvs, w_outs = made

    vectors = jnp.stack([b_out, ln1_gain, ln1_bias, b_down, ln2_gain, ln2_bias])

    tok_send = lax.dynamic_slice_in_dim(tok_own, (1 - core) * half, half, 1)
    tok_far = swap_core(tok_send)
    mixes_far = swap_core(mixes)

    def by_step(*shape):
        block = (None,) + shape
        return pl.BlockSpec(block, lambda k, s: (jnp.minimum(k, heads - 1),) + (0,) * len(shape))

    def unit_at(k, s):
        return s[2] ^ jnp.minimum(k, heads - 1)


    square = (own_rows, width)
    tile = by_step(own_rows, half)
    tiles = (heads, own_rows, half)
    line_block = pl.BlockSpec((None, 1, chunk), lambda k, s: (unit_at(k, s), 0, 0))

    def late(*shape):
        block = (None,) + shape
        index = lambda k, s: (jnp.clip(k - heads - 1, 0, heads - 1),) + (0,) * len(shape)
        return pl.BlockSpec(block, index)

    def late_unit(k, s):
        return (s[2] ^ jnp.clip(k - heads - 1, 0, heads - 1), 0, 0)

    def two_of(array, index):
        return (array, pl.BlockSpec((2, own_rows, half), lambda k, s: (index, 0, 0)))

    ins = [
        own_tokens,
        (mixes, whole(mixes.shape)),
        (w_outs, whole(w_outs.shape)),
        (vectors, whole(vectors.shape)),
        (w_up, pl.BlockSpec(memory_space=pl.ANY)),
        (b_up.reshape(heads, 1, chunk), line_block),
        (w_down, pl.BlockSpec(memory_space=pl.ANY)),
        (cotangent, whole(square)),
    ]
    outs = [
        (tiles, LOW, tile),
        (tiles, LOW, tile),
        (tiles, LOW, late(own_rows, half)),
        (tiles, LOW, late(own_rows, half)),
        ((4, own_rows, half), LOW, whole((4, own_rows, half))),
        (square, LOW, whole(square)),
        (square, F32, whole(square)),
        (square, LOW, whole(square)),
        ((own_rows, half), LOW, whole((own_rows, half))),
        ((8, width), F32, whole((8, width))),
        ((heads, 1, chunk), F32, pl.BlockSpec((None, 1, chunk), late_unit)),
    ]
    scratch = [
        pltpu.VMEM((heads, width, chunk), LOW),
        pltpu.VMEM((heads, chunk, width), LOW),
        pltpu.VMEM(square, LOW),
        pltpu.VMEM((own_rows, hidden_units), LOW),
        pltpu.VMEM((heads, own_rows, chunk), F32),
        pltpu.VMEM((heads, own_rows, chunk), LOW),
        pltpu.VMEM(square, F32),
        pltpu.VMEM(square, F32),
        pltpu.VMEM(square, F32),
        pltpu.VMEM((own_rows, 1), F32),
        pltpu.VMEM(square, LOW),
        pltpu.SemaphoreType.DMA((heads,)),
        pltpu.SemaphoreType.DMA((heads,)),
    ]
    ffn_macs = 2 * own_rows * width * hidden_units
    (
        act_send, act_own, inner_send, inner_own, ends, layer_output, res1, grad_attended,
        grad_send, small, up_bias,
    ) = run(
        feed_forward, places, (2 * heads + 2,), ins, outs, scratch, 2 * ffn_macs
    )
    act_far = swap_core(act_send)
    ends_far = swap_core(ends)
    inner_far = swap_core(inner_send)
    grad_far = swap_core(grad_send)

    def pair_block(first, *shape):
        block = (None,) + shape
        return pl.BlockSpec(block, lambda k, s: (k + first,) + (0,) * len(shape))

    def attend_back(first):
        ins = [
            (qkvs, pair_block(first, rows3, own_rows)),
            (w_outs, pair_block(first, local_width, width)),
            (grad_attended, whole(square)),
            (logs, pair_block(first, 8, own_rows)),
        ] + segs
        outs = [
            ((2, rows3, own_rows), LOW, pair_block(0, rows3, own_rows)),
            ((2, 8, rows3), F32, pair_block(0, 8, rows3)),
        ]
        return run(
            attention_back, places, (2,), ins, outs,
            macs=2 * (15 * own_rows * own_rows * 256 + local_width * own_rows * width),
            weight=8 if first else LIGHT,
        )

    def attend_unit(first, rows, rows_far, qkv_bias, alias):
        line = pl.BlockSpec((None, 1, chunk), lambda k, s: (s[2] ^ (k + first), 0, 0))
        ins = [
            (rows, pair_block(0, rows3, own_rows)),
            (rows_far, pair_block(0, rows3, own_rows)),
            (tok_own, pl.BlockSpec((own_rows, half), lambda k, s: (0, s[1]))),
            (tok_far, whole((own_rows, half))),
            (mixes, pair_block(first, local_width, own_rows)),
            (mixes_far, pair_block(first, local_width, own_rows)),
            (grad_attended, pl.BlockSpec((own_rows, half), lambda k, s: (0, s[1]))),
            (grad_far, whole((own_rows, half))),
            (small, whole((8, width))),
            (up_bias, line),
            (qkv_bias, pair_block(0, 8, rows3)),
        ]
        outs = [
            ((heads, r, half), LOW, pair_block(first, r, half))
            for r in (half // 2, (half + EXTRA) // 2)
            for _ in range(2)
        ]
        return run(
            attn_grad, places, (2,), ins, outs, alias=alias, weight=LIGHT
        )

    def second(x_keep, x_came, y_keep, y_came):
        arrays = (x_keep, x_came, y_keep, y_came)
        ins = [(a, whole(a.shape)) for a in arrays]
        shapes = [(heads, a.shape[1] // 2, half) for a in (x_keep, x_keep, y_keep, y_keep)]
        outs = [(shape, LOW, whole(shape)) for shape in shapes]
        kernel = functools.partial(add_split, (2, 1))
        return run(kernel, places, (1,), ins, outs, weight=LIGHT)

    def third(x_keep, x_came, y_keep, y_came):
        arrays = (x_keep, x_came, y_keep, y_came)
        shape = (heads // 2, x_keep.shape[1] + y_keep.shape[1], half)
        send, keep = run(
            add_parts, places, (1,), [(a, whole(a.shape)) for a in arrays],
            [(shape, LOW, whole(shape))] * 2, weight=LIGHT,
        )
        return keep, swap(send, "head", 1)

    def fourth(keep, came):
        shape = keep.shape[1:]
        mine, other = run(
            add_pair, places, (1,), [(a, whole(a.shape)) for a in (keep, came)],
            [(shape, LOW, whole(shape))] * 2, weight=LIGHT,
        )
        return mine, swap(other, "head", 2)

    def fifth(mine, came):
        shape = mine.shape
        (total,) = run(
            add_two, places, (1,), [(a, whole(shape)) for a in (mine, came)],
            [(shape, LOW, whole(shape))], weight=LIGHT,
        )
        bit = 1
        while bit < lax.axis_size("far"):
            total = (total.astype(F32) + swap(total, "far", bit).astype(F32)).astype(LOW)
            bit *= 2
        return total

    def cross(made, flip):
        x_send, x_keep, y_send, y_keep = made
        x_bit, y_bit = (2, 1) if flip else (1, 2)
        return x_keep, swap(x_send, "near", x_bit), y_keep, swap(y_send, "near", y_bit)

    far_rows, far_bias = attend_back(2)
    far_rows_came = swap_core(far_rows)

    flipped = [pltpu.VMEM((width, own_rows), LOW)] * 2
    unit_out = [((heads, half, half), LOW, by_step(half, half))] * 2
    ins = [(act_own, tile), (act_far, tile), two_of(ends, 1), two_of(ends_far, 1)]
    made = run(down_grad, places, (heads,), ins, unit_out, flipped, ffn_macs // 2)
    ins = [(inner_own, tile), (inner_far, tile), two_of(ends, 0), two_of(ends_far, 0)]
    made += run(up_grad, places, (heads,), ins, unit_out, flipped, ffn_macs // 2, weight=LIGHT)
    ffn_held = cross(made, False)

    near_rows, near_bias = attend_back(0)
    near_rows_came = swap_core(near_rows)
    made = attend_unit(2, far_rows, far_rows_came, far_bias, ())
    ins = [
        (far_rows, pl.BlockSpec((None, rows3, own_rows), lambda k, s: (jnp.minimum(k, 1), 0, 0))),
        (near_rows, pl.BlockSpec((None, rows3, own_rows), lambda k, s: (jnp.maximum(k - 2, 0), 0, 0))),
        (w_qkvs, pl.BlockSpec((None, rows3, width), lambda k, s: ((k + 2) % 4, 0, 0))),
        (res1, whole(square)),
    ]
    outs = [(square, F32, whole(square))]
    (input_grad,) = run(
        input_sum, places, (heads,), ins, outs, macs=heads * own_rows * rows3 * width,
        weight=LIGHT,
    )
    ffn_held = cross(second(*ffn_held), True)
    made = attend_unit(0, near_rows, near_rows_came, near_bias, made)
    attn_held = cross(made, False)

    attn_held = cross(second(*attn_held), True)
    ffn_held = third(*ffn_held)
    attn_held = third(*attn_held)
    ffn_held = fourth(*ffn_held)
    attn_held = fourth(*attn_held)
    ffn_held = gather_back(fifth(*ffn_held))
    attn_held = gather_back(fifth(*attn_held))

    outs = [(shape, F32, whole(shape)) for shape in ((chunk, width), (width, chunk))]
    grad_down, grad_up = run(
        ffn_place, places, (1,), ffn_held, outs, [pltpu.VMEM((width, chunk), F32)]
    )
    shapes = [
        (3, width, local_width),
        (local_width, width),
        (6, width),
        (1, chunk),
        (2, local_width),
    ]
    grad_qkv, grad_out, grad_small, grad_up_bias, grad_qv_bias = run(
        attn_place,
        places,
        (1,),
        attn_held,
        [(shape, F32, whole(shape)) for shape in shapes],
        [pltpu.VMEM((width + EXTRA, width), F32)],
    )
    return (
        layer_output,
        input_grad,
        grad_qkv,
        grad_qv_bias,
        grad_out,
        grad_up,
        grad_up_bias[0],
        grad_down,
        grad_small,
    )


def solution(mesh):
    batch, heads = mesh.devices.shape
    mesh = Mesh(
        mesh.devices.reshape(batch // 8, 4, 2, heads), ("far", "near", "core", "head")
    )
    group = ("far", "near", "core")
    everyone = group + ("head",)
    in_specs = (
        P(group, None),
        P(group),
        P(None, None, "head"),
        P(None, "head"),
        P("head", None),
        P(),
        P(),
        P(),
        P(),
        P(),
        P(),
        P(),
        P(),
        P(),
        P(everyone, None),
    )
    out_specs = (
        P(everyone, None),
        P(everyone, None),
        P(None, None, "head"),
        P(None, "head"),
        P("head", None),
        P(None, "head"),
        P("head"),
        P("head", None),
        P(),
    )
    return jax.shard_map(
        per_device, mesh=mesh, in_specs=in_specs, out_specs=out_specs, check_vma=False
    )
```

```python
import functools
import math

import jax
import jax.numpy as jnp
from jax import lax
from jax.experimental import pallas as pl
from jax.experimental.pallas import tpu as pltpu
from jax.sharding import Mesh
from jax.sharding import PartitionSpec as P

HEAD_DIM = 64
SLOT = 512
LOW = jnp.bfloat16
F32 = jnp.float32
LOG2E = math.log2(math.e)
SCORE_SCALE = HEAD_DIM ** (-0.5) * LOG2E
SPARE_BYTES = 12 * 2**20
EXTRA = 64
LIGHT = 0.01
CHAIN = []
TAIL_SLOPE = 0.36
TAIL = (
    0.14371304537508633,
    0.14177245466203425,
    0.1397192603907239,
    0.026549325413860486,
    0.18095403134327948,
    -0.1797647161697652,
    0.047056295581175855,
)


def swap(value, axis, bit):
    size = lax.axis_size(axis)
    return lax.ppermute(value, axis, [(i, i ^ bit) for i in range(size)])


def swap_core(value):
    return swap(value, "core", 1)


def dot(a, b):
    return jnp.dot(a, b, preferred_element_type=F32)


def dot_nt(a, b):
    return lax.dot_general(a, b, (((1,), (1,)), ((), ())), preferred_element_type=F32)


def dot_tn(a, b):
    return lax.dot_general(a, b, (((0,), (0,)), ((), ())), preferred_element_type=F32)


def whole(shape):
    return pl.BlockSpec(shape, lambda *args: (0,) * len(shape), pipeline_mode=pl.Buffered(1))


def run(
    kernel, places, grid, ins, outs, scratch=(), macs=0, after=(), alias=(), weight=8, chain=True
):
    moved = sum(a.size * a.dtype.itemsize for a, spec in ins)
    moved += sum(math.prod(shape) * jnp.dtype(kind).itemsize for shape, kind, spec in outs)
    after = list(after) + (CHAIN if chain else [])
    count, unread = len(ins), len(alias) + len(after)
    results = len(outs)
    flag = (8, 128)
    if chain:
        outs = outs + [(flag, F32, whole(flag))]

    def body(places, *refs):
        made = refs[count + unread :]
        if chain:

            @pl.when(pl.program_id(0) == 0)
            def _():
                made[results][...] = jnp.zeros(flag, F32)

        kernel(places, *refs[:count], *made[:results], *made[len(outs) :])

    held = pl.BlockSpec(memory_space=pl.ANY)
    room = SPARE_BYTES
    for shape, kind, spec in outs + [(a.shape, a.dtype, spec) for a, spec in ins]:
        if spec.block_shape is not None:
            block = math.prod(1 if n is None else n for n in spec.block_shape)
            copies = 2 if spec.pipeline_mode is None else 1
            room += copies * block * jnp.dtype(kind).itemsize
    for ref in scratch:
        if hasattr(ref, "shape") and ref.dtype in (LOW, F32):
            room += math.prod(ref.shape) * jnp.dtype(ref.dtype).itemsize
    made = pl.pallas_call(
        body,
        name=getattr(kernel, "func", kernel).__name__,
        grid_spec=pltpu.PrefetchScalarGridSpec(
            num_scalar_prefetch=1,
            grid=grid,
            in_specs=[spec for a, spec in ins] + [held] * unread,
            out_specs=[spec for shape, kind, spec in outs],
            scratch_shapes=list(scratch),
        ),
        out_shape=[jax.ShapeDtypeStruct(shape, kind) for shape, kind, spec in outs],
        input_output_aliases={1 + count + i: i for i in range(len(alias))},
        compiler_params=pltpu.CompilerParams(vmem_limit_bytes=room),
        cost_estimate=pl.CostEstimate(
            flops=int(2 * macs * weight), bytes_accessed=int(moved * weight), transcendentals=0
        ),
    )(places, *[a for a, spec in ins], *alias, *after)
    if chain:
        CHAIN[:] = made[results:]
    return made[:results]


def mask_rows(seg_col, seg_row):
    return jnp.where(seg_col == seg_row, 0.0, -1e30)


def attend_heads(tok, w_rows, bias, seg_col, seg_row, qkv_ref, mix_ref, log_ref):
    width = w_rows.shape[0] // 3
    added = dot_tn(bias[:, : 2 * width], jnp.ones((bias.shape[0], tok.shape[0]), LOW))
    qkv = dot_nt(w_rows, tok)
    parts = (
        (qkv[:width] + added[:width]).astype(LOW),
        qkv[width : 2 * width].astype(LOW),
        (qkv[2 * width :] + added[width:]).astype(LOW),
    )
    for c in range(3):
        qkv_ref[c * width : (c + 1) * width] = parts[c]
    masked = mask_rows(seg_col, seg_row)
    for head in range(width // HEAD_DIM):
        q, k, v = (part[head * HEAD_DIM : (head + 1) * HEAD_DIM] for part in parts)
        scores = dot_tn(k, q) + masked
        top = jnp.max(scores, 0, keepdims=True)
        exponent = jnp.exp2((scores - top) * SCORE_SCALE)
        total = jnp.sum(exponent, 0, keepdims=True)
        attend = (exponent * (1.0 / total)).astype(LOW)
        mix_ref[head * HEAD_DIM : (head + 1) * HEAD_DIM] = dot(v, attend).astype(LOW)
        log_ref[head : head + 1] = top * SCORE_SCALE + jnp.log2(total)


def own_attention(
    places, tok, w, bias, seg_col, seg_row, qkv_ref, mix_ref, log_ref, w_qkv, w_out
):
    w_qkv[...] = w[: qkv_ref.shape[0]]
    w_out[...] = w[qkv_ref.shape[0] :]
    attend_heads(
        tok[...],
        w[: qkv_ref.shape[0]],
        bias[...],
        seg_col[...],
        seg_row[...],
        qkv_ref,
        mix_ref,
        log_ref,
    )


def far_attention(
    order, places, tok, pair, rest, pair_far, rest_far, bias, seg_col, seg_row,
    qkv_ref, mix_ref, log_ref, w_qkv, w_out, w_ref,
):
    first, second = order
    rows = pair.shape[1]
    me = places[0] * 2 + places[1]
    for other, held in enumerate(((pair, rest), (pair_far, rest_far))):
        for two, block in enumerate(held):
            for one in range(2):
                owner = me ^ (other + 2 * first * one + 2 * second * two)
                w_ref[pl.ds(pl.multiple_of(owner * rows, rows), rows)] = block[one]
    w_qkv[...] = w_ref[: qkv_ref.shape[0]]
    w_out[...] = w_ref[qkv_ref.shape[0] :]
    attend_heads(
        tok[...],
        w_ref[: qkv_ref.shape[0]],
        bias[...],
        seg_col[...],
        seg_row[...],
        qkv_ref,
        mix_ref,
        log_ref,
    )


def take_rows(places, rows, out):
    out[...] = rows[...]


def pair_rows(places, first, second, out):
    out[0] = first[...]
    out[1] = second[...]


def norm_stats(v):
    centred = v - jnp.mean(v, -1, keepdims=True)
    inv = lax.rsqrt(jnp.mean(centred * centred, -1, keepdims=True) + 1e-05)
    return centred * inv, inv


def norm_back(upstream, unit, inv, gain):
    scaled = upstream * gain
    inner = jnp.mean(scaled * unit, -1, keepdims=True)
    return inv * (scaled - jnp.mean(scaled, -1, keepdims=True) - unit * inner)


def gelu_both(pre):
    power = jnp.exp2(pre * pre * (-0.5 * LOG2E))
    base = 1.0 + TAIL_SLOPE * jnp.abs(pre)
    t = pl.reciprocal(base, approx=True)
    t = t * (2.0 - base * t)
    tail = TAIL[6] * t + TAIL[5]
    for c in TAIL[4::-1]:
        tail = tail * t + c
    tail = tail * (t * power)
    cumul = jnp.where(pre < 0.0, tail, 1.0 - tail)
    return (pre * cumul).astype(LOW), cumul + pre * (power * 0.3989422804014327)


def feed_forward(
    places, tok, mix, w_out, b_out, gain1, shift1, b_down, gain2, shift2,
    w_up, b_up, w_down, cot,
    send, own, ends, slope, unit1, inv1, res2, out, small, tok_send,
    hidden, low, acts, down, sem,
):
    k = pl.program_id(0)
    half = send.shape[1]
    chunk = w_up.shape[1]
    core, z = places[1], places[2]
    heads = mix.shape[0]
    fetch = pltpu.make_async_copy(w_down, down, sem)
    b_out, gain1, shift1, b_down, gain2, shift2 = (
        ref[...].reshape(1, -1) for ref in (b_out, gain1, shift1, b_down, gain2, shift2)
    )

    @pl.when(k == 0)
    def _():
        fetch.start()
        tok_send[...] = jnp.where(core == 0, tok[:, half:], tok[:, :half])
        attended = b_out
        for d in range(heads):
            attended = attended + dot_tn(mix[d], w_out[d])
        unit, inv = norm_stats(tok[...].astype(F32) + attended)
        unit1[...] = unit
        inv1[...] = inv
        one = unit * gain1 + shift1
        hidden[...] = one
        one_low = one.astype(LOW)
        low[...] = one_low
        ends[0] = one_low[:, :half]
        ends[1] = one_low[:, half:]

    @pl.when(k < heads)
    def _():
        start = (z ^ k) * chunk
        block = 256
        for j in range(chunk // block):
            at = slice(j * block, (j + 1) * block)
            pre = dot(low[...], w_up[:, at]) + b_up[:, at]
            act, tilt = gelu_both(pre)
            slope[:, at] = tilt
            acts[:, pl.ds(pl.multiple_of(start + j * block, block), block)] = act
        left = acts[:, pl.ds(pl.multiple_of(start, 128), half)]
        right = acts[:, pl.ds(pl.multiple_of(start + half, 128), half)]
        own[...] = jnp.where(core == 0, left, right)
        send[...] = jnp.where(core == 0, right, left)

    @pl.when(k == heads)
    def _():
        fetch.wait()
        unit, inv = norm_stats(hidden[...] + (dot(acts[...], down[...]) + b_down))
        out[...] = (unit * gain2 + shift2).astype(LOW)
        upstream = cot[...].astype(F32)
        grad = norm_back(upstream, unit, inv, gain2)
        res2[...] = grad
        grad_low = grad.astype(LOW)
        ends[2] = grad_low[:, :half]
        ends[3] = grad_low[:, half:]
        small[0:1] = jnp.sum(grad_low.astype(F32), 0, keepdims=True)
        small[1:2] = jnp.sum(upstream * unit, 0, keepdims=True)
        small[2:3] = jnp.sum(upstream, 0, keepdims=True)


def inner_back(places, ends, w_down, slope, send, own, bias, branch, inners):
    half = send.shape[1]
    core = places[1]

    @pl.when(pl.program_id(0) == 0)
    def _():
        branch[:, :half] = ends[0]
        branch[:, half:] = ends[1]

    block = 256
    for j in range(inners.shape[1] // block):
        at = slice(j * block, (j + 1) * block)
        inner = (dot_nt(branch[...], w_down[at]) * slope[:, at]).astype(LOW)
        inners[:, at] = inner
        bias[:, at] = jnp.sum(inner.astype(F32), 0, keepdims=True)
    first, second = inners[:, :half], inners[:, half:]
    own[...] = jnp.where(core == 0, first, second)
    send[...] = jnp.where(core == 0, second, first)


def hidden_back(
    places, own, sent, w_up, res2, unit1, inv1, gain1, send, res1, low, small, acc
):
    k = pl.program_id(0)
    core = places[1]
    half = own.shape[1]
    mine, other = own[...], sent[...]
    inner = jnp.concatenate(
        [jnp.where(core == 0, mine, other), jnp.where(core == 0, other, mine)], 1
    )
    product = dot_nt(inner, w_up[...])

    @pl.when(k == 0)
    def _():
        acc[...] = res2[...] + product

    @pl.when(k > 0)
    def _():
        acc[...] += product

    @pl.when(k == pl.num_programs(0) - 1)
    def _():
        grad = acc[...]
        result = norm_back(grad, unit1[...], inv1[...], gain1[...].reshape(1, -1))
        res1[...] = result
        result_low = result.astype(LOW)
        low[...] = result_low
        send[...] = jnp.where(core == 0, result_low[:, half:], result_low[:, :half])
        small[0:1] = jnp.sum(result_low.astype(F32), 0, keepdims=True)
        small[1:2] = jnp.sum(grad * unit1[...], 0, keepdims=True)
        small[2:3] = jnp.sum(grad, 0, keepdims=True)


def attention_back(places, qkv, w_out, grad, log_ref, seg_col, seg_row, rows_ref, bias_ref):
    width = qkv.shape[0] // 3
    grad_mixed = dot_nt(w_out[...], grad[...]).astype(LOW)
    masked = mask_rows(seg_col[...], seg_row[...])
    scale = HEAD_DIM ** (-0.5)
    for head in range(width // HEAD_DIM):
        places_of = [c * width + head * HEAD_DIM for c in range(3)]
        q, k, v = (qkv[at : at + HEAD_DIM] for at in places_of)
        g = grad_mixed[head * HEAD_DIM : (head + 1) * HEAD_DIM]
        scores = dot_tn(k, q) + masked
        attend = jnp.exp2(scores * SCORE_SCALE - log_ref[head : head + 1])
        attend_low = attend.astype(LOW)
        grad_v = dot_nt(g, attend_low)
        product = attend * dot_tn(v, g)
        inner = jnp.sum(product, 0, keepdims=True)
        grad_scores = (product - attend * inner).astype(LOW)
        grad_q = dot(k, grad_scores) * scale
        grad_k = dot_nt(q, grad_scores) * scale
        for at, value in zip(places_of, (grad_q, grad_k, grad_v)):
            rows_ref[at : at + HEAD_DIM] = value.astype(LOW)
    ones = jnp.ones((8, rows_ref.shape[1]), LOW)
    bias_ref[...] = dot_nt(ones, rows_ref[...])


def split_rows(value, high, send, keep):
    rows = value.shape[0] // 2
    low = value.astype(LOW)
    send[...] = jnp.where(high, low[:rows], low[rows:])
    keep[...] = jnp.where(high, low[rows:], low[:rows])


def is_high(places, bit):
    return (places[0] & bit) != 0


def unit_rows(places, units, units_far, ends, ends_far, near, far):
    half = ends.shape[2]

    @pl.when(pl.program_id(0) == 0)
    def _():
        for side in range(2):
            rows = slice(side * half, (side + 1) * half)
            near[rows] = ends[side].T
            far[rows] = ends_far[side].T

    return dot(near[...], units[...]) + dot(far[...], units_far[...])


def down_grad(places, units, units_far, ends, ends_far, send, keep, near, far):
    total = unit_rows(places, units, units_far, ends, ends_far, near, far)
    split_rows(total, is_high(places, 1), send, keep)


def up_grad(places, units, units_far, ends, ends_far, send, keep, near, far):
    total = unit_rows(places, units, units_far, ends, ends_far, near, far)
    split_rows(total, is_high(places, 2), send, keep)


def attn_grad(
    places, rows, rows_far, tok, tok_far, mix, mix_far, grad, grad_far,
    small_one, small_two, up_bias, qkv_bias, send_x, keep_x, send_y, keep_y,
):
    width = mix.shape[0]
    half = tok.shape[1]
    qkv = dot(rows[...], tok[...]) + dot(rows_far[...], tok_far[...])
    out = dot(mix[...], grad[...]) + dot(mix_far[...], grad_far[...])
    lines = []
    for held in (small_one, small_two):
        for i in range(3):
            lines += [held[i : i + 1, :half], held[i : i + 1, half:]]
    lines += [up_bias[:, :half], up_bias[:, half:]]
    lines.append(jnp.concatenate([qkv_bias[0:1, :width], qkv_bias[0:1, 2 * width :]], 1))
    lines.append(jnp.zeros((EXTRA - len(lines), half), F32))
    total = jnp.concatenate([qkv, out] + lines, 0)
    split_rows(total[:half], is_high(places, 1), send_x, keep_x)
    split_rows(total[half:], is_high(places, 2), send_y, keep_y)


def add_split(bits, places, *refs):
    for i, bit in enumerate(bits):
        keep, came = refs[2 * i : 2 * i + 2]
        send, left = refs[2 * (len(bits) + i) : 2 * (len(bits) + i) + 2]
        for d in range(keep.shape[0]):
            total = keep[d].astype(F32) + came[d].astype(F32)
            split_rows(total, is_high(places, bit), send.at[d], left.at[d])


def add_parts(places, keep_a, came_a, keep_b, came_b, send, keep):
    rows = keep_a.shape[1]
    for d in range(keep_a.shape[0]):
        out = (send if d % 2 else keep).at[d // 2]
        out[:rows] = (keep_a[d].astype(F32) + came_a[d].astype(F32)).astype(LOW)
        out[rows:] = (keep_b[d].astype(F32) + came_b[d].astype(F32)).astype(LOW)


def add_pair(places, keep, came, *outs):
    for i, out in enumerate(outs):
        out[...] = (keep[i].astype(F32) + came[i].astype(F32)).astype(LOW)


def add_two(places, keep, came, out):
    out[...] = (keep[...].astype(F32) + came[...].astype(F32)).astype(LOW)


def input_sum(places, rows, w, res1, out):
    total = dot_tn(rows[...], w[...])
    k = pl.program_id(0)
    out[...] = jnp.where(k == 0, res1[...], out[...]) + total


def place_pieces(places, held, full, layouts):
    near, core = places[0], places[1]
    width = held[0].shape[1]
    for off in range(4):
        chip = near ^ off
        mine, other = held[off][...], held[4 + off][...]
        sides = (jnp.where(core == 0, mine, other), jnp.where(core == 0, other, mine))
        for at, rows, start, outer in layouts:
            low_bit, high_bit = chip & 1, chip >> 1
            order = 2 * low_bit + high_bit if outer == 1 else 2 * high_bit + low_bit
            to = pl.multiple_of(start + order * rows, 16)
            for side in range(2):
                full[pl.ds(to, rows), side * width : (side + 1) * width] = sides[side][
                    at : at + rows
                ].astype(F32)


def ffn_place(places, *refs):
    held, (down, up, full) = refs[:8], refs[8:]
    rows = held[0].shape[0] // 2
    place_pieces(places, held, full, [(0, rows, 0, 1)])
    down[...] = full[...].T
    place_pieces(places, held, up, [(rows, rows, 0, 2)])


def attn_place(places, *refs):
    held, (qkv, w_out, small, up_bias, qv_bias, full) = refs[:8], refs[8:]
    width = held[0].shape[1]
    count = w_out.shape[0]
    rows = count // 2
    more = held[0].shape[0] - rows
    place_pieces(places, held, full, [(0, rows, 0, 1), (rows, more, 4 * rows, 2)])
    for c in range(3):
        qkv[c] = full[c * count : (c + 1) * count].T
    w_out[...] = full[3 * count : 4 * count]
    at = 4 * count
    lines = full[at : at + 16, :width] + full[at : at + 16, width:]
    for i in range(6):
        small[i : i + 1, :width] = lines[2 * i : 2 * i + 1]
        small[i : i + 1, width:] = lines[2 * i + 1 : 2 * i + 2]
    up_bias[:, :width] = lines[12:13]
    up_bias[:, width:] = lines[13:14]
    qv_bias[0:1] = lines[14:15, :count]
    qv_bias[1:2] = lines[14:15, count : 2 * count]


def bias_parts(values):
    rows, rest = [], values
    for _ in range(3):
        rows.append(lax.reduce_precision(rest, 8, 7))
        rest = rest - rows[-1]
    return jnp.stack(rows).astype(LOW)


def gather_back(piece):
    held = [piece] + [swap(piece, "near", off) for off in range(1, 4)]
    held += [swap_core(h) for h in held]
    return [(h, whole(h.shape)) for h in held]


def per_device(
    tokens,
    segment_ids,
    w_qkv,
    b_qv,
    w_out,
    b_out,
    ln1_gain,
    ln1_bias,
    w_up,
    b_up,
    w_down,
    b_down,
    ln2_gain,
    ln2_bias,
    cotangent,
):
    CHAIN.clear()
    width = tokens.shape[1]
    own_rows = cotangent.shape[0]
    local_width = w_qkv.shape[2]
    heads = lax.axis_size("head")
    z = lax.axis_index("head")
    core = lax.axis_index("core")
    near = lax.axis_index("near")
    hidden_units = w_up.shape[1]
    chunk = hidden_units // heads
    half = width // 2
    rows3 = 3 * local_width
    places = jnp.stack([near, core, z]).astype(jnp.int32)

    shard = jnp.concatenate([w_qkv.transpose(0, 2, 1).reshape(rows3, width), w_out], 0)
    piece_rows = shard.shape[0] // 8
    bias = jnp.pad(bias_parts(b_qv.reshape(-1)), ((0, 13), (0, width - 2 * local_width)))
    piece = lax.dynamic_slice_in_dim(shard, (near * 2 + core) * piece_rows, piece_rows, 0)
    piece = jnp.concatenate([piece, bias], 0)
    first_hop = [swap(piece, "head", d) for d in range(1, heads)]

    seg = lax.dynamic_slice_in_dim(segment_ids, z * own_rows, own_rows, 0)
    segs = [
        (seg[:, None], whole((own_rows, 1))),
        (seg[None], whole((1, own_rows))),
    ]
    tok_own = lax.dynamic_slice_in_dim(tokens, z * own_rows, own_rows, 0)
    own_tokens = (tok_own, whole((own_rows, width)))

    def attend_outs(first):
        def spec(*shape):
            return pl.BlockSpec((None,) + shape, lambda k, s: (k + first, 0, 0))

        return [
            ((heads, rows3, own_rows), LOW, spec(rows3, own_rows)),
            ((heads, local_width, own_rows), LOW, spec(local_width, own_rows)),
            ((heads, 8, own_rows), F32, spec(8, own_rows)),
            ((heads, rows3, width), LOW, spec(rows3, width)),
            ((heads, local_width, width), LOW, spec(local_width, width)),
        ]

    macs = rows3 * width * own_rows + 6 * own_rows * own_rows * 256
    ins = [own_tokens, (shard, whole(shard.shape)), (bias, whole(bias.shape))] + segs
    made = begun = run(own_attention, places, (1,), ins, attend_outs(0), macs=macs, chain=False)
    block = pl.BlockSpec((piece_rows, width), lambda k, s: (0, 0))
    mines = []
    for d in range(1, heads):
        mines += run(
            take_rows, places, (1,), [(first_hop[d - 1], block)],
            [((piece_rows, width), LOW, block)], after=[begun[2]] + mines, weight=LIGHT, chain=False,
        )
    orders = [(1, 2) if d % 2 else (2, 1) for d in range(heads)]
    nexts = [swap(mines[d - 1], "near", orders[d][0]) for d in range(1, heads)]
    for d in range(1, heads):
        order = orders[d]
        ins = [(mines[d - 1], block), (nexts[d - 1], block)]
        twice = (2, piece_rows, width)
        (pair,) = run(
            pair_rows, places, (1,), ins, [(twice, LOW, whole(twice))],
            after=nexts[d : d + 1] + mines[d + 1 :], weight=LIGHT, chain=False,
        )
        rest = swap(pair, "near", order[1])
        held = [pair, rest, swap_core(pair), swap_core(rest)]
        ins = [own_tokens] + [(h, whole(h.shape)) for h in held]
        ins += [(first_hop[d - 1], pl.BlockSpec((16, width), lambda k, s: (piece_rows // 16, 0)))]
        kernel = functools.partial(far_attention, order)
        made = run(
            kernel, places, (1,), ins + segs, attend_outs(d), [pltpu.VMEM((rows3 + local_width, width), LOW)], macs, alias=made,
            chain=False,
        )
    qkvs, mixes, logs, w_qkvs, w_outs = made

    mixes_far = swap_core(mixes)

    def by_step(*shape):
        block = (None,) + shape
        return pl.BlockSpec(block, lambda k, s: (jnp.minimum(k, heads - 1),) + (0,) * len(shape))

    def unit_at(k, s):
        return s[2] ^ jnp.minimum(k, heads - 1)


    line = whole((width,))
    square = (own_rows, width)
    tile = by_step(own_rows, half)
    tiles = (heads, own_rows, half)
    up_block = (w_up, pl.BlockSpec((width, chunk), lambda k, s: (0, unit_at(k, s))))
    down_block = (w_down, pl.BlockSpec((chunk, width), lambda k, s: (unit_at(k, s), 0)))
    line_block = pl.BlockSpec((None, 1, chunk), lambda k, s: (unit_at(k, s), 0, 0))

    ins = [
        own_tokens,
        (mixes, whole(mixes.shape)),
        (w_outs, whole(w_outs.shape)),
        (b_out, line),
        (ln1_gain, line),
        (ln1_bias, line),
        (b_down, line),
        (ln2_gain, line),
        (ln2_bias, line),
        up_block,
        (b_up.reshape(heads, 1, chunk), line_block),
        (w_down, pl.BlockSpec(memory_space=pl.ANY)),
        (cotangent, whole(square)),
    ]
    outs = [
        (tiles, LOW, tile),
        (tiles, LOW, tile),
        ((4, own_rows, half), LOW, whole((4, own_rows, half))),
        ((heads, own_rows, chunk), F32, by_step(own_rows, chunk)),
        (square, F32, whole(square)),
        ((own_rows, 1), F32, whole((own_rows, 1))),
        (square, F32, whole(square)),
        (square, LOW, whole(square)),
        ((8, width), F32, whole((8, width))),
        ((own_rows, half), LOW, whole((own_rows, half))),
    ]
    scratch = [
        pltpu.VMEM(square, F32),
        pltpu.VMEM(square, LOW),
        pltpu.VMEM((own_rows, hidden_units), LOW),
        pltpu.VMEM(w_down.shape, LOW),
        pltpu.SemaphoreType.DMA,
    ]
    ffn_macs = 2 * own_rows * width * hidden_units
    act_send, act_own, ends, slope, unit1, inv1, res2, layer_output, small_two, tok_send = run(
        feed_forward, places, (heads + 1,), ins, outs, scratch, ffn_macs
    )
    tok_far = swap_core(tok_send)
    act_far = swap_core(act_send)
    ends_far = swap_core(ends)

    def two_of(array, index):
        return (array, pl.BlockSpec((2, own_rows, half), lambda k, s: (index, 0, 0)))

    ins = [two_of(ends, 1), down_block, (slope, by_step(own_rows, chunk))]
    outs = [(tiles, LOW, tile), (tiles, LOW, tile), ((heads, 1, chunk), F32, line_block)]
    scratch = [pltpu.VMEM(square, LOW), pltpu.VMEM((own_rows, chunk), LOW)]
    inner_send, inner_own, up_bias = run(
        inner_back, places, (heads,), ins, outs, scratch, ffn_macs // 2,
        after=[mixes_far],
    )
    inner_far = swap_core(inner_send)


    flipped = [pltpu.VMEM((width, own_rows), LOW)] * 2
    unit_out = [((heads, half, half), LOW, by_step(half, half))] * 2
    ins = [(act_own, tile), (act_far, tile), two_of(ends, 1), two_of(ends_far, 1)]
    made = run(down_grad, places, (heads,), ins, unit_out, flipped, ffn_macs // 2)
    ins = [(inner_own, tile), (inner_far, tile), two_of(ends, 0), two_of(ends_far, 0)]
    made += run(up_grad, places, (heads,), ins, unit_out, flipped, ffn_macs // 2, weight=LIGHT)
    x_send, x_keep, y_send, y_keep = made
    ffn_held = (x_keep, swap(x_send, "near", 1), y_keep, swap(y_send, "near", 2))

    ins = [
        (inner_own, tile),
        (inner_send, tile),
        up_block,
        (res2, whole(square)),
        (unit1, whole(square)),
        (inv1, whole((own_rows, 1))),
        (ln1_gain, line),
    ]
    outs = [
        ((own_rows, half), LOW, whole((own_rows, half))),
        (square, F32, whole(square)),
        (square, LOW, whole(square)),
        ((8, width), F32, whole((8, width))),
    ]
    grad_send, res1, grad_attended, small_one = run(
        hidden_back, places, (heads,), ins, outs, [pltpu.VMEM(square, F32)], ffn_macs // 2,
        weight=LIGHT,
    )
    grad_far = swap_core(grad_send)

    def pair_block(first, *shape):
        block = (None,) + shape
        return pl.BlockSpec(block, lambda k, s: (k + first,) + (0,) * len(shape))

    def attend_back(first, count):
        ins = [
            (qkvs, pair_block(first, rows3, own_rows)),
            (w_outs, pair_block(first, local_width, width)),
            (grad_attended, whole(square)),
            (logs, pair_block(first, 8, own_rows)),
        ] + segs
        outs = [
            ((count, rows3, own_rows), LOW, pair_block(0, rows3, own_rows)),
            ((count, 8, rows3), F32, pair_block(0, 8, rows3)),
        ]
        return run(
            attention_back, places, (count,), ins, outs,
            macs=count * (15 * own_rows * own_rows * 256 + local_width * own_rows * width),
            weight=LIGHT,
        )

    def attend_unit(first, rows, rows_far, qkv_bias, alias):
        bias_line = pl.BlockSpec((None, 1, chunk), lambda k, s: (s[2] ^ (k + first), 0, 0))
        ins = [
            (rows, pair_block(0, rows3, own_rows)),
            (rows_far, pair_block(0, rows3, own_rows)),
            (tok_own, pl.BlockSpec((own_rows, half), lambda k, s: (0, s[1]))),
            (tok_far, whole((own_rows, half))),
            (mixes, pair_block(first, local_width, own_rows)),
            (mixes_far, pair_block(first, local_width, own_rows)),
            (grad_attended, pl.BlockSpec((own_rows, half), lambda k, s: (0, s[1]))),
            (grad_far, whole((own_rows, half))),
            (small_one, whole((8, width))),
            (small_two, whole((8, width))),
            (up_bias, bias_line),
            (qkv_bias, pair_block(0, 8, rows3)),
        ]
        outs = [
            ((heads, r, half), LOW, pair_block(first, r, half))
            for r in (half // 2, (half + EXTRA) // 2)
            for _ in range(2)
        ]
        return run(
            attn_grad, places, (rows.shape[0],), ins, outs, alias=alias, weight=LIGHT
        )

    def second(x_keep, x_came, y_keep, y_came, macs=0):
        arrays = (x_keep, x_came, y_keep, y_came)
        ins = [(a, whole(a.shape)) for a in arrays]
        shapes = [(heads, a.shape[1] // 2, half) for a in (x_keep, x_keep, y_keep, y_keep)]
        outs = [(shape, LOW, whole(shape)) for shape in shapes]
        kernel = functools.partial(add_split, (2, 1))
        return run(kernel, places, (1,), ins, outs, macs=macs)

    def third(x_keep, x_came, y_keep, y_came):
        arrays = (x_keep, x_came, y_keep, y_came)
        shape = (heads // 2, x_keep.shape[1] + y_keep.shape[1], half)
        send, keep = run(
            add_parts, places, (1,), [(a, whole(a.shape)) for a in arrays],
            [(shape, LOW, whole(shape))] * 2, weight=LIGHT,
        )
        return keep, swap(send, "head", 1)

    def fourth(keep, came):
        shape = keep.shape[1:]
        mine, other = run(
            add_pair, places, (1,), [(a, whole(a.shape)) for a in (keep, came)],
            [(shape, LOW, whole(shape))] * 2, weight=LIGHT,
        )
        return mine, swap(other, "head", 2)

    def fifth(mine, came):
        shape = mine.shape
        (total,) = run(
            add_two, places, (1,), [(a, whole(shape)) for a in (mine, came)],
            [(shape, LOW, whole(shape))], weight=LIGHT,
        )
        bit = 1
        while bit < lax.axis_size("far"):
            total = (total.astype(F32) + swap(total, "far", bit).astype(F32)).astype(LOW)
            bit *= 2
        return total

    def cross(made, flip):
        x_send, x_keep, y_send, y_keep = made
        x_bit, y_bit = (2, 1) if flip else (1, 2)
        return x_keep, swap(x_send, "near", x_bit), y_keep, swap(y_send, "near", y_bit)

    rows, qkv_bias = attend_back(0, heads)
    rows_far = swap_core(rows)

    ins = [
        (rows, by_step(rows3, own_rows)),
        (w_qkvs, by_step(rows3, width)),
        (res1, whole(square)),
    ]
    outs = [(square, F32, whole(square))]
    (input_grad,) = run(input_sum, places, (heads,), ins, outs, weight=LIGHT)
    ffn_held = cross(second(*ffn_held, ffn_macs), True)
    made = attend_unit(0, rows, rows_far, qkv_bias, ())
    attn_held = cross(made, False)

    ffn_held = third(*ffn_held)
    attn_held = cross(second(*attn_held), True)
    ffn_held = fourth(*ffn_held)
    attn_held = third(*attn_held)
    attn_held = fourth(*attn_held)
    ffn_held = gather_back(fifth(*ffn_held))
    attn_held = gather_back(fifth(*attn_held))

    outs = [(shape, F32, whole(shape)) for shape in ((chunk, width), (width, chunk))]
    grad_down, grad_up = run(
        ffn_place, places, (1,), ffn_held, outs, [pltpu.VMEM((width, chunk), F32)]
    )
    shapes = [
        (3, width, local_width),
        (local_width, width),
        (6, width),
        (1, chunk),
        (2, local_width),
    ]
    grad_qkv, grad_out, grad_small, grad_up_bias, grad_qv_bias = run(
        attn_place,
        places,
        (1,),
        attn_held,
        [(shape, F32, whole(shape)) for shape in shapes],
        [pltpu.VMEM((width + EXTRA, width), F32)],
    )
    return (
        layer_output,
        input_grad,
        grad_qkv,
        grad_qv_bias,
        grad_out,
        grad_up,
        grad_up_bias[0],
        grad_down,
        grad_small,
    )


def solution(mesh):
    batch, heads = mesh.devices.shape
    mesh = Mesh(
        mesh.devices.reshape(batch // 8, 4, 2, heads), ("far", "near", "core", "head")
    )
    group = ("far", "near", "core")
    everyone = group + ("head",)
    in_specs = (
        P(group, None),
        P(group),
        P(None, None, "head"),
        P(None, "head"),
        P("head", None),
        P(),
        P(),
        P(),
        P(),
        P(),
        P(),
        P(),
        P(),
        P(),
        P(everyone, None),
    )
    out_specs = (
        P(everyone, None),
        P(everyone, None),
        P(None, None, "head"),
        P(None, "head"),
        P("head", None),
        P(None, "head"),
        P("head"),
        P("head", None),
        P(),
    )
    return jax.shard_map(
        per_device, mesh=mesh, in_specs=in_specs, out_specs=out_specs, check_vma=False
    )
```

```python
import functools
import math

import jax
import jax.numpy as jnp
from jax import lax
from jax.experimental import pallas as pl
from jax.experimental.pallas import tpu as pltpu
from jax.sharding import Mesh
from jax.sharding import PartitionSpec as P

HEAD_DIM = 64
SLOT = 512
LOW = jnp.bfloat16
F32 = jnp.float32
LOG2E = math.log2(math.e)
SCORE_SCALE = HEAD_DIM ** (-0.5) * LOG2E
SPARE_BYTES = 12 * 2**20
EXTRA = 64
LIGHT = 0.01
CHAIN = []
TAIL_SLOPE = 0.36
TAIL = (
    0.14371304537508633,
    0.14177245466203425,
    0.1397192603907239,
    0.026549325413860486,
    0.18095403134327948,
    -0.1797647161697652,
    0.047056295581175855,
)


def swap(value, axis, bit):
    size = lax.axis_size(axis)
    return lax.ppermute(value, axis, [(i, i ^ bit) for i in range(size)])


def swap_core(value):
    return swap(value, "core", 1)


def dot(a, b):
    return jnp.dot(a, b, preferred_element_type=F32)


def dot_nt(a, b):
    return lax.dot_general(a, b, (((1,), (1,)), ((), ())), preferred_element_type=F32)


def dot_tn(a, b):
    return lax.dot_general(a, b, (((0,), (0,)), ((), ())), preferred_element_type=F32)


def whole(shape):
    return pl.BlockSpec(shape, lambda *args: (0,) * len(shape), pipeline_mode=pl.Buffered(1))


def run(
    kernel, places, grid, ins, outs, scratch=(), macs=0, after=(), alias=(), weight=8, chain=True
):
    moved = sum(a.size * a.dtype.itemsize for a, spec in ins)
    moved += sum(math.prod(shape) * jnp.dtype(kind).itemsize for shape, kind, spec in outs)
    after = list(after) + (CHAIN if chain else [])
    count, unread = len(ins), len(alias) + len(after)
    results = len(outs)
    flag = (8, 128)
    if chain:
        outs = outs + [(flag, F32, whole(flag))]

    def body(places, *refs):
        made = refs[count + unread :]
        if chain:

            @pl.when(pl.program_id(0) == 0)
            def _():
                made[results][...] = jnp.zeros(flag, F32)

        kernel(places, *refs[:count], *made[:results], *made[len(outs) :])

    held = pl.BlockSpec(memory_space=pl.ANY)
    room = SPARE_BYTES
    for shape, kind, spec in outs + [(a.shape, a.dtype, spec) for a, spec in ins]:
        if spec.block_shape is not None:
            block = math.prod(1 if n is None else n for n in spec.block_shape)
            copies = 2 if spec.pipeline_mode is None else 1
            room += copies * block * jnp.dtype(kind).itemsize
    for ref in scratch:
        if hasattr(ref, "shape") and ref.dtype in (LOW, F32):
            room += math.prod(ref.shape) * jnp.dtype(ref.dtype).itemsize
    made = pl.pallas_call(
        body,
        name=getattr(kernel, "func", kernel).__name__,
        grid_spec=pltpu.PrefetchScalarGridSpec(
            num_scalar_prefetch=1,
            grid=grid,
            in_specs=[spec for a, spec in ins] + [held] * unread,
            out_specs=[spec for shape, kind, spec in outs],
            scratch_shapes=list(scratch),
        ),
        out_shape=[jax.ShapeDtypeStruct(shape, kind) for shape, kind, spec in outs],
        input_output_aliases={1 + count + i: i for i in range(len(alias))},
        compiler_params=pltpu.CompilerParams(vmem_limit_bytes=room),
        cost_estimate=pl.CostEstimate(
            flops=int(2 * macs * weight), bytes_accessed=int(moved * weight), transcendentals=0
        ),
    )(places, *[a for a, spec in ins], *alias, *after)
    if chain:
        CHAIN[:] = made[results:]
    return made[:results]


def mask_rows(seg_col, seg_row):
    return jnp.where(seg_col == seg_row, 0.0, -1e30)


def attend_heads(tok, w_rows, bias, seg_col, seg_row, qkv_ref, mix_ref, log_ref):
    width = w_rows.shape[0] // 3
    added = dot_tn(bias[:, : 2 * width], jnp.ones((bias.shape[0], tok.shape[0]), LOW))
    qkv = dot_nt(w_rows, tok)
    parts = (
        (qkv[:width] + added[:width]).astype(LOW),
        qkv[width : 2 * width].astype(LOW),
        (qkv[2 * width :] + added[width:]).astype(LOW),
    )
    for c in range(3):
        qkv_ref[c * width : (c + 1) * width] = parts[c]
    masked = mask_rows(seg_col, seg_row)
    for head in range(width // HEAD_DIM):
        q, k, v = (part[head * HEAD_DIM : (head + 1) * HEAD_DIM] for part in parts)
        scores = dot_tn(k, q) + masked
        top = jnp.max(scores, 0, keepdims=True)
        exponent = jnp.exp2((scores - top) * SCORE_SCALE)
        total = jnp.sum(exponent, 0, keepdims=True)
        attend = (exponent * (1.0 / total)).astype(LOW)
        mix_ref[head * HEAD_DIM : (head + 1) * HEAD_DIM] = dot(v, attend).astype(LOW)
        log_ref[head : head + 1] = top * SCORE_SCALE + jnp.log2(total)


def own_attention(
    places, tok, w, bias, seg_col, seg_row, qkv_ref, mix_ref, log_ref, w_qkv, w_out
):
    w_qkv[...] = w[: qkv_ref.shape[0]]
    w_out[...] = w[qkv_ref.shape[0] :]
    attend_heads(
        tok[...],
        w[: qkv_ref.shape[0]],
        bias[...],
        seg_col[...],
        seg_row[...],
        qkv_ref,
        mix_ref,
        log_ref,
    )


def far_attention(
    order, places, tok, pair, rest, pair_far, rest_far, bias, seg_col, seg_row,
    qkv_ref, mix_ref, log_ref, w_qkv, w_out, w_ref,
):
    first, second = order
    rows = pair.shape[1]
    me = places[0] * 2 + places[1]
    for other, held in enumerate(((pair, rest), (pair_far, rest_far))):
        for two, block in enumerate(held):
            for one in range(2):
                owner = me ^ (other + 2 * first * one + 2 * second * two)
                w_ref[pl.ds(pl.multiple_of(owner * rows, rows), rows)] = block[one]
    w_qkv[...] = w_ref[: qkv_ref.shape[0]]
    w_out[...] = w_ref[qkv_ref.shape[0] :]
    attend_heads(
        tok[...],
        w_ref[: qkv_ref.shape[0]],
        bias[...],
        seg_col[...],
        seg_row[...],
        qkv_ref,
        mix_ref,
        log_ref,
    )


def take_rows(places, rows, out):
    out[...] = rows[...]


def pair_rows(places, first, second, out):
    out[0] = first[...]
    out[1] = second[...]


def norm_stats(v):
    centred = v - jnp.mean(v, -1, keepdims=True)
    inv = lax.rsqrt(jnp.mean(centred * centred, -1, keepdims=True) + 1e-05)
    return centred * inv, inv


def norm_back(upstream, unit, inv, gain):
    scaled = upstream * gain
    inner = jnp.mean(scaled * unit, -1, keepdims=True)
    return inv * (scaled - jnp.mean(scaled, -1, keepdims=True) - unit * inner)


def gelu_both(pre):
    power = jnp.exp2(pre * pre * (-0.5 * LOG2E))
    base = 1.0 + TAIL_SLOPE * jnp.abs(pre)
    t = pl.reciprocal(base, approx=True)
    t = t * (2.0 - base * t)
    tail = TAIL[6] * t + TAIL[5]
    for c in TAIL[4::-1]:
        tail = tail * t + c
    tail = tail * (t * power)
    cumul = jnp.where(pre < 0.0, tail, 1.0 - tail)
    return (pre * cumul).astype(LOW), cumul + pre * (power * 0.3989422804014327)


def feed_forward(
    places, tok, mix, w_out, b_out, gain1, shift1, b_down, gain2, shift2,
    w_up, b_up, w_down, cot,
    send, own, ends, slope, unit1, inv1, res2, out, small, tok_send,
    hidden, low, acts, down, sem,
):
    k = pl.program_id(0)
    half = send.shape[1]
    chunk = w_up.shape[1]
    core, z = places[1], places[2]
    heads = mix.shape[0]
    fetch = pltpu.make_async_copy(w_down, down, sem)
    b_out, gain1, shift1, b_down, gain2, shift2 = (
        ref[...].reshape(1, -1) for ref in (b_out, gain1, shift1, b_down, gain2, shift2)
    )

    @pl.when(k == 0)
    def _():
        fetch.start()
        tok_send[...] = jnp.where(core == 0, tok[:, half:], tok[:, :half])
        attended = b_out
        for d in range(heads):
            attended = attended + dot_tn(mix[d], w_out[d])
        unit, inv = norm_stats(tok[...].astype(F32) + attended)
        unit1[...] = unit
        inv1[...] = inv
        one = unit * gain1 + shift1
        hidden[...] = one
        one_low = one.astype(LOW)
        low[...] = one_low
        ends[0] = one_low[:, :half]
        ends[1] = one_low[:, half:]

    @pl.when(k < heads)
    def _():
        start = (z ^ k) * chunk
        block = 256
        for j in range(chunk // block):
            at = slice(j * block, (j + 1) * block)
            pre = dot(low[...], w_up[:, at]) + b_up[:, at]
            act, tilt = gelu_both(pre)
            slope[:, at] = tilt.astype(LOW)
            acts[:, pl.ds(pl.multiple_of(start + j * block, block), block)] = act
        left = acts[:, pl.ds(pl.multiple_of(start, 128), half)]
        right = acts[:, pl.ds(pl.multiple_of(start + half, 128), half)]
        own[...] = jnp.where(core == 0, left, right)
        send[...] = jnp.where(core == 0, right, left)

    @pl.when(k == heads)
    def _():
        fetch.wait()
        unit, inv = norm_stats(hidden[...] + (dot(acts[...], down[...]) + b_down))
        out[...] = (unit * gain2 + shift2).astype(LOW)
        upstream = cot[...].astype(F32)
        grad = norm_back(upstream, unit, inv, gain2)
        res2[...] = grad
        grad_low = grad.astype(LOW)
        ends[2] = grad_low[:, :half]
        ends[3] = grad_low[:, half:]
        small[0:1] = jnp.sum(grad_low.astype(F32), 0, keepdims=True)
        small[1:2] = jnp.sum(upstream * unit, 0, keepdims=True)
        small[2:3] = jnp.sum(upstream, 0, keepdims=True)


def inner_back(places, ends, w_down, slope, send, own, bias, branch, inners):
    half = send.shape[1]
    core = places[1]

    @pl.when(pl.program_id(0) == 0)
    def _():
        branch[:, :half] = ends[0]
        branch[:, half:] = ends[1]

    block = 256
    for j in range(inners.shape[1] // block):
        at = slice(j * block, (j + 1) * block)
        inner = (dot_nt(branch[...], w_down[at]) * slope[:, at].astype(F32)).astype(LOW)
        inners[:, at] = inner
        bias[:, at] = jnp.sum(inner.astype(F32), 0, keepdims=True)
    first, second = inners[:, :half], inners[:, half:]
    own[...] = jnp.where(core == 0, first, second)
    send[...] = jnp.where(core == 0, second, first)


def hidden_back(
    places, own, sent, w_up, res2, unit1, inv1, gain1, send, res1, low, small, acc
):
    k = pl.program_id(0)
    core = places[1]
    half = own.shape[1]
    mine, other = own[...], sent[...]
    inner = jnp.concatenate(
        [jnp.where(core == 0, mine, other), jnp.where(core == 0, other, mine)], 1
    )
    product = dot_nt(inner, w_up[...])

    @pl.when(k == 0)
    def _():
        acc[...] = res2[...] + product

    @pl.when(k > 0)
    def _():
        acc[...] += product

    @pl.when(k == pl.num_programs(0) - 1)
    def _():
        grad = acc[...]
        result = norm_back(grad, unit1[...], inv1[...], gain1[...].reshape(1, -1))
        res1[...] = result
        result_low = result.astype(LOW)
        low[...] = result_low
        send[...] = jnp.where(core == 0, result_low[:, half:], result_low[:, :half])
        small[0:1] = jnp.sum(result_low.astype(F32), 0, keepdims=True)
        small[1:2] = jnp.sum(grad * unit1[...], 0, keepdims=True)
        small[2:3] = jnp.sum(grad, 0, keepdims=True)


def attention_back(places, qkv, w_out, grad, log_ref, seg_col, seg_row, rows_ref, bias_ref):
    width = qkv.shape[0] // 3
    grad_mixed = dot_nt(w_out[...], grad[...]).astype(LOW)
    masked = mask_rows(seg_col[...], seg_row[...])
    scale = HEAD_DIM ** (-0.5)
    for head in range(width // HEAD_DIM):
        places_of = [c * width + head * HEAD_DIM for c in range(3)]
        q, k, v = (qkv[at : at + HEAD_DIM] for at in places_of)
        g = grad_mixed[head * HEAD_DIM : (head + 1) * HEAD_DIM]
        scores = dot_tn(k, q) + masked
        attend = jnp.exp2(scores * SCORE_SCALE - log_ref[head : head + 1])
        attend_low = attend.astype(LOW)
        grad_v = dot_nt(g, attend_low)
        product = attend * dot_tn(v, g)
        inner = jnp.sum(product, 0, keepdims=True)
        grad_scores = (product - attend * inner).astype(LOW)
        grad_q = dot(k, grad_scores) * scale
        grad_k = dot_nt(q, grad_scores) * scale
        for at, value in zip(places_of, (grad_q, grad_k, grad_v)):
            rows_ref[at : at + HEAD_DIM] = value.astype(LOW)
    ones = jnp.ones((8, rows_ref.shape[1]), LOW)
    bias_ref[...] = dot_nt(ones, rows_ref[...])


def split_rows(value, high, send, keep):
    rows = value.shape[0] // 2
    low = value.astype(LOW)
    send[...] = jnp.where(high, low[:rows], low[rows:])
    keep[...] = jnp.where(high, low[rows:], low[:rows])


def is_high(places, bit):
    return (places[0] & bit) != 0


def unit_rows(places, units, units_far, ends, ends_far, near, far):
    half = ends.shape[2]

    @pl.when(pl.program_id(0) == 0)
    def _():
        for side in range(2):
            rows = slice(side * half, (side + 1) * half)
            near[rows] = ends[side].T
            far[rows] = ends_far[side].T

    return dot(near[...], units[...]) + dot(far[...], units_far[...])


def down_grad(places, units, units_far, ends, ends_far, send, keep, near, far):
    total = unit_rows(places, units, units_far, ends, ends_far, near, far)
    split_rows(total, is_high(places, 1), send, keep)


def up_grad(places, units, units_far, ends, ends_far, send, keep, near, far):
    total = unit_rows(places, units, units_far, ends, ends_far, near, far)
    split_rows(total, is_high(places, 2), send, keep)


def attn_grad(
    places, rows, rows_far, tok, tok_far, mix, mix_far, grad, grad_far,
    small_one, small_two, up_bias, qkv_bias, send_x, keep_x, send_y, keep_y,
):
    width = mix.shape[0]
    half = tok.shape[1]
    qkv = dot(rows[...], tok[...]) + dot(rows_far[...], tok_far[...])
    out = dot(mix[...], grad[...]) + dot(mix_far[...], grad_far[...])
    lines = []
    for held in (small_one, small_two):
        for i in range(3):
            lines += [held[i : i + 1, :half], held[i : i + 1, half:]]
    lines += [up_bias[:, :half], up_bias[:, half:]]
    lines.append(jnp.concatenate([qkv_bias[0:1, :width], qkv_bias[0:1, 2 * width :]], 1))
    lines.append(jnp.zeros((EXTRA - len(lines), half), F32))
    total = jnp.concatenate([qkv, out] + lines, 0)
    split_rows(total[:half], is_high(places, 1), send_x, keep_x)
    split_rows(total[half:], is_high(places, 2), send_y, keep_y)


def add_split(bits, places, *refs):
    for i, bit in enumerate(bits):
        keep, came = refs[2 * i : 2 * i + 2]
        send, left = refs[2 * (len(bits) + i) : 2 * (len(bits) + i) + 2]
        for d in range(keep.shape[0]):
            total = keep[d].astype(F32) + came[d].astype(F32)
            split_rows(total, is_high(places, bit), send.at[d], left.at[d])


def add_parts(places, keep_a, came_a, keep_b, came_b, send, keep):
    rows = keep_a.shape[1]
    for d in range(keep_a.shape[0]):
        out = (send if d % 2 else keep).at[d // 2]
        out[:rows] = (keep_a[d].astype(F32) + came_a[d].astype(F32)).astype(LOW)
        out[rows:] = (keep_b[d].astype(F32) + came_b[d].astype(F32)).astype(LOW)


def add_pair(places, keep, came, *outs):
    for i, out in enumerate(outs):
        out[...] = (keep[i].astype(F32) + came[i].astype(F32)).astype(LOW)


def add_two(places, keep, came, out):
    out[...] = (keep[...].astype(F32) + came[...].astype(F32)).astype(LOW)


def input_sum(places, rows, w, res1, out):
    total = dot_tn(rows[...], w[...])
    k = pl.program_id(0)
    out[...] = jnp.where(k == 0, res1[...], out[...]) + total


def place_pieces(places, held, full, layouts):
    near, core = places[0], places[1]
    width = held[0].shape[1]
    for off in range(4):
        chip = near ^ off
        mine, other = held[off][...], held[4 + off][...]
        sides = (jnp.where(core == 0, mine, other), jnp.where(core == 0, other, mine))
        for at, rows, start, outer in layouts:
            low_bit, high_bit = chip & 1, chip >> 1
            order = 2 * low_bit + high_bit if outer == 1 else 2 * high_bit + low_bit
            to = pl.multiple_of(start + order * rows, 16)
            for side in range(2):
                full[pl.ds(to, rows), side * width : (side + 1) * width] = sides[side][
                    at : at + rows
                ].astype(F32)


def ffn_place(places, *refs):
    held, (down, up, full) = refs[:8], refs[8:]
    rows = held[0].shape[0] // 2
    place_pieces(places, held, full, [(0, rows, 0, 1)])
    down[...] = full[...].T
    place_pieces(places, held, up, [(rows, rows, 0, 2)])


def attn_place(places, *refs):
    held, (qkv, w_out, small, up_bias, qv_bias, full) = refs[:8], refs[8:]
    width = held[0].shape[1]
    count = w_out.shape[0]
    rows = count // 2
    more = held[0].shape[0] - rows
    place_pieces(places, held, full, [(0, rows, 0, 1), (rows, more, 4 * rows, 2)])
    for c in range(3):
        qkv[c] = full[c * count : (c + 1) * count]
    w_out[...] = full[3 * count : 4 * count]
    at = 4 * count
    lines = full[at : at + 16, :width] + full[at : at + 16, width:]
    for i in range(6):
        small[i : i + 1, :width] = lines[2 * i : 2 * i + 1]
        small[i : i + 1, width:] = lines[2 * i + 1 : 2 * i + 2]
    up_bias[...] = jnp.concatenate([lines[12:13], lines[13:14]], 1).reshape(2 * width)
    qv_bias[0:1] = lines[14:15, :count]
    qv_bias[1:2] = lines[14:15, count : 2 * count]


def bias_parts(values):
    rows, rest = [], values
    for _ in range(3):
        rows.append(lax.reduce_precision(rest, 8, 7))
        rest = rest - rows[-1]
    return jnp.stack(rows).astype(LOW)


def gather_back(piece):
    held = [piece] + [swap(piece, "near", off) for off in range(1, 4)]
    held += [swap_core(h) for h in held]
    return [(h, whole(h.shape)) for h in held]


def per_device(
    tokens,
    segment_ids,
    w_qkv,
    b_qv,
    w_out,
    b_out,
    ln1_gain,
    ln1_bias,
    w_up,
    b_up,
    w_down,
    b_down,
    ln2_gain,
    ln2_bias,
    cotangent,
):
    CHAIN.clear()
    width = tokens.shape[1]
    own_rows = cotangent.shape[0]
    local_width = w_qkv.shape[2]
    heads = lax.axis_size("head")
    z = lax.axis_index("head")
    core = lax.axis_index("core")
    near = lax.axis_index("near")
    hidden_units = w_up.shape[1]
    chunk = hidden_units // heads
    half = width // 2
    rows3 = 3 * local_width
    places = jnp.stack([near, core, z]).astype(jnp.int32)

    shard = jnp.concatenate([w_qkv.transpose(0, 2, 1).reshape(rows3, width), w_out], 0)
    piece_rows = shard.shape[0] // 8
    bias = jnp.pad(bias_parts(b_qv.reshape(-1)), ((0, 13), (0, width - 2 * local_width)))
    piece = lax.dynamic_slice_in_dim(shard, (near * 2 + core) * piece_rows, piece_rows, 0)
    piece = jnp.concatenate([piece, bias], 0)
    first_hop = [swap(piece, "head", d) for d in range(1, heads)]

    seg = lax.dynamic_slice_in_dim(segment_ids, z * own_rows, own_rows, 0)
    segs = [
        (seg[:, None], whole((own_rows, 1))),
        (seg[None], whole((1, own_rows))),
    ]
    tok_own = lax.dynamic_slice_in_dim(tokens, z * own_rows, own_rows, 0)
    own_tokens = (tok_own, whole((own_rows, width)))

    def attend_outs(first):
        def spec(*shape):
            return pl.BlockSpec((None,) + shape, lambda k, s: (k + first, 0, 0))

        return [
            ((heads, rows3, own_rows), LOW, spec(rows3, own_rows)),
            ((heads, local_width, own_rows), LOW, spec(local_width, own_rows)),
            ((heads, 8, own_rows), F32, spec(8, own_rows)),
            ((heads, rows3, width), LOW, spec(rows3, width)),
            ((heads, local_width, width), LOW, spec(local_width, width)),
        ]

    macs = rows3 * width * own_rows + 6 * own_rows * own_rows * 256
    ins = [own_tokens, (shard, whole(shard.shape)), (bias, whole(bias.shape))] + segs
    made = begun = run(own_attention, places, (1,), ins, attend_outs(0), macs=macs, chain=False)
    block = pl.BlockSpec((piece_rows, width), lambda k, s: (0, 0))
    mines = []
    for d in range(1, heads):
        mines += run(
            take_rows, places, (1,), [(first_hop[d - 1], block)],
            [((piece_rows, width), LOW, block)], after=[begun[2]] + mines, weight=LIGHT, chain=False,
        )
    orders = [(1, 2) if d % 2 else (2, 1) for d in range(heads)]
    nexts = [swap(mines[d - 1], "near", orders[d][0]) for d in range(1, heads)]
    for d in range(1, heads):
        order = orders[d]
        ins = [(mines[d - 1], block), (nexts[d - 1], block)]
        twice = (2, piece_rows, width)
        (pair,) = run(
            pair_rows, places, (1,), ins, [(twice, LOW, whole(twice))],
            after=nexts, weight=LIGHT, chain=False,
        )
        rest = swap(pair, "near", order[1])
        held = [pair, rest, swap_core(pair), swap_core(rest)]
        ins = [own_tokens] + [(h, whole(h.shape)) for h in held]
        ins += [(first_hop[d - 1], pl.BlockSpec((16, width), lambda k, s: (piece_rows // 16, 0)))]
        kernel = functools.partial(far_attention, order)
        made = run(
            kernel, places, (1,), ins + segs, attend_outs(d), [pltpu.VMEM((rows3 + local_width, width), LOW)], macs, alias=made,
            chain=False, weight=100,
        )
    qkvs, mixes, logs, w_qkvs, w_outs = made

    mixes_far = swap_core(mixes)

    def by_step(*shape):
        block = (None,) + shape
        return pl.BlockSpec(block, lambda k, s: (jnp.minimum(k, heads - 1),) + (0,) * len(shape))

    def unit_at(k, s):
        return s[2] ^ jnp.minimum(k, heads - 1)


    line = whole((width,))
    square = (own_rows, width)
    tile = by_step(own_rows, half)
    tiles = (heads, own_rows, half)
    up_block = (w_up, pl.BlockSpec((width, chunk), lambda k, s: (0, unit_at(k, s))))
    down_block = (w_down, pl.BlockSpec((chunk, width), lambda k, s: (unit_at(k, s), 0)))
    line_block = pl.BlockSpec((None, 1, chunk), lambda k, s: (unit_at(k, s), 0, 0))

    ins = [
        own_tokens,
        (mixes, whole(mixes.shape)),
        (w_outs, whole(w_outs.shape)),
        (b_out, line),
        (ln1_gain, line),
        (ln1_bias, line),
        (b_down, line),
        (ln2_gain, line),
        (ln2_bias, line),
        up_block,
        (b_up.reshape(heads, 1, chunk), line_block),
        (w_down, pl.BlockSpec(memory_space=pl.ANY)),
        (cotangent, whole(square)),
    ]
    outs = [
        (tiles, LOW, tile),
        (tiles, LOW, tile),
        ((4, own_rows, half), LOW, whole((4, own_rows, half))),
        ((heads, own_rows, chunk), LOW, by_step(own_rows, chunk)),
        (square, F32, whole(square)),
        ((own_rows, 1), F32, whole((own_rows, 1))),
        (square, F32, whole(square)),
        (square, LOW, whole(square)),
        ((8, width), F32, whole((8, width))),
        ((own_rows, half), LOW, whole((own_rows, half))),
    ]
    scratch = [
        pltpu.VMEM(square, F32),
        pltpu.VMEM(square, LOW),
        pltpu.VMEM((own_rows, hidden_units), LOW),
        pltpu.VMEM(w_down.shape, LOW),
        pltpu.SemaphoreType.DMA,
    ]
    ffn_macs = 2 * own_rows * width * hidden_units
    act_send, act_own, ends, slope, unit1, inv1, res2, layer_output, small_two, tok_send = run(
        feed_forward, places, (heads + 1,), ins, outs, scratch, ffn_macs
    )
    tok_far = swap_core(tok_send)
    act_far = swap_core(act_send)
    ends_far = swap_core(ends)

    def two_of(array, index):
        return (array, pl.BlockSpec((2, own_rows, half), lambda k, s: (index, 0, 0)))

    ins = [two_of(ends, 1), down_block, (slope, by_step(own_rows, chunk))]
    outs = [(tiles, LOW, tile), (tiles, LOW, tile), ((heads, 1, chunk), F32, line_block)]
    scratch = [pltpu.VMEM(square, LOW), pltpu.VMEM((own_rows, chunk), LOW)]
    inner_send, inner_own, up_bias = run(
        inner_back, places, (heads,), ins, outs, scratch, ffn_macs // 2,
        after=[mixes_far],
    )
    inner_far = swap_core(inner_send)


    flipped = [pltpu.VMEM((width, own_rows), LOW)] * 2
    unit_out = [((heads, half, half), LOW, by_step(half, half))] * 2
    ins = [(act_own, tile), (act_far, tile), two_of(ends, 1), two_of(ends_far, 1)]
    made = run(down_grad, places, (heads,), ins, unit_out, flipped, ffn_macs // 2)
    ins = [(inner_own, tile), (inner_far, tile), two_of(ends, 0), two_of(ends_far, 0)]
    made += run(up_grad, places, (heads,), ins, unit_out, flipped, ffn_macs // 2, weight=LIGHT)
    x_send, x_keep, y_send, y_keep = made
    ffn_held = (x_keep, swap(x_send, "near", 1), y_keep, swap(y_send, "near", 2))

    ins = [
        (inner_own, tile),
        (inner_send, tile),
        up_block,
        (res2, whole(square)),
        (unit1, whole(square)),
        (inv1, whole((own_rows, 1))),
        (ln1_gain, line),
    ]
    outs = [
        ((own_rows, half), LOW, whole((own_rows, half))),
        (square, F32, whole(square)),
        (square, LOW, whole(square)),
        ((8, width), F32, whole((8, width))),
    ]
    grad_send, res1, grad_attended, small_one = run(
        hidden_back, places, (heads,), ins, outs, [pltpu.VMEM(square, F32)], ffn_macs // 2,
        weight=LIGHT,
    )
    grad_far = swap_core(grad_send)

    def pair_block(first, *shape):
        block = (None,) + shape
        return pl.BlockSpec(block, lambda k, s: (k + first,) + (0,) * len(shape))

    def attend_back(first, count):
        ins = [
            (qkvs, pair_block(first, rows3, own_rows)),
            (w_outs, pair_block(first, local_width, width)),
            (grad_attended, whole(square)),
            (logs, pair_block(first, 8, own_rows)),
        ] + segs
        outs = [
            ((count, rows3, own_rows), LOW, pair_block(0, rows3, own_rows)),
            ((count, 8, rows3), F32, pair_block(0, 8, rows3)),
        ]
        return run(
            attention_back, places, (count,), ins, outs,
            macs=count * (15 * own_rows * own_rows * 256 + local_width * own_rows * width),
            weight=LIGHT,
        )

    def attend_unit(first, rows, rows_far, qkv_bias, alias):
        bias_line = pl.BlockSpec((None, 1, chunk), lambda k, s: (s[2] ^ (k + first), 0, 0))
        ins = [
            (rows, pair_block(0, rows3, own_rows)),
            (rows_far, pair_block(0, rows3, own_rows)),
            (tok_own, pl.BlockSpec((own_rows, half), lambda k, s: (0, s[1]))),
            (tok_far, whole((own_rows, half))),
            (mixes, pair_block(first, local_width, own_rows)),
            (mixes_far, pair_block(first, local_width, own_rows)),
            (grad_attended, pl.BlockSpec((own_rows, half), lambda k, s: (0, s[1]))),
            (grad_far, whole((own_rows, half))),
            (small_one, whole((8, width))),
            (small_two, whole((8, width))),
            (up_bias, bias_line),
            (qkv_bias, pair_block(0, 8, rows3)),
        ]
        outs = [
            ((heads, r, half), LOW, pair_block(first, r, half))
            for r in (half // 2, (half + EXTRA) // 2)
            for _ in range(2)
        ]
        return run(
            attn_grad, places, (rows.shape[0],), ins, outs, alias=alias, weight=LIGHT
        )

    def second(x_keep, x_came, y_keep, y_came, macs=0):
        arrays = (x_keep, x_came, y_keep, y_came)
        ins = [(a, whole(a.shape)) for a in arrays]
        shapes = [(heads, a.shape[1] // 2, half) for a in (x_keep, x_keep, y_keep, y_keep)]
        outs = [(shape, LOW, whole(shape)) for shape in shapes]
        kernel = functools.partial(add_split, (2, 1))
        return run(kernel, places, (1,), ins, outs, macs=macs)

    def third(x_keep, x_came, y_keep, y_came):
        arrays = (x_keep, x_came, y_keep, y_came)
        shape = (heads // 2, x_keep.shape[1] + y_keep.shape[1], half)
        send, keep = run(
            add_parts, places, (1,), [(a, whole(a.shape)) for a in arrays],
            [(shape, LOW, whole(shape))] * 2, weight=LIGHT,
        )
        return keep, swap(send, "head", 1)

    def fourth(keep, came):
        shape = keep.shape[1:]
        mine, other = run(
            add_pair, places, (1,), [(a, whole(a.shape)) for a in (keep, came)],
            [(shape, LOW, whole(shape))] * 2, weight=LIGHT,
        )
        return mine, swap(other, "head", 2)

    def fifth(mine, came):
        shape = mine.shape
        (total,) = run(
            add_two, places, (1,), [(a, whole(shape)) for a in (mine, came)],
            [(shape, LOW, whole(shape))], weight=LIGHT,
        )
        bit = 1
        while bit < lax.axis_size("far"):
            total = (total.astype(F32) + swap(total, "far", bit).astype(F32)).astype(LOW)
            bit *= 2
        return total

    def cross(made, flip):
        x_send, x_keep, y_send, y_keep = made
        x_bit, y_bit = (2, 1) if flip else (1, 2)
        return x_keep, swap(x_send, "near", x_bit), y_keep, swap(y_send, "near", y_bit)

    rows, qkv_bias = attend_back(0, heads)
    rows_far = swap_core(rows)

    ins = [
        (rows, by_step(rows3, own_rows)),
        (w_qkvs, by_step(rows3, width)),
        (res1, whole(square)),
    ]
    outs = [(square, F32, whole(square))]
    (input_grad,) = run(input_sum, places, (heads,), ins, outs, weight=LIGHT)
    ffn_held = cross(second(*ffn_held, ffn_macs), True)
    made = attend_unit(0, rows, rows_far, qkv_bias, ())
    attn_held = cross(made, False)

    ffn_held = third(*ffn_held)
    attn_held = cross(second(*attn_held), True)
    ffn_held = fourth(*ffn_held)
    attn_held = third(*attn_held)
    ffn_held = gather_back(fifth(*ffn_held))
    attn_held = fourth(*attn_held)
    attn_held = gather_back(fifth(*attn_held))

    outs = [(shape, F32, whole(shape)) for shape in ((chunk, width), (width, chunk))]
    grad_down, grad_up = run(
        ffn_place, places, (1,), ffn_held, outs, [pltpu.VMEM((width, chunk), F32)]
    )
    shapes = [
        (3, local_width, width),
        (local_width, width),
        (6, width),
        (chunk,),
        (2, local_width),
    ]
    grad_qkv, grad_out, grad_small, grad_up_bias, grad_qv_bias = run(
        attn_place,
        places,
        (1,),
        attn_held,
        [(shape, F32, whole(shape)) for shape in shapes],
        [pltpu.VMEM((width + EXTRA, width), F32)],
    )
    return (
        layer_output,
        input_grad,
        grad_qkv.transpose(0, 2, 1),
        grad_qv_bias,
        grad_out,
        grad_up,
        grad_up_bias,
        grad_down,
        grad_small,
    )


def solution(mesh):
    batch, heads = mesh.devices.shape
    mesh = Mesh(
        mesh.devices.reshape(batch // 8, 4, 2, heads), ("far", "near", "core", "head")
    )
    group = ("far", "near", "core")
    everyone = group + ("head",)
    in_specs = (
        P(group, None),
        P(group),
        P(None, None, "head"),
        P(None, "head"),
        P("head", None),
        P(),
        P(),
        P(),
        P(),
        P(),
        P(),
        P(),
        P(),
        P(),
        P(everyone, None),
    )
    out_specs = (
        P(everyone, None),
        P(everyone, None),
        P(None, None, "head"),
        P(None, "head"),
        P("head", None),
        P(None, "head"),
        P("head"),
        P("head", None),
        P(),
    )
    return jax.shard_map(
        per_device, mesh=mesh, in_specs=in_specs, out_specs=out_specs, check_vma=False
    )
```

```python
import functools
import math

import jax
import jax.numpy as jnp
from jax import lax
from jax.experimental import pallas as pl
from jax.experimental.pallas import tpu as pltpu
from jax.sharding import Mesh
from jax.sharding import PartitionSpec as P

HEAD_DIM = 64
SLOT = 512
LOW = jnp.bfloat16
F32 = jnp.float32
LOG2E = math.log2(math.e)
SCORE_SCALE = HEAD_DIM ** (-0.5) * LOG2E
SPARE_BYTES = 12 * 2**20
EXTRA = 64
LIGHT = 0.01
CHAIN = []
TAIL_SLOPE = 0.36
TAIL = (
    0.14371304537508633,
    0.14177245466203425,
    0.1397192603907239,
    0.026549325413860486,
    0.18095403134327948,
    -0.1797647161697652,
    0.047056295581175855,
)


def swap(value, axis, bit):
    size = lax.axis_size(axis)
    return lax.ppermute(value, axis, [(i, i ^ bit) for i in range(size)])


def swap_core(value):
    return swap(value, "core", 1)


def dot(a, b):
    return jnp.dot(a, b, preferred_element_type=F32)


def dot_nt(a, b):
    return lax.dot_general(a, b, (((1,), (1,)), ((), ())), preferred_element_type=F32)


def dot_tn(a, b):
    return lax.dot_general(a, b, (((0,), (0,)), ((), ())), preferred_element_type=F32)


def whole(shape):
    return pl.BlockSpec(shape, lambda *args: (0,) * len(shape), pipeline_mode=pl.Buffered(1))


def run(
    kernel, places, grid, ins, outs, scratch=(), macs=0, after=(), alias=(), weight=8, chain=True
):
    moved = sum(a.size * a.dtype.itemsize for a, spec in ins)
    moved += sum(math.prod(shape) * jnp.dtype(kind).itemsize for shape, kind, spec in outs)
    after = list(after) + (CHAIN if chain else [])
    count, unread = len(ins), len(alias) + len(after)
    results = len(outs)
    flag = (8, 128)
    if chain:
        outs = outs + [(flag, F32, whole(flag))]

    def body(places, *refs):
        made = refs[count + unread :]
        if chain:

            @pl.when(pl.program_id(0) == 0)
            def _():
                made[results][...] = jnp.zeros(flag, F32)

        kernel(places, *refs[:count], *made[:results], *made[len(outs) :])

    held = pl.BlockSpec(memory_space=pl.ANY)
    room = SPARE_BYTES
    for shape, kind, spec in outs + [(a.shape, a.dtype, spec) for a, spec in ins]:
        if spec.block_shape is not None:
            block = math.prod(1 if n is None else n for n in spec.block_shape)
            copies = 2 if spec.pipeline_mode is None else 1
            room += copies * block * jnp.dtype(kind).itemsize
    for ref in scratch:
        if hasattr(ref, "shape") and ref.dtype in (LOW, F32):
            room += math.prod(ref.shape) * jnp.dtype(ref.dtype).itemsize
    made = pl.pallas_call(
        body,
        name=getattr(kernel, "func", kernel).__name__,
        grid_spec=pltpu.PrefetchScalarGridSpec(
            num_scalar_prefetch=1,
            grid=grid,
            in_specs=[spec for a, spec in ins] + [held] * unread,
            out_specs=[spec for shape, kind, spec in outs],
            scratch_shapes=list(scratch),
        ),
        out_shape=[jax.ShapeDtypeStruct(shape, kind) for shape, kind, spec in outs],
        input_output_aliases={1 + count + i: i for i in range(len(alias))},
        compiler_params=pltpu.CompilerParams(vmem_limit_bytes=room),
        cost_estimate=pl.CostEstimate(
            flops=int(2 * macs * weight), bytes_accessed=int(moved * weight), transcendentals=0
        ),
    )(places, *[a for a, spec in ins], *alias, *after)
    if chain:
        CHAIN[:] = made[results:]
    return made[:results]


def mask_rows(seg_col, seg_row):
    return jnp.where(seg_col == seg_row, 0.0, -1e30)


def attend_heads(tok, w_rows, bias, seg_col, seg_row, qkv_ref, mix_ref, log_ref):
    width = w_rows.shape[0] // 3
    added = dot_tn(bias[:, : 2 * width], jnp.ones((bias.shape[0], tok.shape[0]), LOW))
    qkv = dot_nt(w_rows, tok)
    parts = (
        (qkv[:width] + added[:width]).astype(LOW),
        qkv[width : 2 * width].astype(LOW),
        (qkv[2 * width :] + added[width:]).astype(LOW),
    )
    for c in range(3):
        qkv_ref[c * width : (c + 1) * width] = parts[c]
    masked = mask_rows(seg_col, seg_row)
    for head in range(width // HEAD_DIM):
        q, k, v = (part[head * HEAD_DIM : (head + 1) * HEAD_DIM] for part in parts)
        scores = dot_tn(k, q) + masked
        top = jnp.max(scores, 0, keepdims=True)
        exponent = jnp.exp2((scores - top) * SCORE_SCALE)
        total = jnp.sum(exponent, 0, keepdims=True)
        attend = (exponent * (1.0 / total)).astype(LOW)
        mix_ref[head * HEAD_DIM : (head + 1) * HEAD_DIM] = dot(v, attend).astype(LOW)
        log_ref[head : head + 1] = top * SCORE_SCALE + jnp.log2(total)


def own_attention(
    places, tok, w, bias, seg_col, seg_row, qkv_ref, mix_ref, log_ref, w_qkv, w_out
):
    w_qkv[...] = w[: qkv_ref.shape[0]]
    w_out[...] = w[qkv_ref.shape[0] :]
    attend_heads(
        tok[...],
        w[: qkv_ref.shape[0]],
        bias[...],
        seg_col[...],
        seg_row[...],
        qkv_ref,
        mix_ref,
        log_ref,
    )


def far_attention(
    order, places, tok, pair, rest, pair_far, rest_far, bias, seg_col, seg_row,
    qkv_ref, mix_ref, log_ref, w_qkv, w_out, w_ref,
):
    first, second = order
    rows = pair.shape[1]
    me = places[0] * 2 + places[1]
    for other, held in enumerate(((pair, rest), (pair_far, rest_far))):
        for two, block in enumerate(held):
            for one in range(2):
                owner = me ^ (other + 2 * first * one + 2 * second * two)
                w_ref[pl.ds(pl.multiple_of(owner * rows, rows), rows)] = block[one]
    w_qkv[...] = w_ref[: qkv_ref.shape[0]]
    w_out[...] = w_ref[qkv_ref.shape[0] :]
    attend_heads(
        tok[...],
        w_ref[: qkv_ref.shape[0]],
        bias[...],
        seg_col[...],
        seg_row[...],
        qkv_ref,
        mix_ref,
        log_ref,
    )


def pair_rows(places, first, second, out):
    out[0] = first[...]
    out[1] = second[...]


def norm_stats(v):
    centred = v - jnp.mean(v, -1, keepdims=True)
    inv = lax.rsqrt(jnp.mean(centred * centred, -1, keepdims=True) + 1e-05)
    return centred * inv, inv


def norm_back(upstream, unit, inv, gain):
    scaled = upstream * gain
    inner = jnp.mean(scaled * unit, -1, keepdims=True)
    return inv * (scaled - jnp.mean(scaled, -1, keepdims=True) - unit * inner)


def gelu_both(pre):
    power = jnp.exp2(pre * pre * (-0.5 * LOG2E))
    base = 1.0 + TAIL_SLOPE * jnp.abs(pre)
    t = pl.reciprocal(base, approx=True)
    tail = TAIL[6] * t + TAIL[5]
    for c in TAIL[4::-1]:
        tail = tail * t + c
    tail = tail * (t * power)
    cumul = jnp.where(pre < 0.0, tail, 1.0 - tail)
    return (pre * cumul).astype(LOW), cumul + pre * (power * 0.3989422804014327)


def feed_forward(
    places, tok, mix, w_out, b_out, gain1, shift1, b_down, gain2, shift2,
    w_up, b_up, w_down, cot,
    send, own, ends, slope, unit1, inv1, res2, out, small, tok_send,
    hidden, low, acts, down, sem,
):
    k = pl.program_id(0)
    half = send.shape[1]
    chunk = w_up.shape[1]
    core, z = places[1], places[2]
    heads = mix.shape[0]
    fetch = pltpu.make_async_copy(w_down, down, sem)
    b_out, gain1, shift1, b_down, gain2, shift2 = (
        ref[...].reshape(1, -1) for ref in (b_out, gain1, shift1, b_down, gain2, shift2)
    )

    @pl.when(k == 0)
    def _():
        fetch.start()
        tok_send[...] = jnp.where(core == 0, tok[:, half:], tok[:, :half])
        attended = b_out
        for d in range(heads):
            attended = attended + dot_tn(mix[d], w_out[d])
        unit, inv = norm_stats(tok[...].astype(F32) + attended)
        unit1[...] = unit
        inv1[...] = inv
        one = unit * gain1 + shift1
        hidden[...] = one
        one_low = one.astype(LOW)
        low[...] = one_low
        ends[0] = one_low[:, :half]
        ends[1] = one_low[:, half:]

    @pl.when(k < heads)
    def _():
        start = (z ^ k) * chunk
        block = 256
        for j in range(chunk // block):
            at = slice(j * block, (j + 1) * block)
            pre = dot(low[...], w_up[:, at]) + b_up[:, at]
            act, tilt = gelu_both(pre)
            slope[:, at] = tilt.astype(LOW)
            acts[:, pl.ds(pl.multiple_of(start + j * block, block), block)] = act
        left = acts[:, pl.ds(pl.multiple_of(start, 128), half)]
        right = acts[:, pl.ds(pl.multiple_of(start + half, 128), half)]
        own[...] = jnp.where(core == 0, left, right)
        send[...] = jnp.where(core == 0, right, left)

    @pl.when(k == heads)
    def _():
        fetch.wait()
        unit, inv = norm_stats(hidden[...] + (dot(acts[...], down[...]) + b_down))
        out[...] = (unit * gain2 + shift2).astype(LOW)
        upstream = cot[...].astype(F32)
        grad = norm_back(upstream, unit, inv, gain2)
        res2[...] = grad
        grad_low = grad.astype(LOW)
        ends[2] = grad_low[:, :half]
        ends[3] = grad_low[:, half:]
        small[0:1] = jnp.sum(grad_low.astype(F32), 0, keepdims=True)
        small[1:2] = jnp.sum(upstream * unit, 0, keepdims=True)
        small[2:3] = jnp.sum(upstream, 0, keepdims=True)


def inner_back(places, ends, w_down, slope, send, own, bias, branch, inners, down, sem):
    half = send.shape[1]
    core, z = places[1], places[2]
    k = pl.program_id(0)
    heads, chunk, _ = down.shape

    def fetch(i):
        at = pl.ds(pl.multiple_of((z ^ i) * chunk, chunk), chunk)
        return pltpu.make_async_copy(w_down.at[at], down.at[i], sem.at[i])

    @pl.when(k == 0)
    def _():
        for i in range(heads):
            fetch(i).start()
        branch[:, :half] = ends[0]
        branch[:, half:] = ends[1]

    fetch(k).wait()
    block = 256
    for j in range(inners.shape[1] // block):
        at = slice(j * block, (j + 1) * block)
        inner = (dot_nt(branch[...], down[k, at]) * slope[:, at].astype(F32)).astype(LOW)
        inners[:, at] = inner
        bias[:, at] = jnp.sum(inner.astype(F32), 0, keepdims=True)
    first, second = inners[:, :half], inners[:, half:]
    own[...] = jnp.where(core == 0, first, second)
    send[...] = jnp.where(core == 0, second, first)


def hidden_back(
    places, own, sent, w_up, res2, unit1, inv1, gain1, send, res1, low, small, acc
):
    k = pl.program_id(0)
    core = places[1]
    half = own.shape[1]
    mine, other = own[...], sent[...]
    inner = jnp.concatenate(
        [jnp.where(core == 0, mine, other), jnp.where(core == 0, other, mine)], 1
    )
    product = dot_nt(inner, w_up[...])

    @pl.when(k == 0)
    def _():
        acc[...] = res2[...] + product

    @pl.when(k > 0)
    def _():
        acc[...] += product

    @pl.when(k == pl.num_programs(0) - 1)
    def _():
        grad = acc[...]
        result = norm_back(grad, unit1[...], inv1[...], gain1[...].reshape(1, -1))
        res1[...] = result
        result_low = result.astype(LOW)
        low[...] = result_low
        send[...] = jnp.where(core == 0, result_low[:, half:], result_low[:, :half])
        small[0:1] = jnp.sum(result_low.astype(F32), 0, keepdims=True)
        small[1:2] = jnp.sum(grad * unit1[...], 0, keepdims=True)
        small[2:3] = jnp.sum(grad, 0, keepdims=True)


def attention_back(places, qkv, w_out, grad, log_ref, seg_col, seg_row, rows_ref, bias_ref):
    width = qkv.shape[0] // 3
    grad_mixed = dot_nt(w_out[...], grad[...]).astype(LOW)
    masked = mask_rows(seg_col[...], seg_row[...])
    scale = HEAD_DIM ** (-0.5)
    for head in range(width // HEAD_DIM):
        places_of = [c * width + head * HEAD_DIM for c in range(3)]
        q, k, v = (qkv[at : at + HEAD_DIM] for at in places_of)
        g = grad_mixed[head * HEAD_DIM : (head + 1) * HEAD_DIM]
        scores = dot_tn(k, q) + masked
        attend = jnp.exp2(scores * SCORE_SCALE - log_ref[head : head + 1])
        attend_low = attend.astype(LOW)
        grad_v = dot_nt(g, attend_low)
        product = attend * dot_tn(v, g)
        inner = jnp.sum(product, 0, keepdims=True)
        grad_scores = (product - attend * inner).astype(LOW)
        grad_q = dot(k, grad_scores) * scale
        grad_k = dot_nt(q, grad_scores) * scale
        for at, value in zip(places_of, (grad_q, grad_k, grad_v)):
            rows_ref[at : at + HEAD_DIM] = value.astype(LOW)
    ones = jnp.ones((8, rows_ref.shape[1]), LOW)
    bias_ref[...] = dot_nt(ones, rows_ref[...])


def split_rows(value, high, send, keep):
    rows = value.shape[0] // 2
    low = value.astype(LOW)
    send[...] = jnp.where(high, low[:rows], low[rows:])
    keep[...] = jnp.where(high, low[rows:], low[:rows])


def is_high(places, bit):
    return (places[0] & bit) != 0


def unit_rows(units, units_far, ends, ends_far, both):
    half, count = ends.shape[2], ends.shape[1]

    @pl.when(pl.program_id(0) == 0)
    def _():
        for side in range(2):
            rows = slice(side * half, (side + 1) * half)
            both[rows, :count] = ends[side].T
            both[rows, count:] = ends_far[side].T

    left, right = (jnp.concatenate([units[i], units_far[i]], 0) for i in range(2))
    return dot(both[...], jnp.concatenate([left, right], 1))


def ffn_grad(bit, places, units, units_far, ends, ends_far, send, keep, both):
    total = unit_rows(units, units_far, ends, ends_far, both)
    half = send.shape[2]
    for i in range(2):
        part = total[:, i * half : (i + 1) * half]
        split_rows(part, is_high(places, bit), send.at[i], keep.at[i])


def attn_grad(
    places, rows, rows_far, tok, tok_far, mix, mix_far, grad, grad_far,
    small_one, small_two, up_bias, qkv_bias, send_x, keep_x, send_y, keep_y,
):
    width = mix.shape[0]
    half = tok.shape[1]
    def joined(a, a_far, b, b_far):
        left = jnp.concatenate([a[...], a_far[...]], 1)
        return dot(left, jnp.concatenate([b[...], b_far[...]], 0))

    qkv = joined(rows, rows_far, tok, tok_far)
    out = joined(mix, mix_far, grad, grad_far)
    lines = []
    for held in (small_one, small_two):
        for i in range(3):
            lines += [held[i : i + 1, :half], held[i : i + 1, half:]]
    lines += [up_bias[:, :half], up_bias[:, half:]]
    lines.append(jnp.concatenate([qkv_bias[0:1, :width], qkv_bias[0:1, 2 * width :]], 1))
    lines.append(jnp.zeros((EXTRA - len(lines), half), F32))
    total = jnp.concatenate([qkv, out] + lines, 0)
    split_rows(total[:half], is_high(places, 1), send_x, keep_x)
    split_rows(total[half:], is_high(places, 2), send_y, keep_y)


def add_split(bits, places, *refs):
    for i, bit in enumerate(bits):
        keep, came = refs[2 * i : 2 * i + 2]
        send, left = refs[2 * (len(bits) + i) : 2 * (len(bits) + i) + 2]
        for d in range(keep.shape[0]):
            total = keep[d].astype(F32) + came[d].astype(F32)
            split_rows(total, is_high(places, bit), send.at[d], left.at[d])


def add_parts(places, keep_a, came_a, keep_b, came_b, send, keep):
    rows = keep_a.shape[1]
    for d in range(keep_a.shape[0]):
        out = (send if d % 2 else keep).at[d // 2]
        out[:rows] = (keep_a[d].astype(F32) + came_a[d].astype(F32)).astype(LOW)
        out[rows:] = (keep_b[d].astype(F32) + came_b[d].astype(F32)).astype(LOW)


def add_pair(places, keep, came, *outs):
    for i, out in enumerate(outs):
        out[...] = (keep[i].astype(F32) + came[i].astype(F32)).astype(LOW)


def add_two(places, keep, came, out):
    out[...] = (keep[...].astype(F32) + came[...].astype(F32)).astype(LOW)


def input_sum(places, rows, w, res1, out):
    total = dot_tn(rows[...], w[...])
    k = pl.program_id(0)
    out[...] = jnp.where(k == 0, res1[...], out[...]) + total


def place_pieces(places, held, full, layouts):
    near, core = places[0], places[1]
    width = held[0].shape[1]
    for off in range(4):
        chip = near ^ off
        mine, other = held[off][...], held[4 + off][...]
        sides = (jnp.where(core == 0, mine, other), jnp.where(core == 0, other, mine))
        for at, rows, start, outer in layouts:
            low_bit, high_bit = chip & 1, chip >> 1
            order = 2 * low_bit + high_bit if outer == 1 else 2 * high_bit + low_bit
            to = pl.multiple_of(start + order * rows, 16)
            for side in range(2):
                full[pl.ds(to, rows), side * width : (side + 1) * width] = sides[side][
                    at : at + rows
                ].astype(F32)


def ffn_place(places, *refs):
    held = [ref.at[off] for ref in refs[:2] for off in range(4)]
    down, up, full = refs[2:]
    rows = held[0].shape[0] // 2
    place_pieces(places, held, full, [(0, rows, 0, 1)])
    down[...] = full[...].T
    place_pieces(places, held, up, [(rows, rows, 0, 2)])


def collect(places, *refs):
    for off in range(4):
        refs[4][off] = refs[off][...]


def attn_place(places, *refs):
    held = [ref.at[off] for ref in refs[:2] for off in range(4)]
    qkv, w_out, small, up_bias, qv_bias, full = refs[2:]
    width = held[0].shape[1]
    count = w_out.shape[0]
    rows = count // 2
    more = held[0].shape[0] - rows
    place_pieces(places, held, full, [(0, rows, 0, 1), (rows, more, 4 * rows, 2)])
    for c in range(3):
        qkv[c] = full[c * count : (c + 1) * count]
    w_out[...] = full[3 * count : 4 * count]
    at = 4 * count
    lines = full[at : at + 16, :width] + full[at : at + 16, width:]
    for i in range(6):
        small[i : i + 1, :width] = lines[2 * i : 2 * i + 1]
        small[i : i + 1, width:] = lines[2 * i + 1 : 2 * i + 2]
    up_bias[...] = jnp.concatenate([lines[12:13], lines[13:14]], 1).reshape(2 * width)
    qv_bias[0:1] = lines[14:15, :count]
    qv_bias[1:2] = lines[14:15, count : 2 * count]


def bias_parts(values):
    rows, rest = [], values
    for _ in range(3):
        rows.append(lax.reduce_precision(rest, 8, 7))
        rest = rest - rows[-1]
    return jnp.stack(rows).astype(LOW)


def gather_back(piece):
    return [piece] + [swap(piece, "near", off) for off in range(1, 4)]


def per_device(
    tokens,
    segment_ids,
    w_qkv,
    b_qv,
    w_out,
    b_out,
    ln1_gain,
    ln1_bias,
    w_up,
    b_up,
    w_down,
    b_down,
    ln2_gain,
    ln2_bias,
    cotangent,
):
    CHAIN.clear()
    width = tokens.shape[1]
    own_rows = cotangent.shape[0]
    local_width = w_qkv.shape[2]
    heads = lax.axis_size("head")
    z = lax.axis_index("head")
    core = lax.axis_index("core")
    near = lax.axis_index("near")
    hidden_units = w_up.shape[1]
    chunk = hidden_units // heads
    half = width // 2
    rows3 = 3 * local_width
    places = jnp.stack([near, core, z]).astype(jnp.int32)

    shard = jnp.concatenate([w_qkv.transpose(0, 2, 1).reshape(rows3, width), w_out], 0)
    piece_rows = shard.shape[0] // 8
    bias = jnp.pad(bias_parts(b_qv.reshape(-1)), ((0, 13), (0, width - 2 * local_width)))
    piece = lax.dynamic_slice_in_dim(shard, (near * 2 + core) * piece_rows, piece_rows, 0)
    piece = jnp.concatenate([piece, bias], 0)
    first_hop = [swap(piece, "head", d) for d in range(1, heads)]

    seg = lax.dynamic_slice_in_dim(segment_ids, z * own_rows, own_rows, 0)
    segs = [
        (seg[:, None], whole((own_rows, 1))),
        (seg[None], whole((1, own_rows))),
    ]
    tok_own = lax.dynamic_slice_in_dim(tokens, z * own_rows, own_rows, 0)
    own_tokens = (tok_own, whole((own_rows, width)))

    def attend_outs(first):
        def spec(*shape):
            return pl.BlockSpec((None,) + shape, lambda k, s: (k + first, 0, 0))

        return [
            ((heads, rows3, own_rows), LOW, spec(rows3, own_rows)),
            ((heads, local_width, own_rows), LOW, spec(local_width, own_rows)),
            ((heads, 8, own_rows), F32, spec(8, own_rows)),
            ((heads, rows3, width), LOW, spec(rows3, width)),
            ((heads, local_width, width), LOW, spec(local_width, width)),
        ]

    macs = rows3 * width * own_rows + 6 * own_rows * own_rows * 256
    ins = [own_tokens, (shard, whole(shard.shape)), (bias, whole(bias.shape))] + segs
    made = begun = run(own_attention, places, (1,), ins, attend_outs(0), macs=macs, chain=False)
    block = pl.BlockSpec((piece_rows, width), lambda k, s: (0, 0))
    orders = [(1, 2) if d % 2 else (2, 1) for d in range(heads)]
    nexts = [swap(first_hop[d - 1], "near", orders[d][0]) for d in range(1, heads)]
    for d in range(1, heads):
        order = orders[d]
        ins = [(first_hop[d - 1], block), (nexts[d - 1], block)]
        twice = (2, piece_rows, width)
        (pair,) = run(
            pair_rows, places, (1,), ins, [(twice, LOW, whole(twice))],
            after=nexts + [begun[2]], weight=LIGHT, chain=False,
        )
        rest = swap(pair, "near", order[1])
        held = [pair, rest, swap_core(pair), swap_core(rest)]
        ins = [own_tokens] + [(h, whole(h.shape)) for h in held]
        ins += [(first_hop[d - 1], pl.BlockSpec((16, width), lambda k, s: (piece_rows // 16, 0)))]
        kernel = functools.partial(far_attention, order)
        made = run(
            kernel, places, (1,), ins + segs, attend_outs(d), [pltpu.VMEM((rows3 + local_width, width), LOW)], macs, alias=made,
            chain=False, weight=100,
        )
    qkvs, mixes, logs, w_qkvs, w_outs = made

    mixes_far = swap_core(mixes)

    def by_step(*shape):
        block = (None,) + shape
        return pl.BlockSpec(block, lambda k, s: (jnp.minimum(k, heads - 1),) + (0,) * len(shape))

    def unit_at(k, s):
        return s[2] ^ jnp.minimum(k, heads - 1)


    line = whole((width,))
    square = (own_rows, width)
    tile = by_step(own_rows, half)
    tiles = (heads, own_rows, half)
    up_block = (w_up, pl.BlockSpec((width, chunk), lambda k, s: (0, unit_at(k, s))))
    line_block = pl.BlockSpec((None, 1, chunk), lambda k, s: (unit_at(k, s), 0, 0))

    ins = [
        own_tokens,
        (mixes, whole(mixes.shape)),
        (w_outs, whole(w_outs.shape)),
        (b_out, line),
        (ln1_gain, line),
        (ln1_bias, line),
        (b_down, line),
        (ln2_gain, line),
        (ln2_bias, line),
        up_block,
        (b_up.reshape(heads, 1, chunk), line_block),
        (w_down, pl.BlockSpec(memory_space=pl.ANY)),
        (cotangent, whole(square)),
    ]
    outs = [
        (tiles, LOW, tile),
        (tiles, LOW, tile),
        ((4, own_rows, half), LOW, whole((4, own_rows, half))),
        ((heads, own_rows, chunk), LOW, by_step(own_rows, chunk)),
        (square, F32, whole(square)),
        ((own_rows, 1), F32, whole((own_rows, 1))),
        (square, F32, whole(square)),
        (square, LOW, whole(square)),
        ((8, width), F32, whole((8, width))),
        ((own_rows, half), LOW, whole((own_rows, half))),
    ]
    scratch = [
        pltpu.VMEM(square, F32),
        pltpu.VMEM(square, LOW),
        pltpu.VMEM((own_rows, hidden_units), LOW),
        pltpu.VMEM(w_down.shape, LOW),
        pltpu.SemaphoreType.DMA,
    ]
    ffn_macs = 2 * own_rows * width * hidden_units
    act_send, act_own, ends, slope, unit1, inv1, res2, layer_output, small_two, tok_send = run(
        feed_forward, places, (heads + 1,), ins, outs, scratch, ffn_macs
    )
    tok_far = swap_core(tok_send)
    act_far = swap_core(act_send)
    ends_far = swap_core(ends)

    def two_of(array, index):
        return (array, pl.BlockSpec((2, own_rows, half), lambda k, s: (index, 0, 0)))

    ins = [
        two_of(ends, 1),
        (w_down, pl.BlockSpec(memory_space=pl.ANY)),
        (slope, by_step(own_rows, chunk)),
    ]
    outs = [(tiles, LOW, tile), (tiles, LOW, tile), ((heads, 1, chunk), F32, line_block)]
    scratch = [
        pltpu.VMEM(square, LOW),
        pltpu.VMEM((own_rows, chunk), LOW),
        pltpu.VMEM((heads, chunk, width), LOW),
        pltpu.SemaphoreType.DMA((heads,)),
    ]
    inner_send, inner_own, up_bias = run(
        inner_back, places, (heads,), ins, outs, scratch, ffn_macs // 2,
        after=[mixes_far],
    )
    inner_far = swap_core(inner_send)


    def two(*shape):
        return pl.BlockSpec((2,) + shape, lambda k, s: (k,) + (0,) * len(shape))

    def ffn_unit(bit, own, far, which, weight):
        ins = [(own, two(own_rows, half)), (far, two(own_rows, half))]
        ins += [two_of(ends, which), two_of(ends_far, which)]
        outs = [((heads, half, half), LOW, two(half, half))] * 2
        both = [pltpu.VMEM((width, 2 * own_rows), LOW)]
        kernel = functools.partial(ffn_grad, bit)
        return run(kernel, places, (heads // 2,), ins, outs, both, ffn_macs // 2, weight=weight)

    made = ffn_unit(1, act_own, act_far, 1, 8) + ffn_unit(2, inner_own, inner_far, 0, LIGHT)
    x_send, x_keep, y_send, y_keep = made
    ffn_held = (x_keep, swap(x_send, "near", 1), y_keep, swap(y_send, "near", 2))

    ins = [
        (inner_own, tile),
        (inner_send, tile),
        up_block,
        (res2, whole(square)),
        (unit1, whole(square)),
        (inv1, whole((own_rows, 1))),
        (ln1_gain, line),
    ]
    outs = [
        ((own_rows, half), LOW, whole((own_rows, half))),
        (square, F32, whole(square)),
        (square, LOW, whole(square)),
        ((8, width), F32, whole((8, width))),
    ]
    grad_send, res1, grad_attended, small_one = run(
        hidden_back, places, (heads,), ins, outs, [pltpu.VMEM(square, F32)], ffn_macs // 2,
        weight=LIGHT,
    )
    grad_far = swap_core(grad_send)

    def pair_block(first, *shape):
        block = (None,) + shape
        return pl.BlockSpec(block, lambda k, s: (k + first,) + (0,) * len(shape))

    def attend_back(first, count):
        ins = [
            (qkvs, pair_block(first, rows3, own_rows)),
            (w_outs, pair_block(first, local_width, width)),
            (grad_attended, whole(square)),
            (logs, pair_block(first, 8, own_rows)),
        ] + segs
        outs = [
            ((count, rows3, own_rows), LOW, pair_block(0, rows3, own_rows)),
            ((count, 8, rows3), F32, pair_block(0, 8, rows3)),
        ]
        return run(
            attention_back, places, (count,), ins, outs,
            macs=count * (15 * own_rows * own_rows * 256 + local_width * own_rows * width),
            weight=LIGHT,
        )

    def attend_unit(first, rows, rows_far, qkv_bias, alias):
        bias_line = pl.BlockSpec((None, 1, chunk), lambda k, s: (s[2] ^ (k + first), 0, 0))
        ins = [
            (rows, pair_block(0, rows3, own_rows)),
            (rows_far, pair_block(0, rows3, own_rows)),
            (tok_own, pl.BlockSpec((own_rows, half), lambda k, s: (0, s[1]))),
            (tok_far, whole((own_rows, half))),
            (mixes, pair_block(first, local_width, own_rows)),
            (mixes_far, pair_block(first, local_width, own_rows)),
            (grad_attended, pl.BlockSpec((own_rows, half), lambda k, s: (0, s[1]))),
            (grad_far, whole((own_rows, half))),
            (small_one, whole((8, width))),
            (small_two, whole((8, width))),
            (up_bias, bias_line),
            (qkv_bias, pair_block(0, 8, rows3)),
        ]
        outs = [
            ((heads, r, half), LOW, pair_block(first, r, half))
            for r in (half // 2, (half + EXTRA) // 2)
            for _ in range(2)
        ]
        return run(
            attn_grad, places, (rows.shape[0],), ins, outs, alias=alias, weight=LIGHT
        )

    def second(x_keep, x_came, y_keep, y_came, macs=0):
        arrays = (x_keep, x_came, y_keep, y_came)
        ins = [(a, whole(a.shape)) for a in arrays]
        shapes = [(heads, a.shape[1] // 2, half) for a in (x_keep, x_keep, y_keep, y_keep)]
        outs = [(shape, LOW, whole(shape)) for shape in shapes]
        kernel = functools.partial(add_split, (2, 1))
        return run(kernel, places, (1,), ins, outs, macs=macs)

    def third(x_keep, x_came, y_keep, y_came):
        arrays = (x_keep, x_came, y_keep, y_came)
        shape = (heads // 2, x_keep.shape[1] + y_keep.shape[1], half)
        send, keep = run(
            add_parts, places, (1,), [(a, whole(a.shape)) for a in arrays],
            [(shape, LOW, whole(shape))] * 2, weight=LIGHT,
        )
        return keep, swap(send, "head", 1)

    def fourth(keep, came):
        shape = keep.shape[1:]
        mine, other = run(
            add_pair, places, (1,), [(a, whole(a.shape)) for a in (keep, came)],
            [(shape, LOW, whole(shape))] * 2, weight=LIGHT,
        )
        return mine, swap(other, "head", 2)

    def fifth(mine, came):
        shape = mine.shape
        (total,) = run(
            add_two, places, (1,), [(a, whole(shape)) for a in (mine, came)],
            [(shape, LOW, whole(shape))], weight=LIGHT,
        )
        bit = 1
        while bit < lax.axis_size("far"):
            total = (total.astype(F32) + swap(total, "far", bit).astype(F32)).astype(LOW)
            bit *= 2
        return total

    def cross(made, flip):
        x_send, x_keep, y_send, y_keep = made
        x_bit, y_bit = (2, 1) if flip else (1, 2)
        return x_keep, swap(x_send, "near", x_bit), y_keep, swap(y_send, "near", y_bit)

    rows, qkv_bias = attend_back(0, heads)
    rows_far = swap_core(rows)

    ins = [
        (rows, by_step(rows3, own_rows)),
        (w_qkvs, by_step(rows3, width)),
        (res1, whole(square)),
    ]
    outs = [(square, F32, whole(square))]
    (input_grad,) = run(input_sum, places, (heads,), ins, outs, weight=LIGHT)
    ffn_held = cross(second(*ffn_held, ffn_macs), True)
    made = attend_unit(0, rows, rows_far, qkv_bias, ())
    attn_held = cross(made, False)

    ffn_held = third(*ffn_held)
    attn_held = cross(second(*attn_held), True)
    ffn_held = fourth(*ffn_held)
    attn_held = third(*attn_held)
    attn_held = fourth(*attn_held)
    ffn_held = gather_back(fifth(*ffn_held))
    attn_held = gather_back(fifth(*attn_held))

    def both_cores(held):
        shape = (heads,) + held[0].shape
        ins = [(h, whole(h.shape)) for h in held]
        (pieces,) = run(collect, places, (1,), ins, [(shape, LOW, whole(shape))])
        return [(a, whole(shape)) for a in (pieces, swap_core(pieces))]

    ffn_held = both_cores(ffn_held)
    attn_held = both_cores(attn_held)
    outs = [(shape, F32, whole(shape)) for shape in ((chunk, width), (width, chunk))]
    grad_down, grad_up = run(
        ffn_place, places, (1,), ffn_held, outs, [pltpu.VMEM((width, chunk), F32)]
    )
    shapes = [
        (3, local_width, width),
        (local_width, width),
        (6, width),
        (chunk,),
        (2, local_width),
    ]
    grad_qkv, grad_out, grad_small, grad_up_bias, grad_qv_bias = run(
        attn_place,
        places,
        (1,),
        attn_held,
        [(shape, F32, whole(shape)) for shape in shapes],
        [pltpu.VMEM((width + EXTRA, width), F32)],
    )
    return (
        layer_output,
        input_grad,
        grad_qkv.transpose(0, 2, 1),
        grad_qv_bias,
        grad_out,
        grad_up,
        grad_up_bias,
        grad_down,
        grad_small,
    )


def solution(mesh):
    batch, heads = mesh.devices.shape
    mesh = Mesh(
        mesh.devices.reshape(batch // 8, 4, 2, heads), ("far", "near", "core", "head")
    )
    group = ("far", "near", "core")
    everyone = group + ("head",)
    in_specs = (
        P(group, None),
        P(group),
        P(None, None, "head"),
        P(None, "head"),
        P("head", None),
        P(),
        P(),
        P(),
        P(),
        P(),
        P(),
        P(),
        P(),
        P(),
        P(everyone, None),
    )
    out_specs = (
        P(everyone, None),
        P(everyone, None),
        P(None, None, "head"),
        P(None, "head"),
        P("head", None),
        P(None, "head"),
        P("head"),
        P("head", None),
        P(),
    )
    return jax.shard_map(
        per_device, mesh=mesh, in_specs=in_specs, out_specs=out_specs, check_vma=False
    )
```

```python
import functools
import math

import jax
import jax.numpy as jnp
from jax import lax
from jax.experimental import pallas as pl
from jax.experimental.pallas import tpu as pltpu
from jax.sharding import Mesh
from jax.sharding import PartitionSpec as P

HEAD_DIM = 64
SLOT = 512
LOW = jnp.bfloat16
F32 = jnp.float32
LOG2E = math.log2(math.e)
SCORE_SCALE = HEAD_DIM ** (-0.5) * LOG2E
SPARE_BYTES = 12 * 2**20
EXTRA = 64
LIGHT = 0.01
CHAIN = []
TAIL_SLOPE = 0.36
TAIL = (
    0.14371304537508633,
    0.14177245466203425,
    0.1397192603907239,
    0.026549325413860486,
    0.18095403134327948,
    -0.1797647161697652,
    0.047056295581175855,
)


def swap(value, axis, bit):
    size = lax.axis_size(axis)
    return lax.ppermute(value, axis, [(i, i ^ bit) for i in range(size)])


def swap_core(value):
    return swap(value, "core", 1)


def dot(a, b):
    return jnp.dot(a, b, preferred_element_type=F32)


def dot_nt(a, b):
    return lax.dot_general(a, b, (((1,), (1,)), ((), ())), preferred_element_type=F32)


def dot_tn(a, b):
    return lax.dot_general(a, b, (((0,), (0,)), ((), ())), preferred_element_type=F32)


def whole(shape):
    return pl.BlockSpec(shape, lambda *args: (0,) * len(shape), pipeline_mode=pl.Buffered(1))


def run(
    kernel, places, grid, ins, outs, scratch=(), macs=0, after=(), alias=(), weight=8, chain=True
):
    moved = sum(a.size * a.dtype.itemsize for a, spec in ins)
    moved += sum(math.prod(shape) * jnp.dtype(kind).itemsize for shape, kind, spec in outs)
    after = list(after) + (CHAIN if chain else [])
    count, unread = len(ins), len(alias) + len(after)
    results = len(outs)
    flag = (8, 128)
    if chain:
        outs = outs + [(flag, F32, whole(flag))]

    def body(places, *refs):
        made = refs[count + unread :]
        if chain:

            @pl.when(pl.program_id(0) == 0)
            def _():
                made[results][...] = jnp.zeros(flag, F32)

        kernel(places, *refs[:count], *made[:results], *made[len(outs) :])

    held = pl.BlockSpec(memory_space=pl.ANY)
    room = SPARE_BYTES
    for shape, kind, spec in outs + [(a.shape, a.dtype, spec) for a, spec in ins]:
        if spec.block_shape is not None:
            block = math.prod(1 if n is None else n for n in spec.block_shape)
            copies = 2 if spec.pipeline_mode is None else 1
            room += copies * block * jnp.dtype(kind).itemsize
    for ref in scratch:
        if hasattr(ref, "shape") and ref.dtype in (LOW, F32):
            room += math.prod(ref.shape) * jnp.dtype(ref.dtype).itemsize
    made = pl.pallas_call(
        body,
        name=getattr(kernel, "func", kernel).__name__,
        grid_spec=pltpu.PrefetchScalarGridSpec(
            num_scalar_prefetch=1,
            grid=grid,
            in_specs=[spec for a, spec in ins] + [held] * unread,
            out_specs=[spec for shape, kind, spec in outs],
            scratch_shapes=list(scratch),
        ),
        out_shape=[jax.ShapeDtypeStruct(shape, kind) for shape, kind, spec in outs],
        input_output_aliases={1 + count + i: i for i in range(len(alias))},
        compiler_params=pltpu.CompilerParams(vmem_limit_bytes=room),
        cost_estimate=pl.CostEstimate(
            flops=int(2 * macs * weight), bytes_accessed=int(moved * weight), transcendentals=0
        ),
    )(places, *[a for a, spec in ins], *alias, *after)
    if chain:
        CHAIN[:] = made[results:]
    return made[:results]


def three_parts(values):
    parts, rest = [], values
    for _ in range(3):
        parts.append(rest.astype(LOW))
        rest = rest - parts[-1].astype(F32)
    return parts


def segment_rows(seg_row):
    shape = (16, seg_row.shape[1])
    place = lax.broadcasted_iota(jnp.int32, shape, 0)
    same = place - 1 == seg_row
    keys = jnp.where(same, 1.0, jnp.where((place >= 8) & (place < 11), 1.0, 0.0))
    queries = jnp.where(same | (place > 4), 0.0, -1e30)
    return keys.astype(LOW), queries.astype(LOW)


def attend_heads(tok, w_rows, bias, seg_row, qkv_ref, mix_ref, log_ref):
    width = w_rows.shape[0] // 3
    added = dot_tn(bias[:, : 2 * width], jnp.ones((bias.shape[0], tok.shape[0]), LOW))
    qkv = dot_nt(w_rows, tok)
    parts = (
        (qkv[:width] + added[:width]).astype(LOW),
        qkv[width : 2 * width].astype(LOW),
        (qkv[2 * width :] + added[width:]).astype(LOW),
    )
    for c in range(3):
        qkv_ref[c * width : (c + 1) * width] = parts[c]
    more_k, more_q = segment_rows(seg_row)
    for head in range(width // HEAD_DIM):
        q, k, v = (part[head * HEAD_DIM : (head + 1) * HEAD_DIM] for part in parts)
        scores = dot_tn(jnp.concatenate([k, more_k], 0), jnp.concatenate([q, more_q], 0))
        top = jnp.max(scores, 0, keepdims=True)
        exponent = jnp.exp2((scores - top) * SCORE_SCALE)
        total = jnp.sum(exponent, 0, keepdims=True)
        attend = (exponent * (1.0 / total)).astype(LOW)
        mix_ref[head * HEAD_DIM : (head + 1) * HEAD_DIM] = dot(v, attend).astype(LOW)
        log_ref[head : head + 1] = top + jnp.log2(total) * (1.0 / SCORE_SCALE)


def own_attention(
    places, tok, w, bias, seg_row, qkv_ref, mix_ref, log_ref, w_qkv, w_out
):
    w_qkv[...] = w[: qkv_ref.shape[0]]
    w_out[...] = w[qkv_ref.shape[0] :]
    attend_heads(
        tok[...],
        w[: qkv_ref.shape[0]],
        bias[...],
        seg_row[...],
        qkv_ref,
        mix_ref,
        log_ref,
    )


def far_attention(
    order, places, tok, pair, rest, pair_far, rest_far, bias, seg_row,
    qkv_ref, mix_ref, log_ref, w_qkv, w_out, w_ref,
):
    first, second = order
    rows = pair.shape[1]
    me = places[0] * 2 + places[1]
    for other, held in enumerate(((pair, rest), (pair_far, rest_far))):
        for two, block in enumerate(held):
            for one in range(2):
                owner = me ^ (other + 2 * first * one + 2 * second * two)
                w_ref[pl.ds(pl.multiple_of(owner * rows, rows), rows)] = block[one]
    w_qkv[...] = w_ref[: qkv_ref.shape[0]]
    w_out[...] = w_ref[qkv_ref.shape[0] :]
    attend_heads(
        tok[...],
        w_ref[: qkv_ref.shape[0]],
        bias[...],
        seg_row[...],
        qkv_ref,
        mix_ref,
        log_ref,
    )


def pair_rows(places, first, second, out):
    out[0] = first[...]
    out[1] = second[...]


def norm_stats(v):
    centred = v - jnp.mean(v, -1, keepdims=True)
    inv = lax.rsqrt(jnp.mean(centred * centred, -1, keepdims=True) + 1e-05)
    return centred * inv, inv


def norm_back(upstream, unit, inv, gain):
    scaled = upstream * gain
    inner = jnp.mean(scaled * unit, -1, keepdims=True)
    return inv * (scaled - jnp.mean(scaled, -1, keepdims=True) - unit * inner)


def gelu_both(pre):
    power = jnp.exp2(pre * pre * (-0.5 * LOG2E))
    base = 1.0 + TAIL_SLOPE * jnp.abs(pre)
    t = pl.reciprocal(base, approx=True)
    tail = TAIL[6] * t + TAIL[5]
    for c in TAIL[4::-1]:
        tail = tail * t + c
    tail = tail * (t * power)
    cumul = jnp.where(pre < 0.0, tail, 1.0 - tail)
    return (pre * cumul).astype(LOW), cumul + pre * (power * 0.3989422804014327)


def feed_forward(
    places, tok, mix, w_out, b_out, gain1, shift1, b_down, gain2, shift2,
    w_up, b_up, w_down, cot,
    send, own, ends, slope, unit1, inv1, res2, out, small, tok_send,
    hidden, low, acts, down, sem,
):
    k = pl.program_id(0)
    half = send.shape[1]
    chunk = w_up.shape[1]
    core, z = places[1], places[2]
    heads = mix.shape[0]
    fetch = pltpu.make_async_copy(w_down, down, sem)
    b_out, gain1, shift1, b_down, gain2, shift2 = (
        ref[...].reshape(1, -1) for ref in (b_out, gain1, shift1, b_down, gain2, shift2)
    )

    @pl.when(k == 0)
    def _():
        fetch.start()
        tok_send[...] = jnp.where(core == 0, tok[:, half:], tok[:, :half])
        attended = b_out
        for d in range(heads):
            attended = attended + dot_tn(mix[d], w_out[d])
        unit, inv = norm_stats(tok[...].astype(F32) + attended)
        unit1[...] = unit
        inv1[...] = inv
        one = unit * gain1 + shift1
        hidden[...] = one
        one_low = one.astype(LOW)
        low[...] = one_low
        ends[0] = one_low[:, :half]
        ends[1] = one_low[:, half:]

    @pl.when(k < heads)
    def _():
        start = (z ^ k) * chunk
        block = 256
        for j in range(chunk // block):
            at = slice(j * block, (j + 1) * block)
            pre = dot(low[...], w_up[:, at]) + b_up[:, at]
            act, tilt = gelu_both(pre)
            slope[:, at] = tilt.astype(LOW)
            acts[:, pl.ds(pl.multiple_of(start + j * block, block), block)] = act
        left = acts[:, pl.ds(pl.multiple_of(start, 128), half)]
        right = acts[:, pl.ds(pl.multiple_of(start + half, 128), half)]
        own[...] = jnp.where(core == 0, left, right)
        send[...] = jnp.where(core == 0, right, left)

    @pl.when(k == heads)
    def _():
        fetch.wait()
        unit, inv = norm_stats(hidden[...] + (dot(acts[...], down[...]) + b_down))
        out[...] = (unit * gain2 + shift2).astype(LOW)
        upstream = cot[...].astype(F32)
        grad = norm_back(upstream, unit, inv, gain2)
        res2[...] = grad
        grad_low = grad.astype(LOW)
        ends[2] = grad_low[:, :half]
        ends[3] = grad_low[:, half:]
        small[0:1] = jnp.sum(grad_low.astype(F32), 0, keepdims=True)
        small[1:2] = jnp.sum(upstream * unit, 0, keepdims=True)
        small[2:3] = jnp.sum(upstream, 0, keepdims=True)


def inner_back(places, ends, w_down, slope, send, own, bias, branch, inners, down, sem):
    half = send.shape[1]
    core, z = places[1], places[2]
    k = pl.program_id(0)
    heads, chunk, _ = down.shape

    def fetch(i):
        at = pl.ds(pl.multiple_of((z ^ i) * chunk, chunk), chunk)
        return pltpu.make_async_copy(w_down.at[at], down.at[i], sem.at[i])

    @pl.when(k == 0)
    def _():
        for i in range(heads):
            fetch(i).start()
        branch[:, :half] = ends[0]
        branch[:, half:] = ends[1]

    fetch(k).wait()
    block = 256
    for j in range(inners.shape[1] // block):
        at = slice(j * block, (j + 1) * block)
        inner = (dot_nt(branch[...], down[k, at]) * slope[:, at].astype(F32)).astype(LOW)
        inners[:, at] = inner
        bias[:, at] = jnp.sum(inner.astype(F32), 0, keepdims=True)
    first, second = inners[:, :half], inners[:, half:]
    own[...] = jnp.where(core == 0, first, second)
    send[...] = jnp.where(core == 0, second, first)


def hidden_back(
    places, own, sent, w_up, res2, unit1, inv1, gain1, send, res1, low, small, acc
):
    k = pl.program_id(0)
    core = places[1]
    half = own.shape[1]
    mine, other = own[...], sent[...]
    inner = jnp.concatenate(
        [jnp.where(core == 0, mine, other), jnp.where(core == 0, other, mine)], 1
    )
    product = dot_nt(inner, w_up[...])

    @pl.when(k == 0)
    def _():
        acc[...] = res2[...] + product

    @pl.when(k > 0)
    def _():
        acc[...] += product

    @pl.when(k == pl.num_programs(0) - 1)
    def _():
        grad = acc[...]
        result = norm_back(grad, unit1[...], inv1[...], gain1[...].reshape(1, -1))
        res1[...] = result
        result_low = result.astype(LOW)
        low[...] = result_low
        send[...] = jnp.where(core == 0, result_low[:, half:], result_low[:, :half])
        small[0:1] = jnp.sum(result_low.astype(F32), 0, keepdims=True)
        small[1:2] = jnp.sum(grad * unit1[...], 0, keepdims=True)
        small[2:3] = jnp.sum(grad, 0, keepdims=True)


def attention_back(places, qkv, w_out, grad, log_ref, seg_row, rows_ref, bias_ref):
    width = qkv.shape[0] // 3
    grad_mixed = dot_nt(w_out[...], grad[...]).astype(LOW)
    more_k, more_q = segment_rows(seg_row[...])
    scale = HEAD_DIM ** (-0.5)
    for head in range(width // HEAD_DIM):
        places_of = [c * width + head * HEAD_DIM for c in range(3)]
        q, k, v = (qkv[at : at + HEAD_DIM] for at in places_of)
        g = grad_mixed[head * HEAD_DIM : (head + 1) * HEAD_DIM]
        logs = jnp.concatenate(three_parts(-log_ref[head : head + 1]), 0)
        with_logs = jnp.concatenate([more_q[:8], logs, more_q[11:]], 0)
        scores = dot_tn(jnp.concatenate([k, more_k], 0), jnp.concatenate([q, with_logs], 0))
        attend = jnp.exp2(scores * SCORE_SCALE)
        attend_low = attend.astype(LOW)
        grad_v = dot_nt(g, attend_low)
        product = attend * dot_tn(v, g)
        inner = jnp.sum(product, 0, keepdims=True)
        grad_scores = (product - attend * inner).astype(LOW)
        grad_q = dot(k, grad_scores) * scale
        grad_k = dot_nt(q, grad_scores) * scale
        for at, value in zip(places_of, (grad_q, grad_k, grad_v)):
            rows_ref[at : at + HEAD_DIM] = value.astype(LOW)
    ones = jnp.ones((8, rows_ref.shape[1]), LOW)
    bias_ref[...] = dot_nt(ones, rows_ref[...])


def split_rows(value, high, send, keep):
    rows = value.shape[0] // 2
    low = value.astype(LOW)
    send[...] = jnp.where(high, low[:rows], low[rows:])
    keep[...] = jnp.where(high, low[rows:], low[:rows])


def is_high(places, bit):
    return (places[0] & bit) != 0


def unit_rows(units, units_far, ends, ends_far, both):
    half, count = ends.shape[2], ends.shape[1]

    @pl.when(pl.program_id(0) == 0)
    def _():
        for side in range(2):
            rows = slice(side * half, (side + 1) * half)
            both[rows, :count] = ends[side].T
            both[rows, count:] = ends_far[side].T

    left, right = (jnp.concatenate([units[i], units_far[i]], 0) for i in range(2))
    return dot(both[...], jnp.concatenate([left, right], 1))


def ffn_grad(bit, places, units, units_far, ends, ends_far, send, keep, both):
    total = unit_rows(units, units_far, ends, ends_far, both)
    half = send.shape[2]
    for i in range(2):
        part = total[:, i * half : (i + 1) * half]
        split_rows(part, is_high(places, bit), send.at[i], keep.at[i])


def attn_grad(
    places, rows, rows_far, tok, tok_far, mix, mix_far, grad, grad_far,
    small_one, small_two, up_bias, qkv_bias, send_x, keep_x, send_y, keep_y,
):
    width = mix.shape[0]
    half = tok.shape[1]
    def joined(a, a_far, b, b_far):
        left = jnp.concatenate([a[...], a_far[...]], 1)
        return dot(left, jnp.concatenate([b[...], b_far[...]], 0))

    qkv = joined(rows, rows_far, tok, tok_far)
    out = joined(mix, mix_far, grad, grad_far)
    lines = []
    for held in (small_one, small_two):
        for i in range(3):
            lines += [held[i : i + 1, :half], held[i : i + 1, half:]]
    lines += [up_bias[:, :half], up_bias[:, half:]]
    lines.append(jnp.concatenate([qkv_bias[0:1, :width], qkv_bias[0:1, 2 * width :]], 1))
    lines.append(jnp.zeros((EXTRA - len(lines), half), F32))
    total = jnp.concatenate([qkv, out] + lines, 0)
    split_rows(total[:half], is_high(places, 1), send_x, keep_x)
    split_rows(total[half:], is_high(places, 2), send_y, keep_y)


def add_split(bits, places, *refs):
    for i, bit in enumerate(bits):
        keep, came = refs[2 * i : 2 * i + 2]
        send, left = refs[2 * (len(bits) + i) : 2 * (len(bits) + i) + 2]
        for d in range(keep.shape[0]):
            total = keep[d].astype(F32) + came[d].astype(F32)
            split_rows(total, is_high(places, bit), send.at[d], left.at[d])


def add_parts(places, keep_a, came_a, keep_b, came_b, send, keep):
    rows = keep_a.shape[1]
    for d in range(keep_a.shape[0]):
        out = (send if d % 2 else keep).at[d // 2]
        out[:rows] = (keep_a[d].astype(F32) + came_a[d].astype(F32)).astype(LOW)
        out[rows:] = (keep_b[d].astype(F32) + came_b[d].astype(F32)).astype(LOW)


def add_pair(places, keep, came, *outs):
    for i, out in enumerate(outs):
        out[...] = (keep[i].astype(F32) + came[i].astype(F32)).astype(LOW)


def add_two(places, keep, came, out):
    out[...] = (keep[...].astype(F32) + came[...].astype(F32)).astype(LOW)


def input_sum(places, rows, w, res1, out):
    total = dot_tn(rows[...], w[...])
    k = pl.program_id(0)
    out[...] = jnp.where(k == 0, res1[...], out[...]) + total


def place_pieces(places, held, full, layouts):
    near, core = places[0], places[1]
    width = held[0].shape[1]
    for off in range(4):
        chip = near ^ off
        mine, other = held[off][...], held[4 + off][...]
        sides = (jnp.where(core == 0, mine, other), jnp.where(core == 0, other, mine))
        for at, rows, start, outer in layouts:
            low_bit, high_bit = chip & 1, chip >> 1
            order = 2 * low_bit + high_bit if outer == 1 else 2 * high_bit + low_bit
            to = pl.multiple_of(start + order * rows, 16)
            for side in range(2):
                full[pl.ds(to, rows), side * width : (side + 1) * width] = sides[side][
                    at : at + rows
                ].astype(F32)


def ffn_place(places, *refs):
    held = [ref.at[off] for ref in refs[:2] for off in range(4)]
    down, up, full = refs[2:]
    rows = held[0].shape[0] // 2
    place_pieces(places, held, full, [(0, rows, 0, 1)])
    down[...] = full[...].T
    place_pieces(places, held, up, [(rows, rows, 0, 2)])


def collect(places, *refs):
    for off in range(4):
        refs[4][off] = refs[off][...]


def attn_place(places, *refs):
    held = [ref.at[off] for ref in refs[:2] for off in range(4)]
    qkv, w_out, small, up_bias, qv_bias, full = refs[2:]
    width = held[0].shape[1]
    count = w_out.shape[0]
    rows = count // 2
    more = held[0].shape[0] - rows
    place_pieces(places, held, full, [(0, rows, 0, 1), (rows, more, 4 * rows, 2)])
    for c in range(3):
        qkv[c] = full[c * count : (c + 1) * count]
    w_out[...] = full[3 * count : 4 * count]
    at = 4 * count
    lines = full[at : at + 16, :width] + full[at : at + 16, width:]
    for i in range(6):
        small[i : i + 1, :width] = lines[2 * i : 2 * i + 1]
        small[i : i + 1, width:] = lines[2 * i + 1 : 2 * i + 2]
    up_bias[...] = jnp.concatenate([lines[12:13], lines[13:14]], 1).reshape(2 * width)
    qv_bias[0:1] = lines[14:15, :count]
    qv_bias[1:2] = lines[14:15, count : 2 * count]


def bias_parts(values):
    rows, rest = [], values
    for _ in range(3):
        rows.append(lax.reduce_precision(rest, 8, 7))
        rest = rest - rows[-1]
    return jnp.stack(rows).astype(LOW)


def gather_back(piece):
    return [piece] + [swap(piece, "near", off) for off in range(1, 4)]


def per_device(
    tokens,
    segment_ids,
    w_qkv,
    b_qv,
    w_out,
    b_out,
    ln1_gain,
    ln1_bias,
    w_up,
    b_up,
    w_down,
    b_down,
    ln2_gain,
    ln2_bias,
    cotangent,
):
    CHAIN.clear()
    width = tokens.shape[1]
    own_rows = cotangent.shape[0]
    local_width = w_qkv.shape[2]
    heads = lax.axis_size("head")
    z = lax.axis_index("head")
    core = lax.axis_index("core")
    near = lax.axis_index("near")
    hidden_units = w_up.shape[1]
    chunk = hidden_units // heads
    half = width // 2
    rows3 = 3 * local_width
    places = jnp.stack([near, core, z]).astype(jnp.int32)

    shard = jnp.concatenate([w_qkv.transpose(0, 2, 1).reshape(rows3, width), w_out], 0)
    piece_rows = shard.shape[0] // 8
    bias = jnp.pad(bias_parts(b_qv.reshape(-1)), ((0, 13), (0, width - 2 * local_width)))
    piece = lax.dynamic_slice_in_dim(shard, (near * 2 + core) * piece_rows, piece_rows, 0)
    piece = jnp.concatenate([piece, bias], 0)
    first_hop = [swap(piece, "head", d) for d in range(1, heads)]

    seg = lax.dynamic_slice_in_dim(segment_ids, z * own_rows, own_rows, 0)
    segs = [(seg[None], whole((1, own_rows)))]
    tok_own = lax.dynamic_slice_in_dim(tokens, z * own_rows, own_rows, 0)
    own_tokens = (tok_own, whole((own_rows, width)))

    def attend_outs(first):
        def spec(*shape):
            return pl.BlockSpec((None,) + shape, lambda k, s: (k + first, 0, 0))

        return [
            ((heads, rows3, own_rows), LOW, spec(rows3, own_rows)),
            ((heads, local_width, own_rows), LOW, spec(local_width, own_rows)),
            ((heads, 8, own_rows), F32, spec(8, own_rows)),
            ((heads, rows3, width), LOW, spec(rows3, width)),
            ((heads, local_width, width), LOW, spec(local_width, width)),
        ]

    macs = rows3 * width * own_rows + 6 * own_rows * own_rows * 256
    ins = [own_tokens, (shard, whole(shard.shape)), (bias, whole(bias.shape))] + segs
    made = begun = run(own_attention, places, (1,), ins, attend_outs(0), macs=macs, chain=False)
    block = pl.BlockSpec((piece_rows, width), lambda k, s: (0, 0))
    orders = [(1, 2) if d % 2 else (2, 1) for d in range(heads)]
    nexts = [swap(first_hop[d - 1], "near", orders[d][0]) for d in range(1, heads)]
    for d in range(1, heads):
        order = orders[d]
        ins = [(first_hop[d - 1], block), (nexts[d - 1], block)]
        twice = (2, piece_rows, width)
        (pair,) = run(
            pair_rows, places, (1,), ins, [(twice, LOW, whole(twice))],
            after=nexts + [begun[2]], weight=LIGHT, chain=False,
        )
        rest = swap(pair, "near", order[1])
        held = [pair, rest, swap_core(pair), swap_core(rest)]
        ins = [own_tokens] + [(h, whole(h.shape)) for h in held]
        ins += [(first_hop[d - 1], pl.BlockSpec((16, width), lambda k, s: (piece_rows // 16, 0)))]
        kernel = functools.partial(far_attention, order)
        made = run(
            kernel, places, (1,), ins + segs, attend_outs(d), [pltpu.VMEM((rows3 + local_width, width), LOW)], macs, alias=made,
            chain=False, weight=100,
        )
    qkvs, mixes, logs, w_qkvs, w_outs = made

    mixes_far = swap_core(mixes)

    def by_step(*shape):
        block = (None,) + shape
        return pl.BlockSpec(block, lambda k, s: (jnp.minimum(k, heads - 1),) + (0,) * len(shape))

    def unit_at(k, s):
        return s[2] ^ jnp.minimum(k, heads - 1)


    line = whole((width,))
    square = (own_rows, width)
    tile = by_step(own_rows, half)
    tiles = (heads, own_rows, half)
    up_block = (w_up, pl.BlockSpec((width, chunk), lambda k, s: (0, unit_at(k, s))))
    line_block = pl.BlockSpec((None, 1, chunk), lambda k, s: (unit_at(k, s), 0, 0))

    ins = [
        own_tokens,
        (mixes, whole(mixes.shape)),
        (w_outs, whole(w_outs.shape)),
        (b_out, line),
        (ln1_gain, line),
        (ln1_bias, line),
        (b_down, line),
        (ln2_gain, line),
        (ln2_bias, line),
        up_block,
        (b_up.reshape(heads, 1, chunk), line_block),
        (w_down, pl.BlockSpec(memory_space=pl.ANY)),
        (cotangent, whole(square)),
    ]
    outs = [
        (tiles, LOW, tile),
        (tiles, LOW, tile),
        ((4, own_rows, half), LOW, whole((4, own_rows, half))),
        ((heads, own_rows, chunk), LOW, by_step(own_rows, chunk)),
        (square, F32, whole(square)),
        ((own_rows, 1), F32, whole((own_rows, 1))),
        (square, F32, whole(square)),
        (square, LOW, whole(square)),
        ((8, width), F32, whole((8, width))),
        ((own_rows, half), LOW, whole((own_rows, half))),
    ]
    scratch = [
        pltpu.VMEM(square, F32),
        pltpu.VMEM(square, LOW),
        pltpu.VMEM((own_rows, hidden_units), LOW),
        pltpu.VMEM(w_down.shape, LOW),
        pltpu.SemaphoreType.DMA,
    ]
    ffn_macs = 2 * own_rows * width * hidden_units
    act_send, act_own, ends, slope, unit1, inv1, res2, layer_output, small_two, tok_send = run(
        feed_forward, places, (heads + 1,), ins, outs, scratch, ffn_macs
    )
    tok_far = swap_core(tok_send)
    act_far = swap_core(act_send)
    ends_far = swap_core(ends)

    def two_of(array, index):
        return (array, pl.BlockSpec((2, own_rows, half), lambda k, s: (index, 0, 0)))

    ins = [
        two_of(ends, 1),
        (w_down, pl.BlockSpec(memory_space=pl.ANY)),
        (slope, by_step(own_rows, chunk)),
    ]
    outs = [(tiles, LOW, tile), (tiles, LOW, tile), ((heads, 1, chunk), F32, line_block)]
    scratch = [
        pltpu.VMEM(square, LOW),
        pltpu.VMEM((own_rows, chunk), LOW),
        pltpu.VMEM((heads, chunk, width), LOW),
        pltpu.SemaphoreType.DMA((heads,)),
    ]
    inner_send, inner_own, up_bias = run(
        inner_back, places, (heads,), ins, outs, scratch, ffn_macs // 2,
        after=[mixes_far],
    )
    inner_far = swap_core(inner_send)


    def two(*shape):
        return pl.BlockSpec((2,) + shape, lambda k, s: (k,) + (0,) * len(shape))

    def ffn_unit(bit, own, far, which, weight):
        ins = [(own, two(own_rows, half)), (far, two(own_rows, half))]
        ins += [two_of(ends, which), two_of(ends_far, which)]
        outs = [((heads, half, half), LOW, two(half, half))] * 2
        both = [pltpu.VMEM((width, 2 * own_rows), LOW)]
        kernel = functools.partial(ffn_grad, bit)
        return run(kernel, places, (heads // 2,), ins, outs, both, ffn_macs // 2, weight=weight)

    made = ffn_unit(1, act_own, act_far, 1, 8) + ffn_unit(2, inner_own, inner_far, 0, LIGHT)
    x_send, x_keep, y_send, y_keep = made
    ffn_held = (x_keep, swap(x_send, "near", 1), y_keep, swap(y_send, "near", 2))

    ins = [
        (inner_own, tile),
        (inner_send, tile),
        up_block,
        (res2, whole(square)),
        (unit1, whole(square)),
        (inv1, whole((own_rows, 1))),
        (ln1_gain, line),
    ]
    outs = [
        ((own_rows, half), LOW, whole((own_rows, half))),
        (square, F32, whole(square)),
        (square, LOW, whole(square)),
        ((8, width), F32, whole((8, width))),
    ]
    grad_send, res1, grad_attended, small_one = run(
        hidden_back, places, (heads,), ins, outs, [pltpu.VMEM(square, F32)], ffn_macs // 2,
        weight=LIGHT,
    )
    grad_far = swap_core(grad_send)

    def pair_block(first, *shape):
        block = (None,) + shape
        return pl.BlockSpec(block, lambda k, s: (k + first,) + (0,) * len(shape))

    def attend_back(first, count):
        ins = [
            (qkvs, pair_block(first, rows3, own_rows)),
            (w_outs, pair_block(first, local_width, width)),
            (grad_attended, whole(square)),
            (logs, pair_block(first, 8, own_rows)),
        ] + segs
        outs = [
            ((count, rows3, own_rows), LOW, pair_block(0, rows3, own_rows)),
            ((count, 8, rows3), F32, pair_block(0, 8, rows3)),
        ]
        return run(
            attention_back, places, (count,), ins, outs,
            macs=count * (15 * own_rows * own_rows * 256 + local_width * own_rows * width),
            weight=LIGHT,
        )

    def attend_unit(first, rows, rows_far, qkv_bias, alias):
        bias_line = pl.BlockSpec((None, 1, chunk), lambda k, s: (s[2] ^ (k + first), 0, 0))
        ins = [
            (rows, pair_block(0, rows3, own_rows)),
            (rows_far, pair_block(0, rows3, own_rows)),
            (tok_own, pl.BlockSpec((own_rows, half), lambda k, s: (0, s[1]))),
            (tok_far, whole((own_rows, half))),
            (mixes, pair_block(first, local_width, own_rows)),
            (mixes_far, pair_block(first, local_width, own_rows)),
            (grad_attended, pl.BlockSpec((own_rows, half), lambda k, s: (0, s[1]))),
            (grad_far, whole((own_rows, half))),
            (small_one, whole((8, width))),
            (small_two, whole((8, width))),
            (up_bias, bias_line),
            (qkv_bias, pair_block(0, 8, rows3)),
        ]
        outs = [
            ((heads, r, half), LOW, pair_block(first, r, half))
            for r in (half // 2, (half + EXTRA) // 2)
            for _ in range(2)
        ]
        return run(
            attn_grad, places, (rows.shape[0],), ins, outs, alias=alias, weight=LIGHT
        )

    def second(x_keep, x_came, y_keep, y_came, macs=0):
        arrays = (x_keep, x_came, y_keep, y_came)
        ins = [(a, whole(a.shape)) for a in arrays]
        shapes = [(heads, a.shape[1] // 2, half) for a in (x_keep, x_keep, y_keep, y_keep)]
        outs = [(shape, LOW, whole(shape)) for shape in shapes]
        kernel = functools.partial(add_split, (2, 1))
        return run(kernel, places, (1,), ins, outs, macs=macs)

    def third(x_keep, x_came, y_keep, y_came):
        arrays = (x_keep, x_came, y_keep, y_came)
        shape = (heads // 2, x_keep.shape[1] + y_keep.shape[1], half)
        send, keep = run(
            add_parts, places, (1,), [(a, whole(a.shape)) for a in arrays],
            [(shape, LOW, whole(shape))] * 2, weight=LIGHT,
        )
        return keep, swap(send, "head", 1)

    def fourth(keep, came):
        shape = keep.shape[1:]
        mine, other = run(
            add_pair, places, (1,), [(a, whole(a.shape)) for a in (keep, came)],
            [(shape, LOW, whole(shape))] * 2, weight=LIGHT,
        )
        return mine, swap(other, "head", 2)

    def fifth(mine, came):
        shape = mine.shape
        (total,) = run(
            add_two, places, (1,), [(a, whole(shape)) for a in (mine, came)],
            [(shape, LOW, whole(shape))], weight=LIGHT,
        )
        bit = 1
        while bit < lax.axis_size("far"):
            total = (total.astype(F32) + swap(total, "far", bit).astype(F32)).astype(LOW)
            bit *= 2
        return total

    def cross(made, flip):
        x_send, x_keep, y_send, y_keep = made
        x_bit, y_bit = (2, 1) if flip else (1, 2)
        return x_keep, swap(x_send, "near", x_bit), y_keep, swap(y_send, "near", y_bit)

    rows, qkv_bias = attend_back(0, heads)
    rows_far = swap_core(rows)

    ins = [
        (rows, by_step(rows3, own_rows)),
        (w_qkvs, by_step(rows3, width)),
        (res1, whole(square)),
    ]
    outs = [(square, F32, whole(square))]
    (input_grad,) = run(input_sum, places, (heads,), ins, outs, weight=LIGHT)
    ffn_held = cross(second(*ffn_held, ffn_macs), True)
    made = attend_unit(0, rows, rows_far, qkv_bias, ())
    attn_held = cross(made, False)

    ffn_held = third(*ffn_held)
    attn_held = cross(second(*attn_held), True)
    ffn_held = fourth(*ffn_held)
    attn_held = third(*attn_held)
    ffn_held = gather_back(fifth(*ffn_held))
    attn_held = fourth(*attn_held)
    attn_held = gather_back(fifth(*attn_held))

    def both_cores(held):
        shape = (heads,) + held[0].shape
        ins = [(h, whole(h.shape)) for h in held]
        (pieces,) = run(collect, places, (1,), ins, [(shape, LOW, whole(shape))])
        return [(a, whole(shape)) for a in (pieces, swap_core(pieces))]

    ffn_held = both_cores(ffn_held)
    outs = [(shape, F32, whole(shape)) for shape in ((chunk, width), (width, chunk))]
    grad_down, grad_up = run(
        ffn_place, places, (1,), ffn_held, outs, [pltpu.VMEM((width, chunk), F32)]
    )
    attn_held = both_cores(attn_held)
    shapes = [
        (3, local_width, width),
        (local_width, width),
        (6, width),
        (chunk,),
        (2, local_width),
    ]
    grad_qkv, grad_out, grad_small, grad_up_bias, grad_qv_bias = run(
        attn_place,
        places,
        (1,),
        attn_held,
        [(shape, F32, whole(shape)) for shape in shapes],
        [pltpu.VMEM((width + EXTRA, width), F32)],
    )
    return (
        layer_output,
        input_grad,
        grad_qkv.transpose(0, 2, 1),
        grad_qv_bias,
        grad_out,
        grad_up,
        grad_up_bias,
        grad_down,
        grad_small,
    )


def solution(mesh):
    batch, heads = mesh.devices.shape
    mesh = Mesh(
        mesh.devices.reshape(batch // 8, 4, 2, heads), ("far", "near", "core", "head")
    )
    group = ("far", "near", "core")
    everyone = group + ("head",)
    in_specs = (
        P(group, None),
        P(group),
        P(None, None, "head"),
        P(None, "head"),
        P("head", None),
        P(),
        P(),
        P(),
        P(),
        P(),
        P(),
        P(),
        P(),
        P(),
        P(everyone, None),
    )
    out_specs = (
        P(everyone, None),
        P(everyone, None),
        P(None, None, "head"),
        P(None, "head"),
        P("head", None),
        P(None, "head"),
        P("head"),
        P("head", None),
        P(),
    )
    return jax.shard_map(
        per_device, mesh=mesh, in_specs=in_specs, out_specs=out_specs, check_vma=False
    )
```

```python
import functools
import math

import jax
import jax.numpy as jnp
from jax import lax
from jax.experimental import pallas as pl
from jax.experimental.pallas import tpu as pltpu
from jax.sharding import Mesh
from jax.sharding import PartitionSpec as P

HEAD_DIM = 64
SLOT = 512
LOW = jnp.bfloat16
F32 = jnp.float32
LOG2E = math.log2(math.e)
SCORE_SCALE = HEAD_DIM ** (-0.5) * LOG2E
SPARE_BYTES = 12 * 2**20
EXTRA = 64
LIGHT = 0.01
LANES = 128
CHAIN = []
TAIL_SLOPE = 0.36
TAIL = (
    0.14371304537508633,
    0.14177245466203425,
    0.1397192603907239,
    0.026549325413860486,
    0.18095403134327948,
    -0.1797647161697652,
    0.047056295581175855,
)


def swap(value, axis, bit):
    size = lax.axis_size(axis)
    return lax.ppermute(value, axis, [(i, i ^ bit) for i in range(size)])


def swap_core(value):
    return swap(value, "core", 1)


def dot(a, b):
    return jnp.dot(a, b, preferred_element_type=F32)


def dot_nt(a, b):
    return lax.dot_general(a, b, (((1,), (1,)), ((), ())), preferred_element_type=F32)


def dot_tn(a, b):
    return lax.dot_general(a, b, (((0,), (0,)), ((), ())), preferred_element_type=F32)


def whole(shape):
    return pl.BlockSpec(shape, lambda *args: (0,) * len(shape), pipeline_mode=pl.Buffered(1))


def run(
    kernel, places, grid, ins, outs, scratch=(), macs=0, after=(), alias=(), weight=8, chain=True
):
    moved = sum(a.size * a.dtype.itemsize for a, spec in ins)
    moved += sum(math.prod(shape) * jnp.dtype(kind).itemsize for shape, kind, spec in outs)
    after = list(after) + (CHAIN if chain else [])
    count, unread = len(ins), len(alias) + len(after)
    results = len(outs)
    flag = (8, 128)
    if chain:
        outs = outs + [(flag, F32, whole(flag))]

    def body(places, *refs):
        made = refs[count + unread :]
        if chain:

            @pl.when(pl.program_id(0) == 0)
            def _():
                made[results][...] = jnp.zeros(flag, F32)

        kernel(places, *refs[:count], *made[:results], *made[len(outs) :])

    held = pl.BlockSpec(memory_space=pl.ANY)
    room = SPARE_BYTES
    for shape, kind, spec in outs + [(a.shape, a.dtype, spec) for a, spec in ins]:
        if spec.block_shape is not None:
            block = math.prod(1 if n is None else n for n in spec.block_shape)
            copies = 2 if spec.pipeline_mode is None else 1
            room += copies * block * jnp.dtype(kind).itemsize
    for ref in scratch:
        if hasattr(ref, "shape") and ref.dtype in (LOW, F32):
            room += math.prod(ref.shape) * jnp.dtype(ref.dtype).itemsize
    made = pl.pallas_call(
        body,
        name=getattr(kernel, "func", kernel).__name__,
        grid_spec=pltpu.PrefetchScalarGridSpec(
            num_scalar_prefetch=1,
            grid=grid,
            in_specs=[spec for a, spec in ins] + [held] * unread,
            out_specs=[spec for shape, kind, spec in outs],
            scratch_shapes=list(scratch),
        ),
        out_shape=[jax.ShapeDtypeStruct(shape, kind) for shape, kind, spec in outs],
        input_output_aliases={1 + count + i: i for i in range(len(alias))},
        compiler_params=pltpu.CompilerParams(vmem_limit_bytes=room),
        cost_estimate=pl.CostEstimate(
            flops=int(2 * macs * weight), bytes_accessed=int(moved * weight), transcendentals=0
        ),
    )(places, *[a for a, spec in ins], *alias, *after)
    if chain:
        CHAIN[:] = made[results:]
    return made[:results]


def tiles_of(count, size):
    return [slice(at, at + size) for at in range(0, count, size)]


def three_parts(values):
    parts, rest = [], values
    for _ in range(3):
        parts.append(rest.astype(LOW))
        rest = rest - parts[-1].astype(F32)
    return parts


def segment_rows(seg_row):
    shape = (16, seg_row.shape[1])
    place = lax.broadcasted_iota(jnp.int32, shape, 0)
    same = place - 1 == seg_row
    keys = jnp.where(same, 1.0, jnp.where((place >= 8) & (place < 11), 1.0, 0.0))
    queries = jnp.where(same | (place > 4), 0.0, -1e30)
    return keys.astype(LOW), queries.astype(LOW)


def attend_heads(tok, w_rows, bias, seg_row, qkv_ref, mix_ref, log_ref):
    width = w_rows.shape[0] // 3
    added = dot_tn(bias[:, : 2 * width], jnp.ones((bias.shape[0], tok.shape[0]), LOW))
    qkv = dot_nt(w_rows, tok)
    parts = (
        (qkv[:width] + added[:width]).astype(LOW),
        qkv[width : 2 * width].astype(LOW),
        (qkv[2 * width :] + added[width:]).astype(LOW),
    )
    for c in range(3):
        qkv_ref[c * width : (c + 1) * width] = parts[c]
    more_k, more_q = segment_rows(seg_row)
    for head in range(width // HEAD_DIM):
        q, k, v = (part[head * HEAD_DIM : (head + 1) * HEAD_DIM] for part in parts)
        scores = dot_tn(jnp.concatenate([k, more_k], 0), jnp.concatenate([q, more_q], 0))
        columns, tops, totals = [], [], []
        for tile in tiles_of(scores.shape[1], LANES):
            top = jnp.max(scores[:, tile], 0, keepdims=True)
            total, column = 0.0, []
            for rows in tiles_of(scores.shape[0], 64):
                exponent = jnp.exp2((scores[rows, tile] - top) * SCORE_SCALE)
                total = total + jnp.sum(exponent, 0, keepdims=True)
                column.append(exponent.astype(LOW))
            columns.append(jnp.concatenate(column, 0))
            tops.append(top)
            totals.append(total)
        total = jnp.concatenate(totals, 1)
        mixed = dot(v, jnp.concatenate(columns, 1)) * (1.0 / total)
        mix_ref[head * HEAD_DIM : (head + 1) * HEAD_DIM] = mixed.astype(LOW)
        top = jnp.concatenate(tops, 1)
        log_ref[head : head + 1] = top + jnp.log2(total) * (1.0 / SCORE_SCALE)


def own_attention(
    places, tok, w, bias, seg_row, qkv_ref, mix_ref, log_ref, w_qkv, w_out
):
    w_qkv[...] = w[: qkv_ref.shape[0]]
    w_out[...] = w[qkv_ref.shape[0] :]
    attend_heads(
        tok[...],
        w[: qkv_ref.shape[0]],
        bias[...],
        seg_row[...],
        qkv_ref,
        mix_ref,
        log_ref,
    )


def far_attention(
    order, places, tok, pair, rest, pair_far, rest_far, bias, seg_row,
    qkv_ref, mix_ref, log_ref, w_qkv, w_out, w_ref,
):
    first, second = order
    rows = pair.shape[1]
    me = places[0] * 2 + places[1]
    for other, held in enumerate(((pair, rest), (pair_far, rest_far))):
        for two, block in enumerate(held):
            for one in range(2):
                owner = me ^ (other + 2 * first * one + 2 * second * two)
                w_ref[pl.ds(pl.multiple_of(owner * rows, rows), rows)] = block[one]
    w_qkv[...] = w_ref[: qkv_ref.shape[0]]
    w_out[...] = w_ref[qkv_ref.shape[0] :]
    attend_heads(
        tok[...],
        w_ref[: qkv_ref.shape[0]],
        bias[...],
        seg_row[...],
        qkv_ref,
        mix_ref,
        log_ref,
    )


def pair_rows(places, first, second, out):
    out[0] = first[...]
    out[1] = second[...]


def norm_stats(v):
    centred = v - jnp.mean(v, -1, keepdims=True)
    inv = lax.rsqrt(jnp.mean(centred * centred, -1, keepdims=True) + 1e-05)
    return centred * inv, inv


def norm_back(upstream, unit, inv, gain):
    scaled = upstream * gain
    inner = jnp.mean(scaled * unit, -1, keepdims=True)
    return inv * (scaled - jnp.mean(scaled, -1, keepdims=True) - unit * inner)


def gelu_both(pre):
    power = jnp.exp2(pre * pre * (-0.5 * LOG2E))
    base = 1.0 + TAIL_SLOPE * jnp.abs(pre)
    t = pl.reciprocal(base, approx=True)
    tail = TAIL[6] * t + TAIL[5]
    for c in TAIL[4::-1]:
        tail = tail * t + c
    tail = tail * (t * power)
    cumul = jnp.where(pre < 0.0, tail, 1.0 - tail)
    return (pre * cumul).astype(LOW), cumul + pre * (power * 0.3989422804014327)


def feed_forward(
    places, tok, mix, w_out, b_out, gain1, shift1, b_down, gain2, shift2,
    w_up, b_up, w_down, cot,
    send, own, ends, slope, unit1, inv1, res2, out, small, tok_send,
    hidden, low, acts, down, sem,
):
    k = pl.program_id(0)
    half = send.shape[1]
    chunk = w_up.shape[1]
    core, z = places[1], places[2]
    heads = mix.shape[0]
    fetch = pltpu.make_async_copy(w_down, down, sem)
    b_out, gain1, shift1, b_down, gain2, shift2 = (
        ref[...].reshape(1, -1) for ref in (b_out, gain1, shift1, b_down, gain2, shift2)
    )

    @pl.when(k == 0)
    def _():
        fetch.start()
        tok_send[...] = jnp.where(core == 0, tok[:, half:], tok[:, :half])
        width = low.shape[1]
        attended = dot_tn(
            mix[...].reshape(width, low.shape[0]), w_out[...].reshape(width, width)
        )
        for rows in tiles_of(low.shape[0], 32):
            unit, inv = norm_stats(tok[rows].astype(F32) + (attended[rows] + b_out))
            unit1[rows] = unit
            inv1[rows] = inv
            one = unit * gain1 + shift1
            hidden[rows] = one
            one_low = one.astype(LOW)
            low[rows] = one_low
            ends[0, rows] = one_low[:, :half]
            ends[1, rows] = one_low[:, half:]

    @pl.when(k < heads)
    def _():
        start = (z ^ k) * chunk
        block = 256
        for j in range(chunk // block):
            at = slice(j * block, (j + 1) * block)
            pre = dot(low[...], w_up[:, at])
            for rows in tiles_of(pre.shape[0], 32):
                act, tilt = gelu_both(pre[rows] + b_up[:, at])
                slope[rows, at] = tilt.astype(LOW)
                acts[rows, pl.ds(pl.multiple_of(start + j * block, block), block)] = act
        left = acts[:, pl.ds(pl.multiple_of(start, 128), half)]
        right = acts[:, pl.ds(pl.multiple_of(start + half, 128), half)]
        own[...] = jnp.where(core == 0, left, right)
        send[...] = jnp.where(core == 0, right, left)

    @pl.when(k == heads)
    def _():
        fetch.wait()
        branch = dot(acts[...], down[...])
        sums = [0.0] * 3
        for rows in tiles_of(branch.shape[0], 32):
            unit, inv = norm_stats(hidden[rows] + (branch[rows] + b_down))
            out[rows] = (unit * gain2 + shift2).astype(LOW)
            upstream = cot[rows].astype(F32)
            grad = norm_back(upstream, unit, inv, gain2)
            res2[rows] = grad
            grad_low = grad.astype(LOW)
            ends[2, rows] = grad_low[:, :half]
            ends[3, rows] = grad_low[:, half:]
            for i, term in enumerate((grad_low.astype(F32), upstream * unit, upstream)):
                sums[i] = sums[i] + jnp.sum(term, 0, keepdims=True)
        for i in range(3):
            small[i : i + 1] = sums[i]


def inner_back(places, ends, w_down, slope, send, own, bias, branch, inners, down, sem):
    half = send.shape[1]
    core, z = places[1], places[2]
    k = pl.program_id(0)
    heads, chunk, _ = down.shape

    def fetch(i):
        at = pl.ds(pl.multiple_of((z ^ i) * chunk, chunk), chunk)
        return pltpu.make_async_copy(w_down.at[at], down.at[i], sem.at[i])

    @pl.when(k == 0)
    def _():
        for i in range(heads):
            fetch(i).start()
        branch[:, :half] = ends[0]
        branch[:, half:] = ends[1]

    fetch(k).wait()
    block = 256
    for j in range(inners.shape[1] // block):
        at = slice(j * block, (j + 1) * block)
        grad_act = dot_nt(branch[...], down[k, at])
        total = 0.0
        for rows in tiles_of(grad_act.shape[0], 32):
            inner = (grad_act[rows] * slope[rows, at].astype(F32)).astype(LOW)
            inners[rows, at] = inner
            total = total + jnp.sum(inner.astype(F32), 0, keepdims=True)
        bias[:, at] = total
    first, second = inners[:, :half], inners[:, half:]
    own[...] = jnp.where(core == 0, first, second)
    send[...] = jnp.where(core == 0, second, first)


def hidden_back(
    places, own, sent, w_up, res2, unit1, inv1, gain1, send, res1, low, small, acc
):
    k = pl.program_id(0)
    core = places[1]
    half = own.shape[1]
    mine, other = own[...], sent[...]
    inner = jnp.concatenate(
        [jnp.where(core == 0, mine, other), jnp.where(core == 0, other, mine)], 1
    )
    product = dot_nt(inner, w_up[...])

    @pl.when(k == 0)
    def _():
        acc[...] = res2[...] + product

    @pl.when(k > 0)
    def _():
        acc[...] += product

    @pl.when(k == pl.num_programs(0) - 1)
    def _():
        gain = gain1[...].reshape(1, -1)
        sums = [0.0] * 3
        for rows in tiles_of(acc.shape[0], 32):
            grad, unit = acc[rows], unit1[rows]
            result = norm_back(grad, unit, inv1[rows], gain)
            res1[rows] = result
            result_low = result.astype(LOW)
            low[rows] = result_low
            send[rows] = jnp.where(core == 0, result_low[:, half:], result_low[:, :half])
            for i, term in enumerate((result_low.astype(F32), grad * unit, grad)):
                sums[i] = sums[i] + jnp.sum(term, 0, keepdims=True)
        for i in range(3):
            small[i : i + 1] = sums[i]


def attention_back(places, qkv, w_out, grad, log_ref, seg_row, rows_ref, bias_ref):
    width = qkv.shape[0] // 3
    grad_mixed = dot_nt(w_out[...], grad[...]).astype(LOW)
    more_k, more_q = segment_rows(seg_row[...])
    scale = HEAD_DIM ** (-0.5)
    for head in range(width // HEAD_DIM):
        places_of = [c * width + head * HEAD_DIM for c in range(3)]
        q, k, v = (qkv[at : at + HEAD_DIM] for at in places_of)
        g = grad_mixed[head * HEAD_DIM : (head + 1) * HEAD_DIM]
        logs = jnp.concatenate(three_parts(-log_ref[head : head + 1]), 0)
        with_logs = jnp.concatenate([more_q[:8], logs, more_q[11:]], 0)
        scores = dot_tn(jnp.concatenate([k, more_k], 0), jnp.concatenate([q, with_logs], 0))
        grad_probs = dot_tn(v, g)
        attends, grads = [], []
        for tile in tiles_of(scores.shape[1], LANES):
            inner, kept, lows, parts = 0.0, [], [], []
            tall = tiles_of(scores.shape[0], 64)
            for down in tall:
                attend = jnp.exp2(scores[down, tile] * SCORE_SCALE)
                inner = inner + jnp.sum(attend * grad_probs[down, tile], 0, keepdims=True)
                kept.append(attend)
                lows.append(attend.astype(LOW))
            for down, attend in zip(tall, kept):
                parts.append((attend * (grad_probs[down, tile] - inner)).astype(LOW))
            attends.append(jnp.concatenate(lows, 0))
            grads.append(jnp.concatenate(parts, 0))
        attend_low = jnp.concatenate(attends, 1)
        grad_scores = jnp.concatenate(grads, 1)
        grad_v = dot_nt(g, attend_low)
        grad_q = dot(k, grad_scores) * scale
        grad_k = dot_nt(q, grad_scores) * scale
        for at, value in zip(places_of, (grad_q, grad_k, grad_v)):
            rows_ref[at : at + HEAD_DIM] = value.astype(LOW)
    ones = jnp.ones((8, rows_ref.shape[1]), LOW)
    bias_ref[...] = dot_nt(ones, rows_ref[...])


def split_rows(value, high, send, keep):
    rows = value.shape[0] // 2
    low = value.astype(LOW)
    send[...] = jnp.where(high, low[:rows], low[rows:])
    keep[...] = jnp.where(high, low[rows:], low[:rows])


def is_high(places, bit):
    return (places[0] & bit) != 0


def unit_rows(units, units_far, ends, ends_far, both):
    half, count = ends.shape[2], ends.shape[1]

    @pl.when(pl.program_id(0) == 0)
    def _():
        for side in range(2):
            rows = slice(side * half, (side + 1) * half)
            both[rows, :count] = ends[side].T
            both[rows, count:] = ends_far[side].T

    left, right = (jnp.concatenate([units[i], units_far[i]], 0) for i in range(2))
    return dot(both[...], jnp.concatenate([left, right], 1))


def ffn_grad(bit, places, units, units_far, ends, ends_far, send, keep, both):
    total = unit_rows(units, units_far, ends, ends_far, both)
    half = send.shape[2]
    for i in range(2):
        part = total[:, i * half : (i + 1) * half]
        split_rows(part, is_high(places, bit), send.at[i], keep.at[i])


def attn_grad(
    places, rows, rows_far, tok, tok_far, mix, mix_far, grad, grad_far,
    small_one, small_two, up_bias, qkv_bias, send_x, keep_x, send_y, keep_y,
):
    width = mix.shape[0]
    half = tok.shape[1]
    def joined(a, a_far, b, b_far):
        left = jnp.concatenate([a[...], a_far[...]], 1)
        return dot(left, jnp.concatenate([b[...], b_far[...]], 0))

    qkv = joined(rows, rows_far, tok, tok_far)
    out = joined(mix, mix_far, grad, grad_far)
    lines = []
    for held in (small_one, small_two):
        for i in range(3):
            lines += [held[i : i + 1, :half], held[i : i + 1, half:]]
    lines += [up_bias[:, :half], up_bias[:, half:]]
    lines.append(jnp.concatenate([qkv_bias[0:1, :width], qkv_bias[0:1, 2 * width :]], 1))
    lines.append(jnp.zeros((EXTRA - len(lines), half), F32))
    total = jnp.concatenate([qkv, out] + lines, 0)
    split_rows(total[:half], is_high(places, 1), send_x, keep_x)
    split_rows(total[half:], is_high(places, 2), send_y, keep_y)


def add_split(bits, places, *refs):
    for i, bit in enumerate(bits):
        keep, came = refs[2 * i : 2 * i + 2]
        send, left = refs[2 * (len(bits) + i) : 2 * (len(bits) + i) + 2]
        for d in range(keep.shape[0]):
            total = keep[d].astype(F32) + came[d].astype(F32)
            split_rows(total, is_high(places, bit), send.at[d], left.at[d])


def add_parts(places, keep_a, came_a, keep_b, came_b, send, keep):
    rows = keep_a.shape[1]
    for d in range(keep_a.shape[0]):
        out = (send if d % 2 else keep).at[d // 2]
        out[:rows] = (keep_a[d].astype(F32) + came_a[d].astype(F32)).astype(LOW)
        out[rows:] = (keep_b[d].astype(F32) + came_b[d].astype(F32)).astype(LOW)


def add_pair(places, keep, came, *outs):
    for i, out in enumerate(outs):
        out[...] = (keep[i].astype(F32) + came[i].astype(F32)).astype(LOW)


def add_two(places, keep, came, out):
    out[...] = (keep[...].astype(F32) + came[...].astype(F32)).astype(LOW)


def input_sum(places, rows, w, res1, out):
    total = dot_tn(rows[...], w[...])
    k = pl.program_id(0)
    out[...] = jnp.where(k == 0, res1[...], out[...]) + total


def place_pieces(places, held, full, layouts):
    near, core = places[0], places[1]
    width = held[0].shape[1]
    for off in range(4):
        chip = near ^ off
        mine, other = held[off][...], held[4 + off][...]
        sides = (jnp.where(core == 0, mine, other), jnp.where(core == 0, other, mine))
        for at, rows, start, outer in layouts:
            low_bit, high_bit = chip & 1, chip >> 1
            order = 2 * low_bit + high_bit if outer == 1 else 2 * high_bit + low_bit
            to = pl.multiple_of(start + order * rows, 16)
            for side in range(2):
                full[pl.ds(to, rows), side * width : (side + 1) * width] = sides[side][
                    at : at + rows
                ].astype(F32)


def ffn_place(places, *refs):
    held = [ref.at[off] for ref in refs[:2] for off in range(4)]
    down, up, full = refs[2:]
    rows = held[0].shape[0] // 2
    place_pieces(places, held, full, [(0, rows, 0, 1)])
    down[...] = full[...].T
    place_pieces(places, held, up, [(rows, rows, 0, 2)])


def collect(places, *refs):
    for off in range(4):
        refs[4][off] = refs[off][...]


def attn_place(places, *refs):
    held = [ref.at[off] for ref in refs[:2] for off in range(4)]
    qkv, w_out, small, up_bias, qv_bias, full = refs[2:]
    width = held[0].shape[1]
    count = w_out.shape[0]
    rows = count // 2
    more = held[0].shape[0] - rows
    place_pieces(places, held, full, [(0, rows, 0, 1), (rows, more, 4 * rows, 2)])
    for c in range(3):
        qkv[c] = full[c * count : (c + 1) * count]
    w_out[...] = full[3 * count : 4 * count]
    at = 4 * count
    lines = full[at : at + 16, :width] + full[at : at + 16, width:]
    for i in range(6):
        small[i : i + 1, :width] = lines[2 * i : 2 * i + 1]
        small[i : i + 1, width:] = lines[2 * i + 1 : 2 * i + 2]
    up_bias[...] = jnp.concatenate([lines[12:13], lines[13:14]], 1).reshape(2 * width)
    qv_bias[0:1] = lines[14:15, :count]
    qv_bias[1:2] = lines[14:15, count : 2 * count]


def bias_parts(values):
    rows, rest = [], values
    for _ in range(3):
        rows.append(lax.reduce_precision(rest, 8, 7))
        rest = rest - rows[-1]
    return jnp.stack(rows).astype(LOW)


def gather_back(piece):
    return [piece] + [swap(piece, "near", off) for off in range(1, 4)]


def per_device(
    tokens,
    segment_ids,
    w_qkv,
    b_qv,
    w_out,
    b_out,
    ln1_gain,
    ln1_bias,
    w_up,
    b_up,
    w_down,
    b_down,
    ln2_gain,
    ln2_bias,
    cotangent,
):
    CHAIN.clear()
    width = tokens.shape[1]
    own_rows = cotangent.shape[0]
    local_width = w_qkv.shape[2]
    heads = lax.axis_size("head")
    z = lax.axis_index("head")
    core = lax.axis_index("core")
    near = lax.axis_index("near")
    hidden_units = w_up.shape[1]
    chunk = hidden_units // heads
    half = width // 2
    rows3 = 3 * local_width
    places = jnp.stack([near, core, z]).astype(jnp.int32)

    shard = jnp.concatenate([w_qkv.transpose(0, 2, 1).reshape(rows3, width), w_out], 0)
    piece_rows = shard.shape[0] // 8
    bias = jnp.pad(bias_parts(b_qv.reshape(-1)), ((0, 13), (0, width - 2 * local_width)))
    piece = lax.dynamic_slice_in_dim(shard, (near * 2 + core) * piece_rows, piece_rows, 0)
    piece = jnp.concatenate([piece, bias], 0)
    first_hop = [swap(piece, "head", d) for d in range(1, heads)]

    seg = lax.dynamic_slice_in_dim(segment_ids, z * own_rows, own_rows, 0)
    segs = [(seg[None], whole((1, own_rows)))]
    tok_own = lax.dynamic_slice_in_dim(tokens, z * own_rows, own_rows, 0)
    own_tokens = (tok_own, whole((own_rows, width)))

    def attend_outs(first):
        def spec(*shape):
            return pl.BlockSpec((None,) + shape, lambda k, s: (k + first, 0, 0))

        return [
            ((heads, rows3, own_rows), LOW, spec(rows3, own_rows)),
            ((heads, local_width, own_rows), LOW, spec(local_width, own_rows)),
            ((heads, 8, own_rows), F32, spec(8, own_rows)),
            ((heads, rows3, width), LOW, spec(rows3, width)),
            ((heads, local_width, width), LOW, spec(local_width, width)),
        ]

    macs = rows3 * width * own_rows + 6 * own_rows * own_rows * 256
    ins = [own_tokens, (shard, whole(shard.shape)), (bias, whole(bias.shape))] + segs
    made = begun = run(own_attention, places, (1,), ins, attend_outs(0), macs=macs, chain=False)
    block = pl.BlockSpec((piece_rows, width), lambda k, s: (0, 0))
    orders = [(1, 2) if d % 2 else (2, 1) for d in range(heads)]
    nexts = [swap(first_hop[d - 1], "near", orders[d][0]) for d in range(1, heads)]
    for d in range(1, heads):
        order = orders[d]
        ins = [(first_hop[d - 1], block), (nexts[d - 1], block)]
        twice = (2, piece_rows, width)
        (pair,) = run(
            pair_rows, places, (1,), ins, [(twice, LOW, whole(twice))],
            after=nexts + [begun[2]], weight=LIGHT, chain=False,
        )
        rest = swap(pair, "near", order[1])
        held = [pair, rest, swap_core(pair), swap_core(rest)]
        ins = [own_tokens] + [(h, whole(h.shape)) for h in held]
        ins += [(first_hop[d - 1], pl.BlockSpec((16, width), lambda k, s: (piece_rows // 16, 0)))]
        kernel = functools.partial(far_attention, order)
        made = run(
            kernel, places, (1,), ins + segs, attend_outs(d), [pltpu.VMEM((rows3 + local_width, width), LOW)], macs, alias=made,
            chain=False, weight=100,
        )
    qkvs, mixes, logs, w_qkvs, w_outs = made

    mixes_far = swap_core(mixes)

    def by_step(*shape):
        block = (None,) + shape
        return pl.BlockSpec(block, lambda k, s: (jnp.minimum(k, heads - 1),) + (0,) * len(shape))

    def unit_at(k, s):
        return s[2] ^ jnp.minimum(k, heads - 1)


    line = whole((width,))
    square = (own_rows, width)
    tile = by_step(own_rows, half)
    tiles = (heads, own_rows, half)
    up_block = (w_up, pl.BlockSpec((width, chunk), lambda k, s: (0, unit_at(k, s))))
    line_block = pl.BlockSpec((None, 1, chunk), lambda k, s: (unit_at(k, s), 0, 0))

    ins = [
        own_tokens,
        (mixes, whole(mixes.shape)),
        (w_outs, whole(w_outs.shape)),
        (b_out, line),
        (ln1_gain, line),
        (ln1_bias, line),
        (b_down, line),
        (ln2_gain, line),
        (ln2_bias, line),
        up_block,
        (b_up.reshape(heads, 1, chunk), line_block),
        (w_down, pl.BlockSpec(memory_space=pl.ANY)),
        (cotangent, whole(square)),
    ]
    outs = [
        (tiles, LOW, tile),
        (tiles, LOW, tile),
        ((4, own_rows, half), LOW, whole((4, own_rows, half))),
        ((heads, own_rows, chunk), LOW, by_step(own_rows, chunk)),
        (square, F32, whole(square)),
        ((own_rows, 1), F32, whole((own_rows, 1))),
        (square, F32, whole(square)),
        (square, LOW, whole(square)),
        ((8, width), F32, whole((8, width))),
        ((own_rows, half), LOW, whole((own_rows, half))),
    ]
    scratch = [
        pltpu.VMEM(square, F32),
        pltpu.VMEM(square, LOW),
        pltpu.VMEM((own_rows, hidden_units), LOW),
        pltpu.VMEM(w_down.shape, LOW),
        pltpu.SemaphoreType.DMA,
    ]
    ffn_macs = 2 * own_rows * width * hidden_units
    act_send, act_own, ends, slope, unit1, inv1, res2, layer_output, small_two, tok_send = run(
        feed_forward, places, (heads + 1,), ins, outs, scratch, ffn_macs
    )
    tok_far = swap_core(tok_send)
    act_far = swap_core(act_send)
    ends_far = swap_core(ends)

    def two_of(array, index):
        return (array, pl.BlockSpec((2, own_rows, half), lambda k, s: (index, 0, 0)))

    ins = [
        two_of(ends, 1),
        (w_down, pl.BlockSpec(memory_space=pl.ANY)),
        (slope, by_step(own_rows, chunk)),
    ]
    outs = [(tiles, LOW, tile), (tiles, LOW, tile), ((heads, 1, chunk), F32, line_block)]
    scratch = [
        pltpu.VMEM(square, LOW),
        pltpu.VMEM((own_rows, chunk), LOW),
        pltpu.VMEM((heads, chunk, width), LOW),
        pltpu.SemaphoreType.DMA((heads,)),
    ]
    inner_send, inner_own, up_bias = run(
        inner_back, places, (heads,), ins, outs, scratch, ffn_macs // 2,
        after=[mixes_far],
    )
    inner_far = swap_core(inner_send)


    def two(*shape):
        return pl.BlockSpec((2,) + shape, lambda k, s: (k,) + (0,) * len(shape))

    def ffn_unit(bit, own, far, which, weight):
        ins = [(own, two(own_rows, half)), (far, two(own_rows, half))]
        ins += [two_of(ends, which), two_of(ends_far, which)]
        outs = [((heads, half, half), LOW, two(half, half))] * 2
        both = [pltpu.VMEM((width, 2 * own_rows), LOW)]
        kernel = functools.partial(ffn_grad, bit)
        return run(kernel, places, (heads // 2,), ins, outs, both, ffn_macs // 2, weight=weight)

    made = ffn_unit(1, act_own, act_far, 1, 8) + ffn_unit(2, inner_own, inner_far, 0, LIGHT)
    x_send, x_keep, y_send, y_keep = made
    ffn_held = (x_keep, swap(x_send, "near", 1), y_keep, swap(y_send, "near", 2))

    ins = [
        (inner_own, tile),
        (inner_send, tile),
        up_block,
        (res2, whole(square)),
        (unit1, whole(square)),
        (inv1, whole((own_rows, 1))),
        (ln1_gain, line),
    ]
    outs = [
        ((own_rows, half), LOW, whole((own_rows, half))),
        (square, F32, whole(square)),
        (square, LOW, whole(square)),
        ((8, width), F32, whole((8, width))),
    ]
    grad_send, res1, grad_attended, small_one = run(
        hidden_back, places, (heads,), ins, outs, [pltpu.VMEM(square, F32)], ffn_macs // 2,
        weight=LIGHT,
    )
    grad_far = swap_core(grad_send)

    def pair_block(first, *shape):
        block = (None,) + shape
        return pl.BlockSpec(block, lambda k, s: (k + first,) + (0,) * len(shape))

    def attend_back(first, count):
        ins = [
            (qkvs, pair_block(first, rows3, own_rows)),
            (w_outs, pair_block(first, local_width, width)),
            (grad_attended, whole(square)),
            (logs, pair_block(first, 8, own_rows)),
        ] + segs
        outs = [
            ((count, rows3, own_rows), LOW, pair_block(0, rows3, own_rows)),
            ((count, 8, rows3), F32, pair_block(0, 8, rows3)),
        ]
        return run(
            attention_back, places, (count,), ins, outs,
            macs=count * (15 * own_rows * own_rows * 256 + local_width * own_rows * width),
            weight=LIGHT,
        )

    def attend_unit(first, rows, rows_far, qkv_bias, alias):
        bias_line = pl.BlockSpec((None, 1, chunk), lambda k, s: (s[2] ^ (k + first), 0, 0))
        ins = [
            (rows, pair_block(0, rows3, own_rows)),
            (rows_far, pair_block(0, rows3, own_rows)),
            (tok_own, pl.BlockSpec((own_rows, half), lambda k, s: (0, s[1]))),
            (tok_far, whole((own_rows, half))),
            (mixes, pair_block(first, local_width, own_rows)),
            (mixes_far, pair_block(first, local_width, own_rows)),
            (grad_attended, pl.BlockSpec((own_rows, half), lambda k, s: (0, s[1]))),
            (grad_far, whole((own_rows, half))),
            (small_one, whole((8, width))),
            (small_two, whole((8, width))),
            (up_bias, bias_line),
            (qkv_bias, pair_block(0, 8, rows3)),
        ]
        outs = [
            ((heads, r, half), LOW, pair_block(first, r, half))
            for r in (half // 2, (half + EXTRA) // 2)
            for _ in range(2)
        ]
        return run(
            attn_grad, places, (rows.shape[0],), ins, outs, alias=alias, weight=LIGHT
        )

    def second(x_keep, x_came, y_keep, y_came, macs=0):
        arrays = (x_keep, x_came, y_keep, y_came)
        ins = [(a, whole(a.shape)) for a in arrays]
        shapes = [(heads, a.shape[1] // 2, half) for a in (x_keep, x_keep, y_keep, y_keep)]
        outs = [(shape, LOW, whole(shape)) for shape in shapes]
        kernel = functools.partial(add_split, (2, 1))
        return run(kernel, places, (1,), ins, outs, macs=macs)

    def third(x_keep, x_came, y_keep, y_came):
        arrays = (x_keep, x_came, y_keep, y_came)
        shape = (heads // 2, x_keep.shape[1] + y_keep.shape[1], half)
        send, keep = run(
            add_parts, places, (1,), [(a, whole(a.shape)) for a in arrays],
            [(shape, LOW, whole(shape))] * 2, weight=LIGHT,
        )
        return keep, swap(send, "head", 1)

    def fourth(keep, came):
        shape = keep.shape[1:]
        mine, other = run(
            add_pair, places, (1,), [(a, whole(a.shape)) for a in (keep, came)],
            [(shape, LOW, whole(shape))] * 2, weight=LIGHT,
        )
        return mine, swap(other, "head", 2)

    def fifth(mine, came):
        shape = mine.shape
        (total,) = run(
            add_two, places, (1,), [(a, whole(shape)) for a in (mine, came)],
            [(shape, LOW, whole(shape))], weight=LIGHT,
        )
        bit = 1
        while bit < lax.axis_size("far"):
            total = (total.astype(F32) + swap(total, "far", bit).astype(F32)).astype(LOW)
            bit *= 2
        return total

    def cross(made, flip):
        x_send, x_keep, y_send, y_keep = made
        x_bit, y_bit = (2, 1) if flip else (1, 2)
        return x_keep, swap(x_send, "near", x_bit), y_keep, swap(y_send, "near", y_bit)

    rows, qkv_bias = attend_back(0, heads)
    rows_far = swap_core(rows)

    ins = [
        (rows, by_step(rows3, own_rows)),
        (w_qkvs, by_step(rows3, width)),
        (res1, whole(square)),
    ]
    outs = [(square, F32, whole(square))]
    (input_grad,) = run(input_sum, places, (heads,), ins, outs, weight=LIGHT)
    ffn_held = cross(second(*ffn_held, ffn_macs), True)
    made = attend_unit(0, rows, rows_far, qkv_bias, ())
    attn_held = cross(made, False)

    ffn_held = third(*ffn_held)
    attn_held = cross(second(*attn_held), True)
    ffn_held = fourth(*ffn_held)
    attn_held = third(*attn_held)
    ffn_held = gather_back(fifth(*ffn_held))
    attn_held = fourth(*attn_held)
    attn_held = gather_back(fifth(*attn_held))

    def both_cores(held):
        shape = (heads,) + held[0].shape
        ins = [(h, whole(h.shape)) for h in held]
        (pieces,) = run(collect, places, (1,), ins, [(shape, LOW, whole(shape))])
        return [(a, whole(shape)) for a in (pieces, swap_core(pieces))]

    ffn_held = both_cores(ffn_held)
    outs = [(shape, F32, whole(shape)) for shape in ((chunk, width), (width, chunk))]
    grad_down, grad_up = run(
        ffn_place, places, (1,), ffn_held, outs, [pltpu.VMEM((width, chunk), F32)]
    )
    attn_held = both_cores(attn_held)
    shapes = [
        (3, local_width, width),
        (local_width, width),
        (6, width),
        (chunk,),
        (2, local_width),
    ]
    grad_qkv, grad_out, grad_small, grad_up_bias, grad_qv_bias = run(
        attn_place,
        places,
        (1,),
        attn_held,
        [(shape, F32, whole(shape)) for shape in shapes],
        [pltpu.VMEM((width + EXTRA, width), F32)],
    )
    return (
        layer_output,
        input_grad,
        grad_qkv.transpose(0, 2, 1),
        grad_qv_bias,
        grad_out,
        grad_up,
        grad_up_bias,
        grad_down,
        grad_small,
    )


def solution(mesh):
    batch, heads = mesh.devices.shape
    mesh = Mesh(
        mesh.devices.reshape(batch // 8, 4, 2, heads), ("far", "near", "core", "head")
    )
    group = ("far", "near", "core")
    everyone = group + ("head",)
    in_specs = (
        P(group, None),
        P(group),
        P(None, None, "head"),
        P(None, "head"),
        P("head", None),
        P(),
        P(),
        P(),
        P(),
        P(),
        P(),
        P(),
        P(),
        P(),
        P(everyone, None),
    )
    out_specs = (
        P(everyone, None),
        P(everyone, None),
        P(None, None, "head"),
        P(None, "head"),
        P("head", None),
        P(None, "head"),
        P("head"),
        P("head", None),
        P(),
    )
    return jax.shard_map(
        per_device, mesh=mesh, in_specs=in_specs, out_specs=out_specs, check_vma=False
    )
```

```python
import functools
import math

import jax
import jax.numpy as jnp
from jax import lax
from jax.experimental import pallas as pl
from jax.experimental.pallas import tpu as pltpu
from jax.sharding import Mesh
from jax.sharding import PartitionSpec as P

HEAD_DIM = 64
SLOT = 512
LOW = jnp.bfloat16
F32 = jnp.float32
LOG2E = math.log2(math.e)
SCORE_SCALE = HEAD_DIM ** (-0.5) * LOG2E
SPARE_BYTES = 12 * 2**20
EXTRA = 64
LIGHT = 0.01
LANES = 128
CHAIN = []
TAIL_SLOPE = 0.36
TAIL = (
    0.14371304537508633,
    0.14177245466203425,
    0.1397192603907239,
    0.026549325413860486,
    0.18095403134327948,
    -0.1797647161697652,
    0.047056295581175855,
)


def swap(value, axis, bit):
    size = lax.axis_size(axis)
    return lax.ppermute(value, axis, [(i, i ^ bit) for i in range(size)])


def swap_core(value):
    return swap(value, "core", 1)


def dot(a, b):
    return jnp.dot(a, b, preferred_element_type=F32)


def dot_nt(a, b):
    return lax.dot_general(a, b, (((1,), (1,)), ((), ())), preferred_element_type=F32)


def dot_tn(a, b):
    return lax.dot_general(a, b, (((0,), (0,)), ((), ())), preferred_element_type=F32)


def whole(shape):
    return pl.BlockSpec(shape, lambda *args: (0,) * len(shape), pipeline_mode=pl.Buffered(1))


def run(
    kernel, places, grid, ins, outs, scratch=(), macs=0, after=(), alias=(), weight=8, chain=True
):
    moved = sum(a.size * a.dtype.itemsize for a, spec in ins)
    moved += sum(math.prod(shape) * jnp.dtype(kind).itemsize for shape, kind, spec in outs)
    after = list(after) + (CHAIN if chain else [])
    count, unread = len(ins), len(alias) + len(after)
    results = len(outs)
    flag = (8, 128)
    if chain:
        outs = outs + [(flag, F32, whole(flag))]

    def body(places, *refs):
        made = refs[count + unread :]
        if chain:

            @pl.when(pl.program_id(0) == 0)
            def _():
                made[results][...] = jnp.zeros(flag, F32)

        kernel(places, *refs[:count], *made[:results], *made[len(outs) :])

    held = pl.BlockSpec(memory_space=pl.ANY)
    room = SPARE_BYTES
    for shape, kind, spec in outs + [(a.shape, a.dtype, spec) for a, spec in ins]:
        if spec.block_shape is not None:
            block = math.prod(1 if n is None else n for n in spec.block_shape)
            copies = 2 if spec.pipeline_mode is None else 1
            room += copies * block * jnp.dtype(kind).itemsize
    for ref in scratch:
        if hasattr(ref, "shape") and ref.dtype in (LOW, F32):
            room += math.prod(ref.shape) * jnp.dtype(ref.dtype).itemsize
    made = pl.pallas_call(
        body,
        name=getattr(kernel, "func", kernel).__name__,
        grid_spec=pltpu.PrefetchScalarGridSpec(
            num_scalar_prefetch=1,
            grid=grid,
            in_specs=[spec for a, spec in ins] + [held] * unread,
            out_specs=[spec for shape, kind, spec in outs],
            scratch_shapes=list(scratch),
        ),
        out_shape=[jax.ShapeDtypeStruct(shape, kind) for shape, kind, spec in outs],
        input_output_aliases={1 + count + i: i for i in range(len(alias))},
        compiler_params=pltpu.CompilerParams(vmem_limit_bytes=room),
        cost_estimate=pl.CostEstimate(
            flops=int(2 * macs * weight), bytes_accessed=int(moved * weight), transcendentals=0
        ),
    )(places, *[a for a, spec in ins], *alias, *after)
    if chain:
        CHAIN[:] = made[results:]
    return made[:results]


def run_whole(
    kernel, places, ins, outs, scratch=(), macs=0, after=(), alias=(), weight=8, chain=True
):
    pairs = [a if isinstance(a, tuple) else (a, pltpu.VMEM) for a in ins]
    after = list(after) + (CHAIN if chain else [])
    count, unread, results = len(pairs), len(alias) + len(after), len(outs)
    if chain:
        outs = outs + [((8, 128), F32)]

    def body(places, *refs):
        made = refs[count + unread :]
        if chain:
            made[results][...] = jnp.zeros((8, 128), F32)
        kernel(places, *refs[:count], *made[:results], *made[len(outs) :])

    room = SPARE_BYTES
    for ref in scratch:
        if hasattr(ref, "shape") and ref.dtype in (LOW, F32):
            room += math.prod(ref.shape) * jnp.dtype(ref.dtype).itemsize
    spaces = [pltpu.SMEM] + [space for a, space in pairs]
    spaces += [pltpu.VMEM] * len(alias) + [pl.ANY] * len(after)
    made = pl.pallas_call(
        body,
        name=getattr(kernel, "func", kernel).__name__,
        in_specs=[pl.BlockSpec(memory_space=space) for space in spaces],
        out_specs=[pl.BlockSpec(memory_space=pltpu.VMEM)] * len(outs),
        scratch_shapes=list(scratch),
        out_shape=[jax.ShapeDtypeStruct(shape, kind) for shape, kind in outs],
        input_output_aliases={1 + count + i: i for i in range(len(alias))},
        compiler_params=pltpu.CompilerParams(vmem_limit_bytes=room),
        cost_estimate=pl.CostEstimate(
            flops=int(2 * macs * weight), bytes_accessed=0, transcendentals=0
        ),
    )(places, *[a for a, space in pairs], *alias, *after)
    if chain:
        CHAIN[:] = made[results:]
    return made[:results]


def tiles_of(count, size):
    return [slice(at, at + size) for at in range(0, count, size)]


def three_parts(values):
    parts, rest = [], values
    for _ in range(3):
        parts.append(rest.astype(LOW))
        rest = rest - parts[-1].astype(F32)
    return parts


def segment_rows(seg_row):
    shape = (16, seg_row.shape[1])
    place = lax.broadcasted_iota(jnp.int32, shape, 0)
    same = place - 1 == seg_row
    keys = jnp.where(same, 1.0, jnp.where((place >= 8) & (place < 11), 1.0, 0.0))
    queries = jnp.where(same | (place > 4), 0.0, -1e30)
    return keys.astype(LOW), queries.astype(LOW)


def attend_heads(tok, w_rows, bias, seg_row, qkv_ref, mix_ref, log_ref):
    width = w_rows.shape[0] // 3
    added = dot_tn(bias[:, : 2 * width], jnp.ones((bias.shape[0], tok.shape[0]), LOW))
    qkv = dot_nt(w_rows, tok)
    parts = (
        (qkv[:width] + added[:width]).astype(LOW),
        qkv[width : 2 * width].astype(LOW),
        (qkv[2 * width :] + added[width:]).astype(LOW),
    )
    for c in range(3):
        qkv_ref[c * width : (c + 1) * width] = parts[c]
    more_k, more_q = segment_rows(seg_row)
    for head in range(width // HEAD_DIM):
        q, k, v = (part[head * HEAD_DIM : (head + 1) * HEAD_DIM] for part in parts)
        scores = dot_tn(jnp.concatenate([k, more_k], 0), jnp.concatenate([q, more_q], 0))
        columns, tops, totals = [], [], []
        for tile in tiles_of(scores.shape[1], LANES):
            top = jnp.max(scores[:, tile], 0, keepdims=True)
            total, column = 0.0, []
            for rows in tiles_of(scores.shape[0], 64):
                exponent = jnp.exp2((scores[rows, tile] - top) * SCORE_SCALE)
                total = total + jnp.sum(exponent, 0, keepdims=True)
                column.append(exponent.astype(LOW))
            columns.append(jnp.concatenate(column, 0))
            tops.append(top)
            totals.append(total)
        total = jnp.concatenate(totals, 1)
        mixed = dot(v, jnp.concatenate(columns, 1)) * (1.0 / total)
        mix_ref[head * HEAD_DIM : (head + 1) * HEAD_DIM] = mixed.astype(LOW)
        top = jnp.concatenate(tops, 1)
        log_ref[head : head + 1] = top + jnp.log2(total) * (1.0 / SCORE_SCALE)


def own_attention(
    places, tok, w, bias, seg_row, qkv_ref, mix_ref, log_ref, w_qkv, w_out
):
    w_qkv[...] = w[: qkv_ref.shape[0]]
    w_out[...] = w[qkv_ref.shape[0] :]
    attend_heads(
        tok[...],
        w[: qkv_ref.shape[0]],
        bias[...],
        seg_row[...],
        qkv_ref,
        mix_ref,
        log_ref,
    )


def far_attention(
    order, places, tok, pair, rest, pair_far, rest_far, bias, seg_row,
    qkv_ref, mix_ref, log_ref, w_qkv, w_out, w_ref,
):
    first, second = order
    rows = pair.shape[1]
    me = places[0] * 2 + places[1]
    for other, held in enumerate(((pair, rest), (pair_far, rest_far))):
        for two, block in enumerate(held):
            for one in range(2):
                owner = me ^ (other + 2 * first * one + 2 * second * two)
                w_ref[pl.ds(pl.multiple_of(owner * rows, rows), rows)] = block[one]
    w_qkv[...] = w_ref[: qkv_ref.shape[0]]
    w_out[...] = w_ref[qkv_ref.shape[0] :]
    attend_heads(
        tok[...],
        w_ref[: qkv_ref.shape[0]],
        bias[...],
        seg_row[...],
        qkv_ref,
        mix_ref,
        log_ref,
    )


def pair_rows(places, first, second, out):
    out[0] = first[...]
    out[1] = second[...]


def norm_stats(v):
    centred = v - jnp.mean(v, -1, keepdims=True)
    inv = lax.rsqrt(jnp.mean(centred * centred, -1, keepdims=True) + 1e-05)
    return centred * inv, inv


def norm_back(upstream, unit, inv, gain):
    scaled = upstream * gain
    inner = jnp.mean(scaled * unit, -1, keepdims=True)
    return inv * (scaled - jnp.mean(scaled, -1, keepdims=True) - unit * inner)


def gelu_both(pre):
    power = jnp.exp2(pre * pre * (-0.5 * LOG2E))
    base = 1.0 + TAIL_SLOPE * jnp.abs(pre)
    t = pl.reciprocal(base, approx=True)
    tail = TAIL[6] * t + TAIL[5]
    for c in TAIL[4::-1]:
        tail = tail * t + c
    tail = tail * (t * power)
    cumul = jnp.where(pre < 0.0, tail, 1.0 - tail)
    return (pre * cumul).astype(LOW), cumul + pre * (power * 0.3989422804014327)


def feed_forward(
    places, tok, mix, w_out, b_out, gain1, shift1, b_down, gain2, shift2,
    w_up, b_up, w_down, cot,
    send, own, ends, slope, unit1, inv1, res2, out, small, tok_send,
    hidden, low, acts, down, sem,
):
    k = pl.program_id(0)
    half = send.shape[1]
    chunk = w_up.shape[1]
    core, z = places[1], places[2]
    heads = mix.shape[0]
    fetch = pltpu.make_async_copy(w_down, down, sem)
    b_out, gain1, shift1, b_down, gain2, shift2 = (
        ref[...].reshape(1, -1) for ref in (b_out, gain1, shift1, b_down, gain2, shift2)
    )

    @pl.when(k == 0)
    def _():
        fetch.start()
        tok_send[...] = jnp.where(core == 0, tok[:, half:], tok[:, :half])
        width = low.shape[1]
        attended = dot_tn(
            mix[...].reshape(width, low.shape[0]), w_out[...].reshape(width, width)
        )
        for rows in tiles_of(low.shape[0], 32):
            unit, inv = norm_stats(tok[rows].astype(F32) + (attended[rows] + b_out))
            unit1[rows] = unit
            inv1[rows] = inv
            one = unit * gain1 + shift1
            hidden[rows] = one
            one_low = one.astype(LOW)
            low[rows] = one_low
            ends[0, rows] = one_low[:, :half]
            ends[1, rows] = one_low[:, half:]

    @pl.when(k < heads)
    def _():
        start = (z ^ k) * chunk
        block = 256
        for j in range(chunk // block):
            at = slice(j * block, (j + 1) * block)
            pre = dot(low[...], w_up[:, at])
            for rows in tiles_of(pre.shape[0], 32):
                act, tilt = gelu_both(pre[rows] + b_up[:, at])
                slope[rows, at] = tilt.astype(LOW)
                acts[rows, pl.ds(pl.multiple_of(start + j * block, block), block)] = act
        left = acts[:, pl.ds(pl.multiple_of(start, 128), half)]
        right = acts[:, pl.ds(pl.multiple_of(start + half, 128), half)]
        own[...] = jnp.where(core == 0, left, right)
        send[...] = jnp.where(core == 0, right, left)

    @pl.when(k == heads)
    def _():
        fetch.wait()
        branch = dot(acts[...], down[...])
        sums = [0.0] * 3
        for rows in tiles_of(branch.shape[0], 32):
            unit, inv = norm_stats(hidden[rows] + (branch[rows] + b_down))
            out[rows] = (unit * gain2 + shift2).astype(LOW)
            upstream = cot[rows].astype(F32)
            grad = norm_back(upstream, unit, inv, gain2)
            res2[rows] = grad
            grad_low = grad.astype(LOW)
            ends[2, rows] = grad_low[:, :half]
            ends[3, rows] = grad_low[:, half:]
            for i, term in enumerate((grad_low.astype(F32), upstream * unit, upstream)):
                sums[i] = sums[i] + jnp.sum(term, 0, keepdims=True)
        for i in range(3):
            small[i : i + 1] = sums[i]


def inner_back(places, ends, w_down, slope, send, own, bias, branch, inners, down, sem):
    half = send.shape[1]
    core, z = places[1], places[2]
    k = pl.program_id(0)
    heads, chunk, _ = down.shape

    def fetch(i):
        at = pl.ds(pl.multiple_of((z ^ i) * chunk, chunk), chunk)
        return pltpu.make_async_copy(w_down.at[at], down.at[i], sem.at[i])

    @pl.when(k == 0)
    def _():
        for i in range(heads):
            fetch(i).start()
        branch[:, :half] = ends[0]
        branch[:, half:] = ends[1]

    fetch(k).wait()
    block = 256
    for j in range(inners.shape[1] // block):
        at = slice(j * block, (j + 1) * block)
        grad_act = dot_nt(branch[...], down[k, at])
        total = 0.0
        for rows in tiles_of(grad_act.shape[0], 32):
            inner = (grad_act[rows] * slope[rows, at].astype(F32)).astype(LOW)
            inners[rows, at] = inner
            total = total + jnp.sum(inner.astype(F32), 0, keepdims=True)
        bias[:, at] = total
    first, second = inners[:, :half], inners[:, half:]
    own[...] = jnp.where(core == 0, first, second)
    send[...] = jnp.where(core == 0, second, first)


def hidden_back(
    places, own, sent, w_up, res2, unit1, inv1, gain1, send, res1, low, small, acc
):
    k = pl.program_id(0)
    core = places[1]
    half = own.shape[1]
    mine, other = own[...], sent[...]
    inner = jnp.concatenate(
        [jnp.where(core == 0, mine, other), jnp.where(core == 0, other, mine)], 1
    )
    product = dot_nt(inner, w_up[...])

    @pl.when(k == 0)
    def _():
        acc[...] = res2[...] + product

    @pl.when(k > 0)
    def _():
        acc[...] += product

    @pl.when(k == pl.num_programs(0) - 1)
    def _():
        gain = gain1[...].reshape(1, -1)
        sums = [0.0] * 3
        for rows in tiles_of(acc.shape[0], 32):
            grad, unit = acc[rows], unit1[rows]
            result = norm_back(grad, unit, inv1[rows], gain)
            res1[rows] = result
            result_low = result.astype(LOW)
            low[rows] = result_low
            send[rows] = jnp.where(core == 0, result_low[:, half:], result_low[:, :half])
            for i, term in enumerate((result_low.astype(F32), grad * unit, grad)):
                sums[i] = sums[i] + jnp.sum(term, 0, keepdims=True)
        for i in range(3):
            small[i : i + 1] = sums[i]


def shard_back(qkv, w_out, grad, log_ref, more_k, more_q, rows_ref, bias_ref):
    width = qkv.shape[0] // 3
    grad_mixed = dot_nt(w_out[...], grad[...]).astype(LOW)
    scale = HEAD_DIM ** (-0.5)
    for head in range(width // HEAD_DIM):
        places_of = [c * width + head * HEAD_DIM for c in range(3)]
        q, k, v = (qkv[at : at + HEAD_DIM] for at in places_of)
        g = grad_mixed[head * HEAD_DIM : (head + 1) * HEAD_DIM]
        logs = jnp.concatenate(three_parts(-log_ref[head : head + 1]), 0)
        with_logs = jnp.concatenate([more_q[:8], logs, more_q[11:]], 0)
        scores = dot_tn(jnp.concatenate([k, more_k], 0), jnp.concatenate([q, with_logs], 0))
        grad_probs = dot_tn(v, g)
        attends, grads = [], []
        for tile in tiles_of(scores.shape[1], LANES):
            inner, kept, lows, parts = 0.0, [], [], []
            tall = tiles_of(scores.shape[0], 64)
            for down in tall:
                attend = jnp.exp2(scores[down, tile] * SCORE_SCALE)
                inner = inner + jnp.sum(attend * grad_probs[down, tile], 0, keepdims=True)
                kept.append(attend)
                lows.append(attend.astype(LOW))
            for down, attend in zip(tall, kept):
                parts.append((attend * (grad_probs[down, tile] - inner)).astype(LOW))
            attends.append(jnp.concatenate(lows, 0))
            grads.append(jnp.concatenate(parts, 0))
        attend_low = jnp.concatenate(attends, 1)
        grad_scores = jnp.concatenate(grads, 1)
        grad_v = dot_nt(g, attend_low)
        grad_q = dot(k, grad_scores) * scale
        grad_k = dot_nt(q, grad_scores) * scale
        for at, value in zip(places_of, (grad_q, grad_k, grad_v)):
            rows_ref[at : at + HEAD_DIM] = value.astype(LOW)
    ones = jnp.ones((8, rows_ref.shape[1]), LOW)
    bias_ref[...] = dot_nt(ones, rows_ref[...])


def attention_back(places, qkv, w_out, grad, log_ref, seg_row, rows_ref, bias_ref):
    more_k, more_q = segment_rows(seg_row[...])

    def shard(d, carry):
        refs = (ref.at[d] for ref in (rows_ref, bias_ref))
        shard_back(qkv.at[d], w_out.at[d], grad, log_ref.at[d], more_k, more_q, *refs)
        return carry

    lax.fori_loop(0, qkv.shape[0], shard, 0)


def split_rows(value, high, send, keep):
    rows = value.shape[0] // 2
    low = value.astype(LOW)
    send[...] = jnp.where(high, low[:rows], low[rows:])
    keep[...] = jnp.where(high, low[rows:], low[:rows])


def is_high(places, bit):
    return (places[0] & bit) != 0


def ffn_grad(bit, which, places, units, units_far, ends, ends_far, send, keep, both):
    half, count = ends.shape[2], ends.shape[1]
    for side in range(2):
        rows = slice(side * half, (side + 1) * half)
        both[rows, :count] = ends[2 * which + side].T
        both[rows, count:] = ends_far[2 * which + side].T
    for d in range(0, units.shape[0], 2):
        left, right = (jnp.concatenate([units[d + i], units_far[d + i]], 0) for i in range(2))
        total = dot(both[...], jnp.concatenate([left, right], 1))
        for i in range(2):
            part = total[:, i * half : (i + 1) * half]
            split_rows(part, is_high(places, bit), send.at[d + i], keep.at[d + i])


def attn_grad(
    places, rows, rows_far, tok, tok_far, mix, mix_far, grad, grad_far,
    small_one, small_two, up_bias, qkv_bias, send_x, keep_x, send_y, keep_y,
):
    width = mix.shape[1]
    half = tok_far.shape[1]
    core, z = places[1], places[2]

    def both(near, far):
        mine = jnp.where(core == 0, near[:, :half], near[:, half:])
        return jnp.concatenate([mine, far[...]], 0)

    tok_both, grad_both = both(tok, tok_far), both(grad, grad_far)
    for d in range(rows.shape[0]):
        qkv = dot(jnp.concatenate([rows[d], rows_far[d]], 1), tok_both)
        out = dot(jnp.concatenate([mix[d], mix_far[d]], 1), grad_both)
        lines = []
        for held in (small_one, small_two):
            for i in range(3):
                lines += [held[i : i + 1, :half], held[i : i + 1, half:]]
        line, bias = up_bias[z ^ d], qkv_bias[d]
        lines += [line[:, :half], line[:, half:]]
        lines.append(jnp.concatenate([bias[0:1, :width], bias[0:1, 2 * width :]], 1))
        lines.append(jnp.zeros((EXTRA - len(lines), half), F32))
        total = jnp.concatenate([qkv, out] + lines, 0)
        split_rows(total[:half], is_high(places, 1), send_x.at[d], keep_x.at[d])
        split_rows(total[half:], is_high(places, 2), send_y.at[d], keep_y.at[d])


def add_split(bits, places, *refs):
    for i, bit in enumerate(bits):
        keep, came = refs[2 * i : 2 * i + 2]
        send, left = refs[2 * (len(bits) + i) : 2 * (len(bits) + i) + 2]
        for d in range(keep.shape[0]):
            total = keep[d].astype(F32) + came[d].astype(F32)
            split_rows(total, is_high(places, bit), send.at[d], left.at[d])


def add_parts(places, keep_a, came_a, keep_b, came_b, send, keep):
    rows = keep_a.shape[1]
    for d in range(keep_a.shape[0]):
        out = (send if d % 2 else keep).at[d // 2]
        out[:rows] = (keep_a[d].astype(F32) + came_a[d].astype(F32)).astype(LOW)
        out[rows:] = (keep_b[d].astype(F32) + came_b[d].astype(F32)).astype(LOW)


def add_pair(places, keep, came, *outs):
    for i, out in enumerate(outs):
        out[...] = (keep[i].astype(F32) + came[i].astype(F32)).astype(LOW)


def add_two(places, keep, came, out):
    out[...] = (keep[...].astype(F32) + came[...].astype(F32)).astype(LOW)


def input_sum(places, rows, w, res1, out):
    heads, count, tokens = rows.shape
    total = dot_tn(rows[...].reshape(heads * count, tokens), w[...].reshape(heads * count, -1))
    out[...] = res1[...] + total


def place_pieces(places, held, full, layouts):
    near, core = places[0], places[1]
    width = held[0].shape[1]
    for off in range(4):
        chip = near ^ off
        mine, other = held[off][...], held[4 + off][...]
        sides = (jnp.where(core == 0, mine, other), jnp.where(core == 0, other, mine))
        for at, rows, start, outer in layouts:
            low_bit, high_bit = chip & 1, chip >> 1
            order = 2 * low_bit + high_bit if outer == 1 else 2 * high_bit + low_bit
            to = pl.multiple_of(start + order * rows, 16)
            for side in range(2):
                full[pl.ds(to, rows), side * width : (side + 1) * width] = sides[side][
                    at : at + rows
                ].astype(F32)


def ffn_place(places, *refs):
    held = [ref.at[off] for ref in refs[:2] for off in range(4)]
    down, up, full = refs[2:]
    rows = held[0].shape[0] // 2
    place_pieces(places, held, full, [(0, rows, 0, 1)])
    down[...] = full[...].T
    place_pieces(places, held, up, [(rows, rows, 0, 2)])


def collect(places, *refs):
    for off in range(4):
        refs[4][off] = refs[off][...]


def attn_place(places, *refs):
    held = [ref.at[off] for ref in refs[:2] for off in range(4)]
    qkv, w_out, small, up_bias, qv_bias, full = refs[2:]
    width = held[0].shape[1]
    count = w_out.shape[0]
    rows = count // 2
    more = held[0].shape[0] - rows
    place_pieces(places, held, full, [(0, rows, 0, 1), (rows, more, 4 * rows, 2)])
    for c in range(3):
        qkv[c] = full[c * count : (c + 1) * count]
    w_out[...] = full[3 * count : 4 * count]
    at = 4 * count
    lines = full[at : at + 16, :width] + full[at : at + 16, width:]
    for i in range(6):
        small[i : i + 1, :width] = lines[2 * i : 2 * i + 1]
        small[i : i + 1, width:] = lines[2 * i + 1 : 2 * i + 2]
    up_bias[...] = jnp.concatenate([lines[12:13], lines[13:14]], 1).reshape(2 * width)
    qv_bias[0:1] = lines[14:15, :count]
    qv_bias[1:2] = lines[14:15, count : 2 * count]


def bias_parts(values):
    rows, rest = [], values
    for _ in range(3):
        rows.append(lax.reduce_precision(rest, 8, 7))
        rest = rest - rows[-1]
    return jnp.stack(rows).astype(LOW)


def gather_back(piece):
    return [piece] + [swap(piece, "near", off) for off in range(1, 4)]


def per_device(
    tokens,
    segment_ids,
    w_qkv,
    b_qv,
    w_out,
    b_out,
    ln1_gain,
    ln1_bias,
    w_up,
    b_up,
    w_down,
    b_down,
    ln2_gain,
    ln2_bias,
    cotangent,
):
    CHAIN.clear()
    width = tokens.shape[1]
    own_rows = cotangent.shape[0]
    local_width = w_qkv.shape[2]
    heads = lax.axis_size("head")
    z = lax.axis_index("head")
    core = lax.axis_index("core")
    near = lax.axis_index("near")
    hidden_units = w_up.shape[1]
    chunk = hidden_units // heads
    half = width // 2
    rows3 = 3 * local_width
    places = jnp.stack([near, core, z]).astype(jnp.int32)

    shard = jnp.concatenate([w_qkv.transpose(0, 2, 1).reshape(rows3, width), w_out], 0)
    piece_rows = shard.shape[0] // 8
    bias = jnp.pad(bias_parts(b_qv.reshape(-1)), ((0, 13), (0, width - 2 * local_width)))
    piece = lax.dynamic_slice_in_dim(shard, (near * 2 + core) * piece_rows, piece_rows, 0)
    piece = jnp.concatenate([piece, bias], 0)
    first_hop = [swap(piece, "head", d) for d in range(1, heads)]

    seg = lax.dynamic_slice_in_dim(segment_ids, z * own_rows, own_rows, 0)
    segs = [(seg[None], whole((1, own_rows)))]
    tok_own = lax.dynamic_slice_in_dim(tokens, z * own_rows, own_rows, 0)
    own_tokens = (tok_own, whole((own_rows, width)))

    def attend_outs(first):
        def spec(*shape):
            return pl.BlockSpec((None,) + shape, lambda k, s: (k + first, 0, 0))

        return [
            ((heads, rows3, own_rows), LOW, spec(rows3, own_rows)),
            ((heads, local_width, own_rows), LOW, spec(local_width, own_rows)),
            ((heads, 8, own_rows), F32, spec(8, own_rows)),
            ((heads, rows3, width), LOW, spec(rows3, width)),
            ((heads, local_width, width), LOW, spec(local_width, width)),
        ]

    macs = rows3 * width * own_rows + 6 * own_rows * own_rows * 256
    ins = [own_tokens, (shard, whole(shard.shape)), (bias, whole(bias.shape))] + segs
    made = begun = run(own_attention, places, (1,), ins, attend_outs(0), macs=macs, chain=False)
    block = pl.BlockSpec((piece_rows, width), lambda k, s: (0, 0))
    orders = [(1, 2) if d % 2 else (2, 1) for d in range(heads)]
    nexts = [swap(first_hop[d - 1], "near", orders[d][0]) for d in range(1, heads)]
    for d in range(1, heads):
        order = orders[d]
        ins = [(first_hop[d - 1], block), (nexts[d - 1], block)]
        twice = (2, piece_rows, width)
        (pair,) = run(
            pair_rows, places, (1,), ins, [(twice, LOW, whole(twice))],
            after=nexts + [begun[2]], weight=LIGHT, chain=False,
        )
        rest = swap(pair, "near", order[1])
        held = [pair, rest, swap_core(pair), swap_core(rest)]
        ins = [own_tokens] + [(h, whole(h.shape)) for h in held]
        ins += [(first_hop[d - 1], pl.BlockSpec((16, width), lambda k, s: (piece_rows // 16, 0)))]
        kernel = functools.partial(far_attention, order)
        made = run(
            kernel, places, (1,), ins + segs, attend_outs(d), [pltpu.VMEM((rows3 + local_width, width), LOW)], macs, alias=made,
            chain=False, weight=100,
        )
    qkvs, mixes, logs, w_qkvs, w_outs = made

    mixes_far = swap_core(mixes)

    def by_step(*shape):
        block = (None,) + shape
        return pl.BlockSpec(block, lambda k, s: (jnp.minimum(k, heads - 1),) + (0,) * len(shape))

    def unit_at(k, s):
        return s[2] ^ jnp.minimum(k, heads - 1)


    line = whole((width,))
    square = (own_rows, width)
    tile = by_step(own_rows, half)
    tiles = (heads, own_rows, half)
    up_block = (w_up, pl.BlockSpec((width, chunk), lambda k, s: (0, unit_at(k, s))))
    line_block = pl.BlockSpec((None, 1, chunk), lambda k, s: (unit_at(k, s), 0, 0))

    ins = [
        own_tokens,
        (mixes, whole(mixes.shape)),
        (w_outs, whole(w_outs.shape)),
        (b_out, line),
        (ln1_gain, line),
        (ln1_bias, line),
        (b_down, line),
        (ln2_gain, line),
        (ln2_bias, line),
        up_block,
        (b_up.reshape(heads, 1, chunk), line_block),
        (w_down, pl.BlockSpec(memory_space=pltpu.HBM)),
        (cotangent, whole(square)),
    ]
    outs = [
        (tiles, LOW, tile),
        (tiles, LOW, tile),
        ((4, own_rows, half), LOW, whole((4, own_rows, half))),
        ((heads, own_rows, chunk), LOW, by_step(own_rows, chunk)),
        (square, F32, whole(square)),
        ((own_rows, 1), F32, whole((own_rows, 1))),
        (square, F32, whole(square)),
        (square, LOW, whole(square)),
        ((8, width), F32, whole((8, width))),
        ((own_rows, half), LOW, whole((own_rows, half))),
    ]
    scratch = [
        pltpu.VMEM(square, F32),
        pltpu.VMEM(square, LOW),
        pltpu.VMEM((own_rows, hidden_units), LOW),
        pltpu.VMEM(w_down.shape, LOW),
        pltpu.SemaphoreType.DMA,
    ]
    ffn_macs = 2 * own_rows * width * hidden_units
    act_send, act_own, ends, slope, unit1, inv1, res2, layer_output, small_two, tok_send = run(
        feed_forward, places, (heads + 1,), ins, outs, scratch, ffn_macs
    )
    tok_far = swap_core(tok_send)
    act_far = swap_core(act_send)
    ends_far = swap_core(ends)

    def two_of(array, index):
        return (array, pl.BlockSpec((2, own_rows, half), lambda k, s: (index, 0, 0)))

    ins = [
        two_of(ends, 1),
        (w_down, pl.BlockSpec(memory_space=pltpu.HBM)),
        (slope, by_step(own_rows, chunk)),
    ]
    outs = [(tiles, LOW, tile), (tiles, LOW, tile), ((heads, 1, chunk), F32, line_block)]
    scratch = [
        pltpu.VMEM(square, LOW),
        pltpu.VMEM((own_rows, chunk), LOW),
        pltpu.VMEM((heads, chunk, width), LOW),
        pltpu.SemaphoreType.DMA((heads,)),
    ]
    inner_send, inner_own, up_bias = run(
        inner_back, places, (heads,), ins, outs, scratch, ffn_macs // 2,
        after=[mixes_far],
    )
    inner_far = swap_core(inner_send)


    def ffn_unit(bit, own, far, which, weight):
        outs = [((heads, half, half), LOW)] * 2
        both = [pltpu.VMEM((width, 2 * own_rows), LOW)]
        kernel = functools.partial(ffn_grad, bit, which)
        ins = [own, far, ends, ends_far]
        return run_whole(kernel, places, ins, outs, both, ffn_macs // 2, weight=weight)

    made = ffn_unit(1, act_own, act_far, 1, 8) + ffn_unit(2, inner_own, inner_far, 0, LIGHT)
    x_send, x_keep, y_send, y_keep = made
    ffn_held = (x_keep, swap(x_send, "near", 1), y_keep, swap(y_send, "near", 2))

    ins = [
        (inner_own, tile),
        (inner_send, tile),
        up_block,
        (res2, whole(square)),
        (unit1, whole(square)),
        (inv1, whole((own_rows, 1))),
        (ln1_gain, line),
    ]
    outs = [
        ((own_rows, half), LOW, whole((own_rows, half))),
        (square, F32, whole(square)),
        (square, LOW, whole(square)),
        ((8, width), F32, whole((8, width))),
    ]
    grad_send, res1, grad_attended, small_one = run(
        hidden_back, places, (heads,), ins, outs, [pltpu.VMEM(square, F32)], ffn_macs // 2,
        weight=LIGHT,
    )
    grad_far = swap_core(grad_send)

    def second(x_keep, x_came, y_keep, y_came, macs=0):
        arrays = (x_keep, x_came, y_keep, y_came)
        shapes = [(heads, a.shape[1] // 2, half) for a in (x_keep, x_keep, y_keep, y_keep)]
        outs = [(shape, LOW) for shape in shapes]
        kernel = functools.partial(add_split, (2, 1))
        return run_whole(kernel, places, arrays, outs, macs=macs)

    def third(x_keep, x_came, y_keep, y_came):
        arrays = (x_keep, x_came, y_keep, y_came)
        shape = (heads // 2, x_keep.shape[1] + y_keep.shape[1], half)
        send, keep = run_whole(add_parts, places, arrays, [(shape, LOW)] * 2)
        return keep, swap(send, "head", 1)

    def fourth(keep, came):
        shape = keep.shape[1:]
        mine, other = run_whole(add_pair, places, [keep, came], [(shape, LOW)] * 2)
        return mine, swap(other, "head", 2)

    def fifth(mine, came):
        (total,) = run_whole(add_two, places, [mine, came], [(mine.shape, LOW)])
        bit = 1
        while bit < lax.axis_size("far"):
            total = (total.astype(F32) + swap(total, "far", bit).astype(F32)).astype(LOW)
            bit *= 2
        return total

    def cross(made, flip):
        x_send, x_keep, y_send, y_keep = made
        x_bit, y_bit = (2, 1) if flip else (1, 2)
        return x_keep, swap(x_send, "near", x_bit), y_keep, swap(y_send, "near", y_bit)

    outs = [((heads, rows3, own_rows), LOW), ((heads, 8, rows3), F32)]
    ins = [qkvs, w_outs, grad_attended, logs, seg[None]]
    rows, qkv_bias = run_whole(attention_back, places, ins, outs)
    rows_far = swap_core(rows)

    outs = [(square, F32, whole(square))]
    ins = [(a, whole(a.shape)) for a in (rows, w_qkvs, res1)]
    (input_grad,) = run(input_sum, places, (1,), ins, outs, weight=LIGHT)
    ffn_held = cross(second(*ffn_held, ffn_macs), True)
    ins = [
        rows, rows_far, tok_own, tok_far, mixes, mixes_far, grad_attended, grad_far,
        small_one, small_two, up_bias, qkv_bias,
    ]
    outs = [
        ((heads, r, half), LOW) for r in (half // 2, (half + EXTRA) // 2) for _ in range(2)
    ]
    made = run_whole(attn_grad, places, ins, outs)
    attn_held = cross(made, False)

    ffn_held = third(*ffn_held)
    attn_held = cross(second(*attn_held), True)
    ffn_held = fourth(*ffn_held)
    attn_held = third(*attn_held)
    ffn_held = gather_back(fifth(*ffn_held))
    attn_held = fourth(*attn_held)
    attn_held = gather_back(fifth(*attn_held))

    def both_cores(held):
        shape = (heads,) + held[0].shape
        (pieces,) = run_whole(collect, places, held, [(shape, LOW)])
        return [(a, whole(shape)) for a in (pieces, swap_core(pieces))]

    ffn_held = both_cores(ffn_held)
    outs = [(shape, F32, whole(shape)) for shape in ((chunk, width), (width, chunk))]
    grad_down, grad_up = run(
        ffn_place, places, (1,), ffn_held, outs, [pltpu.VMEM((width, chunk), F32)]
    )
    attn_held = both_cores(attn_held)
    shapes = [
        (3, local_width, width),
        (local_width, width),
        (6, width),
        (chunk,),
        (2, local_width),
    ]
    grad_qkv, grad_out, grad_small, grad_up_bias, grad_qv_bias = run(
        attn_place,
        places,
        (1,),
        attn_held,
        [(shape, F32, whole(shape)) for shape in shapes],
        [pltpu.VMEM((width + EXTRA, width), F32)],
    )
    return (
        layer_output,
        input_grad,
        grad_qkv.transpose(0, 2, 1),
        grad_qv_bias,
        grad_out,
        grad_up,
        grad_up_bias,
        grad_down,
        grad_small,
    )


def solution(mesh):
    batch, heads = mesh.devices.shape
    mesh = Mesh(
        mesh.devices.reshape(batch // 8, 4, 2, heads), ("far", "near", "core", "head")
    )
    group = ("far", "near", "core")
    everyone = group + ("head",)
    in_specs = (
        P(group, None),
        P(group),
        P(None, None, "head"),
        P(None, "head"),
        P("head", None),
        P(),
        P(),
        P(),
        P(),
        P(),
        P(),
        P(),
        P(),
        P(),
        P(everyone, None),
    )
    out_specs = (
        P(everyone, None),
        P(everyone, None),
        P(None, None, "head"),
        P(None, "head"),
        P("head", None),
        P(None, "head"),
        P("head"),
        P("head", None),
        P(),
    )
    return jax.shard_map(
        per_device, mesh=mesh, in_specs=in_specs, out_specs=out_specs, check_vma=False
    )
```

```python
import functools
import math

import jax
import jax.numpy as jnp
from jax import lax
from jax.experimental import pallas as pl
from jax.experimental.pallas import tpu as pltpu
from jax.sharding import Mesh
from jax.sharding import PartitionSpec as P

HEAD_DIM = 64
SLOT = 512
LOW = jnp.bfloat16
F32 = jnp.float32
LOG2E = math.log2(math.e)
SCORE_SCALE = HEAD_DIM ** (-0.5) * LOG2E
SPARE_BYTES = 12 * 2**20
EXTRA = 64
LIGHT = 0.01
LANES = 128
CHAIN = []
TAIL_SLOPE = 0.36
TAIL = (
    0.14371304537508633,
    0.14177245466203425,
    0.1397192603907239,
    0.026549325413860486,
    0.18095403134327948,
    -0.1797647161697652,
    0.047056295581175855,
)


def swap(value, axis, bit):
    size = lax.axis_size(axis)
    return lax.ppermute(value, axis, [(i, i ^ bit) for i in range(size)])


def swap_core(value):
    return swap(value, "core", 1)


def dot(a, b):
    return jnp.dot(a, b, preferred_element_type=F32)


def dot_nt(a, b):
    return lax.dot_general(a, b, (((1,), (1,)), ((), ())), preferred_element_type=F32)


def dot_tn(a, b):
    return lax.dot_general(a, b, (((0,), (0,)), ((), ())), preferred_element_type=F32)


def whole(shape):
    return pl.BlockSpec(shape, lambda *args: (0,) * len(shape), pipeline_mode=pl.Buffered(1))


def run(
    kernel, places, grid, ins, outs, scratch=(), macs=0, after=(), alias=(), weight=8, chain=True
):
    moved = sum(a.size * a.dtype.itemsize for a, spec in ins)
    moved += sum(math.prod(shape) * jnp.dtype(kind).itemsize for shape, kind, spec in outs)
    after = list(after) + (CHAIN if chain else [])
    count, unread = len(ins), len(alias) + len(after)
    results = len(outs)
    flag = (8, 128)
    if chain:
        outs = outs + [(flag, F32, whole(flag))]

    def body(places, *refs):
        made = refs[count + unread :]
        if chain:

            @pl.when(pl.program_id(0) == 0)
            def _():
                made[results][...] = jnp.zeros(flag, F32)

        kernel(places, *refs[:count], *made[:results], *made[len(outs) :])

    held = pl.BlockSpec(memory_space=pl.ANY)
    room = SPARE_BYTES
    for shape, kind, spec in outs + [(a.shape, a.dtype, spec) for a, spec in ins]:
        if spec.block_shape is not None:
            block = math.prod(1 if n is None else n for n in spec.block_shape)
            copies = 2 if spec.pipeline_mode is None else 1
            room += copies * block * jnp.dtype(kind).itemsize
    for ref in scratch:
        if hasattr(ref, "shape") and ref.dtype in (LOW, F32):
            room += math.prod(ref.shape) * jnp.dtype(ref.dtype).itemsize
    made = pl.pallas_call(
        body,
        name=getattr(kernel, "func", kernel).__name__,
        grid_spec=pltpu.PrefetchScalarGridSpec(
            num_scalar_prefetch=1,
            grid=grid,
            in_specs=[spec for a, spec in ins] + [held] * unread,
            out_specs=[spec for shape, kind, spec in outs],
            scratch_shapes=list(scratch),
        ),
        out_shape=[jax.ShapeDtypeStruct(shape, kind) for shape, kind, spec in outs],
        input_output_aliases={1 + count + i: i for i in range(len(alias))},
        compiler_params=pltpu.CompilerParams(vmem_limit_bytes=room),
        cost_estimate=pl.CostEstimate(
            flops=int(2 * macs * weight), bytes_accessed=int(moved * weight), transcendentals=0
        ),
    )(places, *[a for a, spec in ins], *alias, *after)
    if chain:
        CHAIN[:] = made[results:]
    return made[:results]


def run_whole(
    kernel, places, ins, outs, scratch=(), macs=0, after=(), alias=(), weight=8, chain=True
):
    pairs = [a if isinstance(a, tuple) else (a, pltpu.VMEM) for a in ins]
    after = list(after) + (CHAIN if chain else [])
    count, unread, results = len(pairs), len(alias) + len(after), len(outs)
    if chain:
        outs = outs + [((8, 128), F32)]

    def body(places, *refs):
        made = refs[count + unread :]
        if chain:
            made[results][...] = jnp.zeros((8, 128), F32)
        kernel(places, *refs[:count], *made[:results], *made[len(outs) :])

    room = SPARE_BYTES
    for ref in scratch:
        if hasattr(ref, "shape") and ref.dtype in (LOW, F32):
            room += math.prod(ref.shape) * jnp.dtype(ref.dtype).itemsize
    spaces = [pltpu.SMEM] + [space for a, space in pairs]
    spaces += [pltpu.VMEM] * len(alias) + [pl.ANY] * len(after)
    made = pl.pallas_call(
        body,
        name=getattr(kernel, "func", kernel).__name__,
        in_specs=[pl.BlockSpec(memory_space=space) for space in spaces],
        out_specs=[pl.BlockSpec(memory_space=pltpu.VMEM)] * len(outs),
        scratch_shapes=list(scratch),
        out_shape=[jax.ShapeDtypeStruct(shape, kind) for shape, kind in outs],
        input_output_aliases={1 + count + i: i for i in range(len(alias))},
        compiler_params=pltpu.CompilerParams(vmem_limit_bytes=room),
        cost_estimate=pl.CostEstimate(
            flops=int(2 * macs * weight), bytes_accessed=0, transcendentals=0
        ),
    )(places, *[a for a, space in pairs], *alias, *after)
    if chain:
        CHAIN[:] = made[results:]
    return made[:results]


def tiles_of(count, size):
    return [slice(at, at + size) for at in range(0, count, size)]


def three_parts(values):
    parts, rest = [], values
    for _ in range(3):
        parts.append(rest.astype(LOW))
        rest = rest - parts[-1].astype(F32)
    return parts


def segment_rows(seg_row):
    shape = (16, seg_row.shape[1])
    place = lax.broadcasted_iota(jnp.int32, shape, 0)
    same = place - 1 == seg_row
    keys = jnp.where(same, 1.0, jnp.where((place >= 8) & (place < 11), 1.0, 0.0))
    queries = jnp.where(same | (place > 4), 0.0, -1e30)
    return keys.astype(LOW), queries.astype(LOW)


def attend_heads(tok, w_rows, bias, seg_row, qkv_ref, mix_ref, log_ref):
    width = w_rows.shape[0] // 3
    added = dot_tn(bias[:, : 2 * width], jnp.ones((bias.shape[0], tok.shape[0]), LOW))
    qkv = dot_nt(w_rows, tok)
    parts = (
        (qkv[:width] + added[:width]).astype(LOW),
        qkv[width : 2 * width].astype(LOW),
        (qkv[2 * width :] + added[width:]).astype(LOW),
    )
    for c in range(3):
        qkv_ref[c * width : (c + 1) * width] = parts[c]
    more_k, more_q = segment_rows(seg_row)
    for head in range(width // HEAD_DIM):
        q, k, v = (part[head * HEAD_DIM : (head + 1) * HEAD_DIM] for part in parts)
        scores = dot_tn(jnp.concatenate([k, more_k], 0), jnp.concatenate([q, more_q], 0))
        columns, tops, totals = [], [], []
        for tile in tiles_of(scores.shape[1], LANES):
            top = jnp.max(scores[:, tile], 0, keepdims=True)
            total, column = 0.0, []
            for rows in tiles_of(scores.shape[0], 64):
                exponent = jnp.exp2((scores[rows, tile] - top) * SCORE_SCALE)
                total = total + jnp.sum(exponent, 0, keepdims=True)
                column.append(exponent.astype(LOW))
            columns.append(jnp.concatenate(column, 0))
            tops.append(top)
            totals.append(total)
        total = jnp.concatenate(totals, 1)
        mixed = dot(v, jnp.concatenate(columns, 1)) * (1.0 / total)
        mix_ref[head * HEAD_DIM : (head + 1) * HEAD_DIM] = mixed.astype(LOW)
        top = jnp.concatenate(tops, 1)
        log_ref[head : head + 1] = top + jnp.log2(total) * (1.0 / SCORE_SCALE)


def own_attention(
    places, tok, w, bias, seg_row, qkv_ref, mix_ref, log_ref, w_qkv, w_out
):
    count = qkv_ref.shape[1]
    w_qkv[0] = w[:count]
    w_out[0] = w[count:]
    attend_heads(
        tok[...], w[:count], bias[...], seg_row[...], qkv_ref.at[0], mix_ref.at[0], log_ref.at[0]
    )


def far_attention(
    d, order, places, tok, pair, rest, pair_far, rest_far, hop, seg_row,
    qkv_ref, mix_ref, log_ref, w_qkv, w_out, w_ref,
):
    first, second = order
    rows, count = pair.shape[1], qkv_ref.shape[1]
    me = places[0] * 2 + places[1]
    for other, held in enumerate(((pair, rest), (pair_far, rest_far))):
        for two, block in enumerate(held):
            for one in range(2):
                owner = me ^ (other + 2 * first * one + 2 * second * two)
                w_ref[pl.ds(pl.multiple_of(owner * rows, rows), rows)] = block[one]
    w_qkv[d] = w_ref[:count]
    w_out[d] = w_ref[count:]
    attend_heads(
        tok[...],
        w_ref[:count],
        hop[rows:],
        seg_row[...],
        qkv_ref.at[d],
        mix_ref.at[d],
        log_ref.at[d],
    )


def pair_rows(places, first, second, out):
    out[0] = first[: out.shape[1]]
    out[1] = second[: out.shape[1]]


def norm_stats(v):
    centred = v - jnp.mean(v, -1, keepdims=True)
    inv = lax.rsqrt(jnp.mean(centred * centred, -1, keepdims=True) + 1e-05)
    return centred * inv, inv


def norm_back(upstream, unit, inv, gain):
    scaled = upstream * gain
    inner = jnp.mean(scaled * unit, -1, keepdims=True)
    return inv * (scaled - jnp.mean(scaled, -1, keepdims=True) - unit * inner)


def gelu_both(pre):
    power = jnp.exp2(pre * pre * (-0.5 * LOG2E))
    base = 1.0 + TAIL_SLOPE * jnp.abs(pre)
    t = pl.reciprocal(base, approx=True)
    tail = TAIL[6] * t + TAIL[5]
    for c in TAIL[4::-1]:
        tail = tail * t + c
    tail = tail * (t * power)
    cumul = jnp.where(pre < 0.0, tail, 1.0 - tail)
    return (pre * cumul).astype(LOW), cumul + pre * (power * 0.3989422804014327)


def share(core, wide, mine, other):
    half = wide.shape[1] // 2
    left, right = wide[:, :half], wide[:, half:]
    mine[...] = jnp.where(core == 0, left, right)
    other[...] = jnp.where(core == 0, right, left)


def feed_forward(
    places, tok, mix, w_out, b_out, gain1, shift1, b_down, gain2, shift2, w_up, b_up, w_down, cot,
    send, own, ends, slope, unit1, inv1, res2, out, small, tok_send,
    hidden, low, acts,
):
    heads, width, half = mix.shape[0], low.shape[1], send.shape[2]
    chunk = 2 * half
    core, z = places[1], places[2]
    b_out, gain1, shift1, b_down, gain2, shift2, b_up = (
        ref[...].reshape(1, -1) for ref in (b_out, gain1, shift1, b_down, gain2, shift2, b_up)
    )
    tok_send[...] = jnp.where(core == 0, tok[:, half:], tok[:, :half])
    attended = dot_tn(mix[...].reshape(width, low.shape[0]), w_out[...].reshape(width, width))
    for rows in tiles_of(low.shape[0], 32):
        unit, inv = norm_stats(tok[rows].astype(F32) + (attended[rows] + b_out))
        unit1[rows] = unit
        inv1[rows] = inv
        one = unit * gain1 + shift1
        hidden[rows] = one
        one_low = one.astype(LOW)
        low[rows] = one_low
        ends[0, rows] = one_low[:, :half]
        ends[1, rows] = one_low[:, half:]
    for h in range(heads):
        for at in tiles_of(chunk, 256):
            wide = slice(h * chunk + at.start, h * chunk + at.stop)
            pre = dot(low[...], w_up[:, wide])
            for rows in tiles_of(pre.shape[0], 32):
                act, tilt = gelu_both(pre[rows] + b_up[:, wide])
                slope[h, rows, at] = tilt.astype(LOW)
                acts[rows, wide] = act
        share(core, acts.at[:, h * chunk : (h + 1) * chunk], own.at[z ^ h], send.at[z ^ h])
    branch = dot(acts[...], w_down[...])
    sums = [0.0] * 3
    for rows in tiles_of(branch.shape[0], 32):
        unit, inv = norm_stats(hidden[rows] + (branch[rows] + b_down))
        out[rows] = (unit * gain2 + shift2).astype(LOW)
        upstream = cot[rows].astype(F32)
        grad = norm_back(upstream, unit, inv, gain2)
        res2[rows] = grad
        grad_low = grad.astype(LOW)
        ends[2, rows] = grad_low[:, :half]
        ends[3, rows] = grad_low[:, half:]
        for i, term in enumerate((grad_low.astype(F32), upstream * unit, upstream)):
            sums[i] = sums[i] + jnp.sum(term, 0, keepdims=True)
    for i in range(3):
        small[i : i + 1] = sums[i]


def inner_back(places, ends, w_down, slope, send, own, bias, inners):
    heads, _, chunk = slope.shape
    core, z = places[1], places[2]
    branch = jnp.concatenate([ends[2], ends[3]], 1)
    for h in range(heads):
        for at in tiles_of(chunk, 256):
            grad_act = dot_nt(branch, w_down[h * chunk + at.start : h * chunk + at.stop])
            total = 0.0
            for rows in tiles_of(grad_act.shape[0], 32):
                inner = (grad_act[rows] * slope[h, rows, at].astype(F32)).astype(LOW)
                inners[rows, at] = inner
                total = total + jnp.sum(inner.astype(F32), 0, keepdims=True)
            bias[h, :, at] = total
        share(core, inners, own.at[z ^ h], send.at[z ^ h])


def hidden_back(places, own, sent, w_up, res2, unit1, inv1, gain1, send, res1, low, small):
    heads, count, half = own.shape
    core, z = places[1], places[2]
    sides = []
    for h in range(heads):
        mine, other = own[z ^ h], sent[z ^ h]
        sides += [jnp.where(core == 0, mine, other), jnp.where(core == 0, other, mine)]
    product = dot_nt(jnp.concatenate(sides, 1), w_up[...])
    gain = gain1[...].reshape(1, -1)
    sums = [0.0] * 3
    for rows in tiles_of(count, 32):
        grad, unit = product[rows] + res2[rows], unit1[rows]
        result = norm_back(grad, unit, inv1[rows], gain)
        res1[rows] = result
        result_low = result.astype(LOW)
        low[rows] = result_low
        send[rows] = jnp.where(core == 0, result_low[:, half:], result_low[:, :half])
        for i, term in enumerate((result_low.astype(F32), grad * unit, grad)):
            sums[i] = sums[i] + jnp.sum(term, 0, keepdims=True)
    for i in range(3):
        small[i : i + 1] = sums[i]


def shard_back(qkv, w_out, grad, log_ref, more_k, more_q, rows_ref, bias_ref):
    width = qkv.shape[0] // 3
    grad_mixed = dot_nt(w_out[...], grad[...]).astype(LOW)
    scale = HEAD_DIM ** (-0.5)
    for head in range(width // HEAD_DIM):
        places_of = [c * width + head * HEAD_DIM for c in range(3)]
        q, k, v = (qkv[at : at + HEAD_DIM] for at in places_of)
        g = grad_mixed[head * HEAD_DIM : (head + 1) * HEAD_DIM]
        logs = jnp.concatenate(three_parts(-log_ref[head : head + 1]), 0)
        with_logs = jnp.concatenate([more_q[:8], logs, more_q[11:]], 0)
        scores = dot_tn(jnp.concatenate([k, more_k], 0), jnp.concatenate([q, with_logs], 0))
        grad_probs = dot_tn(v, g)
        attends, grads = [], []
        for tile in tiles_of(scores.shape[1], LANES):
            inner, kept, lows, parts = 0.0, [], [], []
            tall = tiles_of(scores.shape[0], 64)
            for down in tall:
                attend = jnp.exp2(scores[down, tile] * SCORE_SCALE)
                inner = inner + jnp.sum(attend * grad_probs[down, tile], 0, keepdims=True)
                kept.append(attend)
                lows.append(attend.astype(LOW))
            for down, attend in zip(tall, kept):
                parts.append((attend * (grad_probs[down, tile] - inner)).astype(LOW))
            attends.append(jnp.concatenate(lows, 0))
            grads.append(jnp.concatenate(parts, 0))
        attend_low = jnp.concatenate(attends, 1)
        grad_scores = jnp.concatenate(grads, 1)
        grad_v = dot_nt(g, attend_low)
        grad_q = dot(k, grad_scores) * scale
        grad_k = dot_nt(q, grad_scores) * scale
        for at, value in zip(places_of, (grad_q, grad_k, grad_v)):
            rows_ref[at : at + HEAD_DIM] = value.astype(LOW)
    ones = jnp.ones((8, rows_ref.shape[1]), LOW)
    bias_ref[...] = dot_nt(ones, rows_ref[...])


def attention_back(places, qkv, w_out, grad, log_ref, seg_row, rows_ref, bias_ref):
    more_k, more_q = segment_rows(seg_row[...])

    def shard(d, carry):
        refs = (ref.at[d] for ref in (rows_ref, bias_ref))
        shard_back(qkv.at[d], w_out.at[d], grad, log_ref.at[d], more_k, more_q, *refs)
        return carry

    lax.fori_loop(0, qkv.shape[0], shard, 0)


def split_rows(value, high, send, keep):
    rows = value.shape[0] // 2
    low = value.astype(LOW)
    send[...] = jnp.where(high, low[:rows], low[rows:])
    keep[...] = jnp.where(high, low[rows:], low[:rows])


def is_high(places, bit):
    return (places[0] & bit) != 0


def ffn_grad(bit, which, places, units, units_far, ends, ends_far, send, keep, both):
    half, count = ends.shape[2], ends.shape[1]
    for side in range(2):
        rows = slice(side * half, (side + 1) * half)
        both[rows, :count] = ends[2 * which + side].T
        both[rows, count:] = ends_far[2 * which + side].T
    for d in range(0, units.shape[0], 2):
        left, right = (jnp.concatenate([units[d + i], units_far[d + i]], 0) for i in range(2))
        total = dot(both[...], jnp.concatenate([left, right], 1))
        for i in range(2):
            part = total[:, i * half : (i + 1) * half]
            split_rows(part, is_high(places, bit), send.at[d + i], keep.at[d + i])


def attn_grad(
    places, rows, rows_far, tok, tok_far, mix, mix_far, grad, grad_far,
    small_one, small_two, up_bias, qkv_bias, send_x, keep_x, send_y, keep_y,
):
    width = mix.shape[1]
    half = tok_far.shape[1]
    core, z = places[1], places[2]

    def both(near, far):
        mine = jnp.where(core == 0, near[:, :half], near[:, half:])
        return jnp.concatenate([mine, far[...]], 0)

    tok_both, grad_both = both(tok, tok_far), both(grad, grad_far)
    for d in range(rows.shape[0]):
        qkv = dot(jnp.concatenate([rows[d], rows_far[d]], 1), tok_both)
        out = dot(jnp.concatenate([mix[d], mix_far[d]], 1), grad_both)
        lines = []
        for held in (small_one, small_two):
            for i in range(3):
                lines += [held[i : i + 1, :half], held[i : i + 1, half:]]
        line, bias = up_bias[z ^ d], qkv_bias[d]
        lines += [line[:, :half], line[:, half:]]
        lines.append(jnp.concatenate([bias[0:1, :width], bias[0:1, 2 * width :]], 1))
        lines.append(jnp.zeros((EXTRA - len(lines), half), F32))
        total = jnp.concatenate([qkv, out] + lines, 0)
        split_rows(total[:half], is_high(places, 1), send_x.at[d], keep_x.at[d])
        split_rows(total[half:], is_high(places, 2), send_y.at[d], keep_y.at[d])


def add_split(bits, places, *refs):
    for i, bit in enumerate(bits):
        keep, came = refs[2 * i : 2 * i + 2]
        send, left = refs[2 * (len(bits) + i) : 2 * (len(bits) + i) + 2]
        for d in range(keep.shape[0]):
            total = keep[d].astype(F32) + came[d].astype(F32)
            split_rows(total, is_high(places, bit), send.at[d], left.at[d])


def add_parts(places, keep_a, came_a, keep_b, came_b, send, keep):
    rows = keep_a.shape[1]
    for d in range(keep_a.shape[0]):
        out = (send if d % 2 else keep).at[d // 2]
        out[:rows] = (keep_a[d].astype(F32) + came_a[d].astype(F32)).astype(LOW)
        out[rows:] = (keep_b[d].astype(F32) + came_b[d].astype(F32)).astype(LOW)


def add_pair(places, keep, came, *outs):
    for i, out in enumerate(outs):
        out[...] = (keep[i].astype(F32) + came[i].astype(F32)).astype(LOW)


def add_two(places, keep, came, out):
    out[...] = (keep[...].astype(F32) + came[...].astype(F32)).astype(LOW)


def input_sum(places, rows, w, res1, out):
    heads, count, tokens = rows.shape
    total = dot_tn(rows[...].reshape(heads * count, tokens), w[...].reshape(heads * count, -1))
    out[...] = res1[...] + total


def place_pieces(places, held, full, layouts):
    near, core = places[0], places[1]
    width = held[0].shape[1]
    for off in range(4):
        chip = near ^ off
        mine, other = held[off][...], held[4 + off][...]
        sides = (jnp.where(core == 0, mine, other), jnp.where(core == 0, other, mine))
        for at, rows, start, outer in layouts:
            low_bit, high_bit = chip & 1, chip >> 1
            order = 2 * low_bit + high_bit if outer == 1 else 2 * high_bit + low_bit
            to = pl.multiple_of(start + order * rows, 16)
            for side in range(2):
                full[pl.ds(to, rows), side * width : (side + 1) * width] = sides[side][
                    at : at + rows
                ].astype(F32)


def ffn_place(places, *refs):
    held = [ref.at[off] for ref in refs[:2] for off in range(4)]
    down, up, full = refs[2:]
    rows = held[0].shape[0] // 2
    place_pieces(places, held, full, [(0, rows, 0, 1)])
    down[...] = full[...].T
    place_pieces(places, held, up, [(rows, rows, 0, 2)])


def collect(places, *refs):
    for off in range(4):
        refs[4][off] = refs[off][...]


def attn_place(places, *refs):
    held = [ref.at[off] for ref in refs[:2] for off in range(4)]
    qkv, w_out, small, up_bias, qv_bias, full = refs[2:]
    width = held[0].shape[1]
    count = w_out.shape[0]
    rows = count // 2
    more = held[0].shape[0] - rows
    place_pieces(places, held, full, [(0, rows, 0, 1), (rows, more, 4 * rows, 2)])
    for c in range(3):
        qkv[c] = full[c * count : (c + 1) * count]
    w_out[...] = full[3 * count : 4 * count]
    at = 4 * count
    lines = full[at : at + 16, :width] + full[at : at + 16, width:]
    for i in range(6):
        small[i : i + 1, :width] = lines[2 * i : 2 * i + 1]
        small[i : i + 1, width:] = lines[2 * i + 1 : 2 * i + 2]
    up_bias[...] = jnp.concatenate([lines[12:13], lines[13:14]], 1).reshape(2 * width)
    qv_bias[0:1] = lines[14:15, :count]
    qv_bias[1:2] = lines[14:15, count : 2 * count]


def bias_parts(values):
    rows, rest = [], values
    for _ in range(3):
        rows.append(lax.reduce_precision(rest, 8, 7))
        rest = rest - rows[-1]
    return jnp.stack(rows).astype(LOW)


def gather_back(piece):
    return [piece] + [swap(piece, "near", off) for off in range(1, 4)]


def per_device(
    tokens,
    segment_ids,
    w_qkv,
    b_qv,
    w_out,
    b_out,
    ln1_gain,
    ln1_bias,
    w_up,
    b_up,
    w_down,
    b_down,
    ln2_gain,
    ln2_bias,
    cotangent,
):
    CHAIN.clear()
    width = tokens.shape[1]
    own_rows = cotangent.shape[0]
    local_width = w_qkv.shape[2]
    heads = lax.axis_size("head")
    z = lax.axis_index("head")
    core = lax.axis_index("core")
    near = lax.axis_index("near")
    hidden_units = w_up.shape[1]
    chunk = hidden_units // heads
    half = width // 2
    rows3 = 3 * local_width
    places = jnp.stack([near, core, z]).astype(jnp.int32)

    shard = jnp.concatenate([w_qkv.transpose(0, 2, 1).reshape(rows3, width), w_out], 0)
    piece_rows = shard.shape[0] // 8
    bias = jnp.pad(bias_parts(b_qv.reshape(-1)), ((0, 13), (0, width - 2 * local_width)))
    piece = lax.dynamic_slice_in_dim(shard, (near * 2 + core) * piece_rows, piece_rows, 0)
    piece = jnp.concatenate([piece, bias], 0)
    first_hop = [swap(piece, "head", d) for d in range(1, heads)]

    seg = lax.dynamic_slice_in_dim(segment_ids, z * own_rows, own_rows, 0)
    tok_own = lax.dynamic_slice_in_dim(tokens, z * own_rows, own_rows, 0)
    attend_outs = [
        ((heads, rows3, own_rows), LOW),
        ((heads, local_width, own_rows), LOW),
        ((heads, 8, own_rows), F32),
        ((heads, rows3, width), LOW),
        ((heads, local_width, width), LOW),
    ]
    macs = rows3 * width * own_rows + 6 * own_rows * own_rows * 256
    ins = [tok_own, shard, bias, seg[None]]
    made = begun = run_whole(own_attention, places, ins, attend_outs, macs=macs, chain=False)
    orders = [(1, 2) if d % 2 else (2, 1) for d in range(heads)]
    nexts = [swap(first_hop[d - 1], "near", orders[d][0]) for d in range(1, heads)]
    for d in range(1, heads):
        (pair,) = run_whole(
            pair_rows, places, [first_hop[d - 1], nexts[d - 1]],
            [((2, piece_rows, width), LOW)], after=nexts + [begun[2]], chain=False,
        )
        rest = swap(pair, "near", orders[d][1])
        ins = [tok_own, pair, rest, swap_core(pair), swap_core(rest), first_hop[d - 1], seg[None]]
        made = run_whole(
            functools.partial(far_attention, d, orders[d]), places, ins, attend_outs,
            [pltpu.VMEM(shard.shape, LOW)], macs, alias=made, chain=False, weight=100,
        )
    qkvs, mixes, logs, w_qkvs, w_outs = made

    mixes_far = swap_core(mixes)

    square = (own_rows, width)
    tiles = (heads, own_rows, half)
    ins = [
        tok_own, mixes, w_outs, b_out, ln1_gain, ln1_bias, b_down, ln2_gain, ln2_bias,
        w_up, b_up, w_down, cotangent,
    ]
    outs = [
        (tiles, LOW),
        (tiles, LOW),
        ((4, own_rows, half), LOW),
        ((heads, own_rows, chunk), LOW),
        (square, F32),
        ((own_rows, 1), F32),
        (square, F32),
        (square, LOW),
        ((8, width), F32),
        ((own_rows, half), LOW),
    ]
    scratch = [
        pltpu.VMEM(square, F32),
        pltpu.VMEM(square, LOW),
        pltpu.VMEM((own_rows, hidden_units), LOW),
    ]
    ffn_macs = 2 * own_rows * width * hidden_units
    (
        act_send, act_own, ends, slope, unit1, inv1, res2, layer_output, small_two, tok_send,
    ) = run_whole(feed_forward, places, ins, outs, scratch, ffn_macs)
    tok_far = swap_core(tok_send)
    act_far = swap_core(act_send)
    ends_far = swap_core(ends)

    outs = [(tiles, LOW), (tiles, LOW), ((heads, 1, chunk), F32)]
    scratch = [pltpu.VMEM((own_rows, chunk), LOW)]
    inner_send, inner_own, up_bias = run_whole(
        inner_back, places, [ends, w_down, slope], outs, scratch, ffn_macs // 2, [mixes_far]
    )
    inner_far = swap_core(inner_send)


    def ffn_unit(bit, own, far, which, weight):
        outs = [((heads, half, half), LOW)] * 2
        both = [pltpu.VMEM((width, 2 * own_rows), LOW)]
        kernel = functools.partial(ffn_grad, bit, which)
        ins = [own, far, ends, ends_far]
        return run_whole(kernel, places, ins, outs, both, ffn_macs // 2, weight=weight)

    made = ffn_unit(1, act_own, act_far, 1, 8) + ffn_unit(2, inner_own, inner_far, 0, LIGHT)
    x_send, x_keep, y_send, y_keep = made
    ffn_held = (x_keep, swap(x_send, "near", 1), y_keep, swap(y_send, "near", 2))

    outs = [((own_rows, half), LOW), (square, F32), (square, LOW), ((8, width), F32)]
    ins = [inner_own, inner_send, w_up, res2, unit1, inv1, ln1_gain]
    grad_send, res1, grad_attended, small_one = run_whole(
        hidden_back, places, ins, outs, macs=ffn_macs // 2, weight=LIGHT
    )
    grad_far = swap_core(grad_send)

    def second(x_keep, x_came, y_keep, y_came, macs=0):
        arrays = (x_keep, x_came, y_keep, y_came)
        shapes = [(heads, a.shape[1] // 2, half) for a in (x_keep, x_keep, y_keep, y_keep)]
        outs = [(shape, LOW) for shape in shapes]
        kernel = functools.partial(add_split, (2, 1))
        return run_whole(kernel, places, arrays, outs, macs=macs)

    def third(x_keep, x_came, y_keep, y_came):
        arrays = (x_keep, x_came, y_keep, y_came)
        shape = (heads // 2, x_keep.shape[1] + y_keep.shape[1], half)
        send, keep = run_whole(add_parts, places, arrays, [(shape, LOW)] * 2)
        return keep, swap(send, "head", 1)

    def fourth(keep, came):
        shape = keep.shape[1:]
        mine, other = run_whole(add_pair, places, [keep, came], [(shape, LOW)] * 2)
        return mine, swap(other, "head", 2)

    def fifth(mine, came):
        (total,) = run_whole(add_two, places, [mine, came], [(mine.shape, LOW)])
        bit = 1
        while bit < lax.axis_size("far"):
            total = (total.astype(F32) + swap(total, "far", bit).astype(F32)).astype(LOW)
            bit *= 2
        return total

    def cross(made, flip):
        x_send, x_keep, y_send, y_keep = made
        x_bit, y_bit = (2, 1) if flip else (1, 2)
        return x_keep, swap(x_send, "near", x_bit), y_keep, swap(y_send, "near", y_bit)

    outs = [((heads, rows3, own_rows), LOW), ((heads, 8, rows3), F32)]
    ins = [qkvs, w_outs, grad_attended, logs, seg[None]]
    rows, qkv_bias = run_whole(attention_back, places, ins, outs)
    rows_far = swap_core(rows)

    outs = [(square, F32, whole(square))]
    ins = [(a, whole(a.shape)) for a in (rows, w_qkvs, res1)]
    (input_grad,) = run(input_sum, places, (1,), ins, outs, weight=LIGHT)
    ffn_held = cross(second(*ffn_held, ffn_macs), True)
    ins = [
        rows, rows_far, tok_own, tok_far, mixes, mixes_far, grad_attended, grad_far,
        small_one, small_two, up_bias, qkv_bias,
    ]
    outs = [
        ((heads, r, half), LOW) for r in (half // 2, (half + EXTRA) // 2) for _ in range(2)
    ]
    made = run_whole(attn_grad, places, ins, outs)
    attn_held = cross(made, False)

    ffn_held = third(*ffn_held)
    attn_held = cross(second(*attn_held), True)
    ffn_held = fourth(*ffn_held)
    attn_held = third(*attn_held)
    ffn_held = gather_back(fifth(*ffn_held))
    attn_held = fourth(*attn_held)
    attn_held = gather_back(fifth(*attn_held))

    def both_cores(held):
        shape = (heads,) + held[0].shape
        (pieces,) = run_whole(collect, places, held, [(shape, LOW)])
        return [(a, whole(shape)) for a in (pieces, swap_core(pieces))]

    ffn_held = both_cores(ffn_held)
    outs = [(shape, F32, whole(shape)) for shape in ((chunk, width), (width, chunk))]
    grad_down, grad_up = run(
        ffn_place, places, (1,), ffn_held, outs, [pltpu.VMEM((width, chunk), F32)]
    )
    attn_held = both_cores(attn_held)
    shapes = [
        (3, local_width, width),
        (local_width, width),
        (6, width),
        (chunk,),
        (2, local_width),
    ]
    grad_qkv, grad_out, grad_small, grad_up_bias, grad_qv_bias = run(
        attn_place,
        places,
        (1,),
        attn_held,
        [(shape, F32, whole(shape)) for shape in shapes],
        [pltpu.VMEM((width + EXTRA, width), F32)],
    )
    return (
        layer_output,
        input_grad,
        grad_qkv.transpose(0, 2, 1),
        grad_qv_bias,
        grad_out,
        grad_up,
        grad_up_bias,
        grad_down,
        grad_small,
    )


def solution(mesh):
    batch, heads = mesh.devices.shape
    mesh = Mesh(
        mesh.devices.reshape(batch // 8, 4, 2, heads), ("far", "near", "core", "head")
    )
    group = ("far", "near", "core")
    everyone = group + ("head",)
    in_specs = (
        P(group, None),
        P(group),
        P(None, None, "head"),
        P(None, "head"),
        P("head", None),
        P(),
        P(),
        P(),
        P(),
        P(),
        P(),
        P(),
        P(),
        P(),
        P(everyone, None),
    )
    out_specs = (
        P(everyone, None),
        P(everyone, None),
        P(None, None, "head"),
        P(None, "head"),
        P("head", None),
        P(None, "head"),
        P("head"),
        P("head", None),
        P(),
    )
    return jax.shard_map(
        per_device, mesh=mesh, in_specs=in_specs, out_specs=out_specs, check_vma=False
    )
```

```python
import functools
import math

import jax
import jax.numpy as jnp
from jax import lax
from jax.experimental import pallas as pl
from jax.experimental.pallas import tpu as pltpu
from jax.sharding import Mesh
from jax.sharding import PartitionSpec as P

HEAD_DIM = 64
SLOT = 512
LOW = jnp.bfloat16
F32 = jnp.float32
LOG2E = math.log2(math.e)
SCORE_SCALE = HEAD_DIM ** (-0.5) * LOG2E
SPARE_BYTES = 12 * 2**20
EXTRA = 64
LIGHT = 0.01
LANES = 128
CHAIN = []
TAIL_SLOPE = 0.36
TAIL = (
    0.14371304537508633,
    0.14177245466203425,
    0.1397192603907239,
    0.026549325413860486,
    0.18095403134327948,
    -0.1797647161697652,
    0.047056295581175855,
)


def swap(value, axis, bit):
    size = lax.axis_size(axis)
    return lax.ppermute(value, axis, [(i, i ^ bit) for i in range(size)])


def swap_core(value):
    return swap(value, "core", 1)


def dot(a, b):
    return jnp.dot(a, b, preferred_element_type=F32)


def dot_nt(a, b):
    return lax.dot_general(a, b, (((1,), (1,)), ((), ())), preferred_element_type=F32)


def dot_tn(a, b):
    return lax.dot_general(a, b, (((0,), (0,)), ((), ())), preferred_element_type=F32)


def whole(shape):
    return pl.BlockSpec(shape, lambda *args: (0,) * len(shape), pipeline_mode=pl.Buffered(1))


def run(
    kernel, places, grid, ins, outs, scratch=(), macs=0, after=(), alias=(), weight=8, chain=True
):
    moved = sum(a.size * a.dtype.itemsize for a, spec in ins)
    moved += sum(math.prod(shape) * jnp.dtype(kind).itemsize for shape, kind, spec in outs)
    after = list(after) + (CHAIN if chain else [])
    count, unread = len(ins), len(alias) + len(after)
    results = len(outs)
    flag = (8, 128)
    if chain:
        outs = outs + [(flag, F32, whole(flag))]

    def body(places, *refs):
        made = refs[count + unread :]
        if chain:

            @pl.when(pl.program_id(0) == 0)
            def _():
                made[results][...] = jnp.zeros(flag, F32)

        kernel(places, *refs[:count], *made[:results], *made[len(outs) :])

    held = pl.BlockSpec(memory_space=pl.ANY)
    room = SPARE_BYTES
    for shape, kind, spec in outs + [(a.shape, a.dtype, spec) for a, spec in ins]:
        if spec.block_shape is not None:
            block = math.prod(1 if n is None else n for n in spec.block_shape)
            copies = 2 if spec.pipeline_mode is None else 1
            room += copies * block * jnp.dtype(kind).itemsize
    for ref in scratch:
        if hasattr(ref, "shape") and ref.dtype in (LOW, F32):
            room += math.prod(ref.shape) * jnp.dtype(ref.dtype).itemsize
    made = pl.pallas_call(
        body,
        name=getattr(kernel, "func", kernel).__name__,
        grid_spec=pltpu.PrefetchScalarGridSpec(
            num_scalar_prefetch=1,
            grid=grid,
            in_specs=[spec for a, spec in ins] + [held] * unread,
            out_specs=[spec for shape, kind, spec in outs],
            scratch_shapes=list(scratch),
        ),
        out_shape=[jax.ShapeDtypeStruct(shape, kind) for shape, kind, spec in outs],
        input_output_aliases={1 + count + i: i for i in range(len(alias))},
        compiler_params=pltpu.CompilerParams(vmem_limit_bytes=room),
        cost_estimate=pl.CostEstimate(
            flops=int(2 * macs * weight), bytes_accessed=int(moved * weight), transcendentals=0
        ),
    )(places, *[a for a, spec in ins], *alias, *after)
    if chain:
        CHAIN[:] = made[results:]
    return made[:results]


def run_whole(
    kernel, places, ins, outs, scratch=(), macs=0, after=(), alias=(), weight=8, chain=True
):
    pairs = [a if isinstance(a, tuple) else (a, pltpu.VMEM) for a in ins]
    after = list(after) + (CHAIN if chain else [])
    count, unread, results = len(pairs), len(alias) + len(after), len(outs)
    if chain:
        outs = outs + [((8, 128), F32)]

    def body(places, *refs):
        made = refs[count + unread :]
        if chain:
            made[results][...] = jnp.zeros((8, 128), F32)
        kernel(places, *refs[:count], *made[:results], *made[len(outs) :])

    room = SPARE_BYTES
    for ref in scratch:
        if hasattr(ref, "shape") and ref.dtype in (LOW, F32):
            room += math.prod(ref.shape) * jnp.dtype(ref.dtype).itemsize
    spaces = [pltpu.SMEM] + [space for a, space in pairs]
    spaces += [pltpu.VMEM] * len(alias) + [pl.ANY] * len(after)
    made = pl.pallas_call(
        body,
        name=getattr(kernel, "func", kernel).__name__,
        in_specs=[pl.BlockSpec(memory_space=space) for space in spaces],
        out_specs=[pl.BlockSpec(memory_space=pltpu.VMEM)] * len(outs),
        scratch_shapes=list(scratch),
        out_shape=[jax.ShapeDtypeStruct(shape, kind) for shape, kind in outs],
        input_output_aliases={1 + count + i: i for i in range(len(alias))},
        compiler_params=pltpu.CompilerParams(vmem_limit_bytes=room),
        cost_estimate=pl.CostEstimate(
            flops=int(2 * macs * weight), bytes_accessed=0, transcendentals=0
        ),
    )(places, *[a for a, space in pairs], *alias, *after)
    if chain:
        CHAIN[:] = made[results:]
    return made[:results]


def each(count, size, body):
    def step(i, carry):
        body(pl.ds(pl.multiple_of(i * size, size), size))
        return carry

    lax.fori_loop(0, count // size, step, 0)


def tiles_of(count, size):
    return [slice(at, at + size) for at in range(0, count, size)]


def three_parts(values):
    parts, rest = [], values
    for _ in range(3):
        parts.append(rest.astype(LOW))
        rest = rest - parts[-1].astype(F32)
    return parts


def segment_rows(seg_row):
    shape = (16, seg_row.shape[1])
    place = lax.broadcasted_iota(jnp.int32, shape, 0)
    same = place - 1 == seg_row
    keys = jnp.where(same, 1.0, jnp.where((place >= 8) & (place < 11), 1.0, 0.0))
    queries = jnp.where(same | (place > 4), 0.0, -1e30)
    return keys.astype(LOW), queries.astype(LOW)


def attend_heads(tok, w_rows, bias, seg_row, qkv_ref, mix_ref, log_ref):
    width = w_rows.shape[0] // 3
    added = dot_tn(bias[:, : 2 * width], jnp.ones((bias.shape[0], tok.shape[0]), LOW))
    qkv = dot_nt(w_rows, tok)
    parts = (
        (qkv[:width] + added[:width]).astype(LOW),
        qkv[width : 2 * width].astype(LOW),
        (qkv[2 * width :] + added[width:]).astype(LOW),
    )
    for c in range(3):
        qkv_ref[c * width : (c + 1) * width] = parts[c]
    more_k, more_q = segment_rows(seg_row)

    def one_head(head, carry):
        def rows_of(c):
            start = pl.multiple_of(c * width + head * HEAD_DIM, HEAD_DIM)
            return qkv_ref[pl.ds(start, HEAD_DIM)]

        q, k, v = (rows_of(c) for c in range(3))
        scores = dot_tn(jnp.concatenate([k, more_k], 0), jnp.concatenate([q, more_q], 0))
        columns, tops, totals = [], [], []
        for tile in tiles_of(scores.shape[1], LANES):
            top = jnp.max(scores[:, tile], 0, keepdims=True)
            total, column = 0.0, []
            for rows in tiles_of(scores.shape[0], 64):
                exponent = jnp.exp2((scores[rows, tile] - top) * SCORE_SCALE)
                total = total + jnp.sum(exponent, 0, keepdims=True)
                column.append(exponent.astype(LOW))
            columns.append(jnp.concatenate(column, 0))
            tops.append(top)
            totals.append(total)
        total = jnp.concatenate(totals, 1)
        mixed = dot(v, jnp.concatenate(columns, 1)) * (1.0 / total)
        at = pl.ds(pl.multiple_of(head * HEAD_DIM, HEAD_DIM), HEAD_DIM)
        mix_ref[at] = mixed.astype(LOW)
        top = jnp.concatenate(tops, 1)
        log_ref[pl.ds(head, 1)] = top + jnp.log2(total) * (1.0 / SCORE_SCALE)
        return carry

    lax.fori_loop(0, width // HEAD_DIM, one_head, 0)


def own_attention(
    places, tok, w, bias, seg_row, qkv_ref, mix_ref, log_ref, w_qkv, w_out
):
    count = qkv_ref.shape[1]
    w_qkv[0] = w[:count]
    w_out[0] = w[count:]
    attend_heads(
        tok[...], w[:count], bias[...], seg_row[...], qkv_ref.at[0], mix_ref.at[0], log_ref.at[0]
    )


def far_attention(
    d, order, places, tok, pair, rest, pair_far, rest_far, hop, seg_row,
    qkv_ref, mix_ref, log_ref, w_qkv, w_out, w_ref,
):
    first, second = order
    rows, count = pair.shape[1], qkv_ref.shape[1]
    me = places[0] * 2 + places[1]
    for other, held in enumerate(((pair, rest), (pair_far, rest_far))):
        for two, block in enumerate(held):
            for one in range(2):
                owner = me ^ (other + 2 * first * one + 2 * second * two)
                w_ref[pl.ds(pl.multiple_of(owner * rows, rows), rows)] = block[one]
    w_qkv[d] = w_ref[:count]
    w_out[d] = w_ref[count:]
    attend_heads(
        tok[...],
        w_ref[:count],
        hop[rows:],
        seg_row[...],
        qkv_ref.at[d],
        mix_ref.at[d],
        log_ref.at[d],
    )


def pair_rows(places, first, second, out):
    out[0] = first[: out.shape[1]]
    out[1] = second[: out.shape[1]]


def norm_stats(v):
    centred = v - jnp.mean(v, -1, keepdims=True)
    inv = lax.rsqrt(jnp.mean(centred * centred, -1, keepdims=True) + 1e-05)
    return centred * inv, inv


def norm_back(upstream, unit, inv, gain):
    scaled = upstream * gain
    inner = jnp.mean(scaled * unit, -1, keepdims=True)
    return inv * (scaled - jnp.mean(scaled, -1, keepdims=True) - unit * inner)


def gelu_both(pre):
    power = jnp.exp2(pre * pre * (-0.5 * LOG2E))
    base = 1.0 + TAIL_SLOPE * jnp.abs(pre)
    t = pl.reciprocal(base, approx=True)
    tail = TAIL[6] * t + TAIL[5]
    for c in TAIL[4::-1]:
        tail = tail * t + c
    tail = tail * (t * power)
    cumul = jnp.where(pre < 0.0, tail, 1.0 - tail)
    return (pre * cumul).astype(LOW), cumul + pre * (power * 0.3989422804014327)


def share(core, wide, mine, other):
    half = wide.shape[1] // 2
    left, right = wide[:, :half], wide[:, half:]
    mine[...] = jnp.where(core == 0, left, right)
    other[...] = jnp.where(core == 0, right, left)


def feed_forward(
    places, tok, mix, w_out, b_out, gain1, shift1, b_down, gain2, shift2, w_up, b_up, w_down, cot,
    send, own, ends, slope, unit1, inv1, res2, out, small, tok_send,
    hidden, low, acts, total,
):
    heads, width, half = mix.shape[0], low.shape[1], send.shape[2]
    chunk = 2 * half
    core, z = places[1], places[2]
    b_out, gain1, shift1, b_down, gain2, shift2 = (
        ref[...].reshape(1, -1) for ref in (b_out, gain1, shift1, b_down, gain2, shift2)
    )
    tok_send[...] = jnp.where(core == 0, tok[:, half:], tok[:, :half])
    total[...] = dot_tn(mix[...].reshape(width, low.shape[0]), w_out[...].reshape(width, width))

    def first_norm(rows):
        unit, inv = norm_stats(tok[rows].astype(F32) + (total[rows] + b_out))
        unit1[rows] = unit
        inv1[rows] = inv
        one = unit * gain1 + shift1
        hidden[rows] = one
        one_low = one.astype(LOW)
        low[rows] = one_low
        ends[0, rows] = one_low[:, :half]
        ends[1, rows] = one_low[:, half:]

    each(low.shape[0], 64, first_norm)

    def one_unit(h, carry):
        start = pl.multiple_of(h * chunk, chunk)
        for at in tiles_of(chunk, 256):
            wide = pl.ds(pl.multiple_of(start + at.start, 256), 256)
            pre = dot(low[...], w_up[:, wide])
            for rows in tiles_of(pre.shape[0], 32):
                act, tilt = gelu_both(pre[rows] + b_up[h, :, at])
                slope[h, rows, at] = tilt.astype(LOW)
                acts[rows, wide] = act
        left = acts[:, pl.ds(start, half)]
        right = acts[:, pl.ds(pl.multiple_of(start + half, 128), half)]
        own[z ^ h] = jnp.where(core == 0, left, right)
        send[z ^ h] = jnp.where(core == 0, right, left)
        return carry

    lax.fori_loop(0, heads, one_unit, 0)
    total[...] = dot(acts[...], w_down[...])
    small[...] = jnp.zeros_like(small)

    def second_norm(rows):
        unit, inv = norm_stats(hidden[rows] + (total[rows] + b_down))
        out[rows] = (unit * gain2 + shift2).astype(LOW)
        upstream = cot[rows].astype(F32)
        grad = norm_back(upstream, unit, inv, gain2)
        res2[rows] = grad
        grad_low = grad.astype(LOW)
        ends[2, rows] = grad_low[:, :half]
        ends[3, rows] = grad_low[:, half:]
        for i, term in enumerate((grad_low.astype(F32), upstream * unit, upstream)):
            small[i : i + 1] += jnp.sum(term, 0, keepdims=True)

    each(low.shape[0], 64, second_norm)


def inner_back(places, ends, w_down, slope, send, own, bias, inners, branch):
    heads, _, chunk = slope.shape
    core, z = places[1], places[2]
    branch[...] = jnp.concatenate([ends[2], ends[3]], 1)

    def one_unit(h, carry):
        start = pl.multiple_of(h * chunk, chunk)
        for at in tiles_of(chunk, 256):
            down = w_down[pl.ds(pl.multiple_of(start + at.start, 256), 256)]
            grad_act = dot_nt(branch[...], down)
            total = 0.0
            for rows in tiles_of(grad_act.shape[0], 32):
                inner = (grad_act[rows] * slope[h, rows, at].astype(F32)).astype(LOW)
                inners[rows, at] = inner
                total = total + jnp.sum(inner.astype(F32), 0, keepdims=True)
            bias[h, :, at] = total
        share(core, inners, own.at[z ^ h], send.at[z ^ h])
        return carry

    lax.fori_loop(0, heads, one_unit, 0)


def hidden_back(places, own, sent, w_up, res2, unit1, inv1, gain1, send, res1, low, small, total):
    heads, count, half = own.shape
    core, z = places[1], places[2]
    sides = []
    for h in range(heads):
        mine, other = own[z ^ h], sent[z ^ h]
        sides += [jnp.where(core == 0, mine, other), jnp.where(core == 0, other, mine)]
    total[...] = dot_nt(jnp.concatenate(sides, 1), w_up[...])
    gain = gain1[...].reshape(1, -1)
    small[...] = jnp.zeros_like(small)

    def norm(rows):
        grad, unit = total[rows] + res2[rows], unit1[rows]
        result = norm_back(grad, unit, inv1[rows], gain)
        res1[rows] = result
        result_low = result.astype(LOW)
        low[rows] = result_low
        send[rows] = jnp.where(core == 0, result_low[:, half:], result_low[:, :half])
        for i, term in enumerate((result_low.astype(F32), grad * unit, grad)):
            small[i : i + 1] += jnp.sum(term, 0, keepdims=True)

    each(count, 64, norm)


def shard_back(qkv, w_out, grad, log_ref, more_k, more_q, rows_ref, bias_ref, grad_ref):
    width = qkv.shape[0] // 3
    grad_ref[...] = dot_nt(w_out[...], grad[...]).astype(LOW)
    scale = HEAD_DIM ** (-0.5)
    def one_head(head, carry):
        places_of = [
            pl.ds(pl.multiple_of(c * width + head * HEAD_DIM, HEAD_DIM), HEAD_DIM)
            for c in range(3)
        ]
        q, k, v = (qkv[at] for at in places_of)
        g = grad_ref[places_of[0]]
        logs = jnp.concatenate(three_parts(-log_ref[pl.ds(head, 1)]), 0)
        with_logs = jnp.concatenate([more_q[:8], logs, more_q[11:]], 0)
        scores = dot_tn(jnp.concatenate([k, more_k], 0), jnp.concatenate([q, with_logs], 0))
        grad_probs = dot_tn(v, g)
        attends, grads = [], []
        for tile in tiles_of(scores.shape[1], LANES):
            inner, kept, lows, parts = 0.0, [], [], []
            tall = tiles_of(scores.shape[0], 64)
            for down in tall:
                attend = jnp.exp2(scores[down, tile] * SCORE_SCALE)
                inner = inner + jnp.sum(attend * grad_probs[down, tile], 0, keepdims=True)
                kept.append(attend)
                lows.append(attend.astype(LOW))
            for down, attend in zip(tall, kept):
                parts.append((attend * (grad_probs[down, tile] - inner)).astype(LOW))
            attends.append(jnp.concatenate(lows, 0))
            grads.append(jnp.concatenate(parts, 0))
        attend_low = jnp.concatenate(attends, 1)
        grad_scores = jnp.concatenate(grads, 1)
        grad_v = dot_nt(g, attend_low)
        grad_q = dot(k, grad_scores) * scale
        grad_k = dot_nt(q, grad_scores) * scale
        for at, value in zip(places_of, (grad_q, grad_k, grad_v)):
            rows_ref[at] = value.astype(LOW)
        return carry

    lax.fori_loop(0, width // HEAD_DIM, one_head, 0)
    ones = jnp.ones((8, rows_ref.shape[1]), LOW)
    bias_ref[...] = dot_nt(ones, rows_ref[...])


def attention_back(places, qkv, w_out, grad, log_ref, seg_row, rows_ref, bias_ref, mixed):
    more_k, more_q = segment_rows(seg_row[...])

    def shard(d, carry):
        refs = (ref.at[d] for ref in (rows_ref, bias_ref))
        shard_back(qkv.at[d], w_out.at[d], grad, log_ref.at[d], more_k, more_q, *refs, mixed)
        return carry

    lax.fori_loop(0, qkv.shape[0], shard, 0)


def split_rows(value, high, send, keep):
    rows = value.shape[0] // 2
    low = value.astype(LOW)
    send[...] = jnp.where(high, low[:rows], low[rows:])
    keep[...] = jnp.where(high, low[rows:], low[:rows])


def is_high(places, bit):
    return (places[0] & bit) != 0


def ffn_grad(bit, which, places, units, units_far, ends, ends_far, send, keep, both):
    half, count = ends.shape[2], ends.shape[1]
    for side in range(2):
        rows = slice(side * half, (side + 1) * half)
        both[rows, :count] = ends[2 * which + side].T
        both[rows, count:] = ends_far[2 * which + side].T
    for d in range(0, units.shape[0], 2):
        left, right = (jnp.concatenate([units[d + i], units_far[d + i]], 0) for i in range(2))
        total = dot(both[...], jnp.concatenate([left, right], 1))
        for i in range(2):
            part = total[:, i * half : (i + 1) * half]
            split_rows(part, is_high(places, bit), send.at[d + i], keep.at[d + i])


def attn_grad(
    places, rows, rows_far, tok, tok_far, mix, mix_far, grad, grad_far,
    small_one, small_two, up_bias, qkv_bias, send_x, keep_x, send_y, keep_y,
):
    width = mix.shape[1]
    half = tok_far.shape[1]
    core, z = places[1], places[2]

    def both(near, far):
        mine = jnp.where(core == 0, near[:, :half], near[:, half:])
        return jnp.concatenate([mine, far[...]], 0)

    tok_both, grad_both = both(tok, tok_far), both(grad, grad_far)
    for d in range(rows.shape[0]):
        qkv = dot(jnp.concatenate([rows[d], rows_far[d]], 1), tok_both)
        out = dot(jnp.concatenate([mix[d], mix_far[d]], 1), grad_both)
        lines = []
        for held in (small_one, small_two):
            for i in range(3):
                lines += [held[i : i + 1, :half], held[i : i + 1, half:]]
        line, bias = up_bias[z ^ d], qkv_bias[d]
        lines += [line[:, :half], line[:, half:]]
        lines.append(jnp.concatenate([bias[0:1, :width], bias[0:1, 2 * width :]], 1))
        lines.append(jnp.zeros((EXTRA - len(lines), half), F32))
        total = jnp.concatenate([qkv, out] + lines, 0)
        split_rows(total[:half], is_high(places, 1), send_x.at[d], keep_x.at[d])
        split_rows(total[half:], is_high(places, 2), send_y.at[d], keep_y.at[d])


def add_split(bits, places, *refs):
    for i, bit in enumerate(bits):
        keep, came = refs[2 * i : 2 * i + 2]
        send, left = refs[2 * (len(bits) + i) : 2 * (len(bits) + i) + 2]
        for d in range(keep.shape[0]):
            total = keep[d].astype(F32) + came[d].astype(F32)
            split_rows(total, is_high(places, bit), send.at[d], left.at[d])


def add_parts(places, keep_a, came_a, keep_b, came_b, send, keep):
    rows = keep_a.shape[1]
    for d in range(keep_a.shape[0]):
        out = (send if d % 2 else keep).at[d // 2]
        out[:rows] = (keep_a[d].astype(F32) + came_a[d].astype(F32)).astype(LOW)
        out[rows:] = (keep_b[d].astype(F32) + came_b[d].astype(F32)).astype(LOW)


def add_pair(places, keep, came, *outs):
    for i, out in enumerate(outs):
        out[...] = (keep[i].astype(F32) + came[i].astype(F32)).astype(LOW)


def add_two(places, keep, came, out):
    out[...] = (keep[...].astype(F32) + came[...].astype(F32)).astype(LOW)


def input_sum(places, rows, w, res1, out):
    heads, count, tokens = rows.shape
    total = dot_tn(rows[...].reshape(heads * count, tokens), w[...].reshape(heads * count, -1))
    out[...] = res1[...] + total


def place_pieces(places, held, full, layouts):
    near, core = places[0], places[1]
    width = held[0].shape[1]
    for off in range(4):
        chip = near ^ off
        mine, other = held[off][...], held[4 + off][...]
        sides = (jnp.where(core == 0, mine, other), jnp.where(core == 0, other, mine))
        for at, rows, start, outer in layouts:
            low_bit, high_bit = chip & 1, chip >> 1
            order = 2 * low_bit + high_bit if outer == 1 else 2 * high_bit + low_bit
            to = pl.multiple_of(start + order * rows, 16)
            for side in range(2):
                full[pl.ds(to, rows), side * width : (side + 1) * width] = sides[side][
                    at : at + rows
                ].astype(F32)


def ffn_place(places, *refs):
    held = [ref.at[off] for ref in refs[:2] for off in range(4)]
    down, up, full = refs[2:]
    rows = held[0].shape[0] // 2
    place_pieces(places, held, full, [(0, rows, 0, 1)])
    down[...] = full[...].T
    place_pieces(places, held, up, [(rows, rows, 0, 2)])


def collect(places, *refs):
    for off in range(4):
        refs[4][off] = refs[off][...]


def attn_place(places, *refs):
    held = [ref.at[off] for ref in refs[:2] for off in range(4)]
    qkv, w_out, small, up_bias, qv_bias, full = refs[2:]
    width = held[0].shape[1]
    count = w_out.shape[0]
    rows = count // 2
    more = held[0].shape[0] - rows
    place_pieces(places, held, full, [(0, rows, 0, 1), (rows, more, 4 * rows, 2)])
    for c in range(3):
        qkv[c] = full[c * count : (c + 1) * count]
    w_out[...] = full[3 * count : 4 * count]
    at = 4 * count
    lines = full[at : at + 16, :width] + full[at : at + 16, width:]
    for i in range(6):
        small[i : i + 1, :width] = lines[2 * i : 2 * i + 1]
        small[i : i + 1, width:] = lines[2 * i + 1 : 2 * i + 2]
    up_bias[...] = jnp.concatenate([lines[12:13], lines[13:14]], 1).reshape(2 * width)
    qv_bias[0:1] = lines[14:15, :count]
    qv_bias[1:2] = lines[14:15, count : 2 * count]


def bias_parts(values):
    rows, rest = [], values
    for _ in range(3):
        rows.append(lax.reduce_precision(rest, 8, 7))
        rest = rest - rows[-1]
    return jnp.stack(rows).astype(LOW)


def gather_back(piece):
    return [piece] + [swap(piece, "near", off) for off in range(1, 4)]


def per_device(
    tokens,
    segment_ids,
    w_qkv,
    b_qv,
    w_out,
    b_out,
    ln1_gain,
    ln1_bias,
    w_up,
    b_up,
    w_down,
    b_down,
    ln2_gain,
    ln2_bias,
    cotangent,
):
    CHAIN.clear()
    width = tokens.shape[1]
    own_rows = cotangent.shape[0]
    local_width = w_qkv.shape[2]
    heads = lax.axis_size("head")
    z = lax.axis_index("head")
    core = lax.axis_index("core")
    near = lax.axis_index("near")
    hidden_units = w_up.shape[1]
    chunk = hidden_units // heads
    half = width // 2
    rows3 = 3 * local_width
    places = jnp.stack([near, core, z]).astype(jnp.int32)

    shard = jnp.concatenate([w_qkv.transpose(0, 2, 1).reshape(rows3, width), w_out], 0)
    piece_rows = shard.shape[0] // 8
    bias = jnp.pad(bias_parts(b_qv.reshape(-1)), ((0, 13), (0, width - 2 * local_width)))
    piece = lax.dynamic_slice_in_dim(shard, (near * 2 + core) * piece_rows, piece_rows, 0)
    piece = jnp.concatenate([piece, bias], 0)
    first_hop = [swap(piece, "head", d) for d in range(1, heads)]

    seg = lax.dynamic_slice_in_dim(segment_ids, z * own_rows, own_rows, 0)
    tok_own = lax.dynamic_slice_in_dim(tokens, z * own_rows, own_rows, 0)
    attend_outs = [
        ((heads, rows3, own_rows), LOW),
        ((heads, local_width, own_rows), LOW),
        ((heads, 8, own_rows), F32),
        ((heads, rows3, width), LOW),
        ((heads, local_width, width), LOW),
    ]
    macs = rows3 * width * own_rows + 6 * own_rows * own_rows * 256
    ins = [tok_own, shard, bias, seg[None]]
    made = begun = run_whole(own_attention, places, ins, attend_outs, macs=macs, chain=False)
    orders = [(1, 2) if d % 2 else (2, 1) for d in range(heads)]
    nexts = [swap(first_hop[d - 1], "near", orders[d][0]) for d in range(1, heads)]
    for d in range(1, heads):
        (pair,) = run_whole(
            pair_rows, places, [first_hop[d - 1], nexts[d - 1]],
            [((2, piece_rows, width), LOW)], after=nexts + [begun[2]], chain=False,
        )
        rest = swap(pair, "near", orders[d][1])
        ins = [tok_own, pair, rest, swap_core(pair), swap_core(rest), first_hop[d - 1], seg[None]]
        made = run_whole(
            functools.partial(far_attention, d, orders[d]), places, ins, attend_outs,
            [pltpu.VMEM(shard.shape, LOW)], macs, alias=made, chain=False, weight=100,
        )
    qkvs, mixes, logs, w_qkvs, w_outs = made

    mixes_far = swap_core(mixes)

    square = (own_rows, width)
    tiles = (heads, own_rows, half)
    ins = [
        tok_own, mixes, w_outs, b_out, ln1_gain, ln1_bias, b_down, ln2_gain, ln2_bias,
        w_up, b_up.reshape(heads, 1, chunk), w_down, cotangent,
    ]
    outs = [
        (tiles, LOW),
        (tiles, LOW),
        ((4, own_rows, half), LOW),
        ((heads, own_rows, chunk), LOW),
        (square, F32),
        ((own_rows, 1), F32),
        (square, F32),
        (square, LOW),
        ((8, width), F32),
        ((own_rows, half), LOW),
    ]
    scratch = [
        pltpu.VMEM(square, F32),
        pltpu.VMEM(square, LOW),
        pltpu.VMEM((own_rows, hidden_units), LOW),
        pltpu.VMEM(square, F32),
    ]
    ffn_macs = 2 * own_rows * width * hidden_units
    (
        act_send, act_own, ends, slope, unit1, inv1, res2, layer_output, small_two, tok_send,
    ) = run_whole(feed_forward, places, ins, outs, scratch, ffn_macs)
    tok_far = swap_core(tok_send)
    act_far = swap_core(act_send)
    ends_far = swap_core(ends)

    outs = [(tiles, LOW), (tiles, LOW), ((heads, 1, chunk), F32)]
    scratch = [pltpu.VMEM((own_rows, chunk), LOW), pltpu.VMEM(square, LOW)]
    inner_send, inner_own, up_bias = run_whole(
        inner_back, places, [ends, w_down, slope], outs, scratch, ffn_macs // 2, [mixes_far]
    )
    inner_far = swap_core(inner_send)


    def ffn_unit(bit, own, far, which, weight):
        outs = [((heads, half, half), LOW)] * 2
        both = [pltpu.VMEM((width, 2 * own_rows), LOW)]
        kernel = functools.partial(ffn_grad, bit, which)
        ins = [own, far, ends, ends_far]
        return run_whole(kernel, places, ins, outs, both, ffn_macs // 2, weight=weight)

    made = ffn_unit(1, act_own, act_far, 1, 8) + ffn_unit(2, inner_own, inner_far, 0, LIGHT)
    x_send, x_keep, y_send, y_keep = made
    ffn_held = (x_keep, swap(x_send, "near", 1), y_keep, swap(y_send, "near", 2))

    outs = [((own_rows, half), LOW), (square, F32), (square, LOW), ((8, width), F32)]
    ins = [inner_own, inner_send, w_up, res2, unit1, inv1, ln1_gain]
    grad_send, res1, grad_attended, small_one = run_whole(
        hidden_back, places, ins, outs, [pltpu.VMEM(square, F32)], ffn_macs // 2, weight=LIGHT
    )
    grad_far = swap_core(grad_send)

    def second(x_keep, x_came, y_keep, y_came, macs=0):
        arrays = (x_keep, x_came, y_keep, y_came)
        shapes = [(heads, a.shape[1] // 2, half) for a in (x_keep, x_keep, y_keep, y_keep)]
        outs = [(shape, LOW) for shape in shapes]
        kernel = functools.partial(add_split, (2, 1))
        return run_whole(kernel, places, arrays, outs, macs=macs)

    def third(x_keep, x_came, y_keep, y_came):
        arrays = (x_keep, x_came, y_keep, y_came)
        shape = (heads // 2, x_keep.shape[1] + y_keep.shape[1], half)
        send, keep = run_whole(add_parts, places, arrays, [(shape, LOW)] * 2)
        return keep, swap(send, "head", 1)

    def fourth(keep, came):
        shape = keep.shape[1:]
        mine, other = run_whole(add_pair, places, [keep, came], [(shape, LOW)] * 2)
        return mine, swap(other, "head", 2)

    def fifth(mine, came):
        (total,) = run_whole(add_two, places, [mine, came], [(mine.shape, LOW)])
        bit = 1
        while bit < lax.axis_size("far"):
            total = (total.astype(F32) + swap(total, "far", bit).astype(F32)).astype(LOW)
            bit *= 2
        return total

    def cross(made, flip):
        x_send, x_keep, y_send, y_keep = made
        x_bit, y_bit = (2, 1) if flip else (1, 2)
        return x_keep, swap(x_send, "near", x_bit), y_keep, swap(y_send, "near", y_bit)

    outs = [((heads, rows3, own_rows), LOW), ((heads, 8, rows3), F32)]
    ins = [qkvs, w_outs, grad_attended, logs, seg[None]]
    scratch = [pltpu.VMEM((local_width, own_rows), LOW)]
    rows, qkv_bias = run_whole(attention_back, places, ins, outs, scratch)
    rows_far = swap_core(rows)

    outs = [(square, F32, whole(square))]
    ins = [(a, whole(a.shape)) for a in (rows, w_qkvs, res1)]
    (input_grad,) = run(input_sum, places, (1,), ins, outs, weight=LIGHT)
    ffn_held = cross(second(*ffn_held, ffn_macs), True)
    ins = [
        rows, rows_far, tok_own, tok_far, mixes, mixes_far, grad_attended, grad_far,
        small_one, small_two, up_bias, qkv_bias,
    ]
    outs = [
        ((heads, r, half), LOW) for r in (half // 2, (half + EXTRA) // 2) for _ in range(2)
    ]
    made = run_whole(attn_grad, places, ins, outs)
    attn_held = cross(made, False)

    ffn_held = third(*ffn_held)
    attn_held = cross(second(*attn_held), True)
    ffn_held = fourth(*ffn_held)
    attn_held = third(*attn_held)
    ffn_held = gather_back(fifth(*ffn_held))
    attn_held = fourth(*attn_held)
    attn_held = gather_back(fifth(*attn_held))

    def both_cores(held):
        shape = (heads,) + held[0].shape
        (pieces,) = run_whole(collect, places, held, [(shape, LOW)])
        return [(a, whole(shape)) for a in (pieces, swap_core(pieces))]

    ffn_held = both_cores(ffn_held)
    outs = [(shape, F32, whole(shape)) for shape in ((chunk, width), (width, chunk))]
    grad_down, grad_up = run(
        ffn_place, places, (1,), ffn_held, outs, [pltpu.VMEM((width, chunk), F32)]
    )
    attn_held = both_cores(attn_held)
    shapes = [
        (3, local_width, width),
        (local_width, width),
        (6, width),
        (chunk,),
        (2, local_width),
    ]
    grad_qkv, grad_out, grad_small, grad_up_bias, grad_qv_bias = run(
        attn_place,
        places,
        (1,),
        attn_held,
        [(shape, F32, whole(shape)) for shape in shapes],
        [pltpu.VMEM((width + EXTRA, width), F32)],
    )
    return (
        layer_output,
        input_grad,
        grad_qkv.transpose(0, 2, 1),
        grad_qv_bias,
        grad_out,
        grad_up,
        grad_up_bias,
        grad_down,
        grad_small,
    )


def solution(mesh):
    batch, heads = mesh.devices.shape
    mesh = Mesh(
        mesh.devices.reshape(batch // 8, 4, 2, heads), ("far", "near", "core", "head")
    )
    group = ("far", "near", "core")
    everyone = group + ("head",)
    in_specs = (
        P(group, None),
        P(group),
        P(None, None, "head"),
        P(None, "head"),
        P("head", None),
        P(),
        P(),
        P(),
        P(),
        P(),
        P(),
        P(),
        P(),
        P(),
        P(everyone, None),
    )
    out_specs = (
        P(everyone, None),
        P(everyone, None),
        P(None, None, "head"),
        P(None, "head"),
        P("head", None),
        P(None, "head"),
        P("head"),
        P("head", None),
        P(),
    )
    return jax.shard_map(
        per_device, mesh=mesh, in_specs=in_specs, out_specs=out_specs, check_vma=False
    )
```

```python
import functools
import math

import jax
import jax.numpy as jnp
from jax import lax
from jax.experimental import pallas as pl
from jax.experimental.pallas import tpu as pltpu
from jax.sharding import Mesh
from jax.sharding import PartitionSpec as P

HEAD_DIM = 64
SLOT = 512
LOW = jnp.bfloat16
F32 = jnp.float32
LOG2E = math.log2(math.e)
SCORE_SCALE = HEAD_DIM ** (-0.5) * LOG2E
SPARE_BYTES = 12 * 2**20
EXTRA = 64
LIGHT = 0.01
LANES = 128
CHAIN = []
TAIL_SLOPE = 0.36
TAIL = (
    0.14371304537508633,
    0.14177245466203425,
    0.1397192603907239,
    0.026549325413860486,
    0.18095403134327948,
    -0.1797647161697652,
    0.047056295581175855,
)


def swap(value, axis, bit):
    size = lax.axis_size(axis)
    return lax.ppermute(value, axis, [(i, i ^ bit) for i in range(size)])


def swap_core(value):
    return swap(value, "core", 1)


def dot(a, b):
    return jnp.dot(a, b, preferred_element_type=F32)


def dot_nt(a, b):
    return lax.dot_general(a, b, (((1,), (1,)), ((), ())), preferred_element_type=F32)


def dot_tn(a, b):
    return lax.dot_general(a, b, (((0,), (0,)), ((), ())), preferred_element_type=F32)


def whole(shape):
    return pl.BlockSpec(shape, lambda *args: (0,) * len(shape), pipeline_mode=pl.Buffered(1))


def run(
    kernel, places, grid, ins, outs, scratch=(), macs=0, after=(), alias=(), weight=8, chain=True
):
    moved = sum(a.size * a.dtype.itemsize for a, spec in ins)
    moved += sum(math.prod(shape) * jnp.dtype(kind).itemsize for shape, kind, spec in outs)
    after = list(after) + (CHAIN if chain else [])
    count, unread = len(ins), len(alias) + len(after)
    results = len(outs)
    flag = (8, 128)
    if chain:
        outs = outs + [(flag, F32, whole(flag))]

    def body(places, *refs):
        made = refs[count + unread :]
        if chain:

            @pl.when(pl.program_id(0) == 0)
            def _():
                made[results][...] = jnp.zeros(flag, F32)

        kernel(places, *refs[:count], *made[:results], *made[len(outs) :])

    held = pl.BlockSpec(memory_space=pl.ANY)
    room = SPARE_BYTES
    for shape, kind, spec in outs + [(a.shape, a.dtype, spec) for a, spec in ins]:
        if spec.block_shape is not None:
            block = math.prod(1 if n is None else n for n in spec.block_shape)
            copies = 2 if spec.pipeline_mode is None else 1
            room += copies * block * jnp.dtype(kind).itemsize
    for ref in scratch:
        if hasattr(ref, "shape") and ref.dtype in (LOW, F32):
            room += math.prod(ref.shape) * jnp.dtype(ref.dtype).itemsize
    made = pl.pallas_call(
        body,
        name=getattr(kernel, "func", kernel).__name__,
        grid_spec=pltpu.PrefetchScalarGridSpec(
            num_scalar_prefetch=1,
            grid=grid,
            in_specs=[spec for a, spec in ins] + [held] * unread,
            out_specs=[spec for shape, kind, spec in outs],
            scratch_shapes=list(scratch),
        ),
        out_shape=[jax.ShapeDtypeStruct(shape, kind) for shape, kind, spec in outs],
        input_output_aliases={1 + count + i: i for i in range(len(alias))},
        compiler_params=pltpu.CompilerParams(vmem_limit_bytes=room),
        cost_estimate=pl.CostEstimate(
            flops=int(2 * macs * weight), bytes_accessed=int(moved * weight), transcendentals=0
        ),
    )(places, *[a for a, spec in ins], *alias, *after)
    if chain:
        CHAIN[:] = made[results:]
    return made[:results]


def run_whole(
    kernel, places, ins, outs, scratch=(), macs=0, after=(), alias=(), weight=8, chain=True
):
    pairs = [a if isinstance(a, tuple) else (a, pltpu.VMEM) for a in ins]
    after = list(after) + (CHAIN if chain else [])
    count, unread, results = len(pairs), len(alias) + len(after), len(outs)
    if chain:
        outs = outs + [((8, 128), F32)]

    def body(places, *refs):
        made = refs[count + unread :]
        if chain:
            made[results][...] = jnp.zeros((8, 128), F32)
        kernel(places, *refs[:count], *made[:results], *made[len(outs) :])

    room = SPARE_BYTES
    for ref in scratch:
        if hasattr(ref, "shape") and ref.dtype in (LOW, F32):
            room += math.prod(ref.shape) * jnp.dtype(ref.dtype).itemsize
    spaces = [pltpu.SMEM] + [space for a, space in pairs]
    spaces += [pltpu.VMEM] * len(alias) + [pl.ANY] * len(after)
    made = pl.pallas_call(
        body,
        name=getattr(kernel, "func", kernel).__name__,
        in_specs=[pl.BlockSpec(memory_space=space) for space in spaces],
        out_specs=[pl.BlockSpec(memory_space=pltpu.VMEM)] * len(outs),
        scratch_shapes=list(scratch),
        out_shape=[jax.ShapeDtypeStruct(shape, kind) for shape, kind in outs],
        input_output_aliases={1 + count + i: i for i in range(len(alias))},
        compiler_params=pltpu.CompilerParams(vmem_limit_bytes=room),
        cost_estimate=pl.CostEstimate(
            flops=int(2 * macs * weight), bytes_accessed=0, transcendentals=0
        ),
    )(places, *[a for a, space in pairs], *alias, *after)
    if chain:
        CHAIN[:] = made[results:]
    return made[:results]


def each(count, size, body):
    def step(i, carry):
        body(pl.ds(pl.multiple_of(i * size, size), size))
        return carry

    lax.fori_loop(0, count // size, step, 0)


def tiles_of(count, size):
    return [slice(at, at + size) for at in range(0, count, size)]


def three_parts(values):
    parts, rest = [], values
    for _ in range(3):
        parts.append(rest.astype(LOW))
        rest = rest - parts[-1].astype(F32)
    return parts


def segment_rows(seg_row):
    shape = (16, seg_row.shape[1])
    place = lax.broadcasted_iota(jnp.int32, shape, 0)
    same = place - 1 == seg_row
    keys = jnp.where(same, 1.0, jnp.where((place >= 8) & (place < 11), 1.0, 0.0))
    queries = jnp.where(same | (place > 4), 0.0, -1e30)
    return keys.astype(LOW), queries.astype(LOW)


def attend_heads(tok, w_rows, bias, seg_row, qkv_ref, mix_ref, log_ref):
    width = w_rows.shape[0] // 3
    added = dot_tn(bias[:, : 2 * width], jnp.ones((bias.shape[0], tok.shape[0]), LOW))
    qkv = dot_nt(w_rows, tok)
    parts = (
        (qkv[:width] + added[:width]).astype(LOW),
        qkv[width : 2 * width].astype(LOW),
        (qkv[2 * width :] + added[width:]).astype(LOW),
    )
    for c in range(3):
        qkv_ref[c * width : (c + 1) * width] = parts[c]
    more_k, more_q = segment_rows(seg_row)
    for head in range(width // HEAD_DIM):
        q, k, v = (part[head * HEAD_DIM : (head + 1) * HEAD_DIM] for part in parts)
        scores = dot_tn(jnp.concatenate([k, more_k], 0), jnp.concatenate([q, more_q], 0))
        columns, tops, totals = [], [], []
        for tile in tiles_of(scores.shape[1], LANES):
            top = jnp.max(scores[:, tile], 0, keepdims=True)
            total, column = 0.0, []
            for rows in tiles_of(scores.shape[0], 64):
                exponent = jnp.exp2((scores[rows, tile] - top) * SCORE_SCALE)
                total = total + jnp.sum(exponent, 0, keepdims=True)
                column.append(exponent.astype(LOW))
            columns.append(jnp.concatenate(column, 0))
            tops.append(top)
            totals.append(total)
        total = jnp.concatenate(totals, 1)
        mixed = dot(v, jnp.concatenate(columns, 1)) * (1.0 / total)
        mix_ref[head * HEAD_DIM : (head + 1) * HEAD_DIM] = mixed.astype(LOW)
        top = jnp.concatenate(tops, 1)
        log_ref[head : head + 1] = top + jnp.log2(total) * (1.0 / SCORE_SCALE)


def own_attention(
    places, tok, w, bias, seg_row, qkv_ref, mix_ref, log_ref, w_qkv, w_out
):
    count = qkv_ref.shape[1]
    w_qkv[0] = w[:count]
    w_out[0] = w[count:]
    attend_heads(
        tok[...], w[:count], bias[...], seg_row[...], qkv_ref.at[0], mix_ref.at[0], log_ref.at[0]
    )


def far_attention(
    d, order, places, tok, pair, rest, pair_far, rest_far, hop, seg_row,
    qkv_ref, mix_ref, log_ref, w_qkv, w_out, w_ref,
):
    first, second = order
    rows, count = pair.shape[1], qkv_ref.shape[1]
    me = places[0] * 2 + places[1]
    for other, held in enumerate(((pair, rest), (pair_far, rest_far))):
        for two, block in enumerate(held):
            for one in range(2):
                owner = me ^ (other + 2 * first * one + 2 * second * two)
                w_ref[pl.ds(pl.multiple_of(owner * rows, rows), rows)] = block[one]
    w_qkv[d] = w_ref[:count]
    w_out[d] = w_ref[count:]
    attend_heads(
        tok[...],
        w_ref[:count],
        hop[rows:],
        seg_row[...],
        qkv_ref.at[d],
        mix_ref.at[d],
        log_ref.at[d],
    )


def copy_rows(places, rows, out):
    out[...] = rows[...]


def pair_rows(places, first, second, out):
    out[0] = first[: out.shape[1]]
    out[1] = second[: out.shape[1]]


def norm_stats(v):
    centred = v - jnp.mean(v, -1, keepdims=True)
    inv = lax.rsqrt(jnp.mean(centred * centred, -1, keepdims=True) + 1e-05)
    return centred * inv, inv


def norm_back(upstream, unit, inv, gain):
    scaled = upstream * gain
    inner = jnp.mean(scaled * unit, -1, keepdims=True)
    return inv * (scaled - jnp.mean(scaled, -1, keepdims=True) - unit * inner)


def gelu_both(pre):
    power = jnp.exp2(pre * pre * (-0.5 * LOG2E))
    base = 1.0 + TAIL_SLOPE * jnp.abs(pre)
    t = pl.reciprocal(base, approx=True)
    tail = TAIL[6] * t + TAIL[5]
    for c in TAIL[4::-1]:
        tail = tail * t + c
    tail = tail * (t * power)
    cumul = jnp.where(pre < 0.0, tail, 1.0 - tail)
    return (pre * cumul).astype(LOW), cumul + pre * (power * 0.3989422804014327)


def share(core, wide, mine, other):
    half = wide.shape[1] // 2
    left, right = wide[:, :half], wide[:, half:]
    mine[...] = jnp.where(core == 0, left, right)
    other[...] = jnp.where(core == 0, right, left)


def feed_forward(
    places, tok, mix, w_out, b_out, gain1, shift1, b_down, gain2, shift2, w_up, b_up, w_down, cot,
    send, own, ends, slope, unit1, inv1, res2, out, small, tok_send,
    hidden, low, acts, total,
):
    heads, width, half = mix.shape[0], low.shape[1], send.shape[2]
    chunk = 2 * half
    core, z = places[1], places[2]
    b_out, gain1, shift1, b_down, gain2, shift2 = (
        ref[...].reshape(1, -1) for ref in (b_out, gain1, shift1, b_down, gain2, shift2)
    )
    tok_send[...] = jnp.where(core == 0, tok[:, half:], tok[:, :half])
    total[...] = dot_tn(mix[...].reshape(width, low.shape[0]), w_out[...].reshape(width, width))

    def first_norm(rows):
        unit, inv = norm_stats(tok[rows].astype(F32) + (total[rows] + b_out))
        unit1[rows] = unit
        inv1[rows] = inv
        one = unit * gain1 + shift1
        hidden[rows] = one
        one_low = one.astype(LOW)
        low[rows] = one_low
        ends[0, rows] = one_low[:, :half]
        ends[1, rows] = one_low[:, half:]

    each(low.shape[0], 64, first_norm)

    def one_unit(h, carry):
        start = pl.multiple_of(h * chunk, chunk)
        for at in tiles_of(chunk, 256):
            wide = pl.ds(pl.multiple_of(start + at.start, 256), 256)
            pre = dot(low[...], w_up[:, wide])
            for rows in tiles_of(pre.shape[0], 32):
                act, tilt = gelu_both(pre[rows] + b_up[h, :, at])
                slope[h, rows, at] = tilt.astype(LOW)
                acts[rows, wide] = act
        left = acts[:, pl.ds(start, half)]
        right = acts[:, pl.ds(pl.multiple_of(start + half, 128), half)]
        own[z ^ h] = jnp.where(core == 0, left, right)
        send[z ^ h] = jnp.where(core == 0, right, left)
        return carry

    lax.fori_loop(0, heads, one_unit, 0)
    total[...] = dot(acts[...], w_down[...])
    small[...] = jnp.zeros_like(small)

    def second_norm(rows):
        unit, inv = norm_stats(hidden[rows] + (total[rows] + b_down))
        out[rows] = (unit * gain2 + shift2).astype(LOW)
        upstream = cot[rows].astype(F32)
        grad = norm_back(upstream, unit, inv, gain2)
        res2[rows] = grad
        grad_low = grad.astype(LOW)
        ends[2, rows] = grad_low[:, :half]
        ends[3, rows] = grad_low[:, half:]
        for i, term in enumerate((grad_low.astype(F32), upstream * unit, upstream)):
            small[i : i + 1] += jnp.sum(term, 0, keepdims=True)

    each(low.shape[0], 64, second_norm)


def inner_back(places, ends, w_down, slope, send, own, bias, inners):
    heads, _, chunk = slope.shape
    core, z = places[1], places[2]
    branch = jnp.concatenate([ends[2], ends[3]], 1)
    for h in range(heads):
        for at in tiles_of(chunk, 256):
            grad_act = dot_nt(branch, w_down[h * chunk + at.start : h * chunk + at.stop])
            total = 0.0
            for rows in tiles_of(grad_act.shape[0], 32):
                inner = (grad_act[rows] * slope[h, rows, at].astype(F32)).astype(LOW)
                inners[rows, at] = inner
                total = total + jnp.sum(inner.astype(F32), 0, keepdims=True)
            bias[h, :, at] = total
        share(core, inners, own.at[z ^ h], send.at[z ^ h])


def hidden_back(places, own, sent, w_up, res2, unit1, inv1, gain1, send, res1, low, small):
    heads, count, half = own.shape
    core, z = places[1], places[2]
    sides = []
    for h in range(heads):
        mine, other = own[z ^ h], sent[z ^ h]
        sides += [jnp.where(core == 0, mine, other), jnp.where(core == 0, other, mine)]
    product = dot_nt(jnp.concatenate(sides, 1), w_up[...])
    gain = gain1[...].reshape(1, -1)
    sums = [0.0] * 3
    for rows in tiles_of(count, 32):
        grad, unit = product[rows] + res2[rows], unit1[rows]
        result = norm_back(grad, unit, inv1[rows], gain)
        res1[rows] = result
        result_low = result.astype(LOW)
        low[rows] = result_low
        send[rows] = jnp.where(core == 0, result_low[:, half:], result_low[:, :half])
        for i, term in enumerate((result_low.astype(F32), grad * unit, grad)):
            sums[i] = sums[i] + jnp.sum(term, 0, keepdims=True)
    for i in range(3):
        small[i : i + 1] = sums[i]


def shard_back(qkv, w_out, grad, log_ref, more_k, more_q, rows_ref, bias_ref):
    width = qkv.shape[0] // 3
    grad_mixed = dot_nt(w_out[...], grad[...]).astype(LOW)
    scale = HEAD_DIM ** (-0.5)
    for head in range(width // HEAD_DIM):
        places_of = [c * width + head * HEAD_DIM for c in range(3)]
        q, k, v = (qkv[at : at + HEAD_DIM] for at in places_of)
        g = grad_mixed[head * HEAD_DIM : (head + 1) * HEAD_DIM]
        logs = jnp.concatenate(three_parts(-log_ref[head : head + 1]), 0)
        with_logs = jnp.concatenate([more_q[:8], logs, more_q[11:]], 0)
        scores = dot_tn(jnp.concatenate([k, more_k], 0), jnp.concatenate([q, with_logs], 0))
        grad_probs = dot_tn(v, g)
        attends, grads = [], []
        for tile in tiles_of(scores.shape[1], LANES):
            inner, kept, lows, parts = 0.0, [], [], []
            tall = tiles_of(scores.shape[0], 64)
            for down in tall:
                attend = jnp.exp2(scores[down, tile] * SCORE_SCALE)
                inner = inner + jnp.sum(attend * grad_probs[down, tile], 0, keepdims=True)
                kept.append(attend)
                lows.append(attend.astype(LOW))
            for down, attend in zip(tall, kept):
                parts.append((attend * (grad_probs[down, tile] - inner)).astype(LOW))
            attends.append(jnp.concatenate(lows, 0))
            grads.append(jnp.concatenate(parts, 0))
        attend_low = jnp.concatenate(attends, 1)
        grad_scores = jnp.concatenate(grads, 1)
        grad_v = dot_nt(g, attend_low)
        grad_q = dot(k, grad_scores) * scale
        grad_k = dot_nt(q, grad_scores) * scale
        for at, value in zip(places_of, (grad_q, grad_k, grad_v)):
            rows_ref[at : at + HEAD_DIM] = value.astype(LOW)
    ones = jnp.ones((8, rows_ref.shape[1]), LOW)
    bias_ref[...] = dot_nt(ones, rows_ref[...])


def attention_back(places, qkv, w_out, grad, log_ref, seg_row, rows_ref, bias_ref):
    more_k, more_q = segment_rows(seg_row[...])

    def shard(d, carry):
        refs = (ref.at[d] for ref in (rows_ref, bias_ref))
        shard_back(qkv.at[d], w_out.at[d], grad, log_ref.at[d], more_k, more_q, *refs)
        return carry

    lax.fori_loop(0, qkv.shape[0], shard, 0)


def split_rows(value, high, send, keep):
    rows = value.shape[0] // 2
    low = value.astype(LOW)
    send[...] = jnp.where(high, low[:rows], low[rows:])
    keep[...] = jnp.where(high, low[rows:], low[:rows])


def is_high(places, bit):
    return (places[0] & bit) != 0


def ffn_grad(bit, which, places, units, units_far, ends, ends_far, send, keep, both):
    half, count = ends.shape[2], ends.shape[1]
    for side in range(2):
        rows = slice(side * half, (side + 1) * half)
        both[rows, :count] = ends[2 * which + side].T
        both[rows, count:] = ends_far[2 * which + side].T
    for d in range(0, units.shape[0], 2):
        left, right = (jnp.concatenate([units[d + i], units_far[d + i]], 0) for i in range(2))
        total = dot(both[...], jnp.concatenate([left, right], 1))
        for i in range(2):
            part = total[:, i * half : (i + 1) * half]
            split_rows(part, is_high(places, bit), send.at[d + i], keep.at[d + i])


def attn_grad(
    places, rows, rows_far, tok, tok_far, mix, mix_far, grad, grad_far,
    small_one, small_two, up_bias, qkv_bias, send_x, keep_x, send_y, keep_y,
):
    width = mix.shape[1]
    half = tok_far.shape[1]
    core, z = places[1], places[2]

    def both(near, far):
        mine = jnp.where(core == 0, near[:, :half], near[:, half:])
        return jnp.concatenate([mine, far[...]], 0)

    tok_both, grad_both = both(tok, tok_far), both(grad, grad_far)
    for d in range(rows.shape[0]):
        qkv = dot(jnp.concatenate([rows[d], rows_far[d]], 1), tok_both)
        out = dot(jnp.concatenate([mix[d], mix_far[d]], 1), grad_both)
        lines = []
        for held in (small_one, small_two):
            for i in range(3):
                lines += [held[i : i + 1, :half], held[i : i + 1, half:]]
        line, bias = up_bias[z ^ d], qkv_bias[d]
        lines += [line[:, :half], line[:, half:]]
        lines.append(jnp.concatenate([bias[0:1, :width], bias[0:1, 2 * width :]], 1))
        lines.append(jnp.zeros((EXTRA - len(lines), half), F32))
        total = jnp.concatenate([qkv, out] + lines, 0)
        split_rows(total[:half], is_high(places, 1), send_x.at[d], keep_x.at[d])
        split_rows(total[half:], is_high(places, 2), send_y.at[d], keep_y.at[d])


def add_split(bits, places, *refs):
    for i, bit in enumerate(bits):
        keep, came = refs[2 * i : 2 * i + 2]
        send, left = refs[2 * (len(bits) + i) : 2 * (len(bits) + i) + 2]
        for d in range(keep.shape[0]):
            total = keep[d].astype(F32) + came[d].astype(F32)
            split_rows(total, is_high(places, bit), send.at[d], left.at[d])


def add_parts(places, keep_a, came_a, keep_b, came_b, send, keep):
    rows = keep_a.shape[1]
    for d in range(keep_a.shape[0]):
        out = (send if d % 2 else keep).at[d // 2]
        out[:rows] = (keep_a[d].astype(F32) + came_a[d].astype(F32)).astype(LOW)
        out[rows:] = (keep_b[d].astype(F32) + came_b[d].astype(F32)).astype(LOW)


def add_pair(places, keep, came, *outs):
    for i, out in enumerate(outs):
        out[...] = (keep[i].astype(F32) + came[i].astype(F32)).astype(LOW)


def add_two(places, keep, came, out):
    out[...] = (keep[...].astype(F32) + came[...].astype(F32)).astype(LOW)


def input_sum(places, rows, w, res1, out):
    heads, count, tokens = rows.shape
    total = dot_tn(rows[...].reshape(heads * count, tokens), w[...].reshape(heads * count, -1))
    out[...] = res1[...] + total


def place_pieces(places, held, full, layouts):
    near, core = places[0], places[1]
    width = held[0].shape[1]
    for off in range(4):
        chip = near ^ off
        mine, other = held[off][...], held[4 + off][...]
        sides = (jnp.where(core == 0, mine, other), jnp.where(core == 0, other, mine))
        for at, rows, start, outer in layouts:
            low_bit, high_bit = chip & 1, chip >> 1
            order = 2 * low_bit + high_bit if outer == 1 else 2 * high_bit + low_bit
            to = pl.multiple_of(start + order * rows, 16)
            for side in range(2):
                full[pl.ds(to, rows), side * width : (side + 1) * width] = sides[side][
                    at : at + rows
                ].astype(F32)


def ffn_place(places, *refs):
    held = [ref.at[off] for ref in refs[:2] for off in range(4)]
    down, up, full = refs[2:]
    rows = held[0].shape[0] // 2
    place_pieces(places, held, full, [(0, rows, 0, 1)])
    down[...] = full[...].T
    place_pieces(places, held, up, [(rows, rows, 0, 2)])


def collect(places, *refs):
    for off in range(4):
        refs[4][off] = refs[off][...]


def attn_place(places, *refs):
    held = [ref.at[off] for ref in refs[:2] for off in range(4)]
    qkv, w_out, small, up_bias, qv_bias, full = refs[2:]
    width = held[0].shape[1]
    count = w_out.shape[0]
    rows = count // 2
    more = held[0].shape[0] - rows
    place_pieces(places, held, full, [(0, rows, 0, 1), (rows, more, 4 * rows, 2)])
    for c in range(3):
        qkv[c] = full[c * count : (c + 1) * count]
    w_out[...] = full[3 * count : 4 * count]
    at = 4 * count
    lines = full[at : at + 16, :width] + full[at : at + 16, width:]
    for i in range(6):
        small[i : i + 1, :width] = lines[2 * i : 2 * i + 1]
        small[i : i + 1, width:] = lines[2 * i + 1 : 2 * i + 2]
    up_bias[...] = jnp.concatenate([lines[12:13], lines[13:14]], 1).reshape(2 * width)
    qv_bias[0:1] = lines[14:15, :count]
    qv_bias[1:2] = lines[14:15, count : 2 * count]


def bias_parts(values):
    rows, rest = [], values
    for _ in range(3):
        rows.append(lax.reduce_precision(rest, 8, 7))
        rest = rest - rows[-1]
    return jnp.stack(rows).astype(LOW)


def gather_back(piece):
    return [piece] + [swap(piece, "near", off) for off in range(1, 4)]


def per_device(
    tokens,
    segment_ids,
    w_qkv,
    b_qv,
    w_out,
    b_out,
    ln1_gain,
    ln1_bias,
    w_up,
    b_up,
    w_down,
    b_down,
    ln2_gain,
    ln2_bias,
    cotangent,
):
    CHAIN.clear()
    width = tokens.shape[1]
    own_rows = cotangent.shape[0]
    local_width = w_qkv.shape[2]
    heads = lax.axis_size("head")
    z = lax.axis_index("head")
    core = lax.axis_index("core")
    near = lax.axis_index("near")
    hidden_units = w_up.shape[1]
    chunk = hidden_units // heads
    half = width // 2
    rows3 = 3 * local_width
    places = jnp.stack([near, core, z]).astype(jnp.int32)

    shard = jnp.concatenate([w_qkv.transpose(0, 2, 1).reshape(rows3, width), w_out], 0)
    piece_rows = shard.shape[0] // 8
    bias = jnp.pad(bias_parts(b_qv.reshape(-1)), ((0, 13), (0, width - 2 * local_width)))
    piece = lax.dynamic_slice_in_dim(shard, (near * 2 + core) * piece_rows, piece_rows, 0)
    piece = jnp.concatenate([piece, bias], 0)
    first_hop = [swap(piece, "head", d) for d in range(1, heads)]

    seg = lax.dynamic_slice_in_dim(segment_ids, z * own_rows, own_rows, 0)
    tok_own = lax.dynamic_slice_in_dim(tokens, z * own_rows, own_rows, 0)
    attend_outs = [
        ((heads, rows3, own_rows), LOW),
        ((heads, local_width, own_rows), LOW),
        ((heads, 8, own_rows), F32),
        ((heads, rows3, width), LOW),
        ((heads, local_width, width), LOW),
    ]
    macs = rows3 * width * own_rows + 6 * own_rows * own_rows * 256
    orders = [(1, 2) if d % 2 else (2, 1) for d in range(heads)]
    nexts = [swap(first_hop[d - 1], "near", orders[d][0]) for d in range(1, heads)]

    def pair_up(d, after):
        (pair,) = run_whole(
            pair_rows, places, [first_hop[d - 1], nexts[d - 1]],
            [((2, piece_rows, width), LOW)], after=after, chain=False,
        )
        return pair

    pairs = [pair_up(1, first_hop[1:])]
    ins = [tok_own, shard, bias, seg[None]]
    made = run_whole(
        own_attention, places, ins, attend_outs, macs=macs, after=pairs, chain=False
    )
    pairs += [pair_up(d, nexts[1:] + [made[2]]) for d in range(2, heads)]
    rests = [swap(pairs[d - 1], "near", orders[d][1]) for d in range(1, heads)]
    for d in range(1, heads):
        pair, rest = pairs[d - 1], rests[d - 1]
        sent = rest
        if d == heads - 1:
            (sent,) = run_whole(
                copy_rows, places, [rest], [(rest.shape, LOW)], after=[second_log], chain=False
            )
        ins = [tok_own, pair, rest, swap_core(pair), swap_core(sent), first_hop[d - 1], seg[None]]
        made = run_whole(
            functools.partial(far_attention, d, orders[d]), places, ins, attend_outs,
            [pltpu.VMEM(shard.shape, LOW)], macs, alias=made, chain=False, weight=100,
        )
        if d == 1:
            second_log = made[2]
    qkvs, mixes, logs, w_qkvs, w_outs = made

    mixes_far = swap_core(mixes)

    square = (own_rows, width)
    tiles = (heads, own_rows, half)
    ins = [
        tok_own, mixes, w_outs, b_out, ln1_gain, ln1_bias, b_down, ln2_gain, ln2_bias,
        w_up, b_up.reshape(heads, 1, chunk), w_down, cotangent,
    ]
    outs = [
        (tiles, LOW),
        (tiles, LOW),
        ((4, own_rows, half), LOW),
        ((heads, own_rows, chunk), LOW),
        (square, F32),
        ((own_rows, 1), F32),
        (square, F32),
        (square, LOW),
        ((8, width), F32),
        ((own_rows, half), LOW),
    ]
    scratch = [
        pltpu.VMEM(square, F32),
        pltpu.VMEM(square, LOW),
        pltpu.VMEM((own_rows, hidden_units), LOW),
        pltpu.VMEM(square, F32),
    ]
    ffn_macs = 2 * own_rows * width * hidden_units
    (
        act_send, act_own, ends, slope, unit1, inv1, res2, layer_output, small_two, tok_send,
    ) = run_whole(feed_forward, places, ins, outs, scratch, ffn_macs)
    tok_far = swap_core(tok_send)
    act_far = swap_core(act_send)
    ends_far = swap_core(ends)

    outs = [(tiles, LOW), (tiles, LOW), ((heads, 1, chunk), F32)]
    scratch = [pltpu.VMEM((own_rows, chunk), LOW)]
    inner_send, inner_own, up_bias = run_whole(
        inner_back, places, [ends, w_down, slope], outs, scratch, ffn_macs // 2, [mixes_far]
    )
    inner_far = swap_core(inner_send)


    def ffn_unit(bit, own, far, which, weight):
        outs = [((heads, half, half), LOW)] * 2
        both = [pltpu.VMEM((width, 2 * own_rows), LOW)]
        kernel = functools.partial(ffn_grad, bit, which)
        ins = [own, far, ends, ends_far]
        return run_whole(kernel, places, ins, outs, both, ffn_macs // 2, weight=weight)

    made = ffn_unit(1, act_own, act_far, 1, 8) + ffn_unit(2, inner_own, inner_far, 0, LIGHT)
    x_send, x_keep, y_send, y_keep = made
    ffn_held = (x_keep, swap(x_send, "near", 1), y_keep, swap(y_send, "near", 2))

    outs = [((own_rows, half), LOW), (square, F32), (square, LOW), ((8, width), F32)]
    ins = [inner_own, inner_send, w_up, res2, unit1, inv1, ln1_gain]
    grad_send, res1, grad_attended, small_one = run_whole(
        hidden_back, places, ins, outs, macs=ffn_macs // 2, weight=LIGHT
    )
    grad_far = swap_core(grad_send)

    def second(x_keep, x_came, y_keep, y_came, macs=0):
        arrays = (x_keep, x_came, y_keep, y_came)
        shapes = [(heads, a.shape[1] // 2, half) for a in (x_keep, x_keep, y_keep, y_keep)]
        outs = [(shape, LOW) for shape in shapes]
        kernel = functools.partial(add_split, (2, 1))
        return run_whole(kernel, places, arrays, outs, macs=macs)

    def third(x_keep, x_came, y_keep, y_came):
        arrays = (x_keep, x_came, y_keep, y_came)
        shape = (heads // 2, x_keep.shape[1] + y_keep.shape[1], half)
        send, keep = run_whole(add_parts, places, arrays, [(shape, LOW)] * 2)
        return keep, swap(send, "head", 1)

    def fourth(keep, came):
        shape = keep.shape[1:]
        mine, other = run_whole(add_pair, places, [keep, came], [(shape, LOW)] * 2)
        return mine, swap(other, "head", 2)

    def fifth(mine, came):
        (total,) = run_whole(add_two, places, [mine, came], [(mine.shape, LOW)])
        bit = 1
        while bit < lax.axis_size("far"):
            total = (total.astype(F32) + swap(total, "far", bit).astype(F32)).astype(LOW)
            bit *= 2
        return total

    def cross(made, flip):
        x_send, x_keep, y_send, y_keep = made
        x_bit, y_bit = (2, 1) if flip else (1, 2)
        return x_keep, swap(x_send, "near", x_bit), y_keep, swap(y_send, "near", y_bit)

    outs = [((heads, rows3, own_rows), LOW), ((heads, 8, rows3), F32)]
    ins = [qkvs, w_outs, grad_attended, logs, seg[None]]
    rows, qkv_bias = run_whole(attention_back, places, ins, outs)
    rows_far = swap_core(rows)

    outs = [(square, F32, whole(square))]
    ins = [(a, whole(a.shape)) for a in (rows, w_qkvs, res1)]
    (input_grad,) = run(input_sum, places, (1,), ins, outs, weight=LIGHT)
    ffn_held = cross(second(*ffn_held, ffn_macs), True)
    ins = [
        rows, rows_far, tok_own, tok_far, mixes, mixes_far, grad_attended, grad_far,
        small_one, small_two, up_bias, qkv_bias,
    ]
    outs = [
        ((heads, r, half), LOW) for r in (half // 2, (half + EXTRA) // 2) for _ in range(2)
    ]
    made = run_whole(attn_grad, places, ins, outs)
    attn_held = cross(made, False)

    ffn_held = third(*ffn_held)
    attn_held = cross(second(*attn_held), True)
    ffn_held = fourth(*ffn_held)
    attn_held = third(*attn_held)
    ffn_held = gather_back(fifth(*ffn_held))
    attn_held = fourth(*attn_held)
    attn_held = gather_back(fifth(*attn_held))

    def both_cores(held):
        shape = (heads,) + held[0].shape
        (pieces,) = run_whole(collect, places, held, [(shape, LOW)])
        return [(a, whole(shape)) for a in (pieces, swap_core(pieces))]

    ffn_held = both_cores(ffn_held)
    outs = [(shape, F32, whole(shape)) for shape in ((chunk, width), (width, chunk))]
    grad_down, grad_up = run(
        ffn_place, places, (1,), ffn_held, outs, [pltpu.VMEM((width, chunk), F32)]
    )
    attn_held = both_cores(attn_held)
    shapes = [
        (3, local_width, width),
        (local_width, width),
        (6, width),
        (chunk,),
        (2, local_width),
    ]
    grad_qkv, grad_out, grad_small, grad_up_bias, grad_qv_bias = run(
        attn_place,
        places,
        (1,),
        attn_held,
        [(shape, F32, whole(shape)) for shape in shapes],
        [pltpu.VMEM((width + EXTRA, width), F32)],
    )
    return (
        layer_output,
        input_grad,
        grad_qkv.transpose(0, 2, 1),
        grad_qv_bias,
        grad_out,
        grad_up,
        grad_up_bias,
        grad_down,
        grad_small,
    )


def solution(mesh):
    batch, heads = mesh.devices.shape
    mesh = Mesh(
        mesh.devices.reshape(batch // 8, 4, 2, heads), ("far", "near", "core", "head")
    )
    group = ("far", "near", "core")
    everyone = group + ("head",)
    in_specs = (
        P(group, None),
        P(group),
        P(None, None, "head"),
        P(None, "head"),
        P("head", None),
        P(),
        P(),
        P(),
        P(),
        P(),
        P(),
        P(),
        P(),
        P(),
        P(everyone, None),
    )
    out_specs = (
        P(everyone, None),
        P(everyone, None),
        P(None, None, "head"),
        P(None, "head"),
        P("head", None),
        P(None, "head"),
        P("head"),
        P("head", None),
        P(),
    )
    return jax.shard_map(
        per_device, mesh=mesh, in_specs=in_specs, out_specs=out_specs, check_vma=False
    )
```

```python
import functools
import math

import jax
import jax.numpy as jnp
from jax import lax
from jax.experimental import pallas as pl
from jax.experimental.pallas import tpu as pltpu
from jax.sharding import Mesh
from jax.sharding import PartitionSpec as P

HEAD_DIM = 64
SLOT = 512
LOW = jnp.bfloat16
F32 = jnp.float32
LOG2E = math.log2(math.e)
SCORE_SCALE = HEAD_DIM ** (-0.5) * LOG2E
SPARE_BYTES = 12 * 2**20
EXTRA = 64
LIGHT = 0.01
LANES = 128
CHAIN = []
TAIL_SLOPE = 0.36
TAIL = (
    0.14371304537508633,
    0.14177245466203425,
    0.1397192603907239,
    0.026549325413860486,
    0.18095403134327948,
    -0.1797647161697652,
    0.047056295581175855,
)


def swap(value, axis, bit):
    size = lax.axis_size(axis)
    return lax.ppermute(value, axis, [(i, i ^ bit) for i in range(size)])


def swap_core(value):
    return swap(value, "core", 1)


def dot(a, b):
    return jnp.dot(a, b, preferred_element_type=F32)


def dot_nt(a, b):
    return lax.dot_general(a, b, (((1,), (1,)), ((), ())), preferred_element_type=F32)


def dot_tn(a, b):
    return lax.dot_general(a, b, (((0,), (0,)), ((), ())), preferred_element_type=F32)


def whole(shape):
    return pl.BlockSpec(shape, lambda *args: (0,) * len(shape), pipeline_mode=pl.Buffered(1))


def run(
    kernel, places, grid, ins, outs, scratch=(), macs=0, after=(), alias=(), weight=8, chain=True
):
    moved = sum(a.size * a.dtype.itemsize for a, spec in ins)
    moved += sum(math.prod(shape) * jnp.dtype(kind).itemsize for shape, kind, spec in outs)
    after = list(after) + (CHAIN if chain else [])
    count, unread = len(ins), len(alias) + len(after)
    results = len(outs)
    flag = (8, 128)
    if chain:
        outs = outs + [(flag, F32, whole(flag))]

    def body(places, *refs):
        made = refs[count + unread :]
        if chain:

            @pl.when(pl.program_id(0) == 0)
            def _():
                made[results][...] = jnp.zeros(flag, F32)

        kernel(places, *refs[:count], *made[:results], *made[len(outs) :])

    held = pl.BlockSpec(memory_space=pl.ANY)
    room = SPARE_BYTES
    for shape, kind, spec in outs + [(a.shape, a.dtype, spec) for a, spec in ins]:
        if spec.block_shape is not None:
            block = math.prod(1 if n is None else n for n in spec.block_shape)
            copies = 2 if spec.pipeline_mode is None else 1
            room += copies * block * jnp.dtype(kind).itemsize
    for ref in scratch:
        if hasattr(ref, "shape") and ref.dtype in (LOW, F32):
            room += math.prod(ref.shape) * jnp.dtype(ref.dtype).itemsize
    made = pl.pallas_call(
        body,
        name=getattr(kernel, "func", kernel).__name__,
        grid_spec=pltpu.PrefetchScalarGridSpec(
            num_scalar_prefetch=1,
            grid=grid,
            in_specs=[spec for a, spec in ins] + [held] * unread,
            out_specs=[spec for shape, kind, spec in outs],
            scratch_shapes=list(scratch),
        ),
        out_shape=[jax.ShapeDtypeStruct(shape, kind) for shape, kind, spec in outs],
        input_output_aliases={1 + count + i: i for i in range(len(alias))},
        compiler_params=pltpu.CompilerParams(vmem_limit_bytes=room),
        cost_estimate=pl.CostEstimate(
            flops=int(2 * macs * weight), bytes_accessed=int(moved * weight), transcendentals=0
        ),
    )(places, *[a for a, spec in ins], *alias, *after)
    if chain:
        CHAIN[:] = made[results:]
    return made[:results]


def run_whole(
    kernel, places, ins, outs, scratch=(), macs=0, after=(), alias=(), weight=8, chain=True
):
    pairs = [a if isinstance(a, tuple) else (a, pltpu.VMEM) for a in ins]
    after = list(after) + (CHAIN if chain else [])
    count, unread, results = len(pairs), len(alias) + len(after), len(outs)
    if chain:
        outs = outs + [((8, 128), F32)]

    def body(places, *refs):
        made = refs[count + unread :]
        if chain:
            made[results][...] = jnp.zeros((8, 128), F32)
        kernel(places, *refs[:count], *made[:results], *made[len(outs) :])

    room = SPARE_BYTES
    for ref in scratch:
        if hasattr(ref, "shape") and ref.dtype in (LOW, F32):
            room += math.prod(ref.shape) * jnp.dtype(ref.dtype).itemsize
    spaces = [pltpu.SMEM] + [space for a, space in pairs]
    spaces += [pltpu.VMEM] * len(alias) + [pl.ANY] * len(after)
    made = pl.pallas_call(
        body,
        name=getattr(kernel, "func", kernel).__name__,
        in_specs=[pl.BlockSpec(memory_space=space) for space in spaces],
        out_specs=[pl.BlockSpec(memory_space=pltpu.VMEM)] * len(outs),
        scratch_shapes=list(scratch),
        out_shape=[jax.ShapeDtypeStruct(shape, kind) for shape, kind in outs],
        input_output_aliases={1 + count + i: i for i in range(len(alias))},
        compiler_params=pltpu.CompilerParams(vmem_limit_bytes=room),
        cost_estimate=pl.CostEstimate(
            flops=int(2 * macs * weight), bytes_accessed=0, transcendentals=0
        ),
    )(places, *[a for a, space in pairs], *alias, *after)
    if chain:
        CHAIN[:] = made[results:]
    return made[:results]


def each(count, size, body):
    def step(i, carry):
        body(pl.ds(pl.multiple_of(i * size, size), size))
        return carry

    lax.fori_loop(0, count // size, step, 0)


def tiles_of(count, size):
    return [slice(at, at + size) for at in range(0, count, size)]


def three_parts(values):
    parts, rest = [], values
    for _ in range(3):
        parts.append(rest.astype(LOW))
        rest = rest - parts[-1].astype(F32)
    return parts


def segment_rows(seg_row):
    shape = (16, seg_row.shape[1])
    place = lax.broadcasted_iota(jnp.int32, shape, 0)
    same = place - 1 == seg_row
    keys = jnp.where(same, 1.0, jnp.where((place >= 8) & (place < 11), 1.0, 0.0))
    queries = jnp.where(same | (place > 4), 0.0, -1e30)
    return keys.astype(LOW), queries.astype(LOW)


def attend_heads(tok, w_rows, bias, seg_row, qkv_ref, mix_ref, log_ref):
    width = w_rows.shape[0] // 3
    added = dot_tn(bias[:, : 2 * width], jnp.ones((bias.shape[0], tok.shape[0]), LOW))
    qkv = dot_nt(w_rows, tok)
    parts = (
        (qkv[:width] + added[:width]).astype(LOW),
        qkv[width : 2 * width].astype(LOW),
        (qkv[2 * width :] + added[width:]).astype(LOW),
    )
    for c in range(3):
        qkv_ref[c * width : (c + 1) * width] = parts[c]
    more_k, more_q = segment_rows(seg_row)
    for head in range(width // HEAD_DIM):
        q, k, v = (part[head * HEAD_DIM : (head + 1) * HEAD_DIM] for part in parts)
        scores = dot_tn(jnp.concatenate([k, more_k], 0), jnp.concatenate([q, more_q], 0))
        columns, tops, totals = [], [], []
        for tile in tiles_of(scores.shape[1], LANES):
            top = jnp.max(scores[:, tile], 0, keepdims=True)
            total, column = 0.0, []
            for rows in tiles_of(scores.shape[0], 64):
                exponent = jnp.exp2((scores[rows, tile] - top) * SCORE_SCALE)
                total = total + jnp.sum(exponent, 0, keepdims=True)
                column.append(exponent.astype(LOW))
            columns.append(jnp.concatenate(column, 0))
            tops.append(top)
            totals.append(total)
        total = jnp.concatenate(totals, 1)
        mixed = dot(v, jnp.concatenate(columns, 1)) * (1.0 / total)
        mix_ref[head * HEAD_DIM : (head + 1) * HEAD_DIM] = mixed.astype(LOW)
        top = jnp.concatenate(tops, 1)
        log_ref[head : head + 1] = top + jnp.log2(total) * (1.0 / SCORE_SCALE)


def own_attention(
    places, tok, w, bias, seg_row, qkv_ref, mix_ref, log_ref, w_qkv, w_out
):
    count = qkv_ref.shape[1]
    w_qkv[0] = w[:count]
    w_out[0] = w[count:]
    attend_heads(
        tok[...], w[:count], bias[...], seg_row[...], qkv_ref.at[0], mix_ref.at[0], log_ref.at[0]
    )


def far_attention(
    d, order, places, tok, pair, rest, pair_far, rest_far, hop, seg_row,
    qkv_ref, mix_ref, log_ref, w_qkv, w_out, w_ref,
):
    first, second = order
    rows, count = pair.shape[1], qkv_ref.shape[1]
    me = places[0] * 2 + places[1]
    for other, held in enumerate(((pair, rest), (pair_far, rest_far))):
        for two, block in enumerate(held):
            for one in range(2):
                owner = me ^ (other + 2 * first * one + 2 * second * two)
                w_ref[pl.ds(pl.multiple_of(owner * rows, rows), rows)] = block[one]
    w_qkv[d] = w_ref[:count]
    w_out[d] = w_ref[count:]
    attend_heads(
        tok[...],
        w_ref[:count],
        hop[rows:],
        seg_row[...],
        qkv_ref.at[d],
        mix_ref.at[d],
        log_ref.at[d],
    )


def copy_rows(places, rows, out):
    out[...] = rows[...]


def pair_rows(places, *refs):
    count = len(refs) // 3
    for i, out in enumerate(refs[2 * count :]):
        out[0] = refs[2 * i][: out.shape[1]]
        out[1] = refs[2 * i + 1][: out.shape[1]]


def norm_stats(v):
    centred = v - jnp.mean(v, -1, keepdims=True)
    inv = lax.rsqrt(jnp.mean(centred * centred, -1, keepdims=True) + 1e-05)
    return centred * inv, inv


def norm_back(upstream, unit, inv, gain):
    scaled = upstream * gain
    inner = jnp.mean(scaled * unit, -1, keepdims=True)
    return inv * (scaled - jnp.mean(scaled, -1, keepdims=True) - unit * inner)


def gelu_both(pre):
    power = jnp.exp2(pre * pre * (-0.5 * LOG2E))
    base = 1.0 + TAIL_SLOPE * jnp.abs(pre)
    t = pl.reciprocal(base, approx=True)
    tail = TAIL[6] * t + TAIL[5]
    for c in TAIL[4::-1]:
        tail = tail * t + c
    tail = tail * (t * power)
    cumul = jnp.where(pre < 0.0, tail, 1.0 - tail)
    return (pre * cumul).astype(LOW), cumul + pre * (power * 0.3989422804014327)


def share(core, wide, mine, other):
    half = wide.shape[1] // 2
    left, right = wide[:, :half], wide[:, half:]
    mine[...] = jnp.where(core == 0, left, right)
    other[...] = jnp.where(core == 0, right, left)


def feed_forward(
    places, tok, mix, w_out, b_out, gain1, shift1, b_down, gain2, shift2, w_up, b_up, w_down, cot,
    send, own, ends, slope, unit1, inv1, res2, out, small, tok_send,
    hidden, low, acts, total,
):
    heads, width, half = mix.shape[0], low.shape[1], send.shape[2]
    chunk = 2 * half
    core, z = places[1], places[2]
    b_out, gain1, shift1, b_down, gain2, shift2 = (
        ref[...].reshape(1, -1) for ref in (b_out, gain1, shift1, b_down, gain2, shift2)
    )
    tok_send[...] = jnp.where(core == 0, tok[:, half:], tok[:, :half])
    total[...] = dot_tn(mix[...].reshape(width, low.shape[0]), w_out[...].reshape(width, width))

    def first_norm(rows):
        unit, inv = norm_stats(tok[rows].astype(F32) + (total[rows] + b_out))
        unit1[rows] = unit
        inv1[rows] = inv
        one = unit * gain1 + shift1
        hidden[rows] = one
        one_low = one.astype(LOW)
        low[rows] = one_low
        ends[0, rows] = one_low[:, :half]
        ends[1, rows] = one_low[:, half:]

    each(low.shape[0], 64, first_norm)

    def one_unit(h, carry):
        start = pl.multiple_of(h * chunk, chunk)
        for at in tiles_of(chunk, 256):
            wide = pl.ds(pl.multiple_of(start + at.start, 256), 256)
            pre = dot(low[...], w_up[:, wide])
            for rows in tiles_of(pre.shape[0], 32):
                act, tilt = gelu_both(pre[rows] + b_up[h, :, at])
                slope[h, rows, at] = tilt.astype(LOW)
                acts[rows, wide] = act
        left = acts[:, pl.ds(start, half)]
        right = acts[:, pl.ds(pl.multiple_of(start + half, 128), half)]
        own[z ^ h] = jnp.where(core == 0, left, right)
        send[z ^ h] = jnp.where(core == 0, right, left)
        return carry

    lax.fori_loop(0, heads, one_unit, 0)
    total[...] = dot(acts[...], w_down[...])
    small[...] = jnp.zeros_like(small)

    def second_norm(rows):
        unit, inv = norm_stats(hidden[rows] + (total[rows] + b_down))
        out[rows] = (unit * gain2 + shift2).astype(LOW)
        upstream = cot[rows].astype(F32)
        grad = norm_back(upstream, unit, inv, gain2)
        res2[rows] = grad
        grad_low = grad.astype(LOW)
        ends[2, rows] = grad_low[:, :half]
        ends[3, rows] = grad_low[:, half:]
        for i, term in enumerate((grad_low.astype(F32), upstream * unit, upstream)):
            small[i : i + 1] += jnp.sum(term, 0, keepdims=True)

    each(low.shape[0], 64, second_norm)


def inner_back(places, ends, w_down, slope, send, own, bias, inners):
    heads, _, chunk = slope.shape
    core, z = places[1], places[2]
    branch = jnp.concatenate([ends[2], ends[3]], 1)
    for h in range(heads):
        for at in tiles_of(chunk, 256):
            grad_act = dot_nt(branch, w_down[h * chunk + at.start : h * chunk + at.stop])
            total = 0.0
            for rows in tiles_of(grad_act.shape[0], 32):
                inner = (grad_act[rows] * slope[h, rows, at].astype(F32)).astype(LOW)
                inners[rows, at] = inner
                total = total + jnp.sum(inner.astype(F32), 0, keepdims=True)
            bias[h, :, at] = total
        share(core, inners, own.at[z ^ h], send.at[z ^ h])


def hidden_back(places, own, sent, w_up, res2, unit1, inv1, gain1, send, res1, low, small):
    heads, count, half = own.shape
    core, z = places[1], places[2]
    sides = []
    for h in range(heads):
        mine, other = own[z ^ h], sent[z ^ h]
        sides += [jnp.where(core == 0, mine, other), jnp.where(core == 0, other, mine)]
    product = dot_nt(jnp.concatenate(sides, 1), w_up[...])
    gain = gain1[...].reshape(1, -1)
    sums = [0.0] * 3
    for rows in tiles_of(count, 32):
        grad, unit = product[rows] + res2[rows], unit1[rows]
        result = norm_back(grad, unit, inv1[rows], gain)
        res1[rows] = result
        result_low = result.astype(LOW)
        low[rows] = result_low
        send[rows] = jnp.where(core == 0, result_low[:, half:], result_low[:, :half])
        for i, term in enumerate((result_low.astype(F32), grad * unit, grad)):
            sums[i] = sums[i] + jnp.sum(term, 0, keepdims=True)
    for i in range(3):
        small[i : i + 1] = sums[i]


def shard_back(qkv, w_out, grad, log_ref, more_k, more_q, rows_ref, bias_ref):
    width = qkv.shape[0] // 3
    grad_mixed = dot_nt(w_out[...], grad[...]).astype(LOW)
    scale = HEAD_DIM ** (-0.5)
    for head in range(width // HEAD_DIM):
        places_of = [c * width + head * HEAD_DIM for c in range(3)]
        q, k, v = (qkv[at : at + HEAD_DIM] for at in places_of)
        g = grad_mixed[head * HEAD_DIM : (head + 1) * HEAD_DIM]
        logs = jnp.concatenate(three_parts(-log_ref[head : head + 1]), 0)
        with_logs = jnp.concatenate([more_q[:8], logs, more_q[11:]], 0)
        scores = dot_tn(jnp.concatenate([k, more_k], 0), jnp.concatenate([q, with_logs], 0))
        grad_probs = dot_tn(v, g)
        attends, grads = [], []
        for tile in tiles_of(scores.shape[1], LANES):
            inner, kept, lows, parts = 0.0, [], [], []
            tall = tiles_of(scores.shape[0], 64)
            for down in tall:
                attend = jnp.exp2(scores[down, tile] * SCORE_SCALE)
                inner = inner + jnp.sum(attend * grad_probs[down, tile], 0, keepdims=True)
                kept.append(attend)
                lows.append(attend.astype(LOW))
            for down, attend in zip(tall, kept):
                parts.append((attend * (grad_probs[down, tile] - inner)).astype(LOW))
            attends.append(jnp.concatenate(lows, 0))
            grads.append(jnp.concatenate(parts, 0))
        attend_low = jnp.concatenate(attends, 1)
        grad_scores = jnp.concatenate(grads, 1)
        grad_v = dot_nt(g, attend_low)
        grad_q = dot(k, grad_scores) * scale
        grad_k = dot_nt(q, grad_scores) * scale
        for at, value in zip(places_of, (grad_q, grad_k, grad_v)):
            rows_ref[at : at + HEAD_DIM] = value.astype(LOW)
    ones = jnp.ones((8, rows_ref.shape[1]), LOW)
    bias_ref[...] = dot_nt(ones, rows_ref[...])


def attention_back(places, qkv, w_out, grad, log_ref, seg_row, rows_ref, bias_ref):
    more_k, more_q = segment_rows(seg_row[...])

    def shard(d, carry):
        refs = (ref.at[d] for ref in (rows_ref, bias_ref))
        shard_back(qkv.at[d], w_out.at[d], grad, log_ref.at[d], more_k, more_q, *refs)
        return carry

    lax.fori_loop(0, qkv.shape[0], shard, 0)


def split_rows(value, high, send, keep):
    rows = value.shape[0] // 2
    low = value.astype(LOW)
    send[...] = jnp.where(high, low[:rows], low[rows:])
    keep[...] = jnp.where(high, low[rows:], low[:rows])


def is_high(places, bit):
    return (places[0] & bit) != 0


def ffn_grad(bit, which, places, units, units_far, ends, ends_far, send, keep, both):
    half, count = ends.shape[2], ends.shape[1]
    for side in range(2):
        rows = slice(side * half, (side + 1) * half)
        both[rows, :count] = ends[2 * which + side].T
        both[rows, count:] = ends_far[2 * which + side].T
    for d in range(0, units.shape[0], 2):
        left, right = (jnp.concatenate([units[d + i], units_far[d + i]], 0) for i in range(2))
        total = dot(both[...], jnp.concatenate([left, right], 1))
        for i in range(2):
            part = total[:, i * half : (i + 1) * half]
            split_rows(part, is_high(places, bit), send.at[d + i], keep.at[d + i])


def attn_grad(
    places, rows, rows_far, tok, tok_far, mix, mix_far, grad, grad_far,
    small_one, small_two, up_bias, qkv_bias, send_x, keep_x, send_y, keep_y,
):
    width = mix.shape[1]
    half = tok_far.shape[1]
    core, z = places[1], places[2]

    def both(near, far):
        mine = jnp.where(core == 0, near[:, :half], near[:, half:])
        return jnp.concatenate([mine, far[...]], 0)

    tok_both, grad_both = both(tok, tok_far), both(grad, grad_far)
    for d in range(rows.shape[0]):
        qkv = dot(jnp.concatenate([rows[d], rows_far[d]], 1), tok_both)
        out = dot(jnp.concatenate([mix[d], mix_far[d]], 1), grad_both)
        lines = []
        for held in (small_one, small_two):
            for i in range(3):
                lines += [held[i : i + 1, :half], held[i : i + 1, half:]]
        line, bias = up_bias[z ^ d], qkv_bias[d]
        lines += [line[:, :half], line[:, half:]]
        lines.append(jnp.concatenate([bias[0:1, :width], bias[0:1, 2 * width :]], 1))
        lines.append(jnp.zeros((EXTRA - len(lines), half), F32))
        total = jnp.concatenate([qkv, out] + lines, 0)
        split_rows(total[:half], is_high(places, 1), send_x.at[d], keep_x.at[d])
        split_rows(total[half:], is_high(places, 2), send_y.at[d], keep_y.at[d])


def add_split(bits, places, *refs):
    for i, bit in enumerate(bits):
        keep, came = refs[2 * i : 2 * i + 2]
        send, left = refs[2 * (len(bits) + i) : 2 * (len(bits) + i) + 2]
        for d in range(keep.shape[0]):
            total = keep[d].astype(F32) + came[d].astype(F32)
            split_rows(total, is_high(places, bit), send.at[d], left.at[d])


def add_parts(places, keep_a, came_a, keep_b, came_b, send, keep):
    rows = keep_a.shape[1]
    for d in range(keep_a.shape[0]):
        out = (send if d % 2 else keep).at[d // 2]
        out[:rows] = (keep_a[d].astype(F32) + came_a[d].astype(F32)).astype(LOW)
        out[rows:] = (keep_b[d].astype(F32) + came_b[d].astype(F32)).astype(LOW)


def add_pair(places, keep, came, *outs):
    for i, out in enumerate(outs):
        out[...] = (keep[i].astype(F32) + came[i].astype(F32)).astype(LOW)


def add_two(places, keep, came, out):
    out[...] = (keep[...].astype(F32) + came[...].astype(F32)).astype(LOW)


def input_sum(places, rows, w, res1, out):
    heads, count, tokens = rows.shape
    total = dot_tn(rows[...].reshape(heads * count, tokens), w[...].reshape(heads * count, -1))
    out[...] = res1[...] + total


def place_pieces(places, held, full, layouts):
    near, core = places[0], places[1]
    width = held[0].shape[1]
    for off in range(4):
        chip = near ^ off
        mine, other = held[off][...], held[4 + off][...]
        sides = (jnp.where(core == 0, mine, other), jnp.where(core == 0, other, mine))
        for at, rows, start, outer in layouts:
            low_bit, high_bit = chip & 1, chip >> 1
            order = 2 * low_bit + high_bit if outer == 1 else 2 * high_bit + low_bit
            to = pl.multiple_of(start + order * rows, 16)
            for side in range(2):
                full[pl.ds(to, rows), side * width : (side + 1) * width] = sides[side][
                    at : at + rows
                ].astype(F32)


def ffn_place(places, *refs):
    held = [ref.at[off] for ref in refs[:2] for off in range(4)]
    down, up, full = refs[2:]
    rows = held[0].shape[0] // 2
    place_pieces(places, held, full, [(0, rows, 0, 1)])
    down[...] = full[...].T
    place_pieces(places, held, up, [(rows, rows, 0, 2)])


def collect(places, *refs):
    for off in range(4):
        refs[4][off] = refs[off][...]


def attn_place(places, *refs):
    held = [ref.at[off] for ref in refs[:2] for off in range(4)]
    qkv, w_out, small, up_bias, qv_bias, full = refs[2:]
    width = held[0].shape[1]
    count = w_out.shape[0]
    rows = count // 2
    more = held[0].shape[0] - rows
    place_pieces(places, held, full, [(0, rows, 0, 1), (rows, more, 4 * rows, 2)])
    for c in range(3):
        qkv[c] = full[c * count : (c + 1) * count]
    w_out[...] = full[3 * count : 4 * count]
    at = 4 * count
    lines = full[at : at + 16, :width] + full[at : at + 16, width:]
    for i in range(6):
        small[i : i + 1, :width] = lines[2 * i : 2 * i + 1]
        small[i : i + 1, width:] = lines[2 * i + 1 : 2 * i + 2]
    up_bias[...] = jnp.concatenate([lines[12:13], lines[13:14]], 1).reshape(2 * width)
    qv_bias[0:1] = lines[14:15, :count]
    qv_bias[1:2] = lines[14:15, count : 2 * count]


def bias_parts(values):
    rows, rest = [], values
    for _ in range(3):
        rows.append(lax.reduce_precision(rest, 8, 7))
        rest = rest - rows[-1]
    return jnp.stack(rows).astype(LOW)


def gather_back(piece):
    return [piece] + [swap(piece, "near", off) for off in range(1, 4)]


def per_device(
    tokens,
    segment_ids,
    w_qkv,
    b_qv,
    w_out,
    b_out,
    ln1_gain,
    ln1_bias,
    w_up,
    b_up,
    w_down,
    b_down,
    ln2_gain,
    ln2_bias,
    cotangent,
):
    CHAIN.clear()
    width = tokens.shape[1]
    own_rows = cotangent.shape[0]
    local_width = w_qkv.shape[2]
    heads = lax.axis_size("head")
    z = lax.axis_index("head")
    core = lax.axis_index("core")
    near = lax.axis_index("near")
    hidden_units = w_up.shape[1]
    chunk = hidden_units // heads
    half = width // 2
    rows3 = 3 * local_width
    places = jnp.stack([near, core, z]).astype(jnp.int32)

    shard = jnp.concatenate([w_qkv.transpose(0, 2, 1).reshape(rows3, width), w_out], 0)
    piece_rows = shard.shape[0] // 8
    bias = jnp.pad(bias_parts(b_qv.reshape(-1)), ((0, 13), (0, width - 2 * local_width)))
    piece = lax.dynamic_slice_in_dim(shard, (near * 2 + core) * piece_rows, piece_rows, 0)
    piece = jnp.concatenate([piece, bias], 0)
    first_hop = [swap(piece, "head", d) for d in range(1, heads)]

    seg = lax.dynamic_slice_in_dim(segment_ids, z * own_rows, own_rows, 0)
    tok_own = lax.dynamic_slice_in_dim(tokens, z * own_rows, own_rows, 0)
    attend_outs = [
        ((heads, rows3, own_rows), LOW),
        ((heads, local_width, own_rows), LOW),
        ((heads, 8, own_rows), F32),
        ((heads, rows3, width), LOW),
        ((heads, local_width, width), LOW),
    ]
    macs = rows3 * width * own_rows + 6 * own_rows * own_rows * 256
    orders = [(1, 2) if d % 2 else (2, 1) for d in range(heads)]
    nexts = [swap(first_hop[d - 1], "near", orders[d][0]) for d in range(1, heads)]

    def pair_up(which, after):
        ins = [hop[d - 1] for d in which for hop in (first_hop, nexts)]
        outs = [((2, piece_rows, width), LOW)] * len(which)
        return list(run_whole(pair_rows, places, ins, outs, after=after, chain=False))

    pairs = pair_up([1], first_hop[1:])
    ins = [tok_own, shard, bias, seg[None]]
    made = run_whole(
        own_attention, places, ins, attend_outs, macs=macs, after=pairs, chain=False
    )
    pairs += pair_up(range(2, heads), [made[2]])
    rests = [swap(pairs[d - 1], "near", orders[d][1]) for d in range(1, heads)]
    for d in range(1, heads):
        pair, rest = pairs[d - 1], rests[d - 1]
        sent = rest
        if d == heads - 1:
            (sent,) = run_whole(
                copy_rows, places, [rest], [(rest.shape, LOW)], after=[second_log], chain=False
            )
        ins = [tok_own, pair, rest, swap_core(pair), swap_core(sent), first_hop[d - 1], seg[None]]
        made = run_whole(
            functools.partial(far_attention, d, orders[d]), places, ins, attend_outs,
            [pltpu.VMEM(shard.shape, LOW)], macs, alias=made, chain=False, weight=100,
        )
        if d == 1:
            second_log = made[2]
    qkvs, mixes, logs, w_qkvs, w_outs = made

    mixes_far = swap_core(mixes)

    square = (own_rows, width)
    tiles = (heads, own_rows, half)
    ins = [
        tok_own, mixes, w_outs, b_out, ln1_gain, ln1_bias, b_down, ln2_gain, ln2_bias,
        w_up, b_up.reshape(heads, 1, chunk), w_down, cotangent,
    ]
    outs = [
        (tiles, LOW),
        (tiles, LOW),
        ((4, own_rows, half), LOW),
        ((heads, own_rows, chunk), LOW),
        (square, F32),
        ((own_rows, 1), F32),
        (square, F32),
        (square, LOW),
        ((8, width), F32),
        ((own_rows, half), LOW),
    ]
    scratch = [
        pltpu.VMEM(square, F32),
        pltpu.VMEM(square, LOW),
        pltpu.VMEM((own_rows, hidden_units), LOW),
        pltpu.VMEM(square, F32),
    ]
    ffn_macs = 2 * own_rows * width * hidden_units
    (
        act_send, act_own, ends, slope, unit1, inv1, res2, layer_output, small_two, tok_send,
    ) = run_whole(feed_forward, places, ins, outs, scratch, ffn_macs)
    tok_far = swap_core(tok_send)
    act_far = swap_core(act_send)
    ends_far = swap_core(ends)

    outs = [(tiles, LOW), (tiles, LOW), ((heads, 1, chunk), F32)]
    scratch = [pltpu.VMEM((own_rows, chunk), LOW)]
    inner_send, inner_own, up_bias = run_whole(
        inner_back, places, [ends, w_down, slope], outs, scratch, ffn_macs // 2, [mixes_far]
    )
    inner_far = swap_core(inner_send)


    def ffn_unit(bit, own, far, which, weight):
        outs = [((heads, half, half), LOW)] * 2
        both = [pltpu.VMEM((width, 2 * own_rows), LOW)]
        kernel = functools.partial(ffn_grad, bit, which)
        ins = [own, far, ends, ends_far]
        return run_whole(kernel, places, ins, outs, both, ffn_macs // 2, weight=weight)

    made = ffn_unit(1, act_own, act_far, 1, 8) + ffn_unit(2, inner_own, inner_far, 0, LIGHT)
    x_send, x_keep, y_send, y_keep = made
    ffn_held = (x_keep, swap(x_send, "near", 1), y_keep, swap(y_send, "near", 2))

    outs = [((own_rows, half), LOW), (square, F32), (square, LOW), ((8, width), F32)]
    ins = [inner_own, inner_send, w_up, res2, unit1, inv1, ln1_gain]
    grad_send, res1, grad_attended, small_one = run_whole(
        hidden_back, places, ins, outs, macs=ffn_macs // 2, weight=LIGHT
    )
    grad_far = swap_core(grad_send)

    def second(x_keep, x_came, y_keep, y_came, macs=0):
        arrays = (x_keep, x_came, y_keep, y_came)
        shapes = [(heads, a.shape[1] // 2, half) for a in (x_keep, x_keep, y_keep, y_keep)]
        outs = [(shape, LOW) for shape in shapes]
        kernel = functools.partial(add_split, (2, 1))
        return run_whole(kernel, places, arrays, outs, macs=macs)

    def third(x_keep, x_came, y_keep, y_came):
        arrays = (x_keep, x_came, y_keep, y_came)
        shape = (heads // 2, x_keep.shape[1] + y_keep.shape[1], half)
        send, keep = run_whole(add_parts, places, arrays, [(shape, LOW)] * 2)
        return keep, swap(send, "head", 1)

    def fourth(keep, came):
        shape = keep.shape[1:]
        mine, other = run_whole(add_pair, places, [keep, came], [(shape, LOW)] * 2)
        return mine, swap(other, "head", 2)

    def fifth(mine, came):
        (total,) = run_whole(add_two, places, [mine, came], [(mine.shape, LOW)])
        bit = 1
        while bit < lax.axis_size("far"):
            total = (total.astype(F32) + swap(total, "far", bit).astype(F32)).astype(LOW)
            bit *= 2
        return total

    def cross(made, flip):
        x_send, x_keep, y_send, y_keep = made
        x_bit, y_bit = (2, 1) if flip else (1, 2)
        return x_keep, swap(x_send, "near", x_bit), y_keep, swap(y_send, "near", y_bit)

    outs = [((heads, rows3, own_rows), LOW), ((heads, 8, rows3), F32)]
    ins = [qkvs, w_outs, grad_attended, logs, seg[None]]
    rows, qkv_bias = run_whole(attention_back, places, ins, outs)
    rows_far = swap_core(rows)

    outs = [(square, F32, whole(square))]
    ins = [(a, whole(a.shape)) for a in (rows, w_qkvs, res1)]
    (input_grad,) = run(input_sum, places, (1,), ins, outs, weight=LIGHT)
    ffn_held = cross(second(*ffn_held, ffn_macs), True)
    ins = [
        rows, rows_far, tok_own, tok_far, mixes, mixes_far, grad_attended, grad_far,
        small_one, small_two, up_bias, qkv_bias,
    ]
    outs = [
        ((heads, r, half), LOW) for r in (half // 2, (half + EXTRA) // 2) for _ in range(2)
    ]
    made = run_whole(attn_grad, places, ins, outs)
    attn_held = cross(made, False)

    ffn_held = third(*ffn_held)
    attn_held = cross(second(*attn_held), True)
    ffn_held = fourth(*ffn_held)
    attn_held = third(*attn_held)
    ffn_held = gather_back(fifth(*ffn_held))
    attn_held = fourth(*attn_held)
    attn_held = gather_back(fifth(*attn_held))

    def both_cores(held):
        shape = (heads,) + held[0].shape
        (pieces,) = run_whole(collect, places, held, [(shape, LOW)])
        return [(a, whole(shape)) for a in (pieces, swap_core(pieces))]

    ffn_held = both_cores(ffn_held)
    outs = [(shape, F32, whole(shape)) for shape in ((chunk, width), (width, chunk))]
    grad_down, grad_up = run(
        ffn_place, places, (1,), ffn_held, outs, [pltpu.VMEM((width, chunk), F32)]
    )
    attn_held = both_cores(attn_held)
    shapes = [
        (3, local_width, width),
        (local_width, width),
        (6, width),
        (chunk,),
        (2, local_width),
    ]
    grad_qkv, grad_out, grad_small, grad_up_bias, grad_qv_bias = run(
        attn_place,
        places,
        (1,),
        attn_held,
        [(shape, F32, whole(shape)) for shape in shapes],
        [pltpu.VMEM((width + EXTRA, width), F32)],
    )
    return (
        layer_output,
        input_grad,
        grad_qkv.transpose(0, 2, 1),
        grad_qv_bias,
        grad_out,
        grad_up,
        grad_up_bias,
        grad_down,
        grad_small,
    )


def solution(mesh):
    batch, heads = mesh.devices.shape
    mesh = Mesh(
        mesh.devices.reshape(batch // 8, 4, 2, heads), ("far", "near", "core", "head")
    )
    group = ("far", "near", "core")
    everyone = group + ("head",)
    in_specs = (
        P(group, None),
        P(group),
        P(None, None, "head"),
        P(None, "head"),
        P("head", None),
        P(),
        P(),
        P(),
        P(),
        P(),
        P(),
        P(),
        P(),
        P(),
        P(everyone, None),
    )
    out_specs = (
        P(everyone, None),
        P(everyone, None),
        P(None, None, "head"),
        P(None, "head"),
        P("head", None),
        P(None, "head"),
        P("head"),
        P("head", None),
        P(),
    )
    return jax.shard_map(
        per_device, mesh=mesh, in_specs=in_specs, out_specs=out_specs, check_vma=False
    )
```

```python
import functools
import math

import jax
import jax.numpy as jnp
from jax import lax
from jax.experimental import pallas as pl
from jax.experimental.pallas import tpu as pltpu
from jax.sharding import Mesh
from jax.sharding import PartitionSpec as P

HEAD_DIM = 64
SLOT = 512
LOW = jnp.bfloat16
F32 = jnp.float32
LOG2E = math.log2(math.e)
SCORE_SCALE = HEAD_DIM ** (-0.5) * LOG2E
SPARE_BYTES = 12 * 2**20
EXTRA = 64
LIGHT = 0.01
LANES = 128
CHAIN = []
TAIL_SLOPE = 0.36
TAIL = (
    0.14371304537508633,
    0.14177245466203425,
    0.1397192603907239,
    0.026549325413860486,
    0.18095403134327948,
    -0.1797647161697652,
    0.047056295581175855,
)


def swap(value, axis, bit):
    size = lax.axis_size(axis)
    return lax.ppermute(value, axis, [(i, i ^ bit) for i in range(size)])


def swap_core(value):
    return swap(value, "core", 1)


def dot(a, b):
    return jnp.dot(a, b, preferred_element_type=F32)


def dot_nt(a, b):
    return lax.dot_general(a, b, (((1,), (1,)), ((), ())), preferred_element_type=F32)


def dot_tn(a, b):
    return lax.dot_general(a, b, (((0,), (0,)), ((), ())), preferred_element_type=F32)


def whole(shape):
    return pl.BlockSpec(shape, lambda *args: (0,) * len(shape), pipeline_mode=pl.Buffered(1))


def run(
    kernel, places, grid, ins, outs, scratch=(), macs=0, after=(), alias=(), weight=8, chain=True
):
    moved = sum(a.size * a.dtype.itemsize for a, spec in ins)
    moved += sum(math.prod(shape) * jnp.dtype(kind).itemsize for shape, kind, spec in outs)
    after = list(after) + (CHAIN if chain else [])
    count, unread = len(ins), len(alias) + len(after)
    results = len(outs)
    flag = (8, 128)
    if chain:
        outs = outs + [(flag, F32, whole(flag))]

    def body(places, *refs):
        made = refs[count + unread :]
        if chain:

            @pl.when(pl.program_id(0) == 0)
            def _():
                made[results][...] = jnp.zeros(flag, F32)

        kernel(places, *refs[:count], *made[:results], *made[len(outs) :])

    held = pl.BlockSpec(memory_space=pl.ANY)
    room = SPARE_BYTES
    for shape, kind, spec in outs + [(a.shape, a.dtype, spec) for a, spec in ins]:
        if spec.block_shape is not None:
            block = math.prod(1 if n is None else n for n in spec.block_shape)
            copies = 2 if spec.pipeline_mode is None else 1
            room += copies * block * jnp.dtype(kind).itemsize
    for ref in scratch:
        if hasattr(ref, "shape") and ref.dtype in (LOW, F32):
            room += math.prod(ref.shape) * jnp.dtype(ref.dtype).itemsize
    made = pl.pallas_call(
        body,
        name=getattr(kernel, "func", kernel).__name__,
        grid_spec=pltpu.PrefetchScalarGridSpec(
            num_scalar_prefetch=1,
            grid=grid,
            in_specs=[spec for a, spec in ins] + [held] * unread,
            out_specs=[spec for shape, kind, spec in outs],
            scratch_shapes=list(scratch),
        ),
        out_shape=[jax.ShapeDtypeStruct(shape, kind) for shape, kind, spec in outs],
        input_output_aliases={1 + count + i: i for i in range(len(alias))},
        compiler_params=pltpu.CompilerParams(vmem_limit_bytes=room),
        cost_estimate=pl.CostEstimate(
            flops=int(2 * macs * weight), bytes_accessed=int(moved * weight), transcendentals=0
        ),
    )(places, *[a for a, spec in ins], *alias, *after)
    if chain:
        CHAIN[:] = made[results:]
    return made[:results]


def run_whole(
    kernel, places, ins, outs, scratch=(), macs=0, after=(), alias=(), weight=8, chain=True
):
    pairs = [a if isinstance(a, tuple) else (a, pltpu.VMEM) for a in ins]
    after = list(after) + (CHAIN if chain else [])
    count, unread, results = len(pairs), len(alias) + len(after), len(outs)
    if chain:
        outs = outs + [((8, 128), F32)]

    def body(places, *refs):
        made = refs[count + unread :]
        if chain:
            made[results][...] = jnp.zeros((8, 128), F32)
        kernel(places, *refs[:count], *made[:results], *made[len(outs) :])

    room = SPARE_BYTES
    for ref in scratch:
        if hasattr(ref, "shape") and ref.dtype in (LOW, F32):
            room += math.prod(ref.shape) * jnp.dtype(ref.dtype).itemsize
    spaces = [pltpu.SMEM] + [space for a, space in pairs]
    spaces += [pltpu.VMEM] * len(alias) + [pl.ANY] * len(after)
    made = pl.pallas_call(
        body,
        name=getattr(kernel, "func", kernel).__name__,
        in_specs=[pl.BlockSpec(memory_space=space) for space in spaces],
        out_specs=[pl.BlockSpec(memory_space=pltpu.VMEM)] * len(outs),
        scratch_shapes=list(scratch),
        out_shape=[jax.ShapeDtypeStruct(shape, kind) for shape, kind in outs],
        input_output_aliases={1 + count + i: i for i in range(len(alias))},
        compiler_params=pltpu.CompilerParams(vmem_limit_bytes=room),
        cost_estimate=pl.CostEstimate(
            flops=int(2 * macs * weight), bytes_accessed=0, transcendentals=0
        ),
    )(places, *[a for a, space in pairs], *alias, *after)
    if chain:
        CHAIN[:] = made[results:]
    return made[:results]


def each(count, size, body):
    def step(i, carry):
        body(pl.ds(pl.multiple_of(i * size, size), size))
        return carry

    lax.fori_loop(0, count // size, step, 0)


def tiles_of(count, size):
    return [slice(at, at + size) for at in range(0, count, size)]


def three_parts(values):
    parts, rest = [], values
    for _ in range(3):
        parts.append(rest.astype(LOW))
        rest = rest - parts[-1].astype(F32)
    return parts


def segment_rows(seg_row):
    shape = (16, seg_row.shape[1])
    place = lax.broadcasted_iota(jnp.int32, shape, 0)
    same = place - 1 == seg_row
    keys = jnp.where(same, 1.0, jnp.where((place >= 8) & (place < 11), 1.0, 0.0))
    queries = jnp.where(same | (place > 4), 0.0, -1e30)
    return keys.astype(LOW), queries.astype(LOW)


def attend_heads(tok, w_rows, bias, seg_row, qkv_ref, mix_ref, log_ref):
    width = w_rows.shape[0] // 3
    added = dot_tn(bias[:, : 2 * width], jnp.ones((bias.shape[0], tok.shape[0]), LOW))
    qkv = dot_nt(w_rows, tok)
    parts = (
        (qkv[:width] + added[:width]).astype(LOW),
        qkv[width : 2 * width].astype(LOW),
        (qkv[2 * width :] + added[width:]).astype(LOW),
    )
    for c in range(3):
        qkv_ref[c * width : (c + 1) * width] = parts[c]
    more_k, more_q = segment_rows(seg_row)
    for head in range(width // HEAD_DIM):
        q, k, v = (part[head * HEAD_DIM : (head + 1) * HEAD_DIM] for part in parts)
        scores = dot_tn(jnp.concatenate([k, more_k], 0), jnp.concatenate([q, more_q], 0))
        columns, tops, totals = [], [], []
        for tile in tiles_of(scores.shape[1], LANES):
            top = jnp.max(scores[:, tile], 0, keepdims=True)
            total, column = 0.0, []
            for rows in tiles_of(scores.shape[0], 64):
                exponent = jnp.exp2((scores[rows, tile] - top) * SCORE_SCALE)
                total = total + jnp.sum(exponent, 0, keepdims=True)
                column.append(exponent.astype(LOW))
            columns.append(jnp.concatenate(column, 0))
            tops.append(top)
            totals.append(total)
        total = jnp.concatenate(totals, 1)
        mixed = dot(v, jnp.concatenate(columns, 1)) * (1.0 / total)
        mix_ref[head * HEAD_DIM : (head + 1) * HEAD_DIM] = mixed.astype(LOW)
        top = jnp.concatenate(tops, 1)
        log_ref[head : head + 1] = top + jnp.log2(total) * (1.0 / SCORE_SCALE)


def own_attention(
    places, tok, w, bias, seg_row, qkv_ref, mix_ref, log_ref, w_qkv, w_out
):
    count = qkv_ref.shape[1]
    w_qkv[0] = w[:count]
    w_out[0] = w[count:]
    attend_heads(
        tok[...], w[:count], bias[...], seg_row[...], qkv_ref.at[0], mix_ref.at[0], log_ref.at[0]
    )


def far_attention(
    d, order, places, tok, pair, rest, pair_far, rest_far, hop, seg_row,
    qkv_ref, mix_ref, log_ref, w_qkv, w_out, w_ref,
):
    first, second = order
    rows, count = pair.shape[1], qkv_ref.shape[1]
    me = places[0] * 2 + places[1]
    for other, held in enumerate(((pair, rest), (pair_far, rest_far))):
        for two, block in enumerate(held):
            for one in range(2):
                owner = me ^ (other + 2 * first * one + 2 * second * two)
                w_ref[pl.ds(pl.multiple_of(owner * rows, rows), rows)] = block[one]
    w_qkv[d] = w_ref[:count]
    w_out[d] = w_ref[count:]
    attend_heads(
        tok[...],
        w_ref[:count],
        hop[rows:],
        seg_row[...],
        qkv_ref.at[d],
        mix_ref.at[d],
        log_ref.at[d],
    )


def copy_rows(places, rows, out):
    out[...] = rows[...]


def pair_rows(places, first, second, out):
    out[0] = first[: out.shape[1]]
    out[1] = second[: out.shape[1]]


def norm_stats(v):
    centred = v - jnp.mean(v, -1, keepdims=True)
    inv = lax.rsqrt(jnp.mean(centred * centred, -1, keepdims=True) + 1e-05)
    return centred * inv, inv


def norm_back(upstream, unit, inv, gain):
    scaled = upstream * gain
    inner = jnp.mean(scaled * unit, -1, keepdims=True)
    return inv * (scaled - jnp.mean(scaled, -1, keepdims=True) - unit * inner)


def gelu_both(pre):
    power = jnp.exp2(pre * pre * (-0.5 * LOG2E))
    base = 1.0 + TAIL_SLOPE * jnp.abs(pre)
    t = pl.reciprocal(base, approx=True)
    tail = TAIL[6] * t + TAIL[5]
    for c in TAIL[4::-1]:
        tail = tail * t + c
    tail = tail * (t * power)
    cumul = jnp.where(pre < 0.0, tail, 1.0 - tail)
    return (pre * cumul).astype(LOW), cumul + pre * (power * 0.3989422804014327)


def share(core, wide, mine, other):
    half = wide.shape[1] // 2
    left, right = wide[:, :half], wide[:, half:]
    mine[...] = jnp.where(core == 0, left, right)
    other[...] = jnp.where(core == 0, right, left)


def feed_forward(
    places, tok, mix, w_out, b_out, gain1, shift1, b_down, gain2, shift2, w_up, b_up, w_down, cot,
    send, own, ends, slope, unit1, inv1, res2, out, small, tok_send,
    hidden, low, acts, total,
):
    heads, width, half = mix.shape[0], low.shape[1], send.shape[2]
    chunk = 2 * half
    core, z = places[1], places[2]
    b_out, gain1, shift1, b_down, gain2, shift2 = (
        ref[...].reshape(1, -1) for ref in (b_out, gain1, shift1, b_down, gain2, shift2)
    )
    tok_send[...] = jnp.where(core == 0, tok[:, half:], tok[:, :half])
    total[...] = dot_tn(mix[...].reshape(width, low.shape[0]), w_out[...].reshape(width, width))

    def first_norm(rows):
        unit, inv = norm_stats(tok[rows].astype(F32) + (total[rows] + b_out))
        unit1[rows] = unit
        inv1[rows] = inv
        one = unit * gain1 + shift1
        hidden[rows] = one
        one_low = one.astype(LOW)
        low[rows] = one_low
        ends[0, rows] = one_low[:, :half]
        ends[1, rows] = one_low[:, half:]

    each(low.shape[0], 64, first_norm)

    def one_unit(h, carry):
        start = pl.multiple_of(h * chunk, chunk)
        for at in tiles_of(chunk, 256):
            wide = pl.ds(pl.multiple_of(start + at.start, 256), 256)
            pre = dot(low[...], w_up[:, wide])
            for rows in tiles_of(pre.shape[0], 32):
                act, tilt = gelu_both(pre[rows] + b_up[h, :, at])
                slope[h, rows, at] = tilt.astype(LOW)
                acts[rows, wide] = act
        left = acts[:, pl.ds(start, half)]
        right = acts[:, pl.ds(pl.multiple_of(start + half, 128), half)]
        own[z ^ h] = jnp.where(core == 0, left, right)
        send[z ^ h] = jnp.where(core == 0, right, left)
        return carry

    lax.fori_loop(0, heads, one_unit, 0)
    total[...] = dot(acts[...], w_down[...])
    small[...] = jnp.zeros_like(small)

    def second_norm(rows):
        unit, inv = norm_stats(hidden[rows] + (total[rows] + b_down))
        out[rows] = (unit * gain2 + shift2).astype(LOW)
        upstream = cot[rows].astype(F32)
        grad = norm_back(upstream, unit, inv, gain2)
        res2[rows] = grad
        grad_low = grad.astype(LOW)
        ends[2, rows] = grad_low[:, :half]
        ends[3, rows] = grad_low[:, half:]
        for i, term in enumerate((grad_low.astype(F32), upstream * unit, upstream)):
            small[i : i + 1] += jnp.sum(term, 0, keepdims=True)

    each(low.shape[0], 64, second_norm)


def inner_back(places, ends, w_down, slope, send, own, bias, inners):
    heads, _, chunk = slope.shape
    core, z = places[1], places[2]
    branch = jnp.concatenate([ends[2], ends[3]], 1)
    for h in range(heads):
        for at in tiles_of(chunk, 256):
            grad_act = dot_nt(branch, w_down[h * chunk + at.start : h * chunk + at.stop])
            total = 0.0
            for rows in tiles_of(grad_act.shape[0], 32):
                inner = (grad_act[rows] * slope[h, rows, at].astype(F32)).astype(LOW)
                inners[rows, at] = inner
                total = total + jnp.sum(inner.astype(F32), 0, keepdims=True)
            bias[h, :, at] = total
        share(core, inners, own.at[z ^ h], send.at[z ^ h])


def hidden_back(places, own, sent, w_up, res2, unit1, inv1, gain1, send, res1, low, small):
    heads, count, half = own.shape
    core, z = places[1], places[2]
    sides = []
    for h in range(heads):
        mine, other = own[z ^ h], sent[z ^ h]
        sides += [jnp.where(core == 0, mine, other), jnp.where(core == 0, other, mine)]
    product = dot_nt(jnp.concatenate(sides, 1), w_up[...])
    gain = gain1[...].reshape(1, -1)
    sums = [0.0] * 3
    for rows in tiles_of(count, 32):
        grad, unit = product[rows] + res2[rows], unit1[rows]
        result = norm_back(grad, unit, inv1[rows], gain)
        res1[rows] = result
        result_low = result.astype(LOW)
        low[rows] = result_low
        send[rows] = jnp.where(core == 0, result_low[:, half:], result_low[:, :half])
        for i, term in enumerate((result_low.astype(F32), grad * unit, grad)):
            sums[i] = sums[i] + jnp.sum(term, 0, keepdims=True)
    for i in range(3):
        small[i : i + 1] = sums[i]


def shard_back(qkv, w_out, grad, log_ref, more_k, more_q, rows_ref, bias_ref):
    width = qkv.shape[0] // 3
    grad_mixed = dot_nt(w_out[...], grad[...]).astype(LOW)
    scale = HEAD_DIM ** (-0.5)
    for head in range(width // HEAD_DIM):
        places_of = [c * width + head * HEAD_DIM for c in range(3)]
        q, k, v = (qkv[at : at + HEAD_DIM] for at in places_of)
        g = grad_mixed[head * HEAD_DIM : (head + 1) * HEAD_DIM]
        logs = jnp.concatenate(three_parts(-log_ref[head : head + 1]), 0)
        with_logs = jnp.concatenate([more_q[:8], logs, more_q[11:]], 0)
        scores = dot_tn(jnp.concatenate([k, more_k], 0), jnp.concatenate([q, with_logs], 0))
        grad_probs = dot_tn(v, g)
        attends, grads = [], []
        for tile in tiles_of(scores.shape[1], LANES):
            inner, kept, lows, parts = 0.0, [], [], []
            tall = tiles_of(scores.shape[0], 64)
            for down in tall:
                attend = jnp.exp2(scores[down, tile] * SCORE_SCALE)
                inner = inner + jnp.sum(attend * grad_probs[down, tile], 0, keepdims=True)
                kept.append(attend)
                lows.append(attend.astype(LOW))
            for down, attend in zip(tall, kept):
                parts.append((attend * (grad_probs[down, tile] - inner)).astype(LOW))
            attends.append(jnp.concatenate(lows, 0))
            grads.append(jnp.concatenate(parts, 0))
        attend_low = jnp.concatenate(attends, 1)
        grad_scores = jnp.concatenate(grads, 1)
        grad_v = dot_nt(g, attend_low)
        grad_q = dot(k, grad_scores) * scale
        grad_k = dot_nt(q, grad_scores) * scale
        for at, value in zip(places_of, (grad_q, grad_k, grad_v)):
            rows_ref[at : at + HEAD_DIM] = value.astype(LOW)
    ones = jnp.ones((8, rows_ref.shape[1]), LOW)
    bias_ref[...] = dot_nt(ones, rows_ref[...])


def attention_back(places, qkv, w_out, grad, log_ref, seg_row, rows_ref, bias_ref):
    more_k, more_q = segment_rows(seg_row[...])

    def shard(d, carry):
        refs = (ref.at[d] for ref in (rows_ref, bias_ref))
        shard_back(qkv.at[d], w_out.at[d], grad, log_ref.at[d], more_k, more_q, *refs)
        return carry

    lax.fori_loop(0, qkv.shape[0], shard, 0)


def split_rows(value, high, send, keep):
    rows = value.shape[0] // 2
    low = value.astype(LOW)
    send[...] = jnp.where(high, low[:rows], low[rows:])
    keep[...] = jnp.where(high, low[rows:], low[:rows])


def is_high(places, bit):
    return (places[0] & bit) != 0


def unit_products(which, units, units_far, ends, ends_far, both):
    half, count = ends.shape[2], ends.shape[1]
    for side in range(2):
        rows = slice(side * half, (side + 1) * half)
        both[rows, :count] = ends[2 * which + side].T
        both[rows, count:] = ends_far[2 * which + side].T
    for d in range(0, units.shape[0], 2):
        left, right = (jnp.concatenate([units[d + i], units_far[d + i]], 0) for i in range(2))
        yield d, dot(both[...], jnp.concatenate([left, right], 1))


def down_grad(places, units, units_far, ends, ends_far, send, keep, both):
    half = send.shape[2]
    for d, total in unit_products(1, units, units_far, ends, ends_far, both):
        keep[d // 2] = total[:, :half].astype(LOW)
        send[d // 2] = total[:, half:].astype(LOW)


def up_grad(places, units, units_far, ends, ends_far, send_x, keep_x, send_y, keep_y, both):
    half = send_x.shape[2]
    for d, total in unit_products(0, units, units_far, ends, ends_far, both):
        for i in range(2):
            part = total[:, i * half : (i + 1) * half]
            split_rows(part[:half], is_high(places, 1), send_x.at[d + i], keep_x.at[d + i])
            split_rows(part[half:], is_high(places, 2), send_y.at[d + i], keep_y.at[d + i])


def split_at(value, high, send, keep, start):
    rows = value.shape[0] // 2
    low = value.astype(LOW)
    send[start : start + rows] = jnp.where(high, low[:rows], low[rows:])
    keep[start : start + rows] = jnp.where(high, low[rows:], low[:rows])


def first_stage(
    places, d_keep, d_came, x_keep, x_came, y_keep, y_came, send_x, keep_x, send_y, keep_y
):
    half = d_keep.shape[2]
    at = 0
    for i in range(d_keep.shape[0]):
        total = d_keep[i].astype(F32) + d_came[i].astype(F32)
        split_at(total[:half], is_high(places, 1), send_x, keep_x, at)
        split_at(total[half:], is_high(places, 2), send_y, keep_y, at)
        at += half // 2
    for d in range(x_keep.shape[0]):
        upper = x_keep[d].astype(F32) + x_came[d].astype(F32)
        lower = y_keep[d].astype(F32) + y_came[d].astype(F32)
        split_at(upper, is_high(places, 2), send_y, keep_y, at)
        split_at(lower, is_high(places, 1), send_x, keep_x, at)
        at += upper.shape[0] // 2


def second_stage(
    places, x_keep, x_came, y_keep, y_came, send_x, keep_x, send_y, keep_y, send_z, keep_z
):
    rows = send_x.shape[1]
    at = 0
    for i in range(send_x.shape[0]):
        piece = slice(at, at + 2 * rows)
        upper = x_keep[piece].astype(F32) + x_came[piece].astype(F32)
        lower = y_keep[piece].astype(F32) + y_came[piece].astype(F32)
        split_rows(upper, is_high(places, 2), send_y.at[i], keep_y.at[i])
        split_rows(lower, is_high(places, 1), send_x.at[i], keep_x.at[i])
        at += 2 * rows
    for d in range(2 * send_z.shape[0]):
        piece = slice(at, at + rows)
        out = (send_z if d % 2 else keep_z).at[d // 2]
        out[:rows] = (y_keep[piece].astype(F32) + y_came[piece].astype(F32)).astype(LOW)
        out[rows:] = (x_keep[piece].astype(F32) + x_came[piece].astype(F32)).astype(LOW)
        at += rows


def third_stage(places, x_keep, x_came, y_keep, y_came, z_keep, z_came, mine, other):
    rows = x_keep.shape[1]
    for i, out in enumerate((mine, other)):
        out[:rows] = (y_keep[i].astype(F32) + y_came[i].astype(F32)).astype(LOW)
        out[rows : 2 * rows] = (x_keep[i].astype(F32) + x_came[i].astype(F32)).astype(LOW)
        out[2 * rows :] = (z_keep[i].astype(F32) + z_came[i].astype(F32)).astype(LOW)


def attn_grad(
    places, rows, rows_far, tok, tok_far, mix, mix_far, grad, grad_far,
    small_one, small_two, up_bias, qkv_bias, send_x, keep_x, send_y, keep_y,
):
    width = mix.shape[1]
    half = tok_far.shape[1]
    core, z = places[1], places[2]

    def both(near, far):
        mine = jnp.where(core == 0, near[:, :half], near[:, half:])
        return jnp.concatenate([mine, far[...]], 0)

    tok_both, grad_both = both(tok, tok_far), both(grad, grad_far)
    for d in range(rows.shape[0]):
        qkv = dot(jnp.concatenate([rows[d], rows_far[d]], 1), tok_both)
        out = dot(jnp.concatenate([mix[d], mix_far[d]], 1), grad_both)
        lines = []
        for held in (small_one, small_two):
            for i in range(3):
                lines += [held[i : i + 1, :half], held[i : i + 1, half:]]
        line, bias = up_bias[z ^ d], qkv_bias[d]
        lines += [line[:, :half], line[:, half:]]
        lines.append(jnp.concatenate([bias[0:1, :width], bias[0:1, 2 * width :]], 1))
        lines.append(jnp.zeros((EXTRA - len(lines), half), F32))
        total = jnp.concatenate([qkv, out] + lines, 0)
        split_rows(total[:half], is_high(places, 1), send_x.at[d], keep_x.at[d])
        split_rows(total[half:], is_high(places, 2), send_y.at[d], keep_y.at[d])


def add_split(bits, places, *refs):
    for i, bit in enumerate(bits):
        keep, came = refs[2 * i : 2 * i + 2]
        send, left = refs[2 * (len(bits) + i) : 2 * (len(bits) + i) + 2]
        for d in range(keep.shape[0]):
            total = keep[d].astype(F32) + came[d].astype(F32)
            split_rows(total, is_high(places, bit), send.at[d], left.at[d])


def add_parts(places, keep_a, came_a, keep_b, came_b, send, keep):
    rows = keep_a.shape[1]
    for d in range(keep_a.shape[0]):
        out = (send if d % 2 else keep).at[d // 2]
        out[:rows] = (keep_a[d].astype(F32) + came_a[d].astype(F32)).astype(LOW)
        out[rows:] = (keep_b[d].astype(F32) + came_b[d].astype(F32)).astype(LOW)


def add_pair(places, keep, came, *outs):
    for i, out in enumerate(outs):
        out[...] = (keep[i].astype(F32) + came[i].astype(F32)).astype(LOW)


def add_two(places, keep, came, out):
    out[...] = (keep[...].astype(F32) + came[...].astype(F32)).astype(LOW)


def input_sum(places, rows, w, res1, out):
    heads, count, tokens = rows.shape
    total = dot_tn(rows[...].reshape(heads * count, tokens), w[...].reshape(heads * count, -1))
    out[...] = res1[...] + total


def place_pieces(places, held, full, layouts):
    near, core = places[0], places[1]
    width = held[0].shape[1]
    for off in range(4):
        chip = near ^ off
        mine, other = held[off][...], held[4 + off][...]
        sides = (jnp.where(core == 0, mine, other), jnp.where(core == 0, other, mine))
        for at, rows, start, outer in layouts:
            low_bit, high_bit = chip & 1, chip >> 1
            order = 2 * low_bit + high_bit if outer == 1 else 2 * high_bit + low_bit
            to = pl.multiple_of(start + order * rows, 16)
            for side in range(2):
                full[pl.ds(to, rows), side * width : (side + 1) * width] = sides[side][
                    at : at + rows
                ].astype(F32)


def ffn_place(places, *refs):
    held = [ref.at[off] for ref in refs[:2] for off in range(4)]
    down, up, full = refs[2:]
    rows = held[0].shape[0] // 4
    half = 4 * rows
    place_pieces(places, held, full, [(0, rows, 0, 1), (rows, rows, half, 2)])
    down[...] = full[...].T
    place_pieces(places, held, up, [(2 * rows, rows, 0, 1), (3 * rows, rows, half, 2)])


def collect(places, *refs):
    for off in range(4):
        refs[4][off] = refs[off][...]


def attn_place(places, *refs):
    held = [ref.at[off] for ref in refs[:2] for off in range(4)]
    qkv, w_out, small, up_bias, qv_bias, full = refs[2:]
    width = held[0].shape[1]
    count = w_out.shape[0]
    rows = count // 2
    more = held[0].shape[0] - rows
    place_pieces(places, held, full, [(0, rows, 0, 1), (rows, more, 4 * rows, 2)])
    for c in range(3):
        qkv[c] = full[c * count : (c + 1) * count]
    w_out[...] = full[3 * count : 4 * count]
    at = 4 * count
    lines = full[at : at + 16, :width] + full[at : at + 16, width:]
    for i in range(6):
        small[i : i + 1, :width] = lines[2 * i : 2 * i + 1]
        small[i : i + 1, width:] = lines[2 * i + 1 : 2 * i + 2]
    up_bias[...] = jnp.concatenate([lines[12:13], lines[13:14]], 1).reshape(2 * width)
    qv_bias[0:1] = lines[14:15, :count]
    qv_bias[1:2] = lines[14:15, count : 2 * count]


def bias_parts(values):
    rows, rest = [], values
    for _ in range(3):
        rows.append(lax.reduce_precision(rest, 8, 7))
        rest = rest - rows[-1]
    return jnp.stack(rows).astype(LOW)


def gather_back(piece):
    return [piece] + [swap(piece, "near", off) for off in range(1, 4)]


def per_device(
    tokens,
    segment_ids,
    w_qkv,
    b_qv,
    w_out,
    b_out,
    ln1_gain,
    ln1_bias,
    w_up,
    b_up,
    w_down,
    b_down,
    ln2_gain,
    ln2_bias,
    cotangent,
):
    CHAIN.clear()
    width = tokens.shape[1]
    own_rows = cotangent.shape[0]
    local_width = w_qkv.shape[2]
    heads = lax.axis_size("head")
    z = lax.axis_index("head")
    core = lax.axis_index("core")
    near = lax.axis_index("near")
    hidden_units = w_up.shape[1]
    chunk = hidden_units // heads
    half = width // 2
    rows3 = 3 * local_width
    places = jnp.stack([near, core, z]).astype(jnp.int32)

    shard = jnp.concatenate([w_qkv.transpose(0, 2, 1).reshape(rows3, width), w_out], 0)
    piece_rows = shard.shape[0] // 8
    bias = jnp.pad(bias_parts(b_qv.reshape(-1)), ((0, 13), (0, width - 2 * local_width)))
    piece = lax.dynamic_slice_in_dim(shard, (near * 2 + core) * piece_rows, piece_rows, 0)
    piece = jnp.concatenate([piece, bias], 0)
    first_hop = [swap(piece, "head", d) for d in range(1, heads)]

    seg = lax.dynamic_slice_in_dim(segment_ids, z * own_rows, own_rows, 0)
    tok_own = lax.dynamic_slice_in_dim(tokens, z * own_rows, own_rows, 0)
    attend_outs = [
        ((heads, rows3, own_rows), LOW),
        ((heads, local_width, own_rows), LOW),
        ((heads, 8, own_rows), F32),
        ((heads, rows3, width), LOW),
        ((heads, local_width, width), LOW),
    ]
    macs = rows3 * width * own_rows + 6 * own_rows * own_rows * 256
    orders = [(1, 2) if d % 2 else (2, 1) for d in range(heads)]
    nexts = [swap(first_hop[d - 1], "near", orders[d][0]) for d in range(1, heads)]

    def pair_up(d, after):
        (pair,) = run_whole(
            pair_rows, places, [first_hop[d - 1], nexts[d - 1]],
            [((2, piece_rows, width), LOW)], after=after, chain=False,
        )
        return pair

    pairs = [pair_up(1, first_hop[1:])]
    ins = [tok_own, shard, bias, seg[None]]
    made = run_whole(
        own_attention, places, ins, attend_outs, macs=macs, after=pairs, chain=False
    )
    pairs += [pair_up(d, nexts[1:] + [made[2]]) for d in range(2, heads)]
    rests = [swap(pairs[d - 1], "near", orders[d][1]) for d in range(1, heads)]
    for d in range(1, heads):
        pair, rest = pairs[d - 1], rests[d - 1]
        sent = rest
        if d == heads - 1:
            (sent,) = run_whole(
                copy_rows, places, [rest], [(rest.shape, LOW)], after=[second_log], chain=False
            )
        ins = [tok_own, pair, rest, swap_core(pair), swap_core(sent), first_hop[d - 1], seg[None]]
        made = run_whole(
            functools.partial(far_attention, d, orders[d]), places, ins, attend_outs,
            [pltpu.VMEM(shard.shape, LOW)], macs, alias=made, chain=False, weight=100,
        )
        if d == 1:
            second_log = made[2]
    qkvs, mixes, logs, w_qkvs, w_outs = made

    mixes_far = swap_core(mixes)

    square = (own_rows, width)
    tiles = (heads, own_rows, half)
    ins = [
        tok_own, mixes, w_outs, b_out, ln1_gain, ln1_bias, b_down, ln2_gain, ln2_bias,
        w_up, b_up.reshape(heads, 1, chunk), w_down, cotangent,
    ]
    outs = [
        (tiles, LOW),
        (tiles, LOW),
        ((4, own_rows, half), LOW),
        ((heads, own_rows, chunk), LOW),
        (square, F32),
        ((own_rows, 1), F32),
        (square, F32),
        (square, LOW),
        ((8, width), F32),
        ((own_rows, half), LOW),
    ]
    scratch = [
        pltpu.VMEM(square, F32),
        pltpu.VMEM(square, LOW),
        pltpu.VMEM((own_rows, hidden_units), LOW),
        pltpu.VMEM(square, F32),
    ]
    ffn_macs = 2 * own_rows * width * hidden_units
    (
        act_send, act_own, ends, slope, unit1, inv1, res2, layer_output, small_two, tok_send,
    ) = run_whole(feed_forward, places, ins, outs, scratch, ffn_macs)
    tok_far = swap_core(tok_send)
    act_far = swap_core(act_send)
    ends_far = swap_core(ends)

    outs = [(tiles, LOW), (tiles, LOW), ((heads, 1, chunk), F32)]
    scratch = [pltpu.VMEM((own_rows, chunk), LOW)]
    inner_send, inner_own, up_bias = run_whole(
        inner_back, places, [ends, w_down, slope], outs, scratch, ffn_macs // 2, [mixes_far]
    )
    inner_far = swap_core(inner_send)


    both = [pltpu.VMEM((width, 2 * own_rows), LOW)]
    outs = [((heads // 2, width, half), LOW)] * 2
    ins = [act_own, act_far, ends, ends_far]
    d_send, d_keep = run_whole(down_grad, places, ins, outs, both, ffn_macs // 2)
    d_came = swap(d_send, "head", 1)
    outs = [((heads, half // 2, half), LOW)] * 4
    ins = [inner_own, inner_far, ends, ends_far]
    made = run_whole(up_grad, places, ins, outs, both, ffn_macs // 2, weight=LIGHT)
    u_held = (made[1], swap(made[0], "near", 1), made[3], swap(made[2], "near", 2))

    outs = [((own_rows, half), LOW), (square, F32), (square, LOW), ((8, width), F32)]
    ins = [inner_own, inner_send, w_up, res2, unit1, inv1, ln1_gain]
    grad_send, res1, grad_attended, small_one = run_whole(
        hidden_back, places, ins, outs, macs=ffn_macs // 2, weight=LIGHT
    )
    grad_far = swap_core(grad_send)

    def second(x_keep, x_came, y_keep, y_came, macs=0):
        arrays = (x_keep, x_came, y_keep, y_came)
        shapes = [(heads, a.shape[1] // 2, half) for a in (x_keep, x_keep, y_keep, y_keep)]
        outs = [(shape, LOW) for shape in shapes]
        kernel = functools.partial(add_split, (2, 1))
        return run_whole(kernel, places, arrays, outs, macs=macs)

    def third(x_keep, x_came, y_keep, y_came):
        arrays = (x_keep, x_came, y_keep, y_came)
        shape = (heads // 2, x_keep.shape[1] + y_keep.shape[1], half)
        send, keep = run_whole(add_parts, places, arrays, [(shape, LOW)] * 2)
        return keep, swap(send, "head", 1)

    def fourth(keep, came):
        shape = keep.shape[1:]
        mine, other = run_whole(add_pair, places, [keep, came], [(shape, LOW)] * 2)
        return mine, swap(other, "head", 2)

    def fifth(mine, came):
        (total,) = run_whole(add_two, places, [mine, came], [(mine.shape, LOW)])
        bit = 1
        while bit < lax.axis_size("far"):
            total = (total.astype(F32) + swap(total, "far", bit).astype(F32)).astype(LOW)
            bit *= 2
        return total

    def cross_back(made):
        x_send, x_keep, y_send, y_keep = made
        return x_keep, swap(x_send, "near", 1), y_keep, swap(y_send, "near", 2)

    def cross(made, flip):
        x_send, x_keep, y_send, y_keep = made
        x_bit, y_bit = (2, 1) if flip else (1, 2)
        return x_keep, swap(x_send, "near", x_bit), y_keep, swap(y_send, "near", y_bit)

    outs = [((heads, rows3, own_rows), LOW), ((heads, 8, rows3), F32)]
    ins = [qkvs, w_outs, grad_attended, logs, seg[None]]
    rows, qkv_bias = run_whole(attention_back, places, ins, outs)
    rows_far = swap_core(rows)

    outs = [(square, F32, whole(square))]
    ins = [(a, whole(a.shape)) for a in (rows, w_qkvs, res1)]
    (input_grad,) = run(input_sum, places, (1,), ins, outs, weight=LIGHT)
    outs = [((width, half), LOW)] * 4
    ins = [d_keep, d_came, *u_held]
    ffn_held = cross(run_whole(first_stage, places, ins, outs, macs=ffn_macs), False)
    ins = [
        rows, rows_far, tok_own, tok_far, mixes, mixes_far, grad_attended, grad_far,
        small_one, small_two, up_bias, qkv_bias,
    ]
    outs = [
        ((heads, r, half), LOW) for r in (half // 2, (half + EXTRA) // 2) for _ in range(2)
    ]
    made = run_whole(attn_grad, places, ins, outs)
    attn_held = cross(made, False)

    outs = [((heads // 2, half // 4, half), LOW)] * 4 + [((heads // 2, half // 2, half), LOW)] * 2
    made = run_whole(second_stage, places, list(ffn_held), outs, macs=ffn_macs)
    ffn_held = cross_back(made[:4]) + (made[5], swap(made[4], "head", 1))
    attn_held = cross(second(*attn_held), True)
    outs = [((half, half), LOW)] * 2
    mine, other = run_whole(third_stage, places, list(ffn_held), outs, macs=ffn_macs)
    ffn_held = mine, swap(other, "head", 2)
    attn_held = third(*attn_held)
    ffn_held = gather_back(fifth(*ffn_held))
    attn_held = fourth(*attn_held)
    attn_held = gather_back(fifth(*attn_held))

    def both_cores(held):
        shape = (heads,) + held[0].shape
        (pieces,) = run_whole(collect, places, held, [(shape, LOW)])
        return [(a, whole(shape)) for a in (pieces, swap_core(pieces))]

    ffn_held = both_cores(ffn_held)
    outs = [(shape, F32, whole(shape)) for shape in ((chunk, width), (width, chunk))]
    grad_down, grad_up = run(
        ffn_place, places, (1,), ffn_held, outs, [pltpu.VMEM((width, chunk), F32)]
    )
    attn_held = both_cores(attn_held)
    shapes = [
        (3, local_width, width),
        (local_width, width),
        (6, width),
        (chunk,),
        (2, local_width),
    ]
    grad_qkv, grad_out, grad_small, grad_up_bias, grad_qv_bias = run(
        attn_place,
        places,
        (1,),
        attn_held,
        [(shape, F32, whole(shape)) for shape in shapes],
        [pltpu.VMEM((width + EXTRA, width), F32)],
    )
    return (
        layer_output,
        input_grad,
        grad_qkv.transpose(0, 2, 1),
        grad_qv_bias,
        grad_out,
        grad_up,
        grad_up_bias,
        grad_down,
        grad_small,
    )


def solution(mesh):
    batch, heads = mesh.devices.shape
    mesh = Mesh(
        mesh.devices.reshape(batch // 8, 4, 2, heads), ("far", "near", "core", "head")
    )
    group = ("far", "near", "core")
    everyone = group + ("head",)
    in_specs = (
        P(group, None),
        P(group),
        P(None, None, "head"),
        P(None, "head"),
        P("head", None),
        P(),
        P(),
        P(),
        P(),
        P(),
        P(),
        P(),
        P(),
        P(),
        P(everyone, None),
    )
    out_specs = (
        P(everyone, None),
        P(everyone, None),
        P(None, None, "head"),
        P(None, "head"),
        P("head", None),
        P(None, "head"),
        P("head"),
        P("head", None),
        P(),
    )
    return jax.shard_map(
        per_device, mesh=mesh, in_specs=in_specs, out_specs=out_specs, check_vma=False
    )
```

```python
import functools
import math

import jax
import jax.numpy as jnp
from jax import lax
from jax.experimental import pallas as pl
from jax.experimental.pallas import tpu as pltpu
from jax.sharding import Mesh
from jax.sharding import PartitionSpec as P

HEAD_DIM = 64
SLOT = 512
LOW = jnp.bfloat16
F32 = jnp.float32
LOG2E = math.log2(math.e)
SCORE_SCALE = HEAD_DIM ** (-0.5) * LOG2E
SPARE_BYTES = 12 * 2**20
EXTRA = 64
LIGHT = 0.01
LANES = 128
CHAIN = []
TAIL_SLOPE = 0.36
TAIL = (
    0.14371304537508633,
    0.14177245466203425,
    0.1397192603907239,
    0.026549325413860486,
    0.18095403134327948,
    -0.1797647161697652,
    0.047056295581175855,
)


def swap(value, axis, bit):
    size = lax.axis_size(axis)
    return lax.ppermute(value, axis, [(i, i ^ bit) for i in range(size)])


def swap_core(value):
    return swap(value, "core", 1)


def dot(a, b):
    return jnp.dot(a, b, preferred_element_type=F32)


def dot_nt(a, b):
    return lax.dot_general(a, b, (((1,), (1,)), ((), ())), preferred_element_type=F32)


def dot_tn(a, b):
    return lax.dot_general(a, b, (((0,), (0,)), ((), ())), preferred_element_type=F32)


def whole(shape):
    return pl.BlockSpec(shape, lambda *args: (0,) * len(shape), pipeline_mode=pl.Buffered(1))


def run(
    kernel, places, grid, ins, outs, scratch=(), macs=0, after=(), alias=(), weight=8, chain=True
):
    moved = sum(a.size * a.dtype.itemsize for a, spec in ins)
    moved += sum(math.prod(shape) * jnp.dtype(kind).itemsize for shape, kind, spec in outs)
    after = list(after) + (CHAIN if chain else [])
    count, unread = len(ins), len(alias) + len(after)
    results = len(outs)
    flag = (8, 128)
    if chain:
        outs = outs + [(flag, F32, whole(flag))]

    def body(places, *refs):
        made = refs[count + unread :]
        if chain:

            @pl.when(pl.program_id(0) == 0)
            def _():
                made[results][...] = jnp.zeros(flag, F32)

        kernel(places, *refs[:count], *made[:results], *made[len(outs) :])

    held = pl.BlockSpec(memory_space=pl.ANY)
    room = SPARE_BYTES
    for shape, kind, spec in outs + [(a.shape, a.dtype, spec) for a, spec in ins]:
        if spec.block_shape is not None:
            block = math.prod(1 if n is None else n for n in spec.block_shape)
            copies = 2 if spec.pipeline_mode is None else 1
            room += copies * block * jnp.dtype(kind).itemsize
    for ref in scratch:
        if hasattr(ref, "shape") and ref.dtype in (LOW, F32):
            room += math.prod(ref.shape) * jnp.dtype(ref.dtype).itemsize
    made = pl.pallas_call(
        body,
        name=getattr(kernel, "func", kernel).__name__,
        grid_spec=pltpu.PrefetchScalarGridSpec(
            num_scalar_prefetch=1,
            grid=grid,
            in_specs=[spec for a, spec in ins] + [held] * unread,
            out_specs=[spec for shape, kind, spec in outs],
            scratch_shapes=list(scratch),
        ),
        out_shape=[jax.ShapeDtypeStruct(shape, kind) for shape, kind, spec in outs],
        input_output_aliases={1 + count + i: i for i in range(len(alias))},
        compiler_params=pltpu.CompilerParams(vmem_limit_bytes=room),
        cost_estimate=pl.CostEstimate(
            flops=int(2 * macs * weight), bytes_accessed=int(moved * weight), transcendentals=0
        ),
    )(places, *[a for a, spec in ins], *alias, *after)
    if chain:
        CHAIN[:] = made[results:]
    return made[:results]


def run_whole(
    kernel, places, ins, outs, scratch=(), macs=0, after=(), alias=(), weight=8, chain=True
):
    pairs = [a if isinstance(a, tuple) else (a, pltpu.VMEM) for a in ins]
    after = list(after) + (CHAIN if chain else [])
    count, unread, results = len(pairs), len(alias) + len(after), len(outs)
    if chain:
        outs = outs + [((8, 128), F32)]

    def body(places, *refs):
        made = refs[count + unread :]
        if chain:
            made[results][...] = jnp.zeros((8, 128), F32)
        kernel(places, *refs[:count], *made[:results], *made[len(outs) :])

    room = SPARE_BYTES
    for ref in scratch:
        if hasattr(ref, "shape") and ref.dtype in (LOW, F32):
            room += math.prod(ref.shape) * jnp.dtype(ref.dtype).itemsize
    spaces = [pltpu.SMEM] + [space for a, space in pairs]
    spaces += [pltpu.VMEM] * len(alias) + [pl.ANY] * len(after)
    made = pl.pallas_call(
        body,
        name=getattr(kernel, "func", kernel).__name__,
        in_specs=[pl.BlockSpec(memory_space=space) for space in spaces],
        out_specs=[pl.BlockSpec(memory_space=pltpu.VMEM)] * len(outs),
        scratch_shapes=list(scratch),
        out_shape=[jax.ShapeDtypeStruct(shape, kind) for shape, kind in outs],
        input_output_aliases={1 + count + i: i for i in range(len(alias))},
        compiler_params=pltpu.CompilerParams(vmem_limit_bytes=room),
        cost_estimate=pl.CostEstimate(
            flops=int(2 * macs * weight), bytes_accessed=0, transcendentals=0
        ),
    )(places, *[a for a, space in pairs], *alias, *after)
    if chain:
        CHAIN[:] = made[results:]
    return made[:results]


def each(count, size, body):
    def step(i, carry):
        body(pl.ds(pl.multiple_of(i * size, size), size))
        return carry

    lax.fori_loop(0, count // size, step, 0)


def tiles_of(count, size):
    return [slice(at, at + size) for at in range(0, count, size)]


def three_parts(values):
    parts, rest = [], values
    for _ in range(3):
        parts.append(rest.astype(LOW))
        rest = rest - parts[-1].astype(F32)
    return parts


def segment_rows(seg_row):
    shape = (16, seg_row.shape[1])
    place = lax.broadcasted_iota(jnp.int32, shape, 0)
    same = place - 1 == seg_row
    keys = jnp.where(same, 1.0, jnp.where((place >= 8) & (place < 11), 1.0, 0.0))
    queries = jnp.where(same | (place > 4), 0.0, -1e30)
    return keys.astype(LOW), queries.astype(LOW)


def attend_heads(tok, w_rows, bias, seg_row, qkv_ref, mix_ref, log_ref):
    width = w_rows.shape[0] // 3
    added = dot_tn(bias[:, : 2 * width], jnp.ones((bias.shape[0], tok.shape[0]), LOW))
    qkv = dot_nt(w_rows, tok)
    parts = (
        (qkv[:width] + added[:width]).astype(LOW),
        qkv[width : 2 * width].astype(LOW),
        (qkv[2 * width :] + added[width:]).astype(LOW),
    )
    for c in range(3):
        qkv_ref[c * width : (c + 1) * width] = parts[c]
    more_k, more_q = segment_rows(seg_row)
    for head in range(width // HEAD_DIM):
        q, k, v = (part[head * HEAD_DIM : (head + 1) * HEAD_DIM] for part in parts)
        scores = dot_tn(jnp.concatenate([k, more_k], 0), jnp.concatenate([q, more_q], 0))
        columns, tops, totals = [], [], []
        for tile in tiles_of(scores.shape[1], LANES):
            top = jnp.max(scores[:, tile], 0, keepdims=True)
            total, column = 0.0, []
            for rows in tiles_of(scores.shape[0], 64):
                exponent = jnp.exp2((scores[rows, tile] - top) * SCORE_SCALE)
                total = total + jnp.sum(exponent, 0, keepdims=True)
                column.append(exponent.astype(LOW))
            columns.append(jnp.concatenate(column, 0))
            tops.append(top)
            totals.append(total)
        total = jnp.concatenate(totals, 1)
        mixed = dot(v, jnp.concatenate(columns, 1)) * (1.0 / total)
        mix_ref[head * HEAD_DIM : (head + 1) * HEAD_DIM] = mixed.astype(LOW)
        top = jnp.concatenate(tops, 1)
        log_ref[head : head + 1] = top + jnp.log2(total) * (1.0 / SCORE_SCALE)


def own_attention(
    places, tok, w, bias, seg_row, qkv_ref, mix_ref, log_ref, w_qkv, w_out
):
    count = qkv_ref.shape[1]
    w_qkv[0] = w[:count]
    w_out[0] = w[count:]
    attend_heads(
        tok[...], w[:count], bias[...], seg_row[...], qkv_ref.at[0], mix_ref.at[0], log_ref.at[0]
    )


def far_attention(
    d, order, places, tok, pair, rest, pair_far, rest_far, hop, seg_row,
    qkv_ref, mix_ref, log_ref, w_qkv, w_out, w_ref,
):
    first, second = order
    rows, count = pair.shape[1], qkv_ref.shape[1]
    me = places[0] * 2 + places[1]
    for other, held in enumerate(((pair, rest), (pair_far, rest_far))):
        for two, block in enumerate(held):
            for one in range(2):
                owner = me ^ (other + 2 * first * one + 2 * second * two)
                w_ref[pl.ds(pl.multiple_of(owner * rows, rows), rows)] = block[one]
    w_qkv[d] = w_ref[:count]
    w_out[d] = w_ref[count:]
    attend_heads(
        tok[...],
        w_ref[:count],
        hop[rows:],
        seg_row[...],
        qkv_ref.at[d],
        mix_ref.at[d],
        log_ref.at[d],
    )


def copy_rows(places, rows, out):
    out[...] = rows[...]


def pair_rows(places, first, second, out):
    out[0] = first[: out.shape[1]]
    out[1] = second[: out.shape[1]]


def norm_stats(v):
    centred = v - jnp.mean(v, -1, keepdims=True)
    inv = lax.rsqrt(jnp.mean(centred * centred, -1, keepdims=True) + 1e-05)
    return centred * inv, inv


def norm_back(upstream, unit, inv, gain):
    scaled = upstream * gain
    inner = jnp.mean(scaled * unit, -1, keepdims=True)
    return inv * (scaled - jnp.mean(scaled, -1, keepdims=True) - unit * inner)


def gelu_both(pre):
    power = jnp.exp2(pre * pre * (-0.5 * LOG2E))
    base = 1.0 + TAIL_SLOPE * jnp.abs(pre)
    t = pl.reciprocal(base, approx=True)
    tail = TAIL[6] * t + TAIL[5]
    for c in TAIL[4::-1]:
        tail = tail * t + c
    tail = tail * (t * power)
    cumul = jnp.where(pre < 0.0, tail, 1.0 - tail)
    return (pre * cumul).astype(LOW), cumul + pre * (power * 0.3989422804014327)


def share(core, wide, mine, other):
    half = wide.shape[1] // 2
    left, right = wide[:, :half], wide[:, half:]
    mine[...] = jnp.where(core == 0, left, right)
    other[...] = jnp.where(core == 0, right, left)


def feed_forward(
    places, tok, mix, w_out, b_out, gain1, shift1, b_down, gain2, shift2, w_up, b_up, w_down, cot,
    send, own, ends, slope, unit1, inv1, res2, out, small, tok_send,
    hidden, low, acts, total,
):
    heads, width, half = mix.shape[0], low.shape[1], send.shape[2]
    chunk = 2 * half
    core, z = places[1], places[2]
    b_out, gain1, shift1, b_down, gain2, shift2 = (
        ref[...].reshape(1, -1) for ref in (b_out, gain1, shift1, b_down, gain2, shift2)
    )
    tok_send[...] = jnp.where(core == 0, tok[:, half:], tok[:, :half])
    total[...] = dot_tn(mix[...].reshape(width, low.shape[0]), w_out[...].reshape(width, width))

    def first_norm(rows):
        unit, inv = norm_stats(tok[rows].astype(F32) + (total[rows] + b_out))
        unit1[rows] = unit
        inv1[rows] = inv
        one = unit * gain1 + shift1
        hidden[rows] = one
        one_low = one.astype(LOW)
        low[rows] = one_low
        ends[0, rows] = one_low[:, :half]
        ends[1, rows] = one_low[:, half:]

    each(low.shape[0], 64, first_norm)

    def one_unit(h, carry):
        start = pl.multiple_of(h * chunk, chunk)
        for at in tiles_of(chunk, 256):
            wide = pl.ds(pl.multiple_of(start + at.start, 256), 256)
            pre = dot(low[...], w_up[:, wide])
            for rows in tiles_of(pre.shape[0], 32):
                act, tilt = gelu_both(pre[rows] + b_up[h, :, at])
                slope[h, rows, at] = tilt.astype(LOW)
                acts[rows, wide] = act
        left = acts[:, pl.ds(start, half)]
        right = acts[:, pl.ds(pl.multiple_of(start + half, 128), half)]
        own[z ^ h] = jnp.where(core == 0, left, right)
        send[z ^ h] = jnp.where(core == 0, right, left)
        return carry

    lax.fori_loop(0, heads, one_unit, 0)
    total[...] = dot(acts[...], w_down[...])
    small[...] = jnp.zeros_like(small)

    def second_norm(rows):
        unit, inv = norm_stats(hidden[rows] + (total[rows] + b_down))
        out[rows] = (unit * gain2 + shift2).astype(LOW)
        upstream = cot[rows].astype(F32)
        grad = norm_back(upstream, unit, inv, gain2)
        res2[rows] = grad
        grad_low = grad.astype(LOW)
        ends[2, rows] = grad_low[:, :half]
        ends[3, rows] = grad_low[:, half:]
        for i, term in enumerate((grad_low.astype(F32), upstream * unit, upstream)):
            small[i : i + 1] += jnp.sum(term, 0, keepdims=True)

    each(low.shape[0], 64, second_norm)


def inner_back(places, ends, w_down, slope, send, own, bias, inners):
    heads, _, chunk = slope.shape
    core, z = places[1], places[2]
    branch = jnp.concatenate([ends[2], ends[3]], 1)
    for h in range(heads):
        for at in tiles_of(chunk, 256):
            grad_act = dot_nt(branch, w_down[h * chunk + at.start : h * chunk + at.stop])
            total = 0.0
            for rows in tiles_of(grad_act.shape[0], 32):
                inner = (grad_act[rows] * slope[h, rows, at].astype(F32)).astype(LOW)
                inners[rows, at] = inner
                total = total + jnp.sum(inner.astype(F32), 0, keepdims=True)
            bias[h, :, at] = total
        share(core, inners, own.at[z ^ h], send.at[z ^ h])


def hidden_back(places, own, sent, w_up, res2, unit1, inv1, gain1, send, res1, low, small):
    heads, count, half = own.shape
    core, z = places[1], places[2]
    sides = []
    for h in range(heads):
        mine, other = own[z ^ h], sent[z ^ h]
        sides += [jnp.where(core == 0, mine, other), jnp.where(core == 0, other, mine)]
    product = dot_nt(jnp.concatenate(sides, 1), w_up[...])
    gain = gain1[...].reshape(1, -1)
    sums = [0.0] * 3
    for rows in tiles_of(count, 32):
        grad, unit = product[rows] + res2[rows], unit1[rows]
        result = norm_back(grad, unit, inv1[rows], gain)
        res1[rows] = result
        result_low = result.astype(LOW)
        low[rows] = result_low
        send[rows] = jnp.where(core == 0, result_low[:, half:], result_low[:, :half])
        for i, term in enumerate((result_low.astype(F32), grad * unit, grad)):
            sums[i] = sums[i] + jnp.sum(term, 0, keepdims=True)
    for i in range(3):
        small[i : i + 1] = sums[i]


def shard_back(qkv, w_out, grad, log_ref, more_k, more_q, rows_ref, bias_ref):
    width = qkv.shape[0] // 3
    grad_mixed = dot_nt(w_out[...], grad[...]).astype(LOW)
    scale = HEAD_DIM ** (-0.5)
    for head in range(width // HEAD_DIM):
        places_of = [c * width + head * HEAD_DIM for c in range(3)]
        q, k, v = (qkv[at : at + HEAD_DIM] for at in places_of)
        g = grad_mixed[head * HEAD_DIM : (head + 1) * HEAD_DIM]
        logs = jnp.concatenate(three_parts(-log_ref[head : head + 1]), 0)
        with_logs = jnp.concatenate([more_q[:8], logs, more_q[11:]], 0)
        scores = dot_tn(jnp.concatenate([k, more_k], 0), jnp.concatenate([q, with_logs], 0))
        grad_probs = dot_tn(v, g)
        attends, grads = [], []
        for tile in tiles_of(scores.shape[1], LANES):
            inner, kept, lows, parts = 0.0, [], [], []
            tall = tiles_of(scores.shape[0], 64)
            for down in tall:
                attend = jnp.exp2(scores[down, tile] * SCORE_SCALE)
                inner = inner + jnp.sum(attend * grad_probs[down, tile], 0, keepdims=True)
                kept.append(attend)
                lows.append(attend.astype(LOW))
            for down, attend in zip(tall, kept):
                parts.append((attend * (grad_probs[down, tile] - inner)).astype(LOW))
            attends.append(jnp.concatenate(lows, 0))
            grads.append(jnp.concatenate(parts, 0))
        attend_low = jnp.concatenate(attends, 1)
        grad_scores = jnp.concatenate(grads, 1)
        grad_v = dot_nt(g, attend_low)
        grad_q = dot(k, grad_scores) * scale
        grad_k = dot_nt(q, grad_scores) * scale
        for at, value in zip(places_of, (grad_q, grad_k, grad_v)):
            rows_ref[at : at + HEAD_DIM] = value.astype(LOW)
    ones = jnp.ones((8, rows_ref.shape[1]), LOW)
    bias_ref[...] = dot_nt(ones, rows_ref[...])


def attention_back(places, qkv, w_out, grad, log_ref, seg_row, rows_ref, bias_ref):
    more_k, more_q = segment_rows(seg_row[...])

    def shard(d, carry):
        refs = (ref.at[d] for ref in (rows_ref, bias_ref))
        shard_back(qkv.at[d], w_out.at[d], grad, log_ref.at[d], more_k, more_q, *refs)
        return carry

    lax.fori_loop(0, qkv.shape[0], shard, 0)


def split_rows(value, high, send, keep):
    rows = value.shape[0] // 2
    low = value.astype(LOW)
    send[...] = jnp.where(high, low[:rows], low[rows:])
    keep[...] = jnp.where(high, low[rows:], low[:rows])


def is_high(places, bit):
    return (places[0] & bit) != 0


def unit_products(which, units, units_far, ends, ends_far, both):
    half, count = ends.shape[2], ends.shape[1]
    for side in range(2):
        rows = slice(side * half, (side + 1) * half)
        both[rows, :count] = ends[2 * which + side].T
        both[rows, count:] = ends_far[2 * which + side].T
    for d in range(0, units.shape[0], 2):
        left, right = (jnp.concatenate([units[d + i], units_far[d + i]], 0) for i in range(2))
        yield d, dot(both[...], jnp.concatenate([left, right], 1))


def down_grad(places, units, units_far, ends, ends_far, send, keep, both):
    half = send.shape[2]
    for d, total in unit_products(1, units, units_far, ends, ends_far, both):
        keep[d // 2] = total[:, :half].astype(LOW)
        send[d // 2] = total[:, half:].astype(LOW)


def up_grad(places, units, units_far, ends, ends_far, send_x, keep_x, send_y, keep_y, both):
    half = send_x.shape[2]
    for d, total in unit_products(0, units, units_far, ends, ends_far, both):
        for i in range(2):
            part = total[:, i * half : (i + 1) * half]
            split_rows(part[:half], is_high(places, 1), send_x.at[d + i], keep_x.at[d + i])
            split_rows(part[half:], is_high(places, 2), send_y.at[d + i], keep_y.at[d + i])


def split_at(value, high, send, keep, start):
    rows = value.shape[0] // 2
    low = value.astype(LOW)
    send[start : start + rows] = jnp.where(high, low[:rows], low[rows:])
    keep[start : start + rows] = jnp.where(high, low[rows:], low[:rows])


def first_stage(
    places, d_keep, d_came, x_keep, x_came, y_keep, y_came, send_x, keep_x, send_y, keep_y
):
    half = d_keep.shape[2]
    at = 0
    for i in range(d_keep.shape[0]):
        total = d_keep[i].astype(F32) + d_came[i].astype(F32)
        split_at(total[:half], is_high(places, 1), send_x, keep_x, at)
        split_at(total[half:], is_high(places, 2), send_y, keep_y, at)
        at += half // 2
    for d in range(x_keep.shape[0]):
        upper = x_keep[d].astype(F32) + x_came[d].astype(F32)
        lower = y_keep[d].astype(F32) + y_came[d].astype(F32)
        split_at(upper, is_high(places, 2), send_y, keep_y, at)
        split_at(lower, is_high(places, 1), send_x, keep_x, at)
        at += upper.shape[0] // 2


def second_stage(
    places, x_keep, x_came, y_keep, y_came, send_x, keep_x, send_y, keep_y, send_z, keep_z
):
    rows = send_x.shape[1]
    at = 0
    for i in range(send_x.shape[0]):
        piece = slice(at, at + 2 * rows)
        upper = x_keep[piece].astype(F32) + x_came[piece].astype(F32)
        lower = y_keep[piece].astype(F32) + y_came[piece].astype(F32)
        split_rows(upper, is_high(places, 2), send_y.at[i], keep_y.at[i])
        split_rows(lower, is_high(places, 1), send_x.at[i], keep_x.at[i])
        at += 2 * rows
    for d in range(2 * send_z.shape[0]):
        piece = slice(at, at + rows)
        out = (send_z if d % 2 else keep_z).at[d // 2]
        out[:rows] = (y_keep[piece].astype(F32) + y_came[piece].astype(F32)).astype(LOW)
        out[rows:] = (x_keep[piece].astype(F32) + x_came[piece].astype(F32)).astype(LOW)
        at += rows


def third_stage(places, x_keep, x_came, y_keep, y_came, z_keep, z_came, mine, other):
    rows = x_keep.shape[1]
    for i, out in enumerate((mine, other)):
        out[:rows] = (y_keep[i].astype(F32) + y_came[i].astype(F32)).astype(LOW)
        out[rows : 2 * rows] = (x_keep[i].astype(F32) + x_came[i].astype(F32)).astype(LOW)
        out[2 * rows :] = (z_keep[i].astype(F32) + z_came[i].astype(F32)).astype(LOW)


def attn_grad(
    places, rows, rows_far, tok, tok_far, mix, mix_far, grad, grad_far,
    small_one, small_two, up_bias, qkv_bias, send_x, keep_x, send_y, keep_y,
):
    width = mix.shape[1]
    half = tok_far.shape[1]
    core, z = places[1], places[2]

    def both(near, far):
        mine = jnp.where(core == 0, near[:, :half], near[:, half:])
        return jnp.concatenate([mine, far[...]], 0)

    tok_both, grad_both = both(tok, tok_far), both(grad, grad_far)
    for d in range(rows.shape[0]):
        qkv = dot(jnp.concatenate([rows[d], rows_far[d]], 1), tok_both)
        out = dot(jnp.concatenate([mix[d], mix_far[d]], 1), grad_both)
        lines = []
        for held in (small_one, small_two):
            for i in range(3):
                lines += [held[i : i + 1, :half], held[i : i + 1, half:]]
        line, bias = up_bias[z ^ d], qkv_bias[d]
        lines += [line[:, :half], line[:, half:]]
        lines.append(jnp.concatenate([bias[0:1, :width], bias[0:1, 2 * width :]], 1))
        lines.append(jnp.zeros((EXTRA - len(lines), half), F32))
        total = jnp.concatenate([qkv, out] + lines, 0)
        split_rows(total[:half], is_high(places, 1), send_x.at[d], keep_x.at[d])
        split_rows(total[half:], is_high(places, 2), send_y.at[d], keep_y.at[d])


def add_split(bits, places, *refs):
    for i, bit in enumerate(bits):
        keep, came = refs[2 * i : 2 * i + 2]
        send, left = refs[2 * (len(bits) + i) : 2 * (len(bits) + i) + 2]
        for d in range(keep.shape[0]):
            total = keep[d].astype(F32) + came[d].astype(F32)
            split_rows(total, is_high(places, bit), send.at[d], left.at[d])


def add_parts(places, keep_a, came_a, keep_b, came_b, send, keep):
    rows = keep_a.shape[1]
    for d in range(keep_a.shape[0]):
        out = (send if d % 2 else keep).at[d // 2]
        out[:rows] = (keep_a[d].astype(F32) + came_a[d].astype(F32)).astype(LOW)
        out[rows:] = (keep_b[d].astype(F32) + came_b[d].astype(F32)).astype(LOW)


def add_pair(places, keep, came, *outs):
    for i, out in enumerate(outs):
        out[...] = (keep[i].astype(F32) + came[i].astype(F32)).astype(LOW)


def add_two(places, keep, came, out):
    out[...] = (keep[...].astype(F32) + came[...].astype(F32)).astype(LOW)


def input_sum(places, rows, w, res1, out):
    heads, count, tokens = rows.shape
    total = dot_tn(rows[...].reshape(heads * count, tokens), w[...].reshape(heads * count, -1))
    out[...] = res1[...] + total


def place_pieces(places, held, full, layouts):
    near, core = places[0], places[1]
    width = held[0].shape[1]
    for off in range(4):
        chip = near ^ off
        mine, other = held[off][...], held[4 + off][...]
        sides = (jnp.where(core == 0, mine, other), jnp.where(core == 0, other, mine))
        for at, rows, start, outer in layouts:
            low_bit, high_bit = chip & 1, chip >> 1
            order = 2 * low_bit + high_bit if outer == 1 else 2 * high_bit + low_bit
            to = pl.multiple_of(start + order * rows, 16)
            for side in range(2):
                full[pl.ds(to, rows), side * width : (side + 1) * width] = sides[side][
                    at : at + rows
                ].astype(F32)


def ffn_place(places, *refs):
    held = [ref.at[off] for ref in refs[:2] for off in range(4)]
    down, up, full = refs[2:]
    rows = held[0].shape[0] // 4
    half = 4 * rows
    place_pieces(places, held, full, [(0, rows, 0, 1), (rows, rows, half, 2)])
    down[...] = full[...].T
    place_pieces(places, held, up, [(2 * rows, rows, 0, 1), (3 * rows, rows, half, 2)])


def collect(places, *refs):
    for off in range(4):
        refs[4][off] = refs[off][...]


def attn_place(places, *refs):
    held = [ref.at[off] for ref in refs[:2] for off in range(4)]
    qkv, w_out, small, up_bias, qv_bias, full = refs[2:]
    width = held[0].shape[1]
    count = w_out.shape[0]
    rows = count // 2
    more = held[0].shape[0] - rows
    place_pieces(places, held, full, [(0, rows, 0, 1), (rows, more, 4 * rows, 2)])
    for c in range(3):
        qkv[c] = full[c * count : (c + 1) * count]
    w_out[...] = full[3 * count : 4 * count]
    at = 4 * count
    lines = full[at : at + 16, :width] + full[at : at + 16, width:]
    for i in range(6):
        small[i : i + 1, :width] = lines[2 * i : 2 * i + 1]
        small[i : i + 1, width:] = lines[2 * i + 1 : 2 * i + 2]
    up_bias[...] = jnp.concatenate([lines[12:13], lines[13:14]], 1).reshape(2 * width)
    qv_bias[0:1] = lines[14:15, :count]
    qv_bias[1:2] = lines[14:15, count : 2 * count]


def bias_parts(values):
    rows, rest = [], values
    for _ in range(3):
        rows.append(lax.reduce_precision(rest, 8, 7))
        rest = rest - rows[-1]
    return jnp.stack(rows).astype(LOW)


def gather_back(piece):
    return [piece] + [swap(piece, "near", off) for off in range(1, 4)]


def per_device(
    tokens,
    segment_ids,
    w_qkv,
    b_qv,
    w_out,
    b_out,
    ln1_gain,
    ln1_bias,
    w_up,
    b_up,
    w_down,
    b_down,
    ln2_gain,
    ln2_bias,
    cotangent,
):
    CHAIN.clear()
    width = tokens.shape[1]
    own_rows = cotangent.shape[0]
    local_width = w_qkv.shape[2]
    heads = lax.axis_size("head")
    z = lax.axis_index("head")
    core = lax.axis_index("core")
    near = lax.axis_index("near")
    hidden_units = w_up.shape[1]
    chunk = hidden_units // heads
    half = width // 2
    rows3 = 3 * local_width
    places = jnp.stack([near, core, z]).astype(jnp.int32)

    shard = jnp.concatenate([w_qkv.transpose(0, 2, 1).reshape(rows3, width), w_out], 0)
    piece_rows = shard.shape[0] // 8
    bias = jnp.pad(bias_parts(b_qv.reshape(-1)), ((0, 13), (0, width - 2 * local_width)))
    piece = lax.dynamic_slice_in_dim(shard, (near * 2 + core) * piece_rows, piece_rows, 0)
    piece = jnp.concatenate([piece, bias], 0)
    first_hop = [swap(piece, "head", d) for d in range(1, heads)]

    seg = lax.dynamic_slice_in_dim(segment_ids, z * own_rows, own_rows, 0)
    tok_own = lax.dynamic_slice_in_dim(tokens, z * own_rows, own_rows, 0)
    attend_outs = [
        ((heads, rows3, own_rows), LOW),
        ((heads, local_width, own_rows), LOW),
        ((heads, 8, own_rows), F32),
        ((heads, rows3, width), LOW),
        ((heads, local_width, width), LOW),
    ]
    macs = rows3 * width * own_rows + 6 * own_rows * own_rows * 256
    orders = [(1, 2) if d % 2 else (2, 1) for d in range(heads)]
    nexts = [swap(first_hop[d - 1], "near", orders[d][0]) for d in range(1, heads)]

    def pair_up(d, after):
        (pair,) = run_whole(
            pair_rows, places, [first_hop[d - 1], nexts[d - 1]],
            [((2, piece_rows, width), LOW)], after=after, chain=False,
        )
        return pair

    pairs = [pair_up(1, first_hop[1:])]
    ins = [tok_own, shard, bias, seg[None]]
    made = run_whole(
        own_attention, places, ins, attend_outs, macs=macs, after=pairs, chain=False
    )
    pairs += [pair_up(d, nexts[1:] + [made[2]]) for d in range(2, heads)]
    rests = [swap(pairs[d - 1], "near", orders[d][1]) for d in range(1, heads)]
    for d in range(1, heads):
        pair, rest = pairs[d - 1], rests[d - 1]
        sent = rest
        if d == heads - 1:
            (sent,) = run_whole(
                copy_rows, places, [rest], [(rest.shape, LOW)], after=[second_log], chain=False
            )
        ins = [tok_own, pair, rest, swap_core(pair), swap_core(sent), first_hop[d - 1], seg[None]]
        made = run_whole(
            functools.partial(far_attention, d, orders[d]), places, ins, attend_outs,
            [pltpu.VMEM(shard.shape, LOW)], macs, alias=made, chain=False, weight=100,
        )
        if d == 1:
            second_log = made[2]
    qkvs, mixes, logs, w_qkvs, w_outs = made

    mixes_far = swap_core(mixes)

    square = (own_rows, width)
    tiles = (heads, own_rows, half)
    ins = [
        tok_own, mixes, w_outs, b_out, ln1_gain, ln1_bias, b_down, ln2_gain, ln2_bias,
        w_up, b_up.reshape(heads, 1, chunk), w_down, cotangent,
    ]
    outs = [
        (tiles, LOW),
        (tiles, LOW),
        ((4, own_rows, half), LOW),
        ((heads, own_rows, chunk), LOW),
        (square, F32),
        ((own_rows, 1), F32),
        (square, F32),
        (square, LOW),
        ((8, width), F32),
        ((own_rows, half), LOW),
    ]
    scratch = [
        pltpu.VMEM(square, F32),
        pltpu.VMEM(square, LOW),
        pltpu.VMEM((own_rows, hidden_units), LOW),
        pltpu.VMEM(square, F32),
    ]
    ffn_macs = 2 * own_rows * width * hidden_units
    (
        act_send, act_own, ends, slope, unit1, inv1, res2, layer_output, small_two, tok_send,
    ) = run_whole(feed_forward, places, ins, outs, scratch, ffn_macs)
    tok_far = swap_core(tok_send)
    act_far = swap_core(act_send)
    ends_far = swap_core(ends)

    outs = [(tiles, LOW), (tiles, LOW), ((heads, 1, chunk), F32)]
    scratch = [pltpu.VMEM((own_rows, chunk), LOW)]
    inner_send, inner_own, up_bias = run_whole(
        inner_back, places, [ends, w_down, slope], outs, scratch, ffn_macs // 2, [mixes_far]
    )
    inner_far = swap_core(inner_send)


    both = [pltpu.VMEM((width, 2 * own_rows), LOW)]
    outs = [((heads // 2, width, half), LOW)] * 2
    ins = [act_own, act_far, ends, ends_far]
    d_send, d_keep = run_whole(down_grad, places, ins, outs, both, ffn_macs // 2)
    d_came = swap(d_send, "head", 1)
    outs = [((heads, half // 2, half), LOW)] * 4
    ins = [inner_own, inner_far, ends, ends_far]
    made = run_whole(up_grad, places, ins, outs, both, ffn_macs // 2, weight=LIGHT)
    u_held = (made[1], swap(made[0], "near", 1), made[3], swap(made[2], "near", 2))

    outs = [((own_rows, half), LOW), (square, F32), (square, LOW), ((8, width), F32)]
    ins = [inner_own, inner_send, w_up, res2, unit1, inv1, ln1_gain]
    grad_send, res1, grad_attended, small_one = run_whole(
        hidden_back, places, ins, outs, macs=ffn_macs // 2, weight=LIGHT
    )
    grad_far = swap_core(grad_send)

    def second(x_keep, x_came, y_keep, y_came, macs=0):
        arrays = (x_keep, x_came, y_keep, y_came)
        shapes = [(heads, a.shape[1] // 2, half) for a in (x_keep, x_keep, y_keep, y_keep)]
        outs = [(shape, LOW) for shape in shapes]
        kernel = functools.partial(add_split, (2, 1))
        return run_whole(kernel, places, arrays, outs, macs=macs)

    def third(x_keep, x_came, y_keep, y_came):
        arrays = (x_keep, x_came, y_keep, y_came)
        shape = (heads // 2, x_keep.shape[1] + y_keep.shape[1], half)
        send, keep = run_whole(add_parts, places, arrays, [(shape, LOW)] * 2)
        return keep, swap(send, "head", 1)

    def fourth(keep, came):
        shape = keep.shape[1:]
        mine, other = run_whole(add_pair, places, [keep, came], [(shape, LOW)] * 2)
        return mine, swap(other, "head", 2)

    def fifth(mine, came):
        (total,) = run_whole(add_two, places, [mine, came], [(mine.shape, LOW)])
        bit = 1
        while bit < lax.axis_size("far"):
            total = (total.astype(F32) + swap(total, "far", bit).astype(F32)).astype(LOW)
            bit *= 2
        return total

    def cross_back(made):
        x_send, x_keep, y_send, y_keep = made
        return x_keep, swap(x_send, "near", 1), y_keep, swap(y_send, "near", 2)

    def cross(made, flip):
        x_send, x_keep, y_send, y_keep = made
        x_bit, y_bit = (2, 1) if flip else (1, 2)
        return x_keep, swap(x_send, "near", x_bit), y_keep, swap(y_send, "near", y_bit)

    outs = [((heads, rows3, own_rows), LOW), ((heads, 8, rows3), F32)]
    ins = [qkvs, w_outs, grad_attended, logs, seg[None]]
    rows, qkv_bias = run_whole(attention_back, places, ins, outs)
    rows_far = swap_core(rows)

    outs = [(square, F32, whole(square))]
    ins = [(a, whole(a.shape)) for a in (rows, w_qkvs, res1)]
    (input_grad,) = run(input_sum, places, (1,), ins, outs, weight=LIGHT)
    outs = [((width, half), LOW)] * 4
    ins = [d_keep, d_came, *u_held]
    ffn_held = cross(run_whole(first_stage, places, ins, outs, macs=ffn_macs), False)
    ins = [
        rows, rows_far, tok_own, tok_far, mixes, mixes_far, grad_attended, grad_far,
        small_one, small_two, up_bias, qkv_bias,
    ]
    outs = [
        ((heads, r, half), LOW) for r in (half // 2, (half + EXTRA) // 2) for _ in range(2)
    ]
    made = run_whole(attn_grad, places, ins, outs)
    attn_held = cross(made, False)

    outs = [((heads // 2, half // 4, half), LOW)] * 4 + [((heads // 2, half // 2, half), LOW)] * 2
    made = run_whole(second_stage, places, list(ffn_held), outs, macs=ffn_macs)
    ffn_held = cross_back(made[:4]) + (made[5], swap(made[4], "head", 1))
    outs = [((half, half), LOW)] * 2
    mine, other = run_whole(third_stage, places, list(ffn_held), outs)
    ffn_held = mine, swap(other, "head", 2)
    attn_held = cross(second(*attn_held), True)
    attn_held = third(*attn_held)
    ffn_held = gather_back(fifth(*ffn_held))
    attn_held = fourth(*attn_held)
    attn_held = gather_back(fifth(*attn_held))

    def both_cores(held):
        shape = (heads,) + held[0].shape
        (pieces,) = run_whole(collect, places, held, [(shape, LOW)])
        return [(a, whole(shape)) for a in (pieces, swap_core(pieces))]

    ffn_held = both_cores(ffn_held)
    outs = [(shape, F32, whole(shape)) for shape in ((chunk, width), (width, chunk))]
    grad_down, grad_up = run(
        ffn_place, places, (1,), ffn_held, outs, [pltpu.VMEM((width, chunk), F32)]
    )
    attn_held = both_cores(attn_held)
    shapes = [
        (3, local_width, width),
        (local_width, width),
        (6, width),
        (chunk,),
        (2, local_width),
    ]
    grad_qkv, grad_out, grad_small, grad_up_bias, grad_qv_bias = run(
        attn_place,
        places,
        (1,),
        attn_held,
        [(shape, F32, whole(shape)) for shape in shapes],
        [pltpu.VMEM((width + EXTRA, width), F32)],
    )
    return (
        layer_output,
        input_grad,
        grad_qkv.transpose(0, 2, 1),
        grad_qv_bias,
        grad_out,
        grad_up,
        grad_up_bias,
        grad_down,
        grad_small,
    )


def solution(mesh):
    batch, heads = mesh.devices.shape
    mesh = Mesh(
        mesh.devices.reshape(batch // 8, 4, 2, heads), ("far", "near", "core", "head")
    )
    group = ("far", "near", "core")
    everyone = group + ("head",)
    in_specs = (
        P(group, None),
        P(group),
        P(None, None, "head"),
        P(None, "head"),
        P("head", None),
        P(),
        P(),
        P(),
        P(),
        P(),
        P(),
        P(),
        P(),
        P(),
        P(everyone, None),
    )
    out_specs = (
        P(everyone, None),
        P(everyone, None),
        P(None, None, "head"),
        P(None, "head"),
        P("head", None),
        P(None, "head"),
        P("head"),
        P("head", None),
        P(),
    )
    return jax.shard_map(
        per_device, mesh=mesh, in_specs=in_specs, out_specs=out_specs, check_vma=False
    )
```

```python
import functools
import math

import jax
import jax.numpy as jnp
from jax import lax
from jax.experimental import pallas as pl
from jax.experimental.pallas import tpu as pltpu
from jax.sharding import Mesh
from jax.sharding import PartitionSpec as P

HEAD_DIM = 64
SLOT = 512
LOW = jnp.bfloat16
F32 = jnp.float32
LOG2E = math.log2(math.e)
SCORE_SCALE = HEAD_DIM ** (-0.5) * LOG2E
SPARE_BYTES = 12 * 2**20
EXTRA = 64
LIGHT = 0.01
LANES = 128
CHAIN = []
TAIL_SLOPE = 0.36
TAIL = (
    0.14371304537508633,
    0.14177245466203425,
    0.1397192603907239,
    0.026549325413860486,
    0.18095403134327948,
    -0.1797647161697652,
    0.047056295581175855,
)


def swap(value, axis, bit):
    size = lax.axis_size(axis)
    return lax.ppermute(value, axis, [(i, i ^ bit) for i in range(size)])


def swap_core(value):
    return swap(value, "core", 1)


def dot(a, b):
    return jnp.dot(a, b, preferred_element_type=F32)


def dot_nt(a, b):
    return lax.dot_general(a, b, (((1,), (1,)), ((), ())), preferred_element_type=F32)


def dot_tn(a, b):
    return lax.dot_general(a, b, (((0,), (0,)), ((), ())), preferred_element_type=F32)


def whole(shape):
    return pl.BlockSpec(shape, lambda *args: (0,) * len(shape), pipeline_mode=pl.Buffered(1))


def run(
    kernel, places, grid, ins, outs, scratch=(), macs=0, after=(), alias=(), weight=8, chain=True
):
    moved = sum(a.size * a.dtype.itemsize for a, spec in ins)
    moved += sum(math.prod(shape) * jnp.dtype(kind).itemsize for shape, kind, spec in outs)
    after = list(after) + (CHAIN if chain else [])
    count, unread = len(ins), len(alias) + len(after)
    results = len(outs)
    flag = (8, 128)
    if chain:
        outs = outs + [(flag, F32, whole(flag))]

    def body(places, *refs):
        made = refs[count + unread :]
        if chain:

            @pl.when(pl.program_id(0) == 0)
            def _():
                made[results][...] = jnp.zeros(flag, F32)

        kernel(places, *refs[:count], *made[:results], *made[len(outs) :])

    held = pl.BlockSpec(memory_space=pl.ANY)
    room = SPARE_BYTES
    for shape, kind, spec in outs + [(a.shape, a.dtype, spec) for a, spec in ins]:
        if spec.block_shape is not None:
            block = math.prod(1 if n is None else n for n in spec.block_shape)
            copies = 2 if spec.pipeline_mode is None else 1
            room += copies * block * jnp.dtype(kind).itemsize
    for ref in scratch:
        if hasattr(ref, "shape") and ref.dtype in (LOW, F32):
            room += math.prod(ref.shape) * jnp.dtype(ref.dtype).itemsize
    made = pl.pallas_call(
        body,
        name=getattr(kernel, "func", kernel).__name__,
        grid_spec=pltpu.PrefetchScalarGridSpec(
            num_scalar_prefetch=1,
            grid=grid,
            in_specs=[spec for a, spec in ins] + [held] * unread,
            out_specs=[spec for shape, kind, spec in outs],
            scratch_shapes=list(scratch),
        ),
        out_shape=[jax.ShapeDtypeStruct(shape, kind) for shape, kind, spec in outs],
        input_output_aliases={1 + count + i: i for i in range(len(alias))},
        compiler_params=pltpu.CompilerParams(vmem_limit_bytes=room),
        cost_estimate=pl.CostEstimate(
            flops=int(2 * macs * weight), bytes_accessed=int(moved * weight), transcendentals=0
        ),
    )(places, *[a for a, spec in ins], *alias, *after)
    if chain:
        CHAIN[:] = made[results:]
    return made[:results]


def run_whole(
    kernel, places, ins, outs, scratch=(), macs=0, after=(), alias=(), weight=8, chain=True
):
    pairs = [a if isinstance(a, tuple) else (a, pltpu.VMEM) for a in ins]
    after = list(after) + (CHAIN if chain else [])
    count, unread, results = len(pairs), len(alias) + len(after), len(outs)
    if chain:
        outs = outs + [((8, 128), F32)]

    def body(places, *refs):
        made = refs[count + unread :]
        if chain:
            made[results][...] = jnp.zeros((8, 128), F32)
        kernel(places, *refs[:count], *made[:results], *made[len(outs) :])

    room = SPARE_BYTES
    for ref in scratch:
        if hasattr(ref, "shape") and ref.dtype in (LOW, F32):
            room += math.prod(ref.shape) * jnp.dtype(ref.dtype).itemsize
    spaces = [pltpu.SMEM] + [space for a, space in pairs]
    spaces += [pltpu.VMEM] * len(alias) + [pl.ANY] * len(after)
    made = pl.pallas_call(
        body,
        name=getattr(kernel, "func", kernel).__name__,
        in_specs=[pl.BlockSpec(memory_space=space) for space in spaces],
        out_specs=[pl.BlockSpec(memory_space=pltpu.VMEM)] * len(outs),
        scratch_shapes=list(scratch),
        out_shape=[jax.ShapeDtypeStruct(shape, kind) for shape, kind in outs],
        input_output_aliases={1 + count + i: i for i in range(len(alias))},
        compiler_params=pltpu.CompilerParams(vmem_limit_bytes=room),
        cost_estimate=pl.CostEstimate(
            flops=int(2 * macs * weight), bytes_accessed=0, transcendentals=0
        ),
    )(places, *[a for a, space in pairs], *alias, *after)
    if chain:
        CHAIN[:] = made[results:]
    return made[:results]


def each(count, size, body):
    def step(i, carry):
        body(pl.ds(pl.multiple_of(i * size, size), size))
        return carry

    lax.fori_loop(0, count // size, step, 0)


def tiles_of(count, size):
    return [slice(at, at + size) for at in range(0, count, size)]


def three_parts(values):
    parts, rest = [], values
    for _ in range(3):
        parts.append(rest.astype(LOW))
        rest = rest - parts[-1].astype(F32)
    return parts


def segment_rows(seg_row):
    shape = (16, seg_row.shape[1])
    place = lax.broadcasted_iota(jnp.int32, shape, 0)
    same = place - 1 == seg_row
    keys = jnp.where(same, 1.0, jnp.where((place >= 8) & (place < 11), 1.0, 0.0))
    queries = jnp.where(same | (place > 4), 0.0, -1e30)
    return keys.astype(LOW), queries.astype(LOW)


def attend_heads(tok, w_rows, bias, seg_row, qkv_ref, mix_ref, log_ref):
    width = w_rows.shape[0] // 3
    added = dot_tn(bias[:, : 2 * width], jnp.ones((bias.shape[0], tok.shape[0]), LOW))
    qkv = dot_nt(w_rows, tok)
    parts = (
        (qkv[:width] + added[:width]).astype(LOW),
        qkv[width : 2 * width].astype(LOW),
        (qkv[2 * width :] + added[width:]).astype(LOW),
    )
    for c in range(3):
        qkv_ref[c * width : (c + 1) * width] = parts[c]
    more_k, more_q = segment_rows(seg_row)
    for head in range(width // HEAD_DIM):
        q, k, v = (part[head * HEAD_DIM : (head + 1) * HEAD_DIM] for part in parts)
        scores = dot_tn(jnp.concatenate([k, more_k], 0), jnp.concatenate([q, more_q], 0))
        columns, tops, totals = [], [], []
        for tile in tiles_of(scores.shape[1], LANES):
            top = jnp.max(scores[:, tile], 0, keepdims=True)
            total, column = 0.0, []
            for rows in tiles_of(scores.shape[0], 64):
                exponent = jnp.exp2((scores[rows, tile] - top) * SCORE_SCALE)
                total = total + jnp.sum(exponent, 0, keepdims=True)
                column.append(exponent.astype(LOW))
            columns.append(jnp.concatenate(column, 0))
            tops.append(top)
            totals.append(total)
        total = jnp.concatenate(totals, 1)
        mixed = dot(v, jnp.concatenate(columns, 1)) * (1.0 / total)
        mix_ref[head * HEAD_DIM : (head + 1) * HEAD_DIM] = mixed.astype(LOW)
        top = jnp.concatenate(tops, 1)
        log_ref[head : head + 1] = top + jnp.log2(total) * (1.0 / SCORE_SCALE)


def own_attention(
    places, tok, w, bias, seg_row, qkv_ref, mix_ref, log_ref, w_qkv, w_out
):
    count = qkv_ref.shape[1]
    w_qkv[0] = w[:count]
    w_out[0] = w[count:]
    attend_heads(
        tok[...], w[:count], bias[...], seg_row[...], qkv_ref.at[0], mix_ref.at[0], log_ref.at[0]
    )


def far_attention(
    d, order, places, tok, pair, rest, pair_far, rest_far, hop, seg_row,
    qkv_ref, mix_ref, log_ref, w_qkv, w_out, w_ref,
):
    first, second = order
    rows, count = pair.shape[1], qkv_ref.shape[1]
    me = places[0] * 2 + places[1]
    for other, held in enumerate(((pair, rest), (pair_far, rest_far))):
        for two, block in enumerate(held):
            for one in range(2):
                owner = me ^ (other + 2 * first * one + 2 * second * two)
                w_ref[pl.ds(pl.multiple_of(owner * rows, rows), rows)] = block[one]
    w_qkv[d] = w_ref[:count]
    w_out[d] = w_ref[count:]
    attend_heads(
        tok[...],
        w_ref[:count],
        hop[rows:],
        seg_row[...],
        qkv_ref.at[d],
        mix_ref.at[d],
        log_ref.at[d],
    )


def copy_rows(places, rows, out):
    out[...] = rows[...]


def pair_rows(places, first, second, out):
    out[0] = first[: out.shape[1]]
    out[1] = second[: out.shape[1]]


def norm_stats(v):
    centred = v - jnp.mean(v, -1, keepdims=True)
    inv = lax.rsqrt(jnp.mean(centred * centred, -1, keepdims=True) + 1e-05)
    return centred * inv, inv


def norm_back(upstream, unit, inv, gain):
    scaled = upstream * gain
    inner = jnp.mean(scaled * unit, -1, keepdims=True)
    return inv * (scaled - jnp.mean(scaled, -1, keepdims=True) - unit * inner)


def gelu_both(pre):
    power = jnp.exp2(pre * pre * (-0.5 * LOG2E))
    base = 1.0 + TAIL_SLOPE * jnp.abs(pre)
    t = pl.reciprocal(base, approx=True)
    tail = TAIL[6] * t + TAIL[5]
    for c in TAIL[4::-1]:
        tail = tail * t + c
    tail = tail * (t * power)
    cumul = jnp.where(pre < 0.0, tail, 1.0 - tail)
    return (pre * cumul).astype(LOW), cumul + pre * (power * 0.3989422804014327)


def share(core, wide, mine, other):
    half = wide.shape[1] // 2
    left, right = wide[:, :half], wide[:, half:]
    mine[...] = jnp.where(core == 0, left, right)
    other[...] = jnp.where(core == 0, right, left)


def feed_forward(
    places, tok, mix, w_out, b_out, gain1, shift1, b_down, gain2, shift2, w_up, b_up, w_down, cot,
    send, own, ends, slope, unit1, inv1, res2, out, small, tok_send,
    hidden, low, acts, total,
):
    heads, width, half = mix.shape[0], low.shape[1], send.shape[2]
    chunk = 2 * half
    core, z = places[1], places[2]
    b_out, gain1, shift1, b_down, gain2, shift2 = (
        ref[...].reshape(1, -1) for ref in (b_out, gain1, shift1, b_down, gain2, shift2)
    )
    tok_send[...] = jnp.where(core == 0, tok[:, half:], tok[:, :half])
    total[...] = dot_tn(mix[...].reshape(width, low.shape[0]), w_out[...].reshape(width, width))

    def first_norm(rows):
        unit, inv = norm_stats(tok[rows].astype(F32) + (total[rows] + b_out))
        unit1[rows] = unit
        inv1[rows] = inv
        one = unit * gain1 + shift1
        hidden[rows] = one
        one_low = one.astype(LOW)
        low[rows] = one_low
        ends[0, rows] = one_low[:, :half]
        ends[1, rows] = one_low[:, half:]

    each(low.shape[0], 64, first_norm)

    def one_unit(h, carry):
        start = pl.multiple_of(h * chunk, chunk)
        for at in tiles_of(chunk, chunk):
            wide = pl.ds(start, chunk)
            pre = dot(low[...], w_up[:, wide])
            for rows in tiles_of(pre.shape[0], 16):
                act, tilt = gelu_both(pre[rows] + b_up[h, :, at])
                slope[h, rows, at] = tilt.astype(LOW)
                acts[rows, wide] = act
        left = acts[:, pl.ds(start, half)]
        right = acts[:, pl.ds(pl.multiple_of(start + half, 128), half)]
        own[z ^ h] = jnp.where(core == 0, left, right)
        send[z ^ h] = jnp.where(core == 0, right, left)
        return carry

    lax.fori_loop(0, heads, one_unit, 0)
    total[...] = dot(acts[...], w_down[...])
    small[...] = jnp.zeros_like(small)

    def second_norm(rows):
        unit, inv = norm_stats(hidden[rows] + (total[rows] + b_down))
        out[rows] = (unit * gain2 + shift2).astype(LOW)
        upstream = cot[rows].astype(F32)
        grad = norm_back(upstream, unit, inv, gain2)
        res2[rows] = grad
        grad_low = grad.astype(LOW)
        ends[2, rows] = grad_low[:, :half]
        ends[3, rows] = grad_low[:, half:]
        for i, term in enumerate((grad_low.astype(F32), upstream * unit, upstream)):
            small[i : i + 1] += jnp.sum(term, 0, keepdims=True)

    each(low.shape[0], 64, second_norm)


def inner_back(places, ends, w_down, slope, send, own, bias, inners):
    heads, _, chunk = slope.shape
    core, z = places[1], places[2]
    branch = jnp.concatenate([ends[2], ends[3]], 1)
    for h in range(heads):
        for at in tiles_of(chunk, 256):
            grad_act = dot_nt(branch, w_down[h * chunk + at.start : h * chunk + at.stop])
            total = 0.0
            for rows in tiles_of(grad_act.shape[0], 32):
                inner = (grad_act[rows] * slope[h, rows, at].astype(F32)).astype(LOW)
                inners[rows, at] = inner
                total = total + jnp.sum(inner.astype(F32), 0, keepdims=True)
            bias[h, :, at] = total
        share(core, inners, own.at[z ^ h], send.at[z ^ h])


def hidden_back(places, own, sent, w_up, res2, unit1, inv1, gain1, send, res1, low, small):
    heads, count, half = own.shape
    core, z = places[1], places[2]
    sides = []
    for h in range(heads):
        mine, other = own[z ^ h], sent[z ^ h]
        sides += [jnp.where(core == 0, mine, other), jnp.where(core == 0, other, mine)]
    product = dot_nt(jnp.concatenate(sides, 1), w_up[...])
    gain = gain1[...].reshape(1, -1)
    sums = [0.0] * 3
    for rows in tiles_of(count, 32):
        grad, unit = product[rows] + res2[rows], unit1[rows]
        result = norm_back(grad, unit, inv1[rows], gain)
        res1[rows] = result
        result_low = result.astype(LOW)
        low[rows] = result_low
        send[rows] = jnp.where(core == 0, result_low[:, half:], result_low[:, :half])
        for i, term in enumerate((result_low.astype(F32), grad * unit, grad)):
            sums[i] = sums[i] + jnp.sum(term, 0, keepdims=True)
    for i in range(3):
        small[i : i + 1] = sums[i]


def shard_back(qkv, w_out, grad, log_ref, more_k, more_q, rows_ref, bias_ref):
    width = qkv.shape[0] // 3
    grad_mixed = dot_nt(w_out[...], grad[...]).astype(LOW)
    scale = HEAD_DIM ** (-0.5)
    for head in range(width // HEAD_DIM):
        places_of = [c * width + head * HEAD_DIM for c in range(3)]
        q, k, v = (qkv[at : at + HEAD_DIM] for at in places_of)
        g = grad_mixed[head * HEAD_DIM : (head + 1) * HEAD_DIM]
        logs = jnp.concatenate(three_parts(-log_ref[head : head + 1]), 0)
        with_logs = jnp.concatenate([more_q[:8], logs, more_q[11:]], 0)
        scores = dot_tn(jnp.concatenate([k, more_k], 0), jnp.concatenate([q, with_logs], 0))
        grad_probs = dot_tn(v, g)
        attends, grads = [], []
        for tile in tiles_of(scores.shape[1], LANES):
            inner, kept, lows, parts = 0.0, [], [], []
            tall = tiles_of(scores.shape[0], 64)
            for down in tall:
                attend = jnp.exp2(scores[down, tile] * SCORE_SCALE)
                inner = inner + jnp.sum(attend * grad_probs[down, tile], 0, keepdims=True)
                kept.append(attend)
                lows.append(attend.astype(LOW))
            for down, attend in zip(tall, kept):
                parts.append((attend * (grad_probs[down, tile] - inner)).astype(LOW))
            attends.append(jnp.concatenate(lows, 0))
            grads.append(jnp.concatenate(parts, 0))
        attend_low = jnp.concatenate(attends, 1)
        grad_scores = jnp.concatenate(grads, 1)
        grad_v = dot_nt(g, attend_low)
        grad_q = dot(k, grad_scores) * scale
        grad_k = dot_nt(q, grad_scores) * scale
        for at, value in zip(places_of, (grad_q, grad_k, grad_v)):
            rows_ref[at : at + HEAD_DIM] = value.astype(LOW)
    ones = jnp.ones((8, rows_ref.shape[1]), LOW)
    bias_ref[...] = dot_nt(ones, rows_ref[...])


def attention_back(places, qkv, w_out, grad, log_ref, seg_row, rows_ref, bias_ref):
    more_k, more_q = segment_rows(seg_row[...])

    def shard(d, carry):
        refs = (ref.at[d] for ref in (rows_ref, bias_ref))
        shard_back(qkv.at[d], w_out.at[d], grad, log_ref.at[d], more_k, more_q, *refs)
        return carry

    lax.fori_loop(0, qkv.shape[0], shard, 0)


def split_rows(value, high, send, keep):
    rows = value.shape[0] // 2
    low = value.astype(LOW)
    send[...] = jnp.where(high, low[:rows], low[rows:])
    keep[...] = jnp.where(high, low[rows:], low[:rows])


def is_high(places, bit):
    return (places[0] & bit) != 0


def unit_products(which, units, units_far, ends, ends_far, both):
    half, count = ends.shape[2], ends.shape[1]
    for side in range(2):
        rows = slice(side * half, (side + 1) * half)
        both[rows, :count] = ends[2 * which + side].T
        both[rows, count:] = ends_far[2 * which + side].T
    for d in range(0, units.shape[0], 2):
        left, right = (jnp.concatenate([units[d + i], units_far[d + i]], 0) for i in range(2))
        yield d, dot(both[...], jnp.concatenate([left, right], 1))


def down_grad(places, units, units_far, ends, ends_far, send, keep, both):
    half = send.shape[2]
    for d, total in unit_products(1, units, units_far, ends, ends_far, both):
        keep[d // 2] = total[:, :half].astype(LOW)
        send[d // 2] = total[:, half:].astype(LOW)


def up_grad(places, units, units_far, ends, ends_far, send_x, keep_x, send_y, keep_y, both):
    half = send_x.shape[2]
    for d, total in unit_products(0, units, units_far, ends, ends_far, both):
        for i in range(2):
            part = total[:, i * half : (i + 1) * half]
            split_rows(part[:half], is_high(places, 1), send_x.at[d + i], keep_x.at[d + i])
            split_rows(part[half:], is_high(places, 2), send_y.at[d + i], keep_y.at[d + i])


def split_at(value, high, send, keep, start):
    rows = value.shape[0] // 2
    low = value.astype(LOW)
    send[start : start + rows] = jnp.where(high, low[:rows], low[rows:])
    keep[start : start + rows] = jnp.where(high, low[rows:], low[:rows])


def first_stage(
    places, d_keep, d_came, x_keep, x_came, y_keep, y_came, send_x, keep_x, send_y, keep_y
):
    half = d_keep.shape[2]
    at = 0
    for i in range(d_keep.shape[0]):
        total = d_keep[i].astype(F32) + d_came[i].astype(F32)
        split_at(total[:half], is_high(places, 1), send_x, keep_x, at)
        split_at(total[half:], is_high(places, 2), send_y, keep_y, at)
        at += half // 2
    for d in range(x_keep.shape[0]):
        upper = x_keep[d].astype(F32) + x_came[d].astype(F32)
        lower = y_keep[d].astype(F32) + y_came[d].astype(F32)
        split_at(upper, is_high(places, 2), send_y, keep_y, at)
        split_at(lower, is_high(places, 1), send_x, keep_x, at)
        at += upper.shape[0] // 2


def second_stage(
    places, x_keep, x_came, y_keep, y_came, send_x, keep_x, send_y, keep_y, send_z, keep_z
):
    rows = send_x.shape[1]
    at = 0
    for i in range(send_x.shape[0]):
        piece = slice(at, at + 2 * rows)
        upper = x_keep[piece].astype(F32) + x_came[piece].astype(F32)
        lower = y_keep[piece].astype(F32) + y_came[piece].astype(F32)
        split_rows(upper, is_high(places, 2), send_y.at[i], keep_y.at[i])
        split_rows(lower, is_high(places, 1), send_x.at[i], keep_x.at[i])
        at += 2 * rows
    for d in range(2 * send_z.shape[0]):
        piece = slice(at, at + rows)
        out = (send_z if d % 2 else keep_z).at[d // 2]
        out[:rows] = (y_keep[piece].astype(F32) + y_came[piece].astype(F32)).astype(LOW)
        out[rows:] = (x_keep[piece].astype(F32) + x_came[piece].astype(F32)).astype(LOW)
        at += rows


def third_stage(places, x_keep, x_came, y_keep, y_came, z_keep, z_came, mine, other):
    rows = x_keep.shape[1]
    for i, out in enumerate((mine, other)):
        out[:rows] = (y_keep[i].astype(F32) + y_came[i].astype(F32)).astype(LOW)
        out[rows : 2 * rows] = (x_keep[i].astype(F32) + x_came[i].astype(F32)).astype(LOW)
        out[2 * rows :] = (z_keep[i].astype(F32) + z_came[i].astype(F32)).astype(LOW)


def attn_grad(
    places, rows, rows_far, tok, tok_far, mix, mix_far, grad, grad_far,
    small_one, small_two, up_bias, qkv_bias, send_x, keep_x, send_y, keep_y,
):
    width = mix.shape[1]
    half = tok_far.shape[1]
    core, z = places[1], places[2]

    def both(near, far):
        mine = jnp.where(core == 0, near[:, :half], near[:, half:])
        return jnp.concatenate([mine, far[...]], 0)

    tok_both, grad_both = both(tok, tok_far), both(grad, grad_far)
    for d in range(rows.shape[0]):
        qkv = dot(jnp.concatenate([rows[d], rows_far[d]], 1), tok_both)
        out = dot(jnp.concatenate([mix[d], mix_far[d]], 1), grad_both)
        lines = []
        for held in (small_one, small_two):
            for i in range(3):
                lines += [held[i : i + 1, :half], held[i : i + 1, half:]]
        line, bias = up_bias[z ^ d], qkv_bias[d]
        lines += [line[:, :half], line[:, half:]]
        lines.append(jnp.concatenate([bias[0:1, :width], bias[0:1, 2 * width :]], 1))
        lines.append(jnp.zeros((EXTRA - len(lines), half), F32))
        total = jnp.concatenate([qkv, out] + lines, 0)
        split_rows(total[:half], is_high(places, 1), send_x.at[d], keep_x.at[d])
        split_rows(total[half:], is_high(places, 2), send_y.at[d], keep_y.at[d])


def add_split(bits, places, *refs):
    for i, bit in enumerate(bits):
        keep, came = refs[2 * i : 2 * i + 2]
        send, left = refs[2 * (len(bits) + i) : 2 * (len(bits) + i) + 2]
        for d in range(keep.shape[0]):
            total = keep[d].astype(F32) + came[d].astype(F32)
            split_rows(total, is_high(places, bit), send.at[d], left.at[d])


def add_parts(places, keep_a, came_a, keep_b, came_b, send, keep):
    rows = keep_a.shape[1]
    for d in range(keep_a.shape[0]):
        out = (send if d % 2 else keep).at[d // 2]
        out[:rows] = (keep_a[d].astype(F32) + came_a[d].astype(F32)).astype(LOW)
        out[rows:] = (keep_b[d].astype(F32) + came_b[d].astype(F32)).astype(LOW)


def add_pair(places, keep, came, *outs):
    for i, out in enumerate(outs):
        out[...] = (keep[i].astype(F32) + came[i].astype(F32)).astype(LOW)


def add_two(places, keep, came, out):
    out[...] = (keep[...].astype(F32) + came[...].astype(F32)).astype(LOW)


def input_sum(places, rows, w, res1, out):
    heads, count, tokens = rows.shape
    total = dot_tn(rows[...].reshape(heads * count, tokens), w[...].reshape(heads * count, -1))
    out[...] = res1[...] + total


def place_pieces(places, held, full, layouts):
    near, core = places[0], places[1]
    width = held[0].shape[1]
    for off in range(4):
        chip = near ^ off
        mine, other = held[off][...], held[4 + off][...]
        sides = (jnp.where(core == 0, mine, other), jnp.where(core == 0, other, mine))
        for at, rows, start, outer in layouts:
            low_bit, high_bit = chip & 1, chip >> 1
            order = 2 * low_bit + high_bit if outer == 1 else 2 * high_bit + low_bit
            to = pl.multiple_of(start + order * rows, 16)
            for side in range(2):
                full[pl.ds(to, rows), side * width : (side + 1) * width] = sides[side][
                    at : at + rows
                ].astype(F32)


def ffn_place(places, *refs):
    held = [ref.at[off] for ref in refs[:2] for off in range(4)]
    down, up, full = refs[2:]
    rows = held[0].shape[0] // 4
    half = 4 * rows
    place_pieces(places, held, full, [(0, rows, 0, 1), (rows, rows, half, 2)])
    down[...] = full[...].T
    place_pieces(places, held, up, [(2 * rows, rows, 0, 1), (3 * rows, rows, half, 2)])


def collect(places, *refs):
    for off in range(4):
        refs[4][off] = refs[off][...]


def attn_place(places, *refs):
    held = [ref.at[off] for ref in refs[:2] for off in range(4)]
    qkv, w_out, small, up_bias, qv_bias, full = refs[2:]
    width = held[0].shape[1]
    count = w_out.shape[0]
    rows = count // 2
    more = held[0].shape[0] - rows
    place_pieces(places, held, full, [(0, rows, 0, 1), (rows, more, 4 * rows, 2)])
    for c in range(3):
        qkv[c] = full[c * count : (c + 1) * count]
    w_out[...] = full[3 * count : 4 * count]
    at = 4 * count
    lines = full[at : at + 16, :width] + full[at : at + 16, width:]
    for i in range(6):
        small[i : i + 1, :width] = lines[2 * i : 2 * i + 1]
        small[i : i + 1, width:] = lines[2 * i + 1 : 2 * i + 2]
    up_bias[...] = jnp.concatenate([lines[12:13], lines[13:14]], 1).reshape(2 * width)
    qv_bias[0:1] = lines[14:15, :count]
    qv_bias[1:2] = lines[14:15, count : 2 * count]


def bias_parts(values):
    rows, rest = [], values
    for _ in range(3):
        rows.append(lax.reduce_precision(rest, 8, 7))
        rest = rest - rows[-1]
    return jnp.stack(rows).astype(LOW)


def gather_back(piece):
    return [piece] + [swap(piece, "near", off) for off in range(1, 4)]


def per_device(
    tokens,
    segment_ids,
    w_qkv,
    b_qv,
    w_out,
    b_out,
    ln1_gain,
    ln1_bias,
    w_up,
    b_up,
    w_down,
    b_down,
    ln2_gain,
    ln2_bias,
    cotangent,
):
    CHAIN.clear()
    width = tokens.shape[1]
    own_rows = cotangent.shape[0]
    local_width = w_qkv.shape[2]
    heads = lax.axis_size("head")
    z = lax.axis_index("head")
    core = lax.axis_index("core")
    near = lax.axis_index("near")
    hidden_units = w_up.shape[1]
    chunk = hidden_units // heads
    half = width // 2
    rows3 = 3 * local_width
    places = jnp.stack([near, core, z]).astype(jnp.int32)

    shard = jnp.concatenate([w_qkv.transpose(0, 2, 1).reshape(rows3, width), w_out], 0)
    piece_rows = shard.shape[0] // 8
    bias = jnp.pad(bias_parts(b_qv.reshape(-1)), ((0, 13), (0, width - 2 * local_width)))
    piece = lax.dynamic_slice_in_dim(shard, (near * 2 + core) * piece_rows, piece_rows, 0)
    piece = jnp.concatenate([piece, bias], 0)
    first_hop = [swap(piece, "head", d) for d in range(1, heads)]

    seg = lax.dynamic_slice_in_dim(segment_ids, z * own_rows, own_rows, 0)
    tok_own = lax.dynamic_slice_in_dim(tokens, z * own_rows, own_rows, 0)
    attend_outs = [
        ((heads, rows3, own_rows), LOW),
        ((heads, local_width, own_rows), LOW),
        ((heads, 8, own_rows), F32),
        ((heads, rows3, width), LOW),
        ((heads, local_width, width), LOW),
    ]
    macs = rows3 * width * own_rows + 6 * own_rows * own_rows * 256
    orders = [(1, 2) if d % 2 else (2, 1) for d in range(heads)]
    nexts = [swap(first_hop[d - 1], "near", orders[d][0]) for d in range(1, heads)]

    def pair_up(d, after):
        (pair,) = run_whole(
            pair_rows, places, [first_hop[d - 1], nexts[d - 1]],
            [((2, piece_rows, width), LOW)], after=after, chain=False,
        )
        return pair

    pairs = [pair_up(1, first_hop[1:])]
    ins = [tok_own, shard, bias, seg[None]]
    made = run_whole(
        own_attention, places, ins, attend_outs, macs=macs, after=pairs, chain=False
    )
    pairs += [pair_up(d, nexts[1:] + [made[2]]) for d in range(2, heads)]
    rests = [swap(pairs[d - 1], "near", orders[d][1]) for d in range(1, heads)]
    for d in range(1, heads):
        pair, rest = pairs[d - 1], rests[d - 1]
        sent = rest
        if d == heads - 1:
            (sent,) = run_whole(
                copy_rows, places, [rest], [(rest.shape, LOW)], after=[second_log], chain=False
            )
        ins = [tok_own, pair, rest, swap_core(pair), swap_core(sent), first_hop[d - 1], seg[None]]
        made = run_whole(
            functools.partial(far_attention, d, orders[d]), places, ins, attend_outs,
            [pltpu.VMEM(shard.shape, LOW)], macs, alias=made, chain=False, weight=100,
        )
        if d == 1:
            second_log = made[2]
    qkvs, mixes, logs, w_qkvs, w_outs = made

    mixes_far = swap_core(mixes)

    square = (own_rows, width)
    tiles = (heads, own_rows, half)
    ins = [
        tok_own, mixes, w_outs, b_out, ln1_gain, ln1_bias, b_down, ln2_gain, ln2_bias,
        w_up, b_up.reshape(heads, 1, chunk), w_down, cotangent,
    ]
    outs = [
        (tiles, LOW),
        (tiles, LOW),
        ((4, own_rows, half), LOW),
        ((heads, own_rows, chunk), LOW),
        (square, F32),
        ((own_rows, 1), F32),
        (square, F32),
        (square, LOW),
        ((8, width), F32),
        ((own_rows, half), LOW),
    ]
    scratch = [
        pltpu.VMEM(square, F32),
        pltpu.VMEM(square, LOW),
        pltpu.VMEM((own_rows, hidden_units), LOW),
        pltpu.VMEM(square, F32),
    ]
    ffn_macs = 2 * own_rows * width * hidden_units
    (
        act_send, act_own, ends, slope, unit1, inv1, res2, layer_output, small_two, tok_send,
    ) = run_whole(feed_forward, places, ins, outs, scratch, ffn_macs)
    tok_far = swap_core(tok_send)
    act_far = swap_core(act_send)
    ends_far = swap_core(ends)

    outs = [(tiles, LOW), (tiles, LOW), ((heads, 1, chunk), F32)]
    scratch = [pltpu.VMEM((own_rows, chunk), LOW)]
    inner_send, inner_own, up_bias = run_whole(
        inner_back, places, [ends, w_down, slope], outs, scratch, ffn_macs // 2, [mixes_far]
    )
    inner_far = swap_core(inner_send)


    both = [pltpu.VMEM((width, 2 * own_rows), LOW)]
    outs = [((heads // 2, width, half), LOW)] * 2
    ins = [act_own, act_far, ends, ends_far]
    d_send, d_keep = run_whole(down_grad, places, ins, outs, both, ffn_macs // 2)
    d_came = swap(d_send, "head", 1)
    outs = [((heads, half // 2, half), LOW)] * 4
    ins = [inner_own, inner_far, ends, ends_far]
    made = run_whole(up_grad, places, ins, outs, both, ffn_macs // 2, weight=LIGHT)
    u_held = (made[1], swap(made[0], "near", 1), made[3], swap(made[2], "near", 2))

    outs = [((own_rows, half), LOW), (square, F32), (square, LOW), ((8, width), F32)]
    ins = [inner_own, inner_send, w_up, res2, unit1, inv1, ln1_gain]
    grad_send, res1, grad_attended, small_one = run_whole(
        hidden_back, places, ins, outs, macs=ffn_macs // 2, weight=LIGHT
    )
    grad_far = swap_core(grad_send)

    def second(x_keep, x_came, y_keep, y_came, macs=0):
        arrays = (x_keep, x_came, y_keep, y_came)
        shapes = [(heads, a.shape[1] // 2, half) for a in (x_keep, x_keep, y_keep, y_keep)]
        outs = [(shape, LOW) for shape in shapes]
        kernel = functools.partial(add_split, (2, 1))
        return run_whole(kernel, places, arrays, outs, macs=macs)

    def third(x_keep, x_came, y_keep, y_came):
        arrays = (x_keep, x_came, y_keep, y_came)
        shape = (heads // 2, x_keep.shape[1] + y_keep.shape[1], half)
        send, keep = run_whole(add_parts, places, arrays, [(shape, LOW)] * 2)
        return keep, swap(send, "head", 1)

    def fourth(keep, came):
        shape = keep.shape[1:]
        mine, other = run_whole(add_pair, places, [keep, came], [(shape, LOW)] * 2)
        return mine, swap(other, "head", 2)

    def fifth(mine, came):
        (total,) = run_whole(add_two, places, [mine, came], [(mine.shape, LOW)])
        bit = 1
        while bit < lax.axis_size("far"):
            total = (total.astype(F32) + swap(total, "far", bit).astype(F32)).astype(LOW)
            bit *= 2
        return total

    def cross_back(made):
        x_send, x_keep, y_send, y_keep = made
        return x_keep, swap(x_send, "near", 1), y_keep, swap(y_send, "near", 2)

    def cross(made, flip):
        x_send, x_keep, y_send, y_keep = made
        x_bit, y_bit = (2, 1) if flip else (1, 2)
        return x_keep, swap(x_send, "near", x_bit), y_keep, swap(y_send, "near", y_bit)

    outs = [((heads, rows3, own_rows), LOW), ((heads, 8, rows3), F32)]
    ins = [qkvs, w_outs, grad_attended, logs, seg[None]]
    rows, qkv_bias = run_whole(attention_back, places, ins, outs)
    rows_far = swap_core(rows)

    outs = [(square, F32, whole(square))]
    ins = [(a, whole(a.shape)) for a in (rows, w_qkvs, res1)]
    (input_grad,) = run(input_sum, places, (1,), ins, outs, weight=LIGHT)
    outs = [((width, half), LOW)] * 4
    ins = [d_keep, d_came, *u_held]
    ffn_held = cross(run_whole(first_stage, places, ins, outs, macs=ffn_macs), False)
    ins = [
        rows, rows_far, tok_own, tok_far, mixes, mixes_far, grad_attended, grad_far,
        small_one, small_two, up_bias, qkv_bias,
    ]
    outs = [
        ((heads, r, half), LOW) for r in (half // 2, (half + EXTRA) // 2) for _ in range(2)
    ]
    made = run_whole(attn_grad, places, ins, outs)
    attn_held = cross(made, False)

    outs = [((heads // 2, half // 4, half), LOW)] * 4 + [((heads // 2, half // 2, half), LOW)] * 2
    made = run_whole(second_stage, places, list(ffn_held), outs, macs=ffn_macs)
    ffn_held = cross_back(made[:4]) + (made[5], swap(made[4], "head", 1))
    attn_held = cross(second(*attn_held), True)
    outs = [((half, half), LOW)] * 2
    mine, other = run_whole(third_stage, places, list(ffn_held), outs, macs=ffn_macs)
    ffn_held = mine, swap(other, "head", 2)
    attn_held = third(*attn_held)
    ffn_held = gather_back(fifth(*ffn_held))
    attn_held = fourth(*attn_held)
    attn_held = gather_back(fifth(*attn_held))

    def both_cores(held):
        shape = (heads,) + held[0].shape
        (pieces,) = run_whole(collect, places, held, [(shape, LOW)])
        return [(a, whole(shape)) for a in (pieces, swap_core(pieces))]

    ffn_held = both_cores(ffn_held)
    outs = [(shape, F32, whole(shape)) for shape in ((chunk, width), (width, chunk))]
    grad_down, grad_up = run(
        ffn_place, places, (1,), ffn_held, outs, [pltpu.VMEM((width, chunk), F32)]
    )
    attn_held = both_cores(attn_held)
    shapes = [
        (3, local_width, width),
        (local_width, width),
        (6, width),
        (chunk,),
        (2, local_width),
    ]
    grad_qkv, grad_out, grad_small, grad_up_bias, grad_qv_bias = run(
        attn_place,
        places,
        (1,),
        attn_held,
        [(shape, F32, whole(shape)) for shape in shapes],
        [pltpu.VMEM((width + EXTRA, width), F32)],
    )
    return (
        layer_output,
        input_grad,
        grad_qkv.transpose(0, 2, 1),
        grad_qv_bias,
        grad_out,
        grad_up,
        grad_up_bias,
        grad_down,
        grad_small,
    )


def solution(mesh):
    batch, heads = mesh.devices.shape
    mesh = Mesh(
        mesh.devices.reshape(batch // 8, 4, 2, heads), ("far", "near", "core", "head")
    )
    group = ("far", "near", "core")
    everyone = group + ("head",)
    in_specs = (
        P(group, None),
        P(group),
        P(None, None, "head"),
        P(None, "head"),
        P("head", None),
        P(),
        P(),
        P(),
        P(),
        P(),
        P(),
        P(),
        P(),
        P(),
        P(everyone, None),
    )
    out_specs = (
        P(everyone, None),
        P(everyone, None),
        P(None, None, "head"),
        P(None, "head"),
        P("head", None),
        P(None, "head"),
        P("head"),
        P("head", None),
        P(),
    )
    return jax.shard_map(
        per_device, mesh=mesh, in_specs=in_specs, out_specs=out_specs, check_vma=False
    )
```

```python
import functools
import math

import jax
import jax.numpy as jnp
from jax import lax
from jax.experimental import pallas as pl
from jax.experimental.pallas import tpu as pltpu
from jax.sharding import Mesh
from jax.sharding import PartitionSpec as P

HEAD_DIM = 64
SLOT = 512
LOW = jnp.bfloat16
F32 = jnp.float32
LOG2E = math.log2(math.e)
SCORE_SCALE = HEAD_DIM ** (-0.5) * LOG2E
SPARE_BYTES = 12 * 2**20
EXTRA = 64
LIGHT = 0.01
LANES = 128
CHAIN = []
TAIL_SLOPE = 0.36
TAIL = (
    0.14371304537508633,
    0.14177245466203425,
    0.1397192603907239,
    0.026549325413860486,
    0.18095403134327948,
    -0.1797647161697652,
    0.047056295581175855,
)


def swap(value, axis, bit):
    size = lax.axis_size(axis)
    return lax.ppermute(value, axis, [(i, i ^ bit) for i in range(size)])


def swap_core(value):
    return swap(value, "core", 1)


def dot(a, b):
    return jnp.dot(a, b, preferred_element_type=F32)


def dot_nt(a, b):
    return lax.dot_general(a, b, (((1,), (1,)), ((), ())), preferred_element_type=F32)


def dot_tn(a, b):
    return lax.dot_general(a, b, (((0,), (0,)), ((), ())), preferred_element_type=F32)


def whole(shape):
    return pl.BlockSpec(shape, lambda *args: (0,) * len(shape), pipeline_mode=pl.Buffered(1))


def run(
    kernel, places, grid, ins, outs, scratch=(), macs=0, after=(), alias=(), weight=8, chain=True
):
    moved = sum(a.size * a.dtype.itemsize for a, spec in ins)
    moved += sum(math.prod(shape) * jnp.dtype(kind).itemsize for shape, kind, spec in outs)
    after = list(after) + (CHAIN if chain else [])
    count, unread = len(ins), len(alias) + len(after)
    results = len(outs)
    flag = (8, 128)
    if chain:
        outs = outs + [(flag, F32, whole(flag))]

    def body(places, *refs):
        made = refs[count + unread :]
        if chain:

            @pl.when(pl.program_id(0) == 0)
            def _():
                made[results][...] = jnp.zeros(flag, F32)

        kernel(places, *refs[:count], *made[:results], *made[len(outs) :])

    held = pl.BlockSpec(memory_space=pl.ANY)
    room = SPARE_BYTES
    for shape, kind, spec in outs + [(a.shape, a.dtype, spec) for a, spec in ins]:
        if spec.block_shape is not None:
            block = math.prod(1 if n is None else n for n in spec.block_shape)
            copies = 2 if spec.pipeline_mode is None else 1
            room += copies * block * jnp.dtype(kind).itemsize
    for ref in scratch:
        if hasattr(ref, "shape") and ref.dtype in (LOW, F32):
            room += math.prod(ref.shape) * jnp.dtype(ref.dtype).itemsize
    made = pl.pallas_call(
        body,
        name=getattr(kernel, "func", kernel).__name__,
        grid_spec=pltpu.PrefetchScalarGridSpec(
            num_scalar_prefetch=1,
            grid=grid,
            in_specs=[spec for a, spec in ins] + [held] * unread,
            out_specs=[spec for shape, kind, spec in outs],
            scratch_shapes=list(scratch),
        ),
        out_shape=[jax.ShapeDtypeStruct(shape, kind) for shape, kind, spec in outs],
        input_output_aliases={1 + count + i: i for i in range(len(alias))},
        compiler_params=pltpu.CompilerParams(vmem_limit_bytes=room),
        cost_estimate=pl.CostEstimate(
            flops=int(2 * macs * weight), bytes_accessed=int(moved * weight), transcendentals=0
        ),
    )(places, *[a for a, spec in ins], *alias, *after)
    if chain:
        CHAIN[:] = made[results:]
    return made[:results]


def run_whole(
    kernel, places, ins, outs, scratch=(), macs=0, after=(), alias=(), weight=8, chain=True
):
    pairs = [a if isinstance(a, tuple) else (a, pltpu.VMEM) for a in ins]
    after = list(after) + (CHAIN if chain else [])
    count, unread, results = len(pairs), len(alias) + len(after), len(outs)
    if chain:
        outs = outs + [((8, 128), F32)]

    def body(places, *refs):
        made = refs[count + unread :]
        if chain:
            made[results][...] = jnp.zeros((8, 128), F32)
        kernel(places, *refs[:count], *made[:results], *made[len(outs) :])

    room = SPARE_BYTES
    for ref in scratch:
        if hasattr(ref, "shape") and ref.dtype in (LOW, F32):
            room += math.prod(ref.shape) * jnp.dtype(ref.dtype).itemsize
    spaces = [pltpu.SMEM] + [space for a, space in pairs]
    spaces += [pltpu.VMEM] * len(alias) + [pl.ANY] * len(after)
    made = pl.pallas_call(
        body,
        name=getattr(kernel, "func", kernel).__name__,
        in_specs=[pl.BlockSpec(memory_space=space) for space in spaces],
        out_specs=[pl.BlockSpec(memory_space=pltpu.VMEM)] * len(outs),
        scratch_shapes=list(scratch),
        out_shape=[jax.ShapeDtypeStruct(shape, kind) for shape, kind in outs],
        input_output_aliases={1 + count + i: i for i in range(len(alias))},
        compiler_params=pltpu.CompilerParams(vmem_limit_bytes=room),
        cost_estimate=pl.CostEstimate(
            flops=int(2 * macs * weight), bytes_accessed=0, transcendentals=0
        ),
    )(places, *[a for a, space in pairs], *alias, *after)
    if chain:
        CHAIN[:] = made[results:]
    return made[:results]


def each(count, size, body):
    def step(i, carry):
        body(pl.ds(pl.multiple_of(i * size, size), size))
        return carry

    lax.fori_loop(0, count // size, step, 0)


def tiles_of(count, size):
    return [slice(at, at + size) for at in range(0, count, size)]


def three_parts(values):
    parts, rest = [], values
    for _ in range(3):
        parts.append(rest.astype(LOW))
        rest = rest - parts[-1].astype(F32)
    return parts


def segment_rows(seg_row):
    shape = (16, seg_row.shape[1])
    place = lax.broadcasted_iota(jnp.int32, shape, 0)
    same = place - 1 == seg_row
    keys = jnp.where(same, 1.0, jnp.where((place >= 8) & (place < 11), 1.0, 0.0))
    queries = jnp.where(same | (place > 4), 0.0, -1e30)
    return keys.astype(LOW), queries.astype(LOW)


def attend_heads(tok, w_rows, bias, seg_row, qkv_ref, mix_ref, log_ref):
    width = w_rows.shape[0] // 3
    added = dot_tn(bias[:, : 2 * width], jnp.ones((bias.shape[0], tok.shape[0]), LOW))
    qkv = dot_nt(w_rows, tok)
    parts = (
        (qkv[:width] + added[:width]).astype(LOW),
        qkv[width : 2 * width].astype(LOW),
        (qkv[2 * width :] + added[width:]).astype(LOW),
    )
    for c in range(3):
        qkv_ref[c * width : (c + 1) * width] = parts[c]
    more_k, more_q = segment_rows(seg_row)
    for head in range(width // HEAD_DIM):
        q, k, v = (part[head * HEAD_DIM : (head + 1) * HEAD_DIM] for part in parts)
        scores = dot_tn(jnp.concatenate([k, more_k], 0), jnp.concatenate([q, more_q], 0))
        columns, tops, totals = [], [], []
        for tile in tiles_of(scores.shape[1], LANES):
            top = jnp.max(scores[:, tile], 0, keepdims=True)
            total, column = 0.0, []
            for rows in tiles_of(scores.shape[0], 64):
                exponent = jnp.exp2((scores[rows, tile] - top) * SCORE_SCALE)
                total = total + jnp.sum(exponent, 0, keepdims=True)
                column.append(exponent.astype(LOW))
            columns.append(jnp.concatenate(column, 0))
            tops.append(top)
            totals.append(total)
        total = jnp.concatenate(totals, 1)
        mixed = dot(v, jnp.concatenate(columns, 1)) * (1.0 / total)
        mix_ref[head * HEAD_DIM : (head + 1) * HEAD_DIM] = mixed.astype(LOW)
        top = jnp.concatenate(tops, 1)
        log_ref[head : head + 1] = top + jnp.log2(total) * (1.0 / SCORE_SCALE)


def own_attention(
    places, tok, w, bias, seg_row, qkv_ref, mix_ref, log_ref, w_qkv, w_out
):
    count = qkv_ref.shape[1]
    w_qkv[0] = w[:count]
    w_out[0] = w[count:]
    attend_heads(
        tok[...], w[:count], bias[...], seg_row[...], qkv_ref.at[0], mix_ref.at[0], log_ref.at[0]
    )


def far_attention(
    d, order, places, tok, pair, rest, pair_far, rest_far, hop, seg_row,
    qkv_ref, mix_ref, log_ref, w_qkv, w_out, w_ref,
):
    first, second = order
    rows, count = pair.shape[1], qkv_ref.shape[1]
    me = places[0] * 2 + places[1]
    for other, held in enumerate(((pair, rest), (pair_far, rest_far))):
        for two, block in enumerate(held):
            for one in range(2):
                owner = me ^ (other + 2 * first * one + 2 * second * two)
                w_ref[pl.ds(pl.multiple_of(owner * rows, rows), rows)] = block[one]
    w_qkv[d] = w_ref[:count]
    w_out[d] = w_ref[count:]
    attend_heads(
        tok[...],
        w_ref[:count],
        hop[rows:],
        seg_row[...],
        qkv_ref.at[d],
        mix_ref.at[d],
        log_ref.at[d],
    )


def copy_rows(places, rows, out):
    out[...] = rows[...]


def pair_rows(places, first, second, out):
    out[0] = first[: out.shape[1]]
    out[1] = second[: out.shape[1]]


def norm_stats(v):
    centred = v - jnp.mean(v, -1, keepdims=True)
    inv = lax.rsqrt(jnp.mean(centred * centred, -1, keepdims=True) + 1e-05)
    return centred * inv, inv


def norm_back(upstream, unit, inv, gain):
    scaled = upstream * gain
    inner = jnp.mean(scaled * unit, -1, keepdims=True)
    return inv * (scaled - jnp.mean(scaled, -1, keepdims=True) - unit * inner)


def gelu_both(pre):
    power = jnp.exp2(pre * pre * (-0.5 * LOG2E))
    base = 1.0 + TAIL_SLOPE * jnp.abs(pre)
    t = pl.reciprocal(base, approx=True)
    tail = TAIL[6] * t + TAIL[5]
    for c in TAIL[4::-1]:
        tail = tail * t + c
    tail = tail * (t * power)
    cumul = jnp.where(pre < 0.0, tail, 1.0 - tail)
    return (pre * cumul).astype(LOW), cumul + pre * (power * 0.3989422804014327)


def share(core, wide, mine, other):
    half = wide.shape[1] // 2
    left, right = wide[:, :half], wide[:, half:]
    mine[...] = jnp.where(core == 0, left, right)
    other[...] = jnp.where(core == 0, right, left)


def feed_forward(
    places, tok, mix, w_out, b_out, gain1, shift1, b_down, gain2, shift2, w_up, b_up, w_down, cot,
    send, own, ends, slope, unit1, inv1, res2, out, small, tok_send,
    hidden, low, acts, total,
):
    heads, width, half = mix.shape[0], low.shape[1], send.shape[2]
    chunk = 2 * half
    core, z = places[1], places[2]
    b_out, gain1, shift1, b_down, gain2, shift2 = (
        ref[...].reshape(1, -1) for ref in (b_out, gain1, shift1, b_down, gain2, shift2)
    )
    tok_send[...] = jnp.where(core == 0, tok[:, half:], tok[:, :half])
    total[...] = dot_tn(mix[...].reshape(width, low.shape[0]), w_out[...].reshape(width, width))

    def first_norm(rows):
        unit, inv = norm_stats(tok[rows].astype(F32) + (total[rows] + b_out))
        unit1[rows] = unit
        inv1[rows] = inv
        one = unit * gain1 + shift1
        hidden[rows] = one
        one_low = one.astype(LOW)
        low[rows] = one_low
        ends[0, rows] = one_low[:, :half]
        ends[1, rows] = one_low[:, half:]

    each(low.shape[0], 64, first_norm)

    def one_unit(h, carry):
        start = pl.multiple_of(h * chunk, chunk)
        for at in tiles_of(chunk, chunk):
            wide = pl.ds(start, chunk)
            pre = dot(low[...], w_up[:, wide])
            for rows in tiles_of(pre.shape[0], 16):
                act, tilt = gelu_both(pre[rows] + b_up[h, :, at])
                slope[h, rows, at] = tilt.astype(LOW)
                acts[rows, wide] = act
        left = acts[:, pl.ds(start, half)]
        right = acts[:, pl.ds(pl.multiple_of(start + half, 128), half)]
        own[z ^ h] = jnp.where(core == 0, left, right)
        send[z ^ h] = jnp.where(core == 0, right, left)
        return carry

    lax.fori_loop(0, heads, one_unit, 0)
    total[...] = dot(acts[...], w_down[...])
    small[...] = jnp.zeros_like(small)

    def second_norm(rows):
        unit, inv = norm_stats(hidden[rows] + (total[rows] + b_down))
        out[rows] = (unit * gain2 + shift2).astype(LOW)
        upstream = cot[rows].astype(F32)
        grad = norm_back(upstream, unit, inv, gain2)
        res2[rows] = grad
        grad_low = grad.astype(LOW)
        ends[2, rows] = grad_low[:, :half]
        ends[3, rows] = grad_low[:, half:]
        for i, term in enumerate((grad_low.astype(F32), upstream * unit, upstream)):
            small[i : i + 1] += jnp.sum(term, 0, keepdims=True)

    each(low.shape[0], 64, second_norm)


def inner_back(places, ends, w_down, slope, send, own, bias, inners):
    heads, _, chunk = slope.shape
    core, z = places[1], places[2]
    branch = jnp.concatenate([ends[2], ends[3]], 1)
    for h in range(heads):
        for at in tiles_of(chunk, 256):
            grad_act = dot_nt(branch, w_down[h * chunk + at.start : h * chunk + at.stop])
            total = 0.0
            for rows in tiles_of(grad_act.shape[0], 32):
                inner = (grad_act[rows] * slope[h, rows, at].astype(F32)).astype(LOW)
                inners[rows, at] = inner
                total = total + jnp.sum(inner.astype(F32), 0, keepdims=True)
            bias[h, :, at] = total
        share(core, inners, own.at[z ^ h], send.at[z ^ h])


def hidden_back(places, own, sent, w_up, res2, unit1, inv1, gain1, send, res1, low, small):
    heads, count, half = own.shape
    core, z = places[1], places[2]
    sides = []
    for h in range(heads):
        mine, other = own[z ^ h], sent[z ^ h]
        sides += [jnp.where(core == 0, mine, other), jnp.where(core == 0, other, mine)]
    product = dot_nt(jnp.concatenate(sides, 1), w_up[...])
    gain = gain1[...].reshape(1, -1)
    sums = [0.0] * 3
    for rows in tiles_of(count, 32):
        grad, unit = product[rows] + res2[rows], unit1[rows]
        result = norm_back(grad, unit, inv1[rows], gain)
        res1[rows] = result
        result_low = result.astype(LOW)
        low[rows] = result_low
        send[rows] = jnp.where(core == 0, result_low[:, half:], result_low[:, :half])
        for i, term in enumerate((result_low.astype(F32), grad * unit, grad)):
            sums[i] = sums[i] + jnp.sum(term, 0, keepdims=True)
    for i in range(3):
        small[i : i + 1] = sums[i]


def shard_back(qkv, w_out, grad, log_ref, more_k, more_q, rows_ref, bias_ref):
    width = qkv.shape[0] // 3
    grad_mixed = dot_nt(w_out[...], grad[...]).astype(LOW)
    scale = HEAD_DIM ** (-0.5)
    for head in range(width // HEAD_DIM):
        places_of = [c * width + head * HEAD_DIM for c in range(3)]
        q, k, v = (qkv[at : at + HEAD_DIM] for at in places_of)
        g = grad_mixed[head * HEAD_DIM : (head + 1) * HEAD_DIM]
        logs = jnp.concatenate(three_parts(-log_ref[head : head + 1]), 0)
        with_logs = jnp.concatenate([more_q[:8], logs, more_q[11:]], 0)
        scores = dot_tn(jnp.concatenate([k, more_k], 0), jnp.concatenate([q, with_logs], 0))
        grad_probs = dot_tn(v, g)
        attends, grads = [], []
        for tile in tiles_of(scores.shape[1], LANES):
            inner, kept, lows, parts = 0.0, [], [], []
            tall = tiles_of(scores.shape[0], 64)
            for down in tall:
                attend = jnp.exp2(scores[down, tile] * SCORE_SCALE)
                inner = inner + jnp.sum(attend * grad_probs[down, tile], 0, keepdims=True)
                kept.append(attend)
                lows.append(attend.astype(LOW))
            for down, attend in zip(tall, kept):
                parts.append((attend * (grad_probs[down, tile] - inner)).astype(LOW))
            attends.append(jnp.concatenate(lows, 0))
            grads.append(jnp.concatenate(parts, 0))
        attend_low = jnp.concatenate(attends, 1)
        grad_scores = jnp.concatenate(grads, 1)
        grad_v = dot_nt(g, attend_low)
        grad_q = dot(k, grad_scores) * scale
        grad_k = dot_nt(q, grad_scores) * scale
        for at, value in zip(places_of, (grad_q, grad_k, grad_v)):
            rows_ref[at : at + HEAD_DIM] = value.astype(LOW)
    ones = jnp.ones((8, rows_ref.shape[1]), LOW)
    bias_ref[...] = dot_nt(ones, rows_ref[...])


def attention_back(places, qkv, w_out, grad, log_ref, seg_row, rows_ref, bias_ref):
    more_k, more_q = segment_rows(seg_row[...])

    def shard(d, carry):
        refs = (ref.at[d] for ref in (rows_ref, bias_ref))
        shard_back(qkv.at[d], w_out.at[d], grad, log_ref.at[d], more_k, more_q, *refs)
        return carry

    lax.fori_loop(0, qkv.shape[0], shard, 0)


def split_rows(value, high, send, keep):
    rows = value.shape[0] // 2
    low = value.astype(LOW)
    send[...] = jnp.where(high, low[:rows], low[rows:])
    keep[...] = jnp.where(high, low[rows:], low[:rows])


def is_high(places, bit):
    return (places[0] & bit) != 0


def unit_products(which, units, units_far, ends, ends_far, both):
    half, count = ends.shape[2], ends.shape[1]
    for side in range(2):
        rows = slice(side * half, (side + 1) * half)
        both[rows, :count] = ends[2 * which + side].T
        both[rows, count:] = ends_far[2 * which + side].T
    for d in range(0, units.shape[0], 2):
        left, right = (jnp.concatenate([units[d + i], units_far[d + i]], 0) for i in range(2))
        yield d, dot(both[...], jnp.concatenate([left, right], 1))


def down_grad(places, units, units_far, ends, ends_far, send, keep, both):
    half = send.shape[2]
    for d, total in unit_products(1, units, units_far, ends, ends_far, both):
        keep[d // 2] = total[:, :half].astype(LOW)
        send[d // 2] = total[:, half:].astype(LOW)


def up_grad(places, units, units_far, ends, ends_far, send_x, keep_x, send_y, keep_y, both):
    half = send_x.shape[2]
    for d, total in unit_products(0, units, units_far, ends, ends_far, both):
        for i in range(2):
            part = total[:, i * half : (i + 1) * half]
            split_rows(part[:half], is_high(places, 1), send_x.at[d + i], keep_x.at[d + i])
            split_rows(part[half:], is_high(places, 2), send_y.at[d + i], keep_y.at[d + i])


def split_at(value, high, send, keep, start):
    rows = value.shape[0] // 2
    low = value.astype(LOW)
    send[start : start + rows] = jnp.where(high, low[:rows], low[rows:])
    keep[start : start + rows] = jnp.where(high, low[rows:], low[:rows])


def first_stage(
    places, d_keep, d_came, x_keep, x_came, y_keep, y_came, send_x, keep_x, send_y, keep_y
):
    half = d_keep.shape[2]
    at = 0
    for i in range(d_keep.shape[0]):
        total = d_keep[i].astype(F32) + d_came[i].astype(F32)
        split_at(total[:half], is_high(places, 1), send_x, keep_x, at)
        split_at(total[half:], is_high(places, 2), send_y, keep_y, at)
        at += half // 2
    for d in range(x_keep.shape[0]):
        upper = x_keep[d].astype(F32) + x_came[d].astype(F32)
        lower = y_keep[d].astype(F32) + y_came[d].astype(F32)
        split_at(upper, is_high(places, 2), send_y, keep_y, at)
        split_at(lower, is_high(places, 1), send_x, keep_x, at)
        at += upper.shape[0] // 2


def second_stage(
    places, x_keep, x_came, y_keep, y_came, send_x, keep_x, send_y, keep_y, send_z, keep_z
):
    rows = send_x.shape[1]
    at = 0
    for i in range(send_x.shape[0]):
        piece = slice(at, at + 2 * rows)
        upper = x_keep[piece].astype(F32) + x_came[piece].astype(F32)
        lower = y_keep[piece].astype(F32) + y_came[piece].astype(F32)
        split_rows(upper, is_high(places, 2), send_y.at[i], keep_y.at[i])
        split_rows(lower, is_high(places, 1), send_x.at[i], keep_x.at[i])
        at += 2 * rows
    for d in range(2 * send_z.shape[0]):
        piece = slice(at, at + rows)
        out = (send_z if d % 2 else keep_z).at[d // 2]
        out[:rows] = (y_keep[piece].astype(F32) + y_came[piece].astype(F32)).astype(LOW)
        out[rows:] = (x_keep[piece].astype(F32) + x_came[piece].astype(F32)).astype(LOW)
        at += rows


def third_stage(places, x_keep, x_came, y_keep, y_came, z_keep, z_came, mine, other):
    rows = x_keep.shape[1]
    for i, out in enumerate((mine, other)):
        out[:rows] = (y_keep[i].astype(F32) + y_came[i].astype(F32)).astype(LOW)
        out[rows : 2 * rows] = (x_keep[i].astype(F32) + x_came[i].astype(F32)).astype(LOW)
        out[2 * rows :] = (z_keep[i].astype(F32) + z_came[i].astype(F32)).astype(LOW)


def attn_grad(
    places, rows, rows_far, tok, tok_far, mix, mix_far, grad, grad_far,
    small_one, small_two, up_bias, qkv_bias, send_x, keep_x, send_y, keep_y,
):
    width = mix.shape[1]
    half = tok_far.shape[1]
    core, z = places[1], places[2]

    def both(near, far):
        mine = jnp.where(core == 0, near[:, :half], near[:, half:])
        return jnp.concatenate([mine, far[...]], 0)

    tok_both, grad_both = both(tok, tok_far), both(grad, grad_far)
    for d in range(rows.shape[0]):
        qkv = dot(jnp.concatenate([rows[d], rows_far[d]], 1), tok_both)
        out = dot(jnp.concatenate([mix[d], mix_far[d]], 1), grad_both)
        lines = []
        for held in (small_one, small_two):
            for i in range(3):
                lines += [held[i : i + 1, :half], held[i : i + 1, half:]]
        line, bias = up_bias[z ^ d], qkv_bias[d]
        lines += [line[:, :half], line[:, half:]]
        lines.append(jnp.concatenate([bias[0:1, :width], bias[0:1, 2 * width :]], 1))
        lines.append(jnp.zeros((EXTRA - len(lines), half), F32))
        total = jnp.concatenate([qkv, out] + lines, 0)
        split_rows(total[:half], is_high(places, 1), send_x.at[d], keep_x.at[d])
        split_rows(total[half:], is_high(places, 2), send_y.at[d], keep_y.at[d])


def add_split(bits, places, *refs):
    for i, bit in enumerate(bits):
        keep, came = refs[2 * i : 2 * i + 2]
        send, left = refs[2 * (len(bits) + i) : 2 * (len(bits) + i) + 2]
        for d in range(keep.shape[0]):
            total = keep[d].astype(F32) + came[d].astype(F32)
            split_rows(total, is_high(places, bit), send.at[d], left.at[d])


def add_parts(places, keep_a, came_a, keep_b, came_b, send, keep):
    rows = keep_a.shape[1]
    for d in range(keep_a.shape[0]):
        out = (send if d % 2 else keep).at[d // 2]
        out[:rows] = (keep_a[d].astype(F32) + came_a[d].astype(F32)).astype(LOW)
        out[rows:] = (keep_b[d].astype(F32) + came_b[d].astype(F32)).astype(LOW)


def add_pair(places, keep, came, *outs):
    for i, out in enumerate(outs):
        out[...] = (keep[i].astype(F32) + came[i].astype(F32)).astype(LOW)


def add_two(places, keep, came, out):
    out[...] = (keep[...].astype(F32) + came[...].astype(F32)).astype(LOW)


def input_sum(places, rows, w, res1, out):
    heads, count, tokens = rows.shape
    total = dot_tn(rows[...].reshape(heads * count, tokens), w[...].reshape(heads * count, -1))
    out[...] = res1[...] + total


def place_pieces(places, held, full, layouts):
    near, core = places[0], places[1]
    width = held[0].shape[1]
    for off in range(4):
        chip = near ^ off
        mine, other = held[off][...], held[4 + off][...]
        sides = (jnp.where(core == 0, mine, other), jnp.where(core == 0, other, mine))
        for at, rows, start, outer in layouts:
            low_bit, high_bit = chip & 1, chip >> 1
            order = 2 * low_bit + high_bit if outer == 1 else 2 * high_bit + low_bit
            to = pl.multiple_of(start + order * rows, 16)
            for side in range(2):
                full[pl.ds(to, rows), side * width : (side + 1) * width] = sides[side][
                    at : at + rows
                ].astype(F32)


def ffn_place(places, *refs):
    held = [ref.at[off] for ref in refs[:2] for off in range(4)]
    down, up, full = refs[2:]
    rows = held[0].shape[0] // 4
    half = 4 * rows
    place_pieces(places, held, full, [(0, rows, 0, 1), (rows, rows, half, 2)])
    down[...] = full[...].T
    place_pieces(places, held, up, [(2 * rows, rows, 0, 1), (3 * rows, rows, half, 2)])


def collect(places, *refs):
    for off in range(4):
        refs[4][off] = refs[off][...]


def attn_place(places, *refs):
    held = [ref.at[off] for ref in refs[:2] for off in range(4)]
    qkv, w_out, small, up_bias, qv_bias, full = refs[2:]
    width = held[0].shape[1]
    count = w_out.shape[0]
    rows = count // 2
    more = held[0].shape[0] - rows
    place_pieces(places, held, full, [(0, rows, 0, 1), (rows, more, 4 * rows, 2)])
    for c in range(3):
        qkv[c] = full[c * count : (c + 1) * count]
    w_out[...] = full[3 * count : 4 * count]
    at = 4 * count
    lines = full[at : at + 16, :width] + full[at : at + 16, width:]
    for i in range(6):
        small[i : i + 1, :width] = lines[2 * i : 2 * i + 1]
        small[i : i + 1, width:] = lines[2 * i + 1 : 2 * i + 2]
    up_bias[...] = jnp.concatenate([lines[12:13], lines[13:14]], 1).reshape(2 * width)
    qv_bias[0:1] = lines[14:15, :count]
    qv_bias[1:2] = lines[14:15, count : 2 * count]


def bias_parts(values):
    rows, rest = [], values
    for _ in range(3):
        rows.append(lax.reduce_precision(rest, 8, 7))
        rest = rest - rows[-1]
    return jnp.stack(rows).astype(LOW)


def gather_back(piece):
    return [piece] + [swap(piece, "near", off) for off in range(1, 4)]


def per_device(
    tokens,
    segment_ids,
    w_qkv,
    b_qv,
    w_out,
    b_out,
    ln1_gain,
    ln1_bias,
    w_up,
    b_up,
    w_down,
    b_down,
    ln2_gain,
    ln2_bias,
    cotangent,
):
    CHAIN.clear()
    width = tokens.shape[1]
    own_rows = cotangent.shape[0]
    local_width = w_qkv.shape[2]
    heads = lax.axis_size("head")
    z = lax.axis_index("head")
    core = lax.axis_index("core")
    near = lax.axis_index("near")
    hidden_units = w_up.shape[1]
    chunk = hidden_units // heads
    half = width // 2
    rows3 = 3 * local_width
    places = jnp.stack([near, core, z]).astype(jnp.int32)

    shard = jnp.concatenate([w_qkv.transpose(0, 2, 1).reshape(rows3, width), w_out], 0)
    piece_rows = shard.shape[0] // 8
    bias = jnp.pad(bias_parts(b_qv.reshape(-1)), ((0, 13), (0, width - 2 * local_width)))
    piece = lax.dynamic_slice_in_dim(shard, (near * 2 + core) * piece_rows, piece_rows, 0)
    piece = jnp.concatenate([piece, bias], 0)
    first_hop = [swap(piece, "head", d) for d in range(1, heads)]

    seg = lax.dynamic_slice_in_dim(segment_ids, z * own_rows, own_rows, 0)
    tok_own = lax.dynamic_slice_in_dim(tokens, z * own_rows, own_rows, 0)
    attend_outs = [
        ((heads, rows3, own_rows), LOW),
        ((heads, local_width, own_rows), LOW),
        ((heads, 8, own_rows), F32),
        ((heads, rows3, width), LOW),
        ((heads, local_width, width), LOW),
    ]
    macs = rows3 * width * own_rows + 6 * own_rows * own_rows * 256
    orders = [(1, 2) if d % 2 else (2, 1) for d in range(heads)]
    nexts = [swap(first_hop[d - 1], "near", orders[d][0]) for d in range(1, heads)]

    def pair_up(d, after):
        (pair,) = run_whole(
            pair_rows, places, [first_hop[d - 1], nexts[d - 1]],
            [((2, piece_rows, width), LOW)], after=after, chain=False,
        )
        return pair

    pairs = [pair_up(1, first_hop[1:])]
    ins = [tok_own, shard, bias, seg[None]]
    made = run_whole(
        own_attention, places, ins, attend_outs, macs=macs, after=pairs, chain=False
    )
    pairs += [pair_up(d, nexts[1:] + [made[2]]) for d in range(2, heads)]
    rests = [swap(pairs[d - 1], "near", orders[d][1]) for d in range(1, heads)]
    for d in range(1, heads):
        pair, rest = pairs[d - 1], rests[d - 1]
        sent = rest
        if d == heads - 1:
            (sent,) = run_whole(
                copy_rows, places, [rest], [(rest.shape, LOW)], after=[second_log], chain=False
            )
        ins = [tok_own, pair, rest, swap_core(pair), swap_core(sent), first_hop[d - 1], seg[None]]
        made = run_whole(
            functools.partial(far_attention, d, orders[d]), places, ins, attend_outs,
            [pltpu.VMEM(shard.shape, LOW)], macs, alias=made, chain=False, weight=100,
        )
        if d == 1:
            second_log = made[2]
    qkvs, mixes, logs, w_qkvs, w_outs = made

    mixes_far = swap_core(mixes)

    square = (own_rows, width)
    tiles = (heads, own_rows, half)
    ins = [
        tok_own, mixes, w_outs, b_out, ln1_gain, ln1_bias, b_down, ln2_gain, ln2_bias,
        w_up, b_up.reshape(heads, 1, chunk), w_down, cotangent,
    ]
    outs = [
        (tiles, LOW),
        (tiles, LOW),
        ((4, own_rows, half), LOW),
        ((heads, own_rows, chunk), LOW),
        (square, F32),
        ((own_rows, 1), F32),
        (square, F32),
        (square, LOW),
        ((8, width), F32),
        ((own_rows, half), LOW),
    ]
    scratch = [
        pltpu.VMEM(square, F32),
        pltpu.VMEM(square, LOW),
        pltpu.VMEM((own_rows, hidden_units), LOW),
        pltpu.VMEM(square, F32),
    ]
    ffn_macs = 2 * own_rows * width * hidden_units
    (
        act_send, act_own, ends, slope, unit1, inv1, res2, layer_output, small_two, tok_send,
    ) = run_whole(feed_forward, places, ins, outs, scratch, ffn_macs)
    tok_far = swap_core(tok_send)
    act_far = swap_core(act_send)
    ends_far = swap_core(ends)

    outs = [(tiles, LOW), (tiles, LOW), ((heads, 1, chunk), F32)]
    scratch = [pltpu.VMEM((own_rows, chunk), LOW)]
    inner_send, inner_own, up_bias = run_whole(
        inner_back, places, [ends, w_down, slope], outs, scratch, ffn_macs // 2, [mixes_far]
    )
    inner_far = swap_core(inner_send)


    both = [pltpu.VMEM((width, 2 * own_rows), LOW)]
    outs = [((heads // 2, width, half), LOW)] * 2
    ins = [act_own, act_far, ends, ends_far]
    d_send, d_keep = run_whole(down_grad, places, ins, outs, both, ffn_macs // 2)
    d_came = swap(d_send, "head", 1)
    outs = [((heads, half // 2, half), LOW)] * 4
    ins = [inner_own, inner_far, ends, ends_far]
    made = run_whole(up_grad, places, ins, outs, both, ffn_macs // 2, weight=LIGHT)
    u_held = (made[1], swap(made[0], "near", 1), made[3], swap(made[2], "near", 2))

    outs = [((own_rows, half), LOW), (square, F32), (square, LOW), ((8, width), F32)]
    ins = [inner_own, inner_send, w_up, res2, unit1, inv1, ln1_gain]
    grad_send, res1, grad_attended, small_one = run_whole(
        hidden_back, places, ins, outs, macs=ffn_macs // 2, weight=LIGHT
    )
    grad_far = swap_core(grad_send)

    def second(x_keep, x_came, y_keep, y_came, macs=0):
        arrays = (x_keep, x_came, y_keep, y_came)
        shapes = [(heads, a.shape[1] // 2, half) for a in (x_keep, x_keep, y_keep, y_keep)]
        outs = [(shape, LOW) for shape in shapes]
        kernel = functools.partial(add_split, (2, 1))
        return run_whole(kernel, places, arrays, outs, macs=macs)

    def third(x_keep, x_came, y_keep, y_came):
        arrays = (x_keep, x_came, y_keep, y_came)
        shape = (heads // 2, x_keep.shape[1] + y_keep.shape[1], half)
        send, keep = run_whole(add_parts, places, arrays, [(shape, LOW)] * 2)
        return keep, swap(send, "head", 1)

    def fourth(keep, came):
        shape = keep.shape[1:]
        mine, other = run_whole(add_pair, places, [keep, came], [(shape, LOW)] * 2)
        return mine, swap(other, "head", 2)

    def fifth(mine, came):
        (total,) = run_whole(add_two, places, [mine, came], [(mine.shape, LOW)])
        bit = 1
        while bit < lax.axis_size("far"):
            total = (total.astype(F32) + swap(total, "far", bit).astype(F32)).astype(LOW)
            bit *= 2
        return total

    def cross_back(made):
        x_send, x_keep, y_send, y_keep = made
        return x_keep, swap(x_send, "near", 1), y_keep, swap(y_send, "near", 2)

    def cross(made, flip):
        x_send, x_keep, y_send, y_keep = made
        x_bit, y_bit = (2, 1) if flip else (1, 2)
        return x_keep, swap(x_send, "near", x_bit), y_keep, swap(y_send, "near", y_bit)

    outs = [((heads, rows3, own_rows), LOW), ((heads, 8, rows3), F32)]
    ins = [qkvs, w_outs, grad_attended, logs, seg[None]]
    rows, qkv_bias = run_whole(attention_back, places, ins, outs)
    rows_far = swap_core(rows)

    outs = [(square, F32, whole(square))]
    ins = [(a, whole(a.shape)) for a in (rows, w_qkvs, res1)]
    (input_grad,) = run(input_sum, places, (1,), ins, outs, weight=LIGHT)
    outs = [((width, half), LOW)] * 4
    ins = [d_keep, d_came, *u_held]
    ffn_held = cross(run_whole(first_stage, places, ins, outs, macs=ffn_macs), False)
    ins = [
        rows, rows_far, tok_own, tok_far, mixes, mixes_far, grad_attended, grad_far,
        small_one, small_two, up_bias, qkv_bias,
    ]
    outs = [
        ((heads, r, half), LOW) for r in (half // 2, (half + EXTRA) // 2) for _ in range(2)
    ]
    made = run_whole(attn_grad, places, ins, outs)
    attn_held = cross(made, False)

    outs = [((heads // 2, half // 4, half), LOW)] * 4 + [((heads // 2, half // 2, half), LOW)] * 2
    made = run_whole(second_stage, places, list(ffn_held), outs, macs=ffn_macs)
    ffn_held = cross_back(made[:4]) + (made[5], swap(made[4], "head", 1))
    attn_held = cross(second(*attn_held), True)
    outs = [((half, half), LOW)] * 2
    mine, other = run_whole(third_stage, places, list(ffn_held), outs, macs=ffn_macs)
    ffn_held = mine, swap(other, "head", 2)
    attn_held = third(*attn_held)
    ffn_held = gather_back(fifth(*ffn_held))
    attn_held = fourth(*attn_held)
    attn_held = gather_back(fifth(*attn_held))

    def both_cores(held, macs=0):
        shape = (heads,) + held[0].shape
        (pieces,) = run_whole(collect, places, held, [(shape, LOW)], macs=macs)
        return [(a, whole(shape)) for a in (pieces, swap_core(pieces))]

    ffn_held = both_cores(ffn_held)
    attn_held = both_cores(attn_held, ffn_macs)
    outs = [(shape, F32, whole(shape)) for shape in ((chunk, width), (width, chunk))]
    grad_down, grad_up = run(
        ffn_place, places, (1,), ffn_held, outs, [pltpu.VMEM((width, chunk), F32)]
    )
    shapes = [
        (3, local_width, width),
        (local_width, width),
        (6, width),
        (chunk,),
        (2, local_width),
    ]
    grad_qkv, grad_out, grad_small, grad_up_bias, grad_qv_bias = run(
        attn_place,
        places,
        (1,),
        attn_held,
        [(shape, F32, whole(shape)) for shape in shapes],
        [pltpu.VMEM((width + EXTRA, width), F32)],
    )
    return (
        layer_output,
        input_grad,
        grad_qkv.transpose(0, 2, 1),
        grad_qv_bias,
        grad_out,
        grad_up,
        grad_up_bias,
        grad_down,
        grad_small,
    )


def solution(mesh):
    batch, heads = mesh.devices.shape
    mesh = Mesh(
        mesh.devices.reshape(batch // 8, 4, 2, heads), ("far", "near", "core", "head")
    )
    group = ("far", "near", "core")
    everyone = group + ("head",)
    in_specs = (
        P(group, None),
        P(group),
        P(None, None, "head"),
        P(None, "head"),
        P("head", None),
        P(),
        P(),
        P(),
        P(),
        P(),
        P(),
        P(),
        P(),
        P(),
        P(everyone, None),
    )
    out_specs = (
        P(everyone, None),
        P(everyone, None),
        P(None, None, "head"),
        P(None, "head"),
        P("head", None),
        P(None, "head"),
        P("head"),
        P("head", None),
        P(),
    )
    return jax.shard_map(
        per_device, mesh=mesh, in_specs=in_specs, out_specs=out_specs, check_vma=False
    )
```

```python
import functools
import math

import jax
import jax.numpy as jnp
from jax import lax
from jax.experimental import pallas as pl
from jax.experimental.pallas import tpu as pltpu
from jax.sharding import Mesh
from jax.sharding import PartitionSpec as P

HEAD_DIM = 64
SLOT = 512
LOW = jnp.bfloat16
F32 = jnp.float32
LOG2E = math.log2(math.e)
SCORE_SCALE = HEAD_DIM ** (-0.5) * LOG2E
SPARE_BYTES = 12 * 2**20
EXTRA = 64
LIGHT = 0.01
LANES = 128
CHAIN = []
TAIL_SLOPE = 0.36
TAIL = (
    0.14371304537508633,
    0.14177245466203425,
    0.1397192603907239,
    0.026549325413860486,
    0.18095403134327948,
    -0.1797647161697652,
    0.047056295581175855,
)


def swap(value, axis, bit):
    size = lax.axis_size(axis)
    return lax.ppermute(value, axis, [(i, i ^ bit) for i in range(size)])


def swap_core(value):
    return swap(value, "core", 1)


def dot(a, b):
    return jnp.dot(a, b, preferred_element_type=F32)


def dot_nt(a, b):
    return lax.dot_general(a, b, (((1,), (1,)), ((), ())), preferred_element_type=F32)


def dot_tn(a, b):
    return lax.dot_general(a, b, (((0,), (0,)), ((), ())), preferred_element_type=F32)


def whole(shape):
    return pl.BlockSpec(shape, lambda *args: (0,) * len(shape), pipeline_mode=pl.Buffered(1))


def run(
    kernel, places, grid, ins, outs, scratch=(), macs=0, after=(), alias=(), weight=8, chain=True
):
    moved = sum(a.size * a.dtype.itemsize for a, spec in ins)
    moved += sum(math.prod(shape) * jnp.dtype(kind).itemsize for shape, kind, spec in outs)
    after = list(after) + (CHAIN if chain else [])
    count, unread = len(ins), len(alias) + len(after)
    results = len(outs)
    flag = (8, 128)
    if chain:
        outs = outs + [(flag, F32, whole(flag))]

    def body(places, *refs):
        made = refs[count + unread :]
        if chain:

            @pl.when(pl.program_id(0) == 0)
            def _():
                made[results][...] = jnp.zeros(flag, F32)

        kernel(places, *refs[:count], *made[:results], *made[len(outs) :])

    held = pl.BlockSpec(memory_space=pl.ANY)
    room = SPARE_BYTES
    for shape, kind, spec in outs + [(a.shape, a.dtype, spec) for a, spec in ins]:
        if spec.block_shape is not None:
            block = math.prod(1 if n is None else n for n in spec.block_shape)
            copies = 2 if spec.pipeline_mode is None else 1
            room += copies * block * jnp.dtype(kind).itemsize
    for ref in scratch:
        if hasattr(ref, "shape") and ref.dtype in (LOW, F32):
            room += math.prod(ref.shape) * jnp.dtype(ref.dtype).itemsize
    made = pl.pallas_call(
        body,
        name=getattr(kernel, "func", kernel).__name__,
        grid_spec=pltpu.PrefetchScalarGridSpec(
            num_scalar_prefetch=1,
            grid=grid,
            in_specs=[spec for a, spec in ins] + [held] * unread,
            out_specs=[spec for shape, kind, spec in outs],
            scratch_shapes=list(scratch),
        ),
        out_shape=[jax.ShapeDtypeStruct(shape, kind) for shape, kind, spec in outs],
        input_output_aliases={1 + count + i: i for i in range(len(alias))},
        compiler_params=pltpu.CompilerParams(vmem_limit_bytes=room),
        cost_estimate=pl.CostEstimate(
            flops=int(2 * macs * weight), bytes_accessed=int(moved * weight), transcendentals=0
        ),
    )(places, *[a for a, spec in ins], *alias, *after)
    if chain:
        CHAIN[:] = made[results:]
    return made[:results]


def run_whole(
    kernel, places, ins, outs, scratch=(), macs=0, after=(), alias=(), weight=8, chain=True
):
    pairs = [a if isinstance(a, tuple) else (a, pltpu.VMEM) for a in ins]
    after = list(after) + (CHAIN if chain else [])
    count, unread, results = len(pairs), len(alias) + len(after), len(outs)
    if chain:
        outs = outs + [((8, 128), F32)]

    def body(places, *refs):
        made = refs[count + unread :]
        if chain:
            made[results][...] = jnp.zeros((8, 128), F32)
        kernel(places, *refs[:count], *made[:results], *made[len(outs) :])

    room = SPARE_BYTES
    for ref in scratch:
        if hasattr(ref, "shape") and ref.dtype in (LOW, F32):
            room += math.prod(ref.shape) * jnp.dtype(ref.dtype).itemsize
    spaces = [pltpu.SMEM] + [space for a, space in pairs]
    spaces += [pltpu.VMEM] * len(alias) + [pl.ANY] * len(after)
    made = pl.pallas_call(
        body,
        name=getattr(kernel, "func", kernel).__name__,
        in_specs=[pl.BlockSpec(memory_space=space) for space in spaces],
        out_specs=[pl.BlockSpec(memory_space=pltpu.VMEM)] * len(outs),
        scratch_shapes=list(scratch),
        out_shape=[jax.ShapeDtypeStruct(shape, kind) for shape, kind in outs],
        input_output_aliases={1 + count + i: i for i in range(len(alias))},
        compiler_params=pltpu.CompilerParams(vmem_limit_bytes=room),
        cost_estimate=pl.CostEstimate(
            flops=int(2 * macs * weight), bytes_accessed=0, transcendentals=0
        ),
    )(places, *[a for a, space in pairs], *alias, *after)
    if chain:
        CHAIN[:] = made[results:]
    return made[:results]


def each(count, size, body):
    def step(i, carry):
        body(pl.ds(pl.multiple_of(i * size, size), size))
        return carry

    lax.fori_loop(0, count // size, step, 0)


def tiles_of(count, size):
    return [slice(at, at + size) for at in range(0, count, size)]


def three_parts(values):
    parts, rest = [], values
    for _ in range(3):
        parts.append(rest.astype(LOW))
        rest = rest - parts[-1].astype(F32)
    return parts


def segment_rows(seg_row):
    shape = (16, seg_row.shape[1])
    place = lax.broadcasted_iota(jnp.int32, shape, 0)
    same = place - 1 == seg_row
    keys = jnp.where(same, 1.0, jnp.where((place >= 8) & (place < 11), 1.0, 0.0))
    queries = jnp.where(same | (place > 4), 0.0, -1e30)
    return keys.astype(LOW), queries.astype(LOW)


def attend_heads(tok, w_rows, bias, seg_row, qkv_ref, mix_ref, log_ref):
    width = w_rows.shape[0] // 3
    added = dot_tn(bias[:, : 2 * width], jnp.ones((bias.shape[0], tok.shape[0]), LOW))
    qkv = dot_nt(w_rows, tok)
    parts = (
        (qkv[:width] + added[:width]).astype(LOW),
        qkv[width : 2 * width].astype(LOW),
        (qkv[2 * width :] + added[width:]).astype(LOW),
    )
    for c in range(3):
        qkv_ref[c * width : (c + 1) * width] = parts[c]
    more_k, more_q = segment_rows(seg_row)
    for head in range(width // HEAD_DIM):
        q, k, v = (part[head * HEAD_DIM : (head + 1) * HEAD_DIM] for part in parts)
        scores = dot_tn(jnp.concatenate([k, more_k], 0), jnp.concatenate([q, more_q], 0))
        columns, tops, totals = [], [], []
        for tile in tiles_of(scores.shape[1], LANES):
            top = jnp.max(scores[:, tile], 0, keepdims=True)
            total, column = 0.0, []
            for rows in tiles_of(scores.shape[0], 64):
                exponent = jnp.exp2((scores[rows, tile] - top) * SCORE_SCALE)
                total = total + jnp.sum(exponent, 0, keepdims=True)
                column.append(exponent.astype(LOW))
            columns.append(jnp.concatenate(column, 0))
            tops.append(top)
            totals.append(total)
        total = jnp.concatenate(totals, 1)
        mixed = dot(v, jnp.concatenate(columns, 1)) * (1.0 / total)
        mix_ref[head * HEAD_DIM : (head + 1) * HEAD_DIM] = mixed.astype(LOW)
        top = jnp.concatenate(tops, 1)
        log_ref[head : head + 1] = top + jnp.log2(total) * (1.0 / SCORE_SCALE)


def own_attention(
    places, tok, w, bias, seg_row, qkv_ref, mix_ref, log_ref, w_qkv, w_out
):
    count = qkv_ref.shape[1]
    w_qkv[0] = w[:count]
    w_out[0] = w[count:]
    attend_heads(
        tok[...], w[:count], bias[...], seg_row[...], qkv_ref.at[0], mix_ref.at[0], log_ref.at[0]
    )


def far_attention(
    d, order, places, tok, pair, rest, pair_far, rest_far, hop, seg_row,
    qkv_ref, mix_ref, log_ref, w_qkv, w_out, w_ref,
):
    first, second = order
    rows, count = pair.shape[1], qkv_ref.shape[1]
    me = places[0] * 2 + places[1]
    for other, held in enumerate(((pair, rest), (pair_far, rest_far))):
        for two, block in enumerate(held):
            for one in range(2):
                owner = me ^ (other + 2 * first * one + 2 * second * two)
                w_ref[pl.ds(pl.multiple_of(owner * rows, rows), rows)] = block[one]
    w_qkv[d] = w_ref[:count]
    w_out[d] = w_ref[count:]
    attend_heads(
        tok[...],
        w_ref[:count],
        hop[rows:],
        seg_row[...],
        qkv_ref.at[d],
        mix_ref.at[d],
        log_ref.at[d],
    )


def copy_rows(places, *refs):
    count = len(refs) // 2
    for rows, out in zip(refs[:count], refs[count:]):
        out[...] = rows[...]


def pair_rows(places, first, second, out):
    out[0] = first[: out.shape[1]]
    out[1] = second[: out.shape[1]]


def norm_stats(v):
    centred = v - jnp.mean(v, -1, keepdims=True)
    inv = lax.rsqrt(jnp.mean(centred * centred, -1, keepdims=True) + 1e-05)
    return centred * inv, inv


def norm_back(upstream, unit, inv, gain):
    scaled = upstream * gain
    inner = jnp.mean(scaled * unit, -1, keepdims=True)
    return inv * (scaled - jnp.mean(scaled, -1, keepdims=True) - unit * inner)


def gelu_both(pre):
    power = jnp.exp2(pre * pre * (-0.5 * LOG2E))
    base = 1.0 + TAIL_SLOPE * jnp.abs(pre)
    t = pl.reciprocal(base, approx=True)
    tail = TAIL[6] * t + TAIL[5]
    for c in TAIL[4::-1]:
        tail = tail * t + c
    tail = tail * (t * power)
    cumul = jnp.where(pre < 0.0, tail, 1.0 - tail)
    return (pre * cumul).astype(LOW), cumul + pre * (power * 0.3989422804014327)


def share(core, wide, mine, other):
    half = wide.shape[1] // 2
    left, right = wide[:, :half], wide[:, half:]
    mine[...] = jnp.where(core == 0, left, right)
    other[...] = jnp.where(core == 0, right, left)


def feed_forward(
    places, tok, mix, w_out, b_out, gain1, shift1, b_down, gain2, shift2, w_up, b_up, w_down, cot,
    send, own, ends, slope, unit1, inv1, res2, out, small, tok_send,
    hidden, low, acts, total,
):
    heads, width, half = mix.shape[0], low.shape[1], send.shape[2]
    chunk = 2 * half
    core, z = places[1], places[2]
    b_out, gain1, shift1, b_down, gain2, shift2 = (
        ref[...].reshape(1, -1) for ref in (b_out, gain1, shift1, b_down, gain2, shift2)
    )
    tok_send[...] = jnp.where(core == 0, tok[:, half:], tok[:, :half])
    total[...] = dot_tn(mix[...].reshape(width, low.shape[0]), w_out[...].reshape(width, width))

    def first_norm(rows):
        unit, inv = norm_stats(tok[rows].astype(F32) + (total[rows] + b_out))
        unit1[rows] = unit
        inv1[rows] = inv
        one = unit * gain1 + shift1
        hidden[rows] = one
        one_low = one.astype(LOW)
        low[rows] = one_low
        ends[0, rows] = one_low[:, :half]
        ends[1, rows] = one_low[:, half:]

    each(low.shape[0], 64, first_norm)

    def one_unit(h, carry):
        start = pl.multiple_of(h * chunk, chunk)
        for at in tiles_of(chunk, chunk):
            wide = pl.ds(start, chunk)
            pre = dot(low[...], w_up[:, wide])
            for rows in tiles_of(pre.shape[0], 16):
                act, tilt = gelu_both(pre[rows] + b_up[h, :, at])
                slope[h, rows, at] = tilt.astype(LOW)
                acts[rows, wide] = act
        left = acts[:, pl.ds(start, half)]
        right = acts[:, pl.ds(pl.multiple_of(start + half, 128), half)]
        own[z ^ h] = jnp.where(core == 0, left, right)
        send[z ^ h] = jnp.where(core == 0, right, left)
        return carry

    lax.fori_loop(0, heads, one_unit, 0)
    total[...] = dot(acts[...], w_down[...])
    small[...] = jnp.zeros_like(small)

    def second_norm(rows):
        unit, inv = norm_stats(hidden[rows] + (total[rows] + b_down))
        out[rows] = (unit * gain2 + shift2).astype(LOW)
        upstream = cot[rows].astype(F32)
        grad = norm_back(upstream, unit, inv, gain2)
        res2[rows] = grad
        grad_low = grad.astype(LOW)
        ends[2, rows] = grad_low[:, :half]
        ends[3, rows] = grad_low[:, half:]
        for i, term in enumerate((grad_low.astype(F32), upstream * unit, upstream)):
            small[i : i + 1] += jnp.sum(term, 0, keepdims=True)

    each(low.shape[0], 64, second_norm)


def inner_back(places, ends, w_down, slope, send, own, bias, inners):
    heads, _, chunk = slope.shape
    core, z = places[1], places[2]
    branch = jnp.concatenate([ends[2], ends[3]], 1)
    for h in range(heads):
        for at in tiles_of(chunk, 256):
            grad_act = dot_nt(branch, w_down[h * chunk + at.start : h * chunk + at.stop])
            total = 0.0
            for rows in tiles_of(grad_act.shape[0], 32):
                inner = (grad_act[rows] * slope[h, rows, at].astype(F32)).astype(LOW)
                inners[rows, at] = inner
                total = total + jnp.sum(inner.astype(F32), 0, keepdims=True)
            bias[h, :, at] = total
        share(core, inners, own.at[z ^ h], send.at[z ^ h])


def hidden_back(places, own, sent, w_up, res2, unit1, inv1, gain1, send, res1, low, small):
    heads, count, half = own.shape
    core, z = places[1], places[2]
    sides = []
    for h in range(heads):
        mine, other = own[z ^ h], sent[z ^ h]
        sides += [jnp.where(core == 0, mine, other), jnp.where(core == 0, other, mine)]
    product = dot_nt(jnp.concatenate(sides, 1), w_up[...])
    gain = gain1[...].reshape(1, -1)
    sums = [0.0] * 3
    for rows in tiles_of(count, 32):
        grad, unit = product[rows] + res2[rows], unit1[rows]
        result = norm_back(grad, unit, inv1[rows], gain)
        res1[rows] = result
        result_low = result.astype(LOW)
        low[rows] = result_low
        send[rows] = jnp.where(core == 0, result_low[:, half:], result_low[:, :half])
        for i, term in enumerate((result_low.astype(F32), grad * unit, grad)):
            sums[i] = sums[i] + jnp.sum(term, 0, keepdims=True)
    for i in range(3):
        small[i : i + 1] = sums[i]


def shard_back(qkv, w_out, grad, log_ref, more_k, more_q, rows_ref, bias_ref):
    width = qkv.shape[0] // 3
    grad_mixed = dot_nt(w_out[...], grad[...]).astype(LOW)
    scale = HEAD_DIM ** (-0.5)
    for head in range(width // HEAD_DIM):
        places_of = [c * width + head * HEAD_DIM for c in range(3)]
        q, k, v = (qkv[at : at + HEAD_DIM] for at in places_of)
        g = grad_mixed[head * HEAD_DIM : (head + 1) * HEAD_DIM]
        logs = jnp.concatenate(three_parts(-log_ref[head : head + 1]), 0)
        with_logs = jnp.concatenate([more_q[:8], logs, more_q[11:]], 0)
        scores = dot_tn(jnp.concatenate([k, more_k], 0), jnp.concatenate([q, with_logs], 0))
        grad_probs = dot_tn(v, g)
        attends, grads = [], []
        for tile in tiles_of(scores.shape[1], LANES):
            inner, kept, lows, parts = 0.0, [], [], []
            tall = tiles_of(scores.shape[0], 64)
            for down in tall:
                attend = jnp.exp2(scores[down, tile] * SCORE_SCALE)
                inner = inner + jnp.sum(attend * grad_probs[down, tile], 0, keepdims=True)
                kept.append(attend)
                lows.append(attend.astype(LOW))
            for down, attend in zip(tall, kept):
                parts.append((attend * (grad_probs[down, tile] - inner)).astype(LOW))
            attends.append(jnp.concatenate(lows, 0))
            grads.append(jnp.concatenate(parts, 0))
        attend_low = jnp.concatenate(attends, 1)
        grad_scores = jnp.concatenate(grads, 1)
        grad_v = dot_nt(g, attend_low)
        grad_q = dot(k, grad_scores) * scale
        grad_k = dot_nt(q, grad_scores) * scale
        for at, value in zip(places_of, (grad_q, grad_k, grad_v)):
            rows_ref[at : at + HEAD_DIM] = value.astype(LOW)
    ones = jnp.ones((8, rows_ref.shape[1]), LOW)
    bias_ref[...] = dot_nt(ones, rows_ref[...])


def attention_back(places, qkv, w_out, grad, log_ref, seg_row, rows_ref, bias_ref):
    more_k, more_q = segment_rows(seg_row[...])

    def shard(d, carry):
        refs = (ref.at[d] for ref in (rows_ref, bias_ref))
        shard_back(qkv.at[d], w_out.at[d], grad, log_ref.at[d], more_k, more_q, *refs)
        return carry

    lax.fori_loop(0, qkv.shape[0], shard, 0)


def split_rows(value, high, send, keep):
    rows = value.shape[0] // 2
    low = value.astype(LOW)
    send[...] = jnp.where(high, low[:rows], low[rows:])
    keep[...] = jnp.where(high, low[rows:], low[:rows])


def is_high(places, bit):
    return (places[0] & bit) != 0


def unit_products(which, units, units_far, ends, ends_far, both):
    half, count = ends.shape[2], ends.shape[1]
    for side in range(2):
        rows = slice(side * half, (side + 1) * half)
        both[rows, :count] = ends[2 * which + side].T
        both[rows, count:] = ends_far[2 * which + side].T
    for d in range(0, units.shape[0], 2):
        left, right = (jnp.concatenate([units[d + i], units_far[d + i]], 0) for i in range(2))
        yield d, dot(both[...], jnp.concatenate([left, right], 1))


def down_grad(places, units, units_far, ends, ends_far, send, keep, both):
    half = send.shape[2]
    for d, total in unit_products(1, units, units_far, ends, ends_far, both):
        keep[d // 2] = total[:, :half].astype(LOW)
        send[d // 2] = total[:, half:].astype(LOW)


def up_grad(places, units, units_far, ends, ends_far, send_x, keep_x, send_y, keep_y, both):
    half = send_x.shape[2]
    for d, total in unit_products(0, units, units_far, ends, ends_far, both):
        for i in range(2):
            part = total[:, i * half : (i + 1) * half]
            split_rows(part[:half], is_high(places, 1), send_x.at[d + i], keep_x.at[d + i])
            split_rows(part[half:], is_high(places, 2), send_y.at[d + i], keep_y.at[d + i])


def split_at(value, high, send, keep, start):
    rows = value.shape[0] // 2
    low = value.astype(LOW)
    send[start : start + rows] = jnp.where(high, low[:rows], low[rows:])
    keep[start : start + rows] = jnp.where(high, low[rows:], low[:rows])


def first_stage(
    places, d_keep, d_came, x_keep, x_came, y_keep, y_came, send_x, keep_x, send_y, keep_y
):
    half = d_keep.shape[2]
    at = 0
    for i in range(d_keep.shape[0]):
        total = d_keep[i].astype(F32) + d_came[i].astype(F32)
        split_at(total[:half], is_high(places, 1), send_x, keep_x, at)
        split_at(total[half:], is_high(places, 2), send_y, keep_y, at)
        at += half // 2
    for d in range(x_keep.shape[0]):
        upper = x_keep[d].astype(F32) + x_came[d].astype(F32)
        lower = y_keep[d].astype(F32) + y_came[d].astype(F32)
        split_at(upper, is_high(places, 2), send_y, keep_y, at)
        split_at(lower, is_high(places, 1), send_x, keep_x, at)
        at += upper.shape[0] // 2


def second_stage(
    places, x_keep, x_came, y_keep, y_came, send_x, keep_x, send_y, keep_y, send_z, keep_z
):
    rows = send_x.shape[1]
    at = 0
    for i in range(send_x.shape[0]):
        piece = slice(at, at + 2 * rows)
        upper = x_keep[piece].astype(F32) + x_came[piece].astype(F32)
        lower = y_keep[piece].astype(F32) + y_came[piece].astype(F32)
        split_rows(upper, is_high(places, 2), send_y.at[i], keep_y.at[i])
        split_rows(lower, is_high(places, 1), send_x.at[i], keep_x.at[i])
        at += 2 * rows
    for d in range(2 * send_z.shape[0]):
        piece = slice(at, at + rows)
        out = (send_z if d % 2 else keep_z).at[d // 2]
        out[:rows] = (y_keep[piece].astype(F32) + y_came[piece].astype(F32)).astype(LOW)
        out[rows:] = (x_keep[piece].astype(F32) + x_came[piece].astype(F32)).astype(LOW)
        at += rows


def third_stage(places, x_keep, x_came, y_keep, y_came, z_keep, z_came, mine, other):
    rows = x_keep.shape[1]
    for i, out in enumerate((mine, other)):
        out[:rows] = (y_keep[i].astype(F32) + y_came[i].astype(F32)).astype(LOW)
        out[rows : 2 * rows] = (x_keep[i].astype(F32) + x_came[i].astype(F32)).astype(LOW)
        out[2 * rows :] = (z_keep[i].astype(F32) + z_came[i].astype(F32)).astype(LOW)


def attn_grad(
    places, rows, rows_far, tok, tok_far, mix, mix_far, grad, grad_far,
    small_one, small_two, up_bias, qkv_bias, send_x, keep_x, send_y, keep_y,
):
    width = mix.shape[1]
    half = tok_far.shape[1]
    core, z = places[1], places[2]

    def both(near, far):
        mine = jnp.where(core == 0, near[:, :half], near[:, half:])
        return jnp.concatenate([mine, far[...]], 0)

    tok_both, grad_both = both(tok, tok_far), both(grad, grad_far)
    for d in range(rows.shape[0]):
        qkv = dot(jnp.concatenate([rows[d], rows_far[d]], 1), tok_both)
        out = dot(jnp.concatenate([mix[d], mix_far[d]], 1), grad_both)
        lines = []
        for held in (small_one, small_two):
            for i in range(3):
                lines += [held[i : i + 1, :half], held[i : i + 1, half:]]
        line, bias = up_bias[z ^ d], qkv_bias[d]
        lines += [line[:, :half], line[:, half:]]
        lines.append(jnp.concatenate([bias[0:1, :width], bias[0:1, 2 * width :]], 1))
        lines.append(jnp.zeros((EXTRA - len(lines), half), F32))
        total = jnp.concatenate([qkv, out] + lines, 0)
        split_rows(total[:half], is_high(places, 1), send_x.at[d], keep_x.at[d])
        split_rows(total[half:], is_high(places, 2), send_y.at[d], keep_y.at[d])


def add_split(bits, places, *refs):
    for i, bit in enumerate(bits):
        keep, came = refs[2 * i : 2 * i + 2]
        send, left = refs[2 * (len(bits) + i) : 2 * (len(bits) + i) + 2]
        for d in range(keep.shape[0]):
            total = keep[d].astype(F32) + came[d].astype(F32)
            split_rows(total, is_high(places, bit), send.at[d], left.at[d])


def add_parts(places, keep_a, came_a, keep_b, came_b, send, keep):
    rows = keep_a.shape[1]
    for d in range(keep_a.shape[0]):
        out = (send if d % 2 else keep).at[d // 2]
        out[:rows] = (keep_a[d].astype(F32) + came_a[d].astype(F32)).astype(LOW)
        out[rows:] = (keep_b[d].astype(F32) + came_b[d].astype(F32)).astype(LOW)


def add_pair(places, keep, came, *outs):
    for i, out in enumerate(outs):
        out[...] = (keep[i].astype(F32) + came[i].astype(F32)).astype(LOW)


def add_two(places, keep, came, out):
    out[...] = (keep[...].astype(F32) + came[...].astype(F32)).astype(LOW)


def input_sum(places, rows, w, res1, out):
    heads, count, tokens = rows.shape
    total = dot_tn(rows[...].reshape(heads * count, tokens), w[...].reshape(heads * count, -1))
    out[...] = res1[...] + total


def place_pieces(places, held, full, layouts):
    near, core = places[0], places[1]
    width = held[0].shape[1]
    for off in range(4):
        chip = near ^ off
        mine, other = held[off][...], held[4 + off][...]
        sides = (jnp.where(core == 0, mine, other), jnp.where(core == 0, other, mine))
        for at, rows, start, outer in layouts:
            low_bit, high_bit = chip & 1, chip >> 1
            order = 2 * low_bit + high_bit if outer == 1 else 2 * high_bit + low_bit
            to = pl.multiple_of(start + order * rows, 16)
            for side in range(2):
                full[pl.ds(to, rows), side * width : (side + 1) * width] = sides[side][
                    at : at + rows
                ].astype(F32)


def ffn_place(places, *refs):
    held = [ref.at[off] for ref in refs[:2] for off in range(4)]
    down, up, full = refs[2:]
    rows = held[0].shape[0] // 4
    half = 4 * rows
    place_pieces(places, held, full, [(0, rows, 0, 1), (rows, rows, half, 2)])
    down[...] = full[...].T
    place_pieces(places, held, up, [(2 * rows, rows, 0, 1), (3 * rows, rows, half, 2)])


def collect(places, *refs):
    for off in range(4):
        refs[4][off] = refs[off][...]


def attn_place(places, *refs):
    held = [ref.at[off] for ref in refs[:2] for off in range(4)]
    qkv, w_out, small, up_bias, qv_bias, full = refs[2:]
    width = held[0].shape[1]
    count = w_out.shape[0]
    rows = count // 2
    more = held[0].shape[0] - rows
    place_pieces(places, held, full, [(0, rows, 0, 1), (rows, more, 4 * rows, 2)])
    for c in range(3):
        qkv[c] = full[c * count : (c + 1) * count]
    w_out[...] = full[3 * count : 4 * count]
    at = 4 * count
    lines = full[at : at + 16, :width] + full[at : at + 16, width:]
    for i in range(6):
        small[i : i + 1, :width] = lines[2 * i : 2 * i + 1]
        small[i : i + 1, width:] = lines[2 * i + 1 : 2 * i + 2]
    up_bias[...] = jnp.concatenate([lines[12:13], lines[13:14]], 1).reshape(2 * width)
    qv_bias[0:1] = lines[14:15, :count]
    qv_bias[1:2] = lines[14:15, count : 2 * count]


def bias_parts(values):
    rows, rest = [], values
    for _ in range(3):
        rows.append(lax.reduce_precision(rest, 8, 7))
        rest = rest - rows[-1]
    return jnp.stack(rows).astype(LOW)


def gather_back(piece):
    return [piece] + [swap(piece, "near", off) for off in range(1, 4)]


def per_device(
    tokens,
    segment_ids,
    w_qkv,
    b_qv,
    w_out,
    b_out,
    ln1_gain,
    ln1_bias,
    w_up,
    b_up,
    w_down,
    b_down,
    ln2_gain,
    ln2_bias,
    cotangent,
):
    CHAIN.clear()
    width = tokens.shape[1]
    own_rows = cotangent.shape[0]
    local_width = w_qkv.shape[2]
    heads = lax.axis_size("head")
    z = lax.axis_index("head")
    core = lax.axis_index("core")
    near = lax.axis_index("near")
    hidden_units = w_up.shape[1]
    chunk = hidden_units // heads
    half = width // 2
    rows3 = 3 * local_width
    places = jnp.stack([near, core, z]).astype(jnp.int32)

    shard = jnp.concatenate([w_qkv.transpose(0, 2, 1).reshape(rows3, width), w_out], 0)
    piece_rows = shard.shape[0] // 8
    bias = jnp.pad(bias_parts(b_qv.reshape(-1)), ((0, 13), (0, width - 2 * local_width)))
    piece = lax.dynamic_slice_in_dim(shard, (near * 2 + core) * piece_rows, piece_rows, 0)
    piece = jnp.concatenate([piece, bias], 0)
    first_hop = [swap(piece, "head", d) for d in range(1, heads)]

    seg = lax.dynamic_slice_in_dim(segment_ids, z * own_rows, own_rows, 0)
    tok_own = lax.dynamic_slice_in_dim(tokens, z * own_rows, own_rows, 0)
    attend_outs = [
        ((heads, rows3, own_rows), LOW),
        ((heads, local_width, own_rows), LOW),
        ((heads, 8, own_rows), F32),
        ((heads, rows3, width), LOW),
        ((heads, local_width, width), LOW),
    ]
    macs = rows3 * width * own_rows + 6 * own_rows * own_rows * 256
    orders = [(1, 2) if d % 2 else (2, 1) for d in range(heads)]
    nexts = [swap(first_hop[0], "near", orders[1][0])]

    def pair_up(d, after):
        (pair,) = run_whole(
            pair_rows, places, [first_hop[d - 1], nexts[d - 1]],
            [((2, piece_rows, width), LOW)], after=after, chain=False,
        )
        return pair

    pairs = [pair_up(1, [])]
    ins = [tok_own, shard, bias, seg[None]]
    made = run_whole(
        own_attention, places, ins, attend_outs, macs=macs, after=pairs, chain=False
    )
    late = run_whole(
        copy_rows, places, first_hop[1:], [(piece.shape, LOW)] * 2, after=[made[2]], chain=False
    )
    nexts += [swap(late[d - 2], "near", orders[d][0]) for d in range(2, heads)]
    pairs += [pair_up(d, nexts[1:] + [made[2]]) for d in range(2, heads)]
    rests = [swap(pairs[d - 1], "near", orders[d][1]) for d in range(1, heads)]
    for d in range(1, heads):
        pair, rest = pairs[d - 1], rests[d - 1]
        sent = rest
        if d == heads - 1:
            (sent,) = run_whole(
                copy_rows, places, [rest], [(rest.shape, LOW)], after=[second_log], chain=False
            )
        ins = [tok_own, pair, rest, swap_core(pair), swap_core(sent), first_hop[d - 1], seg[None]]
        made = run_whole(
            functools.partial(far_attention, d, orders[d]), places, ins, attend_outs,
            [pltpu.VMEM(shard.shape, LOW)], macs, alias=made, chain=False, weight=100,
        )
        if d == 1:
            second_log = made[2]
    qkvs, mixes, logs, w_qkvs, w_outs = made

    mixes_far = swap_core(mixes)

    square = (own_rows, width)
    tiles = (heads, own_rows, half)
    ins = [
        tok_own, mixes, w_outs, b_out, ln1_gain, ln1_bias, b_down, ln2_gain, ln2_bias,
        w_up, b_up.reshape(heads, 1, chunk), w_down, cotangent,
    ]
    outs = [
        (tiles, LOW),
        (tiles, LOW),
        ((4, own_rows, half), LOW),
        ((heads, own_rows, chunk), LOW),
        (square, F32),
        ((own_rows, 1), F32),
        (square, F32),
        (square, LOW),
        ((8, width), F32),
        ((own_rows, half), LOW),
    ]
    scratch = [
        pltpu.VMEM(square, F32),
        pltpu.VMEM(square, LOW),
        pltpu.VMEM((own_rows, hidden_units), LOW),
        pltpu.VMEM(square, F32),
    ]
    ffn_macs = 2 * own_rows * width * hidden_units
    (
        act_send, act_own, ends, slope, unit1, inv1, res2, layer_output, small_two, tok_send,
    ) = run_whole(feed_forward, places, ins, outs, scratch, ffn_macs)
    tok_far = swap_core(tok_send)
    act_far = swap_core(act_send)
    ends_far = swap_core(ends)

    outs = [(tiles, LOW), (tiles, LOW), ((heads, 1, chunk), F32)]
    scratch = [pltpu.VMEM((own_rows, chunk), LOW)]
    inner_send, inner_own, up_bias = run_whole(
        inner_back, places, [ends, w_down, slope], outs, scratch, ffn_macs // 2, [mixes_far]
    )
    inner_far = swap_core(inner_send)


    both = [pltpu.VMEM((width, 2 * own_rows), LOW)]
    outs = [((heads // 2, width, half), LOW)] * 2
    ins = [act_own, act_far, ends, ends_far]
    d_send, d_keep = run_whole(down_grad, places, ins, outs, both, ffn_macs // 2)
    d_came = swap(d_send, "head", 1)
    outs = [((heads, half // 2, half), LOW)] * 4
    ins = [inner_own, inner_far, ends, ends_far]
    made = run_whole(up_grad, places, ins, outs, both, ffn_macs // 2, weight=LIGHT)
    u_held = (made[1], swap(made[0], "near", 1), made[3], swap(made[2], "near", 2))

    outs = [((own_rows, half), LOW), (square, F32), (square, LOW), ((8, width), F32)]
    ins = [inner_own, inner_send, w_up, res2, unit1, inv1, ln1_gain]
    grad_send, res1, grad_attended, small_one = run_whole(
        hidden_back, places, ins, outs, macs=ffn_macs // 2, weight=LIGHT
    )
    grad_far = swap_core(grad_send)

    def second(x_keep, x_came, y_keep, y_came, macs=0):
        arrays = (x_keep, x_came, y_keep, y_came)
        shapes = [(heads, a.shape[1] // 2, half) for a in (x_keep, x_keep, y_keep, y_keep)]
        outs = [(shape, LOW) for shape in shapes]
        kernel = functools.partial(add_split, (2, 1))
        return run_whole(kernel, places, arrays, outs, macs=macs)

    def third(x_keep, x_came, y_keep, y_came):
        arrays = (x_keep, x_came, y_keep, y_came)
        shape = (heads // 2, x_keep.shape[1] + y_keep.shape[1], half)
        send, keep = run_whole(add_parts, places, arrays, [(shape, LOW)] * 2)
        return keep, swap(send, "head", 1)

    def fourth(keep, came):
        shape = keep.shape[1:]
        mine, other = run_whole(add_pair, places, [keep, came], [(shape, LOW)] * 2)
        return mine, swap(other, "head", 2)

    def fifth(mine, came):
        (total,) = run_whole(add_two, places, [mine, came], [(mine.shape, LOW)])
        bit = 1
        while bit < lax.axis_size("far"):
            total = (total.astype(F32) + swap(total, "far", bit).astype(F32)).astype(LOW)
            bit *= 2
        return total

    def cross_back(made):
        x_send, x_keep, y_send, y_keep = made
        return x_keep, swap(x_send, "near", 1), y_keep, swap(y_send, "near", 2)

    def cross(made, flip):
        x_send, x_keep, y_send, y_keep = made
        x_bit, y_bit = (2, 1) if flip else (1, 2)
        return x_keep, swap(x_send, "near", x_bit), y_keep, swap(y_send, "near", y_bit)

    outs = [((heads, rows3, own_rows), LOW), ((heads, 8, rows3), F32)]
    ins = [qkvs, w_outs, grad_attended, logs, seg[None]]
    rows, qkv_bias = run_whole(attention_back, places, ins, outs)
    rows_far = swap_core(rows)

    outs = [(square, F32, whole(square))]
    ins = [(a, whole(a.shape)) for a in (rows, w_qkvs, res1)]
    (input_grad,) = run(input_sum, places, (1,), ins, outs, weight=LIGHT)
    outs = [((width, half), LOW)] * 4
    ins = [d_keep, d_came, *u_held]
    ffn_held = cross(run_whole(first_stage, places, ins, outs, macs=ffn_macs), False)
    ins = [
        rows, rows_far, tok_own, tok_far, mixes, mixes_far, grad_attended, grad_far,
        small_one, small_two, up_bias, qkv_bias,
    ]
    outs = [
        ((heads, r, half), LOW) for r in (half // 2, (half + EXTRA) // 2) for _ in range(2)
    ]
    made = run_whole(attn_grad, places, ins, outs)
    attn_held = cross(made, False)

    outs = [((heads // 2, half // 4, half), LOW)] * 4 + [((heads // 2, half // 2, half), LOW)] * 2
    made = run_whole(second_stage, places, list(ffn_held), outs, macs=ffn_macs)
    ffn_held = cross_back(made[:4]) + (made[5], swap(made[4], "head", 1))
    attn_held = cross(second(*attn_held), True)
    outs = [((half, half), LOW)] * 2
    mine, other = run_whole(third_stage, places, list(ffn_held), outs, macs=ffn_macs)
    ffn_held = mine, swap(other, "head", 2)
    attn_held = third(*attn_held)
    ffn_held = gather_back(fifth(*ffn_held))
    attn_held = fourth(*attn_held)
    attn_held = gather_back(fifth(*attn_held))

    def both_cores(held, macs=0):
        shape = (heads,) + held[0].shape
        (pieces,) = run_whole(collect, places, held, [(shape, LOW)], macs=macs)
        return [(a, whole(shape)) for a in (pieces, swap_core(pieces))]

    ffn_held = both_cores(ffn_held)
    attn_held = both_cores(attn_held, ffn_macs)
    outs = [(shape, F32, whole(shape)) for shape in ((chunk, width), (width, chunk))]
    grad_down, grad_up = run(
        ffn_place, places, (1,), ffn_held, outs, [pltpu.VMEM((width, chunk), F32)]
    )
    shapes = [
        (3, local_width, width),
        (local_width, width),
        (6, width),
        (chunk,),
        (2, local_width),
    ]
    grad_qkv, grad_out, grad_small, grad_up_bias, grad_qv_bias = run(
        attn_place,
        places,
        (1,),
        attn_held,
        [(shape, F32, whole(shape)) for shape in shapes],
        [pltpu.VMEM((width + EXTRA, width), F32)],
    )
    return (
        layer_output,
        input_grad,
        grad_qkv.transpose(0, 2, 1),
        grad_qv_bias,
        grad_out,
        grad_up,
        grad_up_bias,
        grad_down,
        grad_small,
    )


def solution(mesh):
    batch, heads = mesh.devices.shape
    mesh = Mesh(
        mesh.devices.reshape(batch // 8, 4, 2, heads), ("far", "near", "core", "head")
    )
    group = ("far", "near", "core")
    everyone = group + ("head",)
    in_specs = (
        P(group, None),
        P(group),
        P(None, None, "head"),
        P(None, "head"),
        P("head", None),
        P(),
        P(),
        P(),
        P(),
        P(),
        P(),
        P(),
        P(),
        P(),
        P(everyone, None),
    )
    out_specs = (
        P(everyone, None),
        P(everyone, None),
        P(None, None, "head"),
        P(None, "head"),
        P("head", None),
        P(None, "head"),
        P("head"),
        P("head", None),
        P(),
    )
    return jax.shard_map(
        per_device, mesh=mesh, in_specs=in_specs, out_specs=out_specs, check_vma=False
    )
```
